32 devices in a mesh: groups: 2 (over x), shard: 8 (over z, y), mp: 2 (over core).
Axes of the slice: x: 2, y: 2, z: 4, core: 2. Of those that a mesh axis runs over, the one named last changes fastest.
Arguments:
- image_tokens: bfloat16 [4096, 16, 512], P(('groups', 'shard'), None, 'mp'), parts along dimension 0, may hold values from -8 to 8
- pair_owner: int32 [1024, 2], P(('groups', 'shard')), parts along dimension 0, may hold values from 0 to 7, all different within a row; in each aligned block of 64 rows (0 to 63, 64 to 127, ...) at most 32 rows name the same one
- pair_slot: int32 [1024, 2], P(('groups', 'shard')), parts along dimension 0, may hold values from 0 to 255
- gain_attn: float32 [512], replicated, may hold values from 0.1 to 1.9
- w_qk: bfloat16 [512, 512], P(None, 'mp'), may hold values from -0.25 to 0.25
- w_value: bfloat16 [512, 512], P(None, 'mp'), may hold values from -0.25 to 0.25
- logit_scale: float32 [8], P('mp'), may hold values from 0.5 to 30
- w_out: bfloat16 [512, 512], P('mp'), may hold values from -0.25 to 0.25
- gain_mlp: float32 [512], replicated, may hold values from 0.1 to 1.9
- w_in: bfloat16 [512, 2048], P(None, 'mp'), may hold values from -0.25 to 0.25
- bias_in: float32 [2048], P('mp'), may hold values from -3 to 3
- w_back: bfloat16 [2048, 512], P('mp'), may hold values from -0.125 to 0.125
Outputs:
- pair_features: bfloat16 [1024, 512], P(('groups', 'shard')), parts along dimension 0
The draws below stay inside these ranges and needn't reach their ends.
There are 2 independent parts, one for each index of `groups`. The reference program is written for one: setup_inputs(seed, part) draws one part's arguments, and reference() takes and returns one part's arrays. A program takes and returns all parts, laid end to end along the dimension named above; an argument that names none is the same for every part. Nothing has to cross between parts.
Inputs may be any that keep to these rules, and one draw needn't show every extreme that they name: `pair_owner`: the two images of a pair have different owners. Among the 128 images named by the pairs of one index of shard, at most 32 have the same owner; some owner is named exactly 32 times.
All inputs are finite; a program needn't handle non-finite values.
Results may differ from the reference program's by a relative error of at most 0.0095.
Values may be sent and summed in bfloat16 or wider, within the bound.
No kernel may reach another device: no remote copies, remote signals or barrier semaphores. Data moves between devices by JAX's collectives and lax.ppermute only.
A program may use at most 64 MiB of HBM per device.

```python
import math
import jax
import jax.numpy as jnp
import numpy as np
from jax import lax

D = 512
HEADS = 8
FF = 2048
TOK = 16
IMG_DEV = 256
PAIR_DEV = 64
CAP = 32
IMAGES = 2048
PAIRS = 512
N_SHARD = 8


def draw_image_tokens(key, part):
    key = jax.random.fold_in(key, 11)
    noise_key = jax.random.fold_in(key, 0)
    values = jax.random.normal(noise_key, (IMAGES, TOK, D), jnp.float32)
    return jnp.clip(values, -6.0, 6.0).astype(jnp.bfloat16)


def draw_logit_scale(key, part):
    key = jax.random.fold_in(key, 23)
    return jnp.exp(jax.random.uniform(key, (HEADS,), jnp.float32, jnp.log(0.5), jnp.log(4.0)))


def touch_ends(array, stream_key, low, largest):
    longest = array.shape.index(max(array.shape))
    spots = []
    for shift in (0, 1):
        where = [jax.random.randint(jax.random.fold_in(stream_key, axis), (), 0, length) for axis, length in enumerate(array.shape)]
        where[longest] = (where[longest] + shift) % array.shape[longest]
        spots.append(tuple(where))
    return array.at[spots[0]].set(low).at[spots[1]].set(largest)


def levels(key, shape, cuts, least, high):
    loudness = 1.0
    for dim, parts in cuts:
        steps = jax.random.uniform(jax.random.fold_in(jax.random.fold_in(key, 6), dim), (parts,), jnp.float32, least / len(cuts), high / len(cuts))
        loudness = loudness * jnp.repeat(jnp.exp(steps), shape[dim] // parts).reshape((-1,) + (1,) * (len(shape) - 1 - dim))
    return loudness


def shared_out(own_key, own, number, rows, number_of, top, reach, lean):
    order = jax.random.permutation(own_key, number_of)
    packed, usual = load_shares(number_of, rows * top, reach, lean, True), load_shares(number_of, rows * top, reach, lean, False)
    places = jnp.arange(number_of)

    def named(tallies, rotation):
        used = int((tallies > 0).sum())
        fixed = max(1, used // 4)
        passed = fixed + (places - fixed + rotation * (used - fixed)) % max(1, number_of - fixed)
        return jnp.zeros((number_of,), jnp.int32).at[order[jnp.where(places < fixed, places, passed)]].set(jnp.asarray(tallies, jnp.int32))

    tallies = jnp.where(number % 4 == 0, named(packed, number // 4), named(usual, number - number // 4 - 1))
    mixed = jax.random.permutation(jax.random.fold_in(own, 3), number_of)
    giver, sink = mixed[0:number_of // 2 * 2:2], mixed[1:number_of // 2 * 2:2]
    room = jnp.minimum(tallies[giver] - 1, reach - tallies[sink]) // 2
    room = jnp.where((giver == order[0]) | (sink == order[0]) | (tallies[sink] == 0), 0, jnp.maximum(room, 0))
    passed = jax.random.randint(jax.random.fold_in(own, 4), (number_of // 2,), 0, 1 << 20) % (room + 1)
    tallies = tallies.at[giver].add(-passed).at[sink].add(passed)
    items = jnp.searchsorted(jnp.cumsum(tallies), jnp.arange(rows * top), side="right").astype(jnp.int32)
    grid = items.reshape(top, rows).T
    grid = grid[jax.random.permutation(jax.random.fold_in(own, 1), rows)]
    rotation = jax.random.randint(jax.random.fold_in(own, 2), (rows, 1), 0, top)
    return jnp.take_along_axis(grid, (jnp.arange(top)[None, :] + rotation) % top, axis=1)


def load_shares(amount, total, limit, skew, full):
    loads = [(1 << 20) // math.isqrt(grade ** skew) + 1 for grade in range(1, amount + 1)]
    largest = limit if full else min(limit, max(-(-total // amount), total * loads[0] // sum(loads)))
    least = 1 if total - largest >= amount - 1 else 0
    given, surplus = [largest] + [least] * (amount - 1), total - largest - least * (amount - 1)
    while surplus > 0:
        movable = [i for i in range(1, amount) if given[i] < largest] or [i for i in range(1, amount) if given[i] < limit]
        pool, remaining = sum([loads[i] for i in movable]), surplus
        for i in movable:
            more = min(limit - given[i], max(1, remaining * loads[i] // pool), surplus)
            given[i] = given[i] + more
            surplus = surplus - more
    return np.array(given)


def centred(own_key, dims, scale, limit, cuts=(), held_as=jnp.bfloat16):
    entries = jax.random.normal(own_key, dims, jnp.float32) * scale
    if len(cuts) > 0:
        entries = levels(own_key, dims, cuts, -0.22, 0.18) * entries
    return jnp.clip(entries, min=-limit, max=limit).astype(held_as)


def setup_inputs(seed: int = 0, part: int = 0) -> dict:
    streams_of = jax.random.split(jax.random.key(seed), 13)
    own_keys = jax.random.split(jax.random.fold_in(streams_of[12], part), 13)
    image_tokens = draw_image_tokens(jax.random.fold_in(jax.random.fold_in(streams_of[12], part), 71), part)
    pair_owner_keys = jax.random.split(jax.random.fold_in(own_keys[1], 1), PAIRS // PAIR_DEV)
    pair_owner_turns = jax.random.permutation(jax.random.fold_in(own_keys[1], 3), PAIRS // PAIR_DEV)
    pair_owner = jax.vmap(lambda own, number: shared_out(jax.random.fold_in(own_keys[1], 2), own, number, PAIR_DEV, N_SHARD, 2, CAP, 2))(pair_owner_keys, pair_owner_turns).reshape((PAIRS, 2))
    pair_slot = touch_ends(jax.random.randint(own_keys[2], (PAIRS, 2), 0, IMG_DEV), jax.random.fold_in(own_keys[2], 1), 0, IMG_DEV - 1).astype(jnp.int32)
    gain_attn = jnp.clip(1.0 + 0.18 * jax.random.normal(streams_of[3], (D,), jnp.float32), 0.1, 1.9)
    w_qk = centred(streams_of[4], (D, D), D ** -0.5, 0.25, ((1, 2),))
    w_value = centred(streams_of[5], (D, D), D ** -0.5, 0.25, ((1, 2),))
    logit_scale = draw_logit_scale(jax.random.fold_in(streams_of[12], 71), part)
    w_out = centred(streams_of[7], (D, D), D ** -0.5, 0.25, ((0, 2),))
    gain_mlp = jnp.clip(1.0 + 0.18 * jax.random.normal(streams_of[8], (D,), jnp.float32), 0.1, 1.9)
    w_in = centred(streams_of[9], (D, FF), D ** -0.5, 0.25, ((1, 2),))
    bias_in = centred(streams_of[10], (FF,), 0.5, 3.0, ((0, 2),), jnp.float32)
    w_back = centred(streams_of[11], (FF, D), FF ** -0.5, 0.125, ((0, 2),))
    return {"image_tokens": image_tokens, "pair_owner": pair_owner, "pair_slot": pair_slot, "gain_attn": gain_attn, "w_qk": w_qk, "w_value": w_value, "logit_scale": logit_scale, "w_out": w_out, "gain_mlp": gain_mlp, "w_in": w_in, "bias_in": bias_in, "w_back": w_back}


def norm_rows(values, gain):
    center = values - lax.optimization_barrier(jnp.mean(values, axis=-1, keepdims=True))
    spread = lax.optimization_barrier(jnp.mean(center * center, axis=-1, keepdims=True))
    return center * lax.rsqrt(spread + 1e-05) * gain

def compare(tokens, gain_attn, w_qk, w_value, logit_scale, w_out, gain_mlp, w_in, bias_in, w_back):
    count, sides, length, width = tokens.shape
    heads = logit_scale.shape[0]
    inputs = tokens.astype(jnp.float32)
    normed = norm_rows(inputs, gain_attn).astype(jnp.bfloat16)
    query = jnp.einsum('pstd,dk->pstk', normed.astype(jnp.float32), w_qk.astype(jnp.float32)).astype(jnp.bfloat16)
    value = jnp.einsum('pstd,dk->pstk', normed.astype(jnp.float32), w_value.astype(jnp.float32)).astype(jnp.bfloat16)
    query = query.reshape(count, sides, length, heads, -1)
    value = value.reshape(count, sides, length, heads, -1)
    other_keys = query[:, ::-1]
    other_values = value[:, ::-1]
    factor = logit_scale / jnp.sqrt(jnp.float32(query.shape[-1]))
    scores = jnp.einsum('psihe,psjhe->pshij', query.astype(jnp.float32), other_keys.astype(jnp.float32))
    scores = scores * factor[:, None, None]
    probs = jax.nn.softmax(scores, axis=-1).astype(jnp.bfloat16)
    mixed = jnp.einsum('pshij,psjhe->psihe', probs.astype(jnp.float32), other_values.astype(jnp.float32))
    mixed = mixed.astype(jnp.bfloat16).reshape(count, sides, length, width)
    hidden = inputs + jnp.einsum('pstk,kd->pstd', mixed.astype(jnp.float32), w_out.astype(jnp.float32))
    normed_mlp = norm_rows(hidden, gain_mlp).astype(jnp.bfloat16)
    inner = jnp.einsum('pstd,df->pstf', normed_mlp.astype(jnp.float32), w_in.astype(jnp.float32)) + bias_in
    inner = jax.nn.gelu(inner, approximate=True).astype(jnp.bfloat16)
    back = jnp.einsum('pstf,fd->pstd', inner.astype(jnp.float32), w_back.astype(jnp.float32))
    return lax.optimization_barrier(jnp.mean(hidden + back, axis=(1, 2))).astype(jnp.bfloat16)

def reference(image_tokens, pair_owner, pair_slot, gain_attn, w_qk, w_value, logit_scale, w_out, gain_mlp, w_in, bias_in, w_back):
    image_ids = (pair_owner * IMG_DEV + pair_slot).astype(jnp.int32)
    blocks = image_ids.reshape(N_SHARD, PAIR_DEV, 2)

    def one_block(ids):
        tokens = image_tokens[ids]
        return compare(tokens, gain_attn, w_qk, w_value, logit_scale, w_out, gain_mlp, w_in, bias_in, w_back)
    features = lax.map(one_block, blocks)
    return features.reshape(PAIRS, D)
```

```python
import functools

import jax
import jax.numpy as jnp
from jax import lax
from jax.experimental import pallas as pl
from jax.experimental.pallas import tpu as pltpu
from jax.sharding import PartitionSpec as P

LOG2E = 1.4426950408889634


def norm_rows(values, gain):
    center = values - jnp.mean(values, axis=-1, keepdims=True)
    spread = jnp.mean(center * center, axis=-1, keepdims=True)
    return center * lax.rsqrt(spread + 1e-05) * gain


def dot_nt(a, b):
    return lax.dot_general(a, b, (((1,), (1,)), ((), ())), preferred_element_type=jnp.float32)


def dot(a, b):
    return jnp.dot(a, b, preferred_element_type=jnp.float32)


def compare_kernel(
    length,
    head_dim,
    core_ref,
    scale_ref,
    own_ref,
    far_ref,
    gain_attn_ref,
    qk_a_ref,
    qk_b_ref,
    value_a_ref,
    value_b_ref,
    out_a_ref,
    out_b_ref,
    gain_mlp_ref,
    in_a_ref,
    in_b_ref,
    bias_a_ref,
    bias_b_ref,
    back_a_ref,
    back_b_ref,
    result_ref,
    pooled_ref,
    hidden_ref,
):
    half = 8 * length
    rows = 2 * half
    blocks = own_ref.shape[0] // rows
    pair_dim = 2 * head_dim
    first = core_ref[0] == 0
    lane = lax.broadcasted_iota(jnp.int32, (half, pair_dim), 1)
    even = lane < head_dim
    same = (
        lax.broadcasted_iota(jnp.int32, (half, half), 0) // length
        == lax.broadcasted_iota(jnp.int32, (half, half), 1) // length
    )

    def split(values):
        zero = jnp.zeros_like(values)
        return jnp.concatenate(
            [jnp.where(even, values, zero), jnp.where(even, zero, values)], axis=0
        )

    def softmax(scores, factor):
        scores = jnp.where(same, scores, -1e30)
        top = jnp.max(scores, axis=1, keepdims=True)
        weights = jnp.exp2((scores - top) * factor)
        return (weights * (1.0 / jnp.sum(weights, axis=1, keepdims=True))).astype(jnp.bfloat16)

    def block(step, carry):
        span = pl.ds(pl.multiple_of(step * rows, rows), rows)
        own = own_ref[span, :].astype(jnp.float32)
        far = far_ref[span, :].astype(jnp.float32)
        tokens = jnp.concatenate(
            [jnp.where(first, own, far), jnp.where(first, far, own)], axis=1
        )
        normed = norm_rows(tokens, gain_attn_ref[...]).astype(jnp.bfloat16)
        hidden = tokens
        head = 0
        for qk_ref, value_ref, out_ref in (
            (qk_a_ref, value_a_ref, out_a_ref),
            (qk_b_ref, value_b_ref, out_b_ref),
        ):
            query = dot(normed, qk_ref[...]).astype(jnp.bfloat16)
            value = dot(normed, value_ref[...]).astype(jnp.bfloat16)
            mixed = []
            for start in range(0, query.shape[1], pair_dim):
                factors = [scale_ref[head + k] * (LOG2E / head_dim**0.5) for k in range(2)]
                head += 2
                q = query[:, start : start + pair_dim]
                v = value[:, start : start + pair_dim]
                sides = []
                for side in range(2):
                    here = slice(side * half, (side + 1) * half)
                    there = slice((1 - side) * half, (2 - side) * half)
                    scores = dot_nt(q[here], split(q[there]))
                    probs = [
                        softmax(scores[:, k * half : (k + 1) * half], factors[k]) for k in range(2)
                    ]
                    sides.append(
                        dot(jnp.concatenate(probs, axis=1), split(v[there])).astype(jnp.bfloat16)
                    )
                mixed.append(jnp.concatenate(sides, axis=0))
            hidden = hidden + dot(jnp.concatenate(mixed, axis=1), out_ref[...])
        at = pl.ds(pl.multiple_of(step * 8, 8), 8)
        hidden_ref[at, :] = jnp.sum(hidden.reshape(2, 8, length, -1), axis=(0, 2))
        normed = norm_rows(hidden, gain_mlp_ref[...]).astype(jnp.bfloat16)
        offset = 0
        for in_ref, bias_ref in ((in_a_ref, bias_a_ref), (in_b_ref, bias_b_ref)):
            units = in_ref.shape[1]
            tile = min(256, units)
            for start in range(0, units, tile):
                cut = slice(start, start + tile)
                inner = dot(normed, in_ref[:, cut]) + bias_ref[:, cut]
                bent = jnp.tanh(inner * (0.7978845608028654 + 0.035677408136300125 * (inner * inner)))
                inner = inner * bent + inner
                pooled_ref[at, offset + start : offset + start + tile] = jnp.sum(
                    inner.reshape(2, 8, length, -1), axis=(0, 2)
                )
            offset += units
        return carry

    lax.fori_loop(0, blocks, block, 0)
    pooled = pooled_ref[...] * (0.25 / length)
    coarse = pooled.astype(jnp.bfloat16)
    fine = (pooled - coarse.astype(jnp.float32)).astype(jnp.bfloat16)
    both = jnp.concatenate([coarse, fine], axis=0)
    units = back_a_ref.shape[0]
    back = dot(both[:, :units], back_a_ref[...]) + dot(both[:, units:], back_b_ref[...])
    count = result_ref.shape[0]
    mean = hidden_ref[...] * (0.5 / length)
    result_ref[...] = (mean + back[:count] + back[count:]).astype(jnp.bfloat16)


def place_requests(owners, slots, owner_count, capacity):
    flat_owner = owners.reshape(-1)
    flat_slot = slots.reshape(-1)
    onehot = (flat_owner[:, None] == jnp.arange(owner_count, dtype=jnp.int32)[None, :]).astype(
        jnp.int32
    )
    rank = jnp.sum(jnp.cumsum(onehot, axis=0) * onehot, axis=1) - 1
    where = flat_owner * capacity + rank
    wanted = jnp.zeros((owner_count * capacity,), jnp.int32).at[where].set(flat_slot)
    return (where, wanted.reshape(owner_count, capacity))


def on_device(
    image_tokens,
    pair_owner,
    pair_slot,
    gain_attn,
    w_qk,
    w_value,
    logit_scale,
    w_out,
    gain_mlp,
    w_in,
    bias_in,
    w_back,
):
    owner_count = lax.axis_size("shard")
    core = lax.axis_index("mp")
    pair_count = pair_owner.shape[0]
    _, length, features = image_tokens.shape
    width = 2 * features
    head_dim = w_qk.shape[1] // logit_scale.shape[0]
    capacity = max(2, 4 * pair_count // owner_count)
    mine = pair_count // 2

    def swap(values):
        return lax.ppermute(values, "mp", [(0, 1), (1, 0)])

    where, wanted = place_requests(pair_owner, pair_slot, owner_count, capacity)
    incoming = lax.all_to_all(wanted, "shard", split_axis=0, concat_axis=0, tiled=True)
    weights = (w_qk, w_value, w_out, w_in, w_back, bias_in, logit_scale)
    far_qk, far_value, far_out, far_in, far_back, far_bias, far_scale = [swap(w) for w in weights]
    served = image_tokens[incoming]
    returned = lax.all_to_all(served, "shard", split_axis=0, concat_axis=0, tiled=True)
    returned = returned.reshape(owner_count * capacity, length, features)
    order = where.reshape(2, mine // 8, 8, 2).transpose(0, 1, 3, 2).reshape(2, 2 * mine)
    far = swap(returned[order[1 - core]])
    own = returned[order[core]]

    smem = pl.BlockSpec(memory_space=pltpu.SMEM)
    vmem = pl.BlockSpec(memory_space=pltpu.VMEM)
    units = 2 * w_in.shape[1]
    flops = 4 * mine * length * width * (3 * width + units)
    features_here = pl.pallas_call(
        functools.partial(compare_kernel, length, head_dim),
        out_shape=jax.ShapeDtypeStruct((mine, width), jnp.bfloat16),
        in_specs=[smem, smem] + [vmem] * 16,
        out_specs=vmem,
        scratch_shapes=[
            pltpu.VMEM((mine, units), jnp.float32),
            pltpu.VMEM((mine, width), jnp.float32),
        ],
        compiler_params=pltpu.CompilerParams(vmem_limit_bytes=48 * 2**20),
        cost_estimate=pl.CostEstimate(
            flops=flops, bytes_accessed=8 * 2**20, transcendentals=2 * mine * length * units
        ),
    )(
        core.reshape(1),
        jnp.concatenate([logit_scale, far_scale]),
        own.reshape(-1, features),
        far.reshape(-1, features),
        gain_attn.reshape(1, -1),
        w_qk,
        far_qk,
        w_value,
        far_value,
        w_out,
        far_out,
        gain_mlp.reshape(1, -1),
        w_in,
        far_in,
        bias_in.reshape(1, -1),
        far_bias.reshape(1, -1),
        w_back,
        far_back,
    )
    features_there = swap(features_here)
    low = jnp.where(core == 0, features_here, features_there)
    high = jnp.where(core == 0, features_there, features_here)
    return jnp.concatenate([low, high], axis=0)


def solution(mesh):
    in_specs = (
        P(("groups", "shard"), None, "mp"),
        P(("groups", "shard"), None),
        P(("groups", "shard"), None),
        P(),
        P(None, "mp"),
        P(None, "mp"),
        P("mp"),
        P("mp", None),
        P(),
        P(None, "mp"),
        P("mp"),
        P("mp", None),
    )
    out_specs = P(("groups", "shard"), None)
    return jax.shard_map(
        on_device, mesh=mesh, in_specs=in_specs, out_specs=out_specs, check_vma=False
    )
```

```python
import functools

import jax
import jax.numpy as jnp
from jax import lax
from jax.experimental import pallas as pl
from jax.experimental.pallas import tpu as pltpu
from jax.sharding import PartitionSpec as P

LOG2E = 1.4426950408889634


def norm_rows(values, gain):
    center = values - jnp.mean(values, axis=-1, keepdims=True)
    spread = jnp.mean(center * center, axis=-1, keepdims=True)
    return center * lax.rsqrt(spread + 1e-05) * gain


def dot_nt(a, b):
    return lax.dot_general(a, b, (((1,), (1,)), ((), ())), preferred_element_type=jnp.float32)


def dot(a, b):
    return jnp.dot(a, b, preferred_element_type=jnp.float32)


def compare_kernel(
    length,
    head_dim,
    core_ref,
    scale_ref,
    list_ref,
    returned_ref,
    far_ref,
    gain_attn_ref,
    qk_a_ref,
    qk_b_ref,
    value_a_ref,
    value_b_ref,
    out_a_ref,
    out_b_ref,
    gain_mlp_ref,
    in_a_ref,
    in_b_ref,
    bias_a_ref,
    bias_b_ref,
    back_a_ref,
    back_b_ref,
    result_ref,
    own_ref,
    pooled_ref,
    hidden_ref,
    sems,
):
    half = 8 * length
    rows = 2 * half
    blocks = own_ref.shape[0] // 16
    pair_dim = 2 * head_dim
    first = core_ref[0] == 0
    start = core_ref[0] * own_ref.shape[0]

    def begin(index, carry):
        source = returned_ref.at[list_ref[0, start + index]]
        pltpu.make_async_copy(source, own_ref.at[index], sems.at[index // 16]).start()
        return carry

    lax.fori_loop(0, own_ref.shape[0], begin, 0, unroll=8)
    lane = lax.broadcasted_iota(jnp.int32, (half, pair_dim), 1)
    even = lane < head_dim
    same = (
        lax.broadcasted_iota(jnp.int32, (half, half), 0) // length
        == lax.broadcasted_iota(jnp.int32, (half, half), 1) // length
    )

    def split(values):
        zero = jnp.zeros_like(values)
        return jnp.concatenate(
            [jnp.where(even, values, zero), jnp.where(even, zero, values)], axis=0
        )

    def softmax(scores, factor):
        scores = jnp.where(same, scores, -1e30)
        top = jnp.max(scores, axis=1, keepdims=True)
        weights = jnp.exp2((scores - top) * factor)
        return (weights * (1.0 / jnp.sum(weights, axis=1, keepdims=True))).astype(jnp.bfloat16)

    def block(step, carry):
        span = pl.ds(pl.multiple_of(step * 16, 16), 16)
        pltpu.make_async_copy(
            returned_ref.at[pl.ds(0, 16)], own_ref.at[span], sems.at[step]
        ).wait()
        own = own_ref[span].reshape(rows, -1).astype(jnp.float32)
        far = far_ref[span].reshape(rows, -1).astype(jnp.float32)
        tokens = jnp.concatenate(
            [jnp.where(first, own, far), jnp.where(first, far, own)], axis=1
        )
        normed = norm_rows(tokens, gain_attn_ref[...]).astype(jnp.bfloat16)
        hidden = tokens
        head = 0
        for qk_ref, value_ref, out_ref in (
            (qk_a_ref, value_a_ref, out_a_ref),
            (qk_b_ref, value_b_ref, out_b_ref),
        ):
            query = dot(normed, qk_ref[...]).astype(jnp.bfloat16)
            value = dot(normed, value_ref[...]).astype(jnp.bfloat16)
            mixed = []
            for start in range(0, query.shape[1], pair_dim):
                factors = [scale_ref[head + k] * (LOG2E / head_dim**0.5) for k in range(2)]
                head += 2
                q = query[:, start : start + pair_dim]
                v = value[:, start : start + pair_dim]
                sides = []
                for side in range(2):
                    here = slice(side * half, (side + 1) * half)
                    there = slice((1 - side) * half, (2 - side) * half)
                    scores = dot_nt(q[here], split(q[there]))
                    probs = [
                        softmax(scores[:, k * half : (k + 1) * half], factors[k]) for k in range(2)
                    ]
                    sides.append(
                        dot(jnp.concatenate(probs, axis=1), split(v[there])).astype(jnp.bfloat16)
                    )
                mixed.append(jnp.concatenate(sides, axis=0))
            hidden = hidden + dot(jnp.concatenate(mixed, axis=1), out_ref[...])
        at = pl.ds(pl.multiple_of(step * 8, 8), 8)
        hidden_ref[at, :] = jnp.sum(hidden.reshape(2, 8, length, -1), axis=(0, 2))
        normed = norm_rows(hidden, gain_mlp_ref[...]).astype(jnp.bfloat16)
        offset = 0
        for in_ref, bias_ref in ((in_a_ref, bias_a_ref), (in_b_ref, bias_b_ref)):
            units = in_ref.shape[1]
            tile = min(256, units)
            for start in range(0, units, tile):
                cut = slice(start, start + tile)
                inner = dot(normed, in_ref[:, cut]) + bias_ref[:, cut]
                bent = jnp.tanh(inner * (0.7978845608028654 + 0.035677408136300125 * (inner * inner)))
                inner = inner * bent + inner
                pooled_ref[at, offset + start : offset + start + tile] = jnp.sum(
                    inner.reshape(2, 8, length, -1), axis=(0, 2)
                )
            offset += units
        return carry

    lax.fori_loop(0, blocks, block, 0)
    pooled = pooled_ref[...] * (0.25 / length)
    coarse = pooled.astype(jnp.bfloat16)
    fine = (pooled - coarse.astype(jnp.float32)).astype(jnp.bfloat16)
    both = jnp.concatenate([coarse, fine], axis=0)
    units = back_a_ref.shape[0]
    back = dot(both[:, :units], back_a_ref[...]) + dot(both[:, units:], back_b_ref[...])
    count = result_ref.shape[0]
    mean = hidden_ref[...] * (0.5 / length)
    result_ref[...] = (mean + back[:count] + back[count:]).astype(jnp.bfloat16)


def place_kernel(count, capacity, owner_ref, slot_ref, wanted_ref, list_ref):
    owners = wanted_ref.shape[0]
    total = 2 * count
    owner = jnp.concatenate([owner_ref[0:1, :], owner_ref[1:2, :]], axis=1)
    slot = jnp.concatenate([slot_ref[0:1, :], slot_ref[1:2, :]], axis=1)

    def place(dim, size):
        return lax.broadcasted_iota(jnp.int32, (size, total), dim)

    def as_bf16(values):
        return values.astype(jnp.float32).astype(jnp.bfloat16)

    named = place(0, owners) == owner
    until = as_bf16(jnp.where(place(0, total) <= place(1, total), 1, 0))
    tally = dot(as_bf16(jnp.where(named, 1, 0)), until).astype(jnp.int32)
    rank = jnp.sum(jnp.where(named, tally, 0), axis=0, keepdims=True) - 1
    ranked = as_bf16(jnp.where(place(0, total) == rank, 1, 0))
    wanted = dot_nt(as_bf16(jnp.where(named, slot, 0)), ranked).astype(jnp.int32)
    for index in range(owners):
        wanted_ref[index] = wanted[index : index + 1, :capacity]
    where = owner * capacity + rank
    entry = place(1, 1)
    side = entry // count
    pair = entry % count
    mine = count // 2
    seat = pair // mine * count + pair % mine // 8 * 16 + side * 8 + pair % 8
    seated = as_bf16(jnp.where(place(0, total) == seat, 1, 0))
    parts = as_bf16(jnp.where(place(0, 8) == 0, where // 16, where % 16))
    listed = dot_nt(parts, seated).astype(jnp.int32)
    list_ref[...] = listed[0:1] * 16 + listed[1:2]


def place_requests(pair_owner, pair_slot, owner_count, capacity):
    count = pair_owner.shape[0]
    return pl.pallas_call(
        functools.partial(place_kernel, count, capacity),
        out_shape=(
            jax.ShapeDtypeStruct((owner_count, 1, capacity), jnp.int32),
            jax.ShapeDtypeStruct((1, 2 * count), jnp.int32),
        ),
    )(pair_owner.T, pair_slot.T)


def pick_kernel(core_ref, list_ref, returned_ref, picked_ref, sem):
    count = picked_ref.shape[0]
    start = (1 - core_ref[0]) * count

    def begin(index, carry):
        source = returned_ref.at[list_ref[0, start + index]]
        pltpu.make_async_copy(source, picked_ref.at[index], sem).start()
        return carry

    lax.fori_loop(0, count, begin, 0, unroll=8)
    pltpu.make_async_copy(returned_ref.at[pl.ds(0, count)], picked_ref, sem).wait()


def on_device(
    image_tokens,
    pair_owner,
    pair_slot,
    gain_attn,
    w_qk,
    w_value,
    logit_scale,
    w_out,
    gain_mlp,
    w_in,
    bias_in,
    w_back,
):
    owner_count = lax.axis_size("shard")
    core = lax.axis_index("mp")
    pair_count = pair_owner.shape[0]
    _, length, features = image_tokens.shape
    width = 2 * features
    head_dim = w_qk.shape[1] // logit_scale.shape[0]
    capacity = max(2, 4 * pair_count // owner_count)
    mine = pair_count // 2

    def swap(values):
        return lax.ppermute(values, "mp", [(0, 1), (1, 0)])

    smem = pl.BlockSpec(memory_space=pltpu.SMEM)
    vmem = pl.BlockSpec(memory_space=pltpu.VMEM)
    hbm = pl.BlockSpec(memory_space=pl.ANY)

    wanted, order = place_requests(pair_owner, pair_slot, owner_count, capacity)
    incoming = lax.all_to_all(wanted, "shard", split_axis=0, concat_axis=0, tiled=True)
    served = image_tokens[incoming.reshape(-1)]
    served = served.reshape(owner_count, capacity, length, features)
    weights = (w_qk, w_value, w_out, w_in, w_back, bias_in, logit_scale)
    swapped = [swap(w) for w in weights]
    returned = lax.all_to_all(served, "shard", split_axis=0, concat_axis=0, tiled=True)
    returned, *swapped = lax.optimization_barrier((returned, *swapped))
    far_qk, far_value, far_out, far_in, far_back, far_bias, far_scale = swapped
    returned = returned.reshape(owner_count * capacity, length, features)
    core = core.reshape(1)
    picked = pl.pallas_call(
        pick_kernel,
        out_shape=jax.ShapeDtypeStruct((pair_count, length, features), jnp.bfloat16),
        in_specs=[smem, smem, hbm],
        out_specs=hbm,
        scratch_shapes=[pltpu.SemaphoreType.DMA],
    )(core, order, returned)
    far = swap(picked)

    units = 2 * w_in.shape[1]
    flops = 4 * mine * length * width * (3 * width + units)
    features_here = pl.pallas_call(
        functools.partial(compare_kernel, length, head_dim),
        out_shape=jax.ShapeDtypeStruct((mine, width), jnp.bfloat16),
        in_specs=[smem, smem, smem, hbm] + [vmem] * 15,
        out_specs=vmem,
        scratch_shapes=[
            pltpu.VMEM((pair_count, length, features), jnp.bfloat16),
            pltpu.VMEM((mine, units), jnp.float32),
            pltpu.VMEM((mine, width), jnp.float32),
            pltpu.SemaphoreType.DMA((mine // 8,)),
        ],
        compiler_params=pltpu.CompilerParams(vmem_limit_bytes=48 * 2**20),
        cost_estimate=pl.CostEstimate(
            flops=flops, bytes_accessed=8 * 2**20, transcendentals=2 * mine * length * units
        ),
    )(
        core,
        jnp.concatenate([logit_scale, far_scale]),
        order,
        returned,
        far,
        gain_attn.reshape(1, -1),
        w_qk,
        far_qk,
        w_value,
        far_value,
        w_out,
        far_out,
        gain_mlp.reshape(1, -1),
        w_in,
        far_in,
        bias_in.reshape(1, -1),
        far_bias.reshape(1, -1),
        w_back,
        far_back,
    )
    features_there = swap(features_here)
    low = jnp.where(core == 0, features_here, features_there)
    high = jnp.where(core == 0, features_there, features_here)
    return jnp.concatenate([low, high], axis=0)


def solution(mesh):
    in_specs = (
        P(("groups", "shard"), None, "mp"),
        P(("groups", "shard"), None),
        P(("groups", "shard"), None),
        P(),
        P(None, "mp"),
        P(None, "mp"),
        P("mp"),
        P("mp", None),
        P(),
        P(None, "mp"),
        P("mp"),
        P("mp", None),
    )
    out_specs = P(("groups", "shard"), None)
    return jax.shard_map(
        on_device, mesh=mesh, in_specs=in_specs, out_specs=out_specs, check_vma=False
    )
```

```python
import functools

import jax
import jax.numpy as jnp
from jax import lax
from jax.experimental import pallas as pl
from jax.experimental.pallas import tpu as pltpu
from jax.sharding import PartitionSpec as P

LOG2E = 1.4426950408889634


def norm_rows(values, gain):
    center = values - jnp.mean(values, axis=-1, keepdims=True)
    spread = jnp.mean(center * center, axis=-1, keepdims=True)
    return center * lax.rsqrt(spread + 1e-05) * gain


def dot_nt(a, b):
    return lax.dot_general(a, b, (((1,), (1,)), ((), ())), preferred_element_type=jnp.float32)


def dot(a, b):
    return jnp.dot(a, b, preferred_element_type=jnp.float32)


def compare_kernel(
    plan,
    length,
    head_dim,
    core_ref,
    scale_ref,
    list_ref,
    far_ref,
    gain_attn_ref,
    gain_mlp_ref,
    bias_a_ref,
    bias_b_ref,
    *refs,
):
    held_refs, source_refs = refs[:10], refs[10:-16]
    result_ref = refs[-16]
    matrix_refs = refs[-15:-5]
    own_ref, pooled_ref, hidden_ref, sems, matrix_sems = refs[-5:]
    loads = [
        pltpu.make_async_copy(held, ref, matrix_sems.at[k])
        for k, (held, ref) in enumerate(zip(held_refs, matrix_refs))
    ]
    start = core_ref[0] * own_ref.shape[0]

    def begin(index, carry):
        where = list_ref[0, start + index]
        fetch(plan, where, source_refs, own_ref.at[index], sems.at[index // 16])
        return carry

    for load in loads[:4]:
        load.start()
    lax.fori_loop(0, own_ref.shape[0], begin, 0, unroll=4)
    for load in loads[4:]:
        load.start()
    qk_a_ref, qk_b_ref, value_a_ref, value_b_ref, out_a_ref, out_b_ref = matrix_refs[:6]
    in_a_ref, in_b_ref, back_a_ref, back_b_ref = matrix_refs[6:]
    half = 8 * length
    rows = 2 * half
    blocks = own_ref.shape[0] // 16
    pair_dim = 2 * head_dim
    first = core_ref[0] == 0
    lane = lax.broadcasted_iota(jnp.int32, (half, pair_dim), 1)
    even = lane < head_dim
    same = (
        lax.broadcasted_iota(jnp.int32, (half, half), 0) // length
        == lax.broadcasted_iota(jnp.int32, (half, half), 1) // length
    )

    def split(values):
        zero = jnp.zeros_like(values)
        return jnp.concatenate(
            [jnp.where(even, values, zero), jnp.where(even, zero, values)], axis=0
        )

    def softmax(scores, factor):
        scores = jnp.where(same, scores, -1e30)
        top = jnp.max(scores, axis=1, keepdims=True)
        weights = jnp.exp2((scores - top) * factor)
        return (weights * (1.0 / jnp.sum(weights, axis=1, keepdims=True))).astype(jnp.bfloat16)

    def arrive(step, copies):
        @pl.when(step == 0)
        def _():
            for copy in copies:
                copy.wait()

    def block(step, carry):
        span = pl.ds(pl.multiple_of(step * 16, 16), 16)
        pltpu.make_async_copy(
            source_refs[0].at[pl.ds(0, 16)], own_ref.at[span], sems.at[step]
        ).wait()
        own = own_ref[span].reshape(rows, -1).astype(jnp.float32)
        far = far_ref[span].reshape(rows, -1).astype(jnp.float32)
        tokens = jnp.concatenate(
            [jnp.where(first, own, far), jnp.where(first, far, own)], axis=1
        )
        normed = norm_rows(tokens, gain_attn_ref[...]).astype(jnp.bfloat16)
        arrive(step, loads[:6])
        hidden = tokens
        head = 0
        for qk_ref, value_ref, out_ref in (
            (qk_a_ref, value_a_ref, out_a_ref),
            (qk_b_ref, value_b_ref, out_b_ref),
        ):
            query = dot(normed, qk_ref[...]).astype(jnp.bfloat16)
            value = dot(normed, value_ref[...]).astype(jnp.bfloat16)
            mixed = []
            for start in range(0, query.shape[1], pair_dim):
                factors = [scale_ref[head + k] * (LOG2E / head_dim**0.5) for k in range(2)]
                head += 2
                q = query[:, start : start + pair_dim]
                v = value[:, start : start + pair_dim]
                sides = []
                for side in range(2):
                    here = slice(side * half, (side + 1) * half)
                    there = slice((1 - side) * half, (2 - side) * half)
                    scores = dot_nt(q[here], split(q[there]))
                    probs = [
                        softmax(scores[:, k * half : (k + 1) * half], factors[k]) for k in range(2)
                    ]
                    sides.append(
                        dot(jnp.concatenate(probs, axis=1), split(v[there])).astype(jnp.bfloat16)
                    )
                mixed.append(jnp.concatenate(sides, axis=0))
            hidden = hidden + dot(jnp.concatenate(mixed, axis=1), out_ref[...])
        at = pl.ds(pl.multiple_of(step * 8, 8), 8)
        hidden_ref[at, :] = jnp.sum(hidden.reshape(2, 8, length, -1), axis=(0, 2))
        normed = norm_rows(hidden, gain_mlp_ref[...]).astype(jnp.bfloat16)
        arrive(step, loads[6:8])
        offset = 0
        for in_ref, bias_ref in ((in_a_ref, bias_a_ref), (in_b_ref, bias_b_ref)):
            units = in_ref.shape[1]
            tile = min(256, units)
            for start in range(0, units, tile):
                cut = slice(start, start + tile)
                inner = dot(normed, in_ref[:, cut]) + bias_ref[:, cut]
                bent = jnp.tanh(inner * (0.7978845608028654 + 0.035677408136300125 * (inner * inner)))
                inner = inner * bent + inner
                pooled_ref[at, offset + start : offset + start + tile] = jnp.sum(
                    inner.reshape(2, 8, length, -1), axis=(0, 2)
                )
            offset += units
        return carry

    lax.fori_loop(0, blocks, block, 0)
    arrive(0, loads[8:])
    pooled = pooled_ref[...] * (0.25 / length)
    coarse = pooled.astype(jnp.bfloat16)
    fine = (pooled - coarse.astype(jnp.float32)).astype(jnp.bfloat16)
    both = jnp.concatenate([coarse, fine], axis=0)
    units = back_a_ref.shape[0]
    back = dot(both[:, :units], back_a_ref[...]) + dot(both[:, units:], back_b_ref[...])
    count = result_ref.shape[0]
    mean = hidden_ref[...] * (0.5 / length)
    result_ref[...] = (mean + back[:count] + back[count:]).astype(jnp.bfloat16)


class Plan:
    def __init__(self, pair_count, owner_count):
        self.owners = owner_count
        self.capacity = max(2, 4 * pair_count // owner_count)
        self.half = owner_count // 2
        split = self.capacity >= 32 and self.half & (self.half - 1) == 0 and self.half > 0
        self.base = self.capacity // 2 if split else self.capacity
        self.extra = self.capacity - self.base
        self.chunk = 2 * self.extra
        self.part = self.half * self.extra // 2
        self.near_at = owner_count * self.base
        self.far_at = self.near_at + self.half * self.chunk
        self.row = self.capacity + (self.half if split else 0)


def place_kernel(plan, count, shard_ref, owner_ref, slot_ref, wanted_ref, list_ref):
    total = 2 * count
    owners = plan.owners
    owner = jnp.concatenate([owner_ref[0:1, :], owner_ref[1:2, :]], axis=1)
    slot = jnp.concatenate([slot_ref[0:1, :], slot_ref[1:2, :]], axis=1)

    def place(dim, size):
        return lax.broadcasted_iota(jnp.int32, (size, total), dim)

    def as_bf16(values):
        return values.astype(jnp.float32).astype(jnp.bfloat16)

    named = place(0, owners) == owner
    until = as_bf16(jnp.where(place(0, total) <= place(1, total), 1, 0))
    tally = dot(as_bf16(jnp.where(named, 1, 0)), until).astype(jnp.int32)
    rank = jnp.sum(jnp.where(named, tally, 0), axis=0, keepdims=True) - 1
    ranked = as_bf16(jnp.where(place(0, total) == rank, 1, 0))
    wanted = dot_nt(as_bf16(jnp.where(named, slot, 0)), ranked).astype(jnp.int32)
    where = owner * plan.base + rank
    if plan.extra:
        me = shard_ref[0]
        half = plan.half
        over = jnp.maximum(jnp.max(tally, axis=1, keepdims=True) - plan.base, 0)
        row = place(0, owners)
        far_over = jnp.where(row // half != me // half, over, 0)
        before = jnp.zeros((owners, total), jnp.int32)
        for index in range(owners - 1):
            before = before + jnp.where(row > index, far_over[index : index + 1], 0)
        before = jnp.sum(jnp.where(named, before, 0), axis=0, keepdims=True)
        rest = rank - plan.base
        near = plan.near_at + ((owner % half) ^ (me % half)) * plan.chunk + rest
        late = jnp.where(owner // half == me // half, near, plan.far_at + before + rest)
        where = jnp.where(rest < 0, where, late)
        told = place(1, owners) == plan.capacity + row % half
        wanted = wanted + jnp.sum(jnp.where(told, far_over, 0), axis=0, keepdims=True)
    for index in range(owners):
        wanted_ref[index] = wanted[index : index + 1, : plan.row]
    entry = place(1, 1)
    side = entry // count
    pair = entry % count
    mine = count // 2
    seat = pair // mine * count + pair % mine // 8 * 16 + side * 8 + pair % 8
    seated = as_bf16(jnp.where(place(0, total) == seat, 1, 0))
    parts = as_bf16(jnp.where(place(0, 8) == 0, where // 16, where % 16))
    listed = dot_nt(parts, seated).astype(jnp.int32)
    list_ref[...] = listed[0:1] * 16 + listed[1:2]


def serve_base_kernel(plan, incoming_ref, tokens_ref, served_ref):
    for requester in range(plan.owners):

        def copy(index, carry):
            served_ref[requester, index] = tokens_ref[incoming_ref[requester, 0, index]]
            return carry

        lax.fori_loop(0, plan.base, copy, 0, unroll=min(16, plan.base))


def serve_rest_kernel(plan, shard_ref, incoming_ref, tokens_ref, *chunk_refs):
    me = shard_ref[0]
    side = me // plan.half
    for distance, chunk_ref in enumerate(chunk_refs):
        peer = (me % plan.half) ^ distance
        for part in range(2):
            requester = (side ^ part) * plan.half + peer

            def copy(index, carry):
                slot = incoming_ref[requester, 0, plan.base + index]
                chunk_ref[part * plan.extra + index] = tokens_ref[slot]
                return carry

            lax.fori_loop(0, plan.extra, copy, 0, unroll=16)


def relay_kernel(plan, shard_ref, incoming_ref, *refs):
    chunk_refs = refs[: plan.half]
    first_ref, second_ref, sem = refs[plan.half :]
    me = shard_ref[0]
    client = me ^ plan.half
    position = 0
    for owner in range(plan.half):
        amount = incoming_ref[client, 0, plan.capacity + owner]
        for distance, chunk_ref in enumerate(chunk_refs):

            @pl.when((me % plan.half) ^ distance == owner)
            def _():
                def begin(index, carry):
                    source = chunk_ref.at[plan.extra + index]
                    at = position + index

                    @pl.when(at < plan.part)
                    def _():
                        pltpu.make_async_copy(source, first_ref.at[at], sem).start()

                    @pl.when(at >= plan.part)
                    def _():
                        pltpu.make_async_copy(source, second_ref.at[at - plan.part], sem).start()

                    return carry

                lax.fori_loop(0, amount, begin, 0)

        position = position + amount

    def finish(index, carry):
        pltpu.make_async_copy(chunk_refs[0].at[0], first_ref.at[0], sem).wait()
        return carry

    lax.fori_loop(0, position, finish, 0)


def fetch(plan, where, source_refs, target_ref, sem):
    if not plan.extra:
        pltpu.make_async_copy(source_refs[0].at[where], target_ref, sem).start()
        return
    starts = [0] + [plan.near_at + k * plan.chunk for k in range(plan.half)]
    starts += [plan.far_at, plan.far_at + plan.part, plan.far_at + 2 * plan.part]
    for ref, low, high in zip(source_refs, starts[:-1], starts[1:]):

        @pl.when((where >= low) & (where < high))
        def _():
            pltpu.make_async_copy(ref.at[where - low], target_ref, sem).start()


def pick_kernel(plan, core_ref, list_ref, *refs):
    source_refs = refs[:-2]
    picked_ref, sem = refs[-2:]
    count = picked_ref.shape[0]
    start = (1 - core_ref[0]) * count

    def begin(index, carry):
        fetch(plan, list_ref[0, start + index], source_refs, picked_ref.at[index], sem)
        return carry

    lax.fori_loop(0, count, begin, 0, unroll=4)
    pltpu.make_async_copy(source_refs[0].at[pl.ds(0, count)], picked_ref, sem).wait()


def on_device(
    image_tokens,
    pair_owner,
    pair_slot,
    gain_attn,
    w_qk,
    w_value,
    logit_scale,
    w_out,
    gain_mlp,
    w_in,
    bias_in,
    w_back,
):
    owner_count = lax.axis_size("shard")
    groups = lax.axis_size("groups")
    core = lax.axis_index("mp")
    shard = lax.axis_index("shard").reshape(1)
    pair_count = pair_owner.shape[0]
    _, length, features = image_tokens.shape
    width = 2 * features
    head_dim = w_qk.shape[1] // logit_scale.shape[0]
    mine = pair_count // 2
    plan = Plan(pair_count, owner_count)

    def swap(values):
        return lax.ppermute(values, "mp", [(0, 1), (1, 0)])

    def across(values, distance):
        return lax.ppermute(values, "shard", [(k, k ^ distance) for k in range(owner_count)])

    def images(count):
        return jax.ShapeDtypeStruct((count, length, features), jnp.bfloat16)

    smem = pl.BlockSpec(memory_space=pltpu.SMEM)
    vmem = pl.BlockSpec(memory_space=pltpu.VMEM)
    hbm = pl.BlockSpec(memory_space=pl.ANY)

    wanted, order = pl.pallas_call(
        functools.partial(place_kernel, plan, pair_count),
        out_shape=(
            jax.ShapeDtypeStruct((owner_count, 1, plan.row), jnp.int32),
            jax.ShapeDtypeStruct((1, 2 * pair_count), jnp.int32),
        ),
        in_specs=[smem, vmem, vmem],
    )(shard, pair_owner.T, pair_slot.T)
    incoming = lax.all_to_all(wanted, "shard", split_axis=0, concat_axis=0, tiled=True)
    served = pl.pallas_call(
        functools.partial(serve_base_kernel, plan),
        out_shape=jax.ShapeDtypeStruct(
            (owner_count, plan.base, length, features), jnp.bfloat16
        ),
        in_specs=[smem, vmem],
    )(incoming, image_tokens)
    returned = lax.all_to_all(served, "shard", split_axis=0, concat_axis=0, tiled=True)
    returned = returned.reshape(-1, length, features)
    sources = [returned]
    if plan.extra:
        chunks = pl.pallas_call(
            functools.partial(serve_rest_kernel, plan),
            out_shape=[images(plan.chunk)] * plan.half,
            in_specs=[smem, smem, vmem],
        )(shard, incoming, image_tokens)
        chunks = [chunks[0]] + [across(chunks[k], k) for k in range(1, plan.half)]
        first, second = pl.pallas_call(
            functools.partial(relay_kernel, plan),
            out_shape=[images(plan.part)] * 2,
            in_specs=[smem, smem] + [hbm] * plan.half,
            scratch_shapes=[pltpu.SemaphoreType.DMA],
        )(shard, incoming, *chunks)
        first = across(first, plan.half)
        crowded = jnp.max(jnp.sum(incoming[:, 0, plan.capacity :], axis=1)) > plan.part
        crowded = crowded.astype(jnp.int32)
        passed = crowded
        for _ in range(groups - 1):
            passed = lax.ppermute(passed, "groups", [(k, (k + 1) % groups) for k in range(groups)])
            crowded = jnp.maximum(crowded, passed)
        second = lax.cond(
            crowded > 0, lambda part: across(part, plan.half), lambda part: part, second
        )
        sources += [*chunks, first, second]
    weights = (w_qk, w_value, w_out, w_in, w_back, bias_in, logit_scale)
    swapped = [swap(w) for w in weights]
    sources, swapped = lax.optimization_barrier((sources, swapped))
    far_qk, far_value, far_out, far_in, far_back, far_bias, far_scale = swapped
    core = core.reshape(1)
    picked = pl.pallas_call(
        functools.partial(pick_kernel, plan),
        out_shape=images(pair_count),
        in_specs=[smem, smem] + [hbm] * len(sources),
        scratch_shapes=[pltpu.SemaphoreType.DMA],
    )(core, order, *sources)
    far = swap(picked)

    units = 2 * w_in.shape[1]
    flops = 4 * mine * length * width * (3 * width + units)
    matrices = [w_qk, far_qk, w_value, far_value, w_out, far_out, w_in, far_in, w_back, far_back]
    features_here = pl.pallas_call(
        functools.partial(compare_kernel, plan, length, head_dim),
        out_shape=jax.ShapeDtypeStruct((mine, width), jnp.bfloat16),
        in_specs=[smem] * 3 + [vmem] * 5 + [hbm] * (10 + len(sources)),
        out_specs=vmem,
        scratch_shapes=[pltpu.VMEM(m.shape, m.dtype) for m in matrices]
        + [
            pltpu.VMEM((pair_count, length, features), jnp.bfloat16),
            pltpu.VMEM((mine, units), jnp.float32),
            pltpu.VMEM((mine, width), jnp.float32),
            pltpu.SemaphoreType.DMA((mine // 8,)),
            pltpu.SemaphoreType.DMA((10,)),
        ],
        compiler_params=pltpu.CompilerParams(vmem_limit_bytes=32 * 2**20),
        cost_estimate=pl.CostEstimate(
            flops=flops, bytes_accessed=8 * 2**20, transcendentals=2 * mine * length * units
        ),
    )(
        core,
        jnp.concatenate([logit_scale, far_scale]),
        order,
        far,
        gain_attn.reshape(1, -1),
        gain_mlp.reshape(1, -1),
        bias_in.reshape(1, -1),
        far_bias.reshape(1, -1),
        *matrices,
        *sources,
    )
    features_there = swap(features_here)
    low = jnp.where(core == 0, features_here, features_there)
    high = jnp.where(core == 0, features_there, features_here)
    return jnp.concatenate([low, high], axis=0)


def solution(mesh):
    in_specs = (
        P(("groups", "shard"), None, "mp"),
        P(("groups", "shard"), None),
        P(("groups", "shard"), None),
        P(),
        P(None, "mp"),
        P(None, "mp"),
        P("mp"),
        P("mp", None),
        P(),
        P(None, "mp"),
        P("mp"),
        P("mp", None),
    )
    out_specs = P(("groups", "shard"), None)
    return jax.shard_map(
        on_device, mesh=mesh, in_specs=in_specs, out_specs=out_specs, check_vma=False
    )
```

```python
import functools

import jax
import jax.numpy as jnp
from jax import lax
from jax.experimental import pallas as pl
from jax.experimental.pallas import tpu as pltpu
from jax.sharding import PartitionSpec as P

LOG2E = 1.4426950408889634
BLOCK = 8


def norm_rows(values, gain):
    center = values - jnp.mean(values, axis=-1, keepdims=True)
    spread = jnp.mean(center * center, axis=-1, keepdims=True)
    return center * lax.rsqrt(spread + 1e-05) * gain


def dot_nt(a, b):
    return lax.dot_general(a, b, (((1,), (1,)), ((), ())), preferred_element_type=jnp.float32)


def dot(a, b):
    return jnp.dot(a, b, preferred_element_type=jnp.float32)


class Plan:
    def __init__(self, pair_count, owner_count):
        self.owners = owner_count
        self.capacity = max(2, 4 * pair_count // owner_count)
        self.half = owner_count // 2
        split = self.capacity >= 32 and self.half & (self.half - 1) == 0 and self.half > 0
        self.base = self.capacity // 2 if split else self.capacity
        self.extra = self.capacity - self.base
        self.part = self.half * self.extra // 2
        self.far_at = self.half * self.capacity
        self.rest_at = self.far_at + self.half * self.base
        self.row = self.capacity + (self.half if split else 0)
        if split:
            self.starts = [k * self.capacity for k in range(self.half)]
            self.starts += [self.far_at + k * self.base for k in range(self.half)]
            self.starts += [self.rest_at, self.rest_at + self.part]
        else:
            self.starts = [0]


def place_kernel(plan, count, shard_ref, owner_ref, slot_ref, wanted_ref, info_ref, seats_ref):
    total = 2 * count
    owners = plan.owners
    owner = jnp.concatenate([owner_ref[0:1, :], owner_ref[1:2, :]], axis=1)
    slot = jnp.concatenate([slot_ref[0:1, :], slot_ref[1:2, :]], axis=1)

    def place(dim, size):
        return lax.broadcasted_iota(jnp.int32, (size, total), dim)

    def as_bf16(values):
        return values.astype(jnp.float32).astype(jnp.bfloat16)

    row = place(0, owners)
    named = row == owner
    until = as_bf16(jnp.where(place(0, total) <= place(1, total), 1, 0))
    tally = dot(as_bf16(jnp.where(named, 1, 0)), until).astype(jnp.int32)
    rank = jnp.sum(jnp.where(named, tally, 0), axis=0, keepdims=True) - 1
    ranked = as_bf16(jnp.where(place(0, total) == rank, 1, 0))
    wanted = dot_nt(as_bf16(jnp.where(named, slot, 0)), ranked).astype(jnp.int32)
    entry = place(1, 1)
    side = entry // count
    pair = entry % count
    mine = count // 2
    if plan.extra:
        me = shard_ref[0]
        half = plan.half
        over = jnp.maximum(jnp.max(tally, axis=1, keepdims=True) - plan.base, 0)
        far_over = jnp.where(row // half != me // half, over, 0)
        before = jnp.zeros((owners, total), jnp.int32)
        for index in range(owners - 1):
            before = before + jnp.where(row > index, far_over[index : index + 1], 0)
        before = jnp.sum(jnp.where(named, before, 0), axis=0, keepdims=True)
        distance = (owner % half) ^ (me % half)
        rest = plan.rest_at + before + rank - plan.base
        direct = plan.far_at + distance * plan.base + rank
        far = owner // half != me // half
        late = jnp.where(far & (rank >= plan.base), 1, 0)
        where = jnp.where(far, jnp.where(late > 0, rest, direct), distance * plan.capacity + rank)
        told = place(1, owners) == plan.capacity + row % half
        wanted = wanted + jnp.sum(jnp.where(told, far_over, 0), axis=0, keepdims=True)
        late = jnp.maximum(late, jnp.concatenate([late[:, count:], late[:, :count]], axis=1))
        older = (place(0, total) < place(1, total)) & (
            place(0, total) // count == place(1, total) // count
        )
        prompt = as_bf16(jnp.broadcast_to(1 - late, (8, total)))
        ahead = dot(prompt, as_bf16(jnp.where(older, 1, 0))).astype(jnp.int32)[0:1]
        prompt_count = jnp.sum(1 - late, axis=1, keepdims=True) // 2
        seat = jnp.where(late > 0, prompt_count + pair - ahead, ahead)
        full = prompt_count // 2 // BLOCK
    else:
        where = owner * plan.base + rank
        seat = pair
        full = jnp.zeros((1, 1), jnp.int32)
    for index in range(owners):
        wanted_ref[index] = wanted[index : index + 1, : plan.row]
    core = seat % 2
    local = seat // 2
    position = core * count + local // BLOCK * (2 * BLOCK) + side * BLOCK + local % BLOCK
    seated = as_bf16(jnp.where(place(0, total) == position, 1, 0))
    parts = as_bf16(jnp.where(place(0, 8) == 0, where // 16, where % 16))
    listed = dot_nt(parts, seated).astype(jnp.int32)
    info_ref[...] = jnp.where(place(0, 8) == 0, listed[0:1] * 16 + listed[1:2], full)
    lines = place(0, count)
    taken = as_bf16(jnp.where(lines == core * mine + local, 1, 0))
    seats_ref[...] = dot_nt(
        as_bf16(jnp.where(lines == place(1, count), 1, 0)), taken
    ).astype(jnp.bfloat16)


def serve(tokens_ref, incoming_ref, requester, start, served_ref):
    count = served_ref.shape[0]

    def copy(index, carry):
        served_ref[index] = tokens_ref[incoming_ref[requester, 0, start + index]]
        return carry

    lax.fori_loop(0, count, copy, 0, unroll=min(16, count))


def serve_all_kernel(plan, incoming_ref, tokens_ref, served_ref):
    for requester in range(plan.owners):
        serve(tokens_ref, incoming_ref, requester, 0, served_ref.at[requester])


def serve_far_kernel(plan, shard_ref, incoming_ref, tokens_ref, *served_refs):
    for distance, served_ref in enumerate(served_refs):
        relayed = distance < plan.half
        requester = shard_ref[0] ^ (distance + plan.half if relayed else distance)
        serve(tokens_ref, incoming_ref, requester, plan.base if relayed else 0, served_ref)


def serve_near_kernel(plan, shard_ref, incoming_ref, tokens_ref, *served_refs):
    for distance, served_ref in enumerate(served_refs):
        serve(tokens_ref, incoming_ref, shard_ref[0] ^ distance, 0, served_ref)


def relay_kernel(plan, shard_ref, incoming_ref, *refs):
    chunk_refs = refs[: plan.half]
    first_ref, second_ref, sem = refs[plan.half :]
    client = shard_ref[0] ^ plan.half
    position = 0
    for distance, chunk_ref in enumerate(chunk_refs):
        owner = (shard_ref[0] % plan.half) ^ distance
        at = 0
        for index in range(plan.half):
            amount = incoming_ref[client, 0, plan.capacity + index]
            at = at + jnp.where(index < owner, amount, 0)

        def begin(index, carry, chunk_ref=chunk_ref, at=at):
            source = chunk_ref.at[index]

            @pl.when(at + index < plan.part)
            def _():
                pltpu.make_async_copy(source, first_ref.at[at + index], sem).start()

            @pl.when(at + index >= plan.part)
            def _():
                target = second_ref.at[at + index - plan.part]
                pltpu.make_async_copy(source, target, sem).start()

            return carry

        amount = incoming_ref[client, 0, plan.capacity + owner]
        lax.fori_loop(0, amount, begin, 0)
        position = position + amount

    def finish(index, carry):
        pltpu.make_async_copy(chunk_refs[0].at[0], first_ref.at[0], sem).wait()
        return carry

    lax.fori_loop(0, position, finish, 0)


def fetch(plan, where, source_refs, target_ref, sem):
    def among(low, high):
        if high - low == 1:
            source = source_refs[low].at[where - plan.starts[low]]
            pltpu.make_async_copy(source, target_ref, sem).start()
            return
        middle = (low + high) // 2

        @pl.when(where < plan.starts[middle])
        def _():
            among(low, middle)

        @pl.when(where >= plan.starts[middle])
        def _():
            among(middle, high)

    among(0, len(source_refs))


def bounds(plan, phase, info_ref, blocks):
    full = info_ref[1, 0]
    return (0, full) if phase == 0 else (full, blocks)


def pick_kernel(plan, phase, core_ref, info_ref, *refs):
    source_refs = refs[:-2]
    picked_ref, sem = refs[-2:]
    count = picked_ref.shape[0]
    start = (1 - core_ref[0]) * count
    group = 2 * BLOCK
    low, high = bounds(plan, phase, info_ref, count // group)

    def begin(step, carry):
        for index in range(group):
            where = info_ref[0, start + step * group + index]
            fetch(plan, where, source_refs, picked_ref.at[step * group + index], sem)
        return carry

    def finish(step, carry):
        span = pl.ds(0, group)
        pltpu.make_async_copy(source_refs[0].at[span], picked_ref.at[span], sem).wait()
        return carry

    lax.fori_loop(low, high, begin, 0)
    lax.fori_loop(low, high, finish, 0)


def compare_kernel(
    plan,
    phase,
    length,
    head_dim,
    core_ref,
    scale_ref,
    info_ref,
    far_ref,
    gain_attn_ref,
    gain_mlp_ref,
    bias_a_ref,
    bias_b_ref,
    *refs,
):
    if phase:
        earlier_ref, *refs = refs
    held_refs, source_refs = refs[:10], refs[10:-17]
    result_ref = refs[-17]
    matrix_refs = refs[-16:-6]
    own_ref, normed_ref, pooled_ref, hidden_ref, sems, matrix_sems = refs[-6:]
    qk_a_ref, qk_b_ref, value_a_ref, value_b_ref, out_a_ref, out_b_ref = matrix_refs[:6]
    in_a_ref, in_b_ref, back_a_ref, back_b_ref = matrix_refs[6:]
    loads = [
        pltpu.make_async_copy(held, ref, matrix_sems.at[k])
        for k, (held, ref) in enumerate(zip(held_refs, matrix_refs))
    ]
    group = 2 * BLOCK
    half = BLOCK * length
    rows = 2 * half
    blocks = own_ref.shape[0] // group
    low, high = bounds(plan, phase, info_ref, blocks)
    count = result_ref.shape[0]
    pair_dim = 2 * head_dim
    first = core_ref[0] == 0
    start = core_ref[0] * own_ref.shape[0]
    even = lax.broadcasted_iota(jnp.int32, (half, pair_dim), 1) < head_dim
    same = (
        lax.broadcasted_iota(jnp.int32, (half, half), 0) // length
        == lax.broadcasted_iota(jnp.int32, (half, half), 1) // length
    )
    row_pair = lax.broadcasted_iota(jnp.int32, (group, rows), 1) % half // length
    pool = jnp.where(row_pair == lax.broadcasted_iota(jnp.int32, (group, rows), 0), 1.0, 0.0)
    pool = pool.astype(jnp.bfloat16)

    def begin(step, carry):
        for index in range(group):
            at = step * group + index
            fetch(plan, info_ref[0, start + at], source_refs, own_ref.at[at], sems.at[step])
        return carry

    def split(values):
        zero = jnp.zeros_like(values)
        return jnp.concatenate(
            [jnp.where(even, values, zero), jnp.where(even, zero, values)], axis=0
        )

    ones = split(jnp.ones((half, pair_dim), jnp.bfloat16))

    def weigh(scores, factor):
        scores = jnp.where(same, scores, -1e30)
        top = jnp.max(scores, axis=1, keepdims=True)
        return jnp.exp2((scores - top) * factor).astype(jnp.bfloat16)

    def mix(query, value, here, there, factors):
        scores = dot_nt(query[here], split(query[there]))
        weights = [weigh(scores[:, k * half : (k + 1) * half], factors[k]) for k in range(2)]
        mixed = dot(
            jnp.concatenate(weights, axis=1), jnp.concatenate([split(value[there]), ones], axis=1)
        )
        total = mixed[:, pair_dim:]
        inverse = pl.reciprocal(total, approx=True)
        inverse = inverse * (2.0 - total * inverse)
        return (mixed[:, :pair_dim] * inverse).astype(jnp.bfloat16)

    def pair_rows(step):
        return pl.ds(pl.multiple_of(step * BLOCK, BLOCK), BLOCK)

    def attend(step, between):
        span = pl.ds(step * group, group)
        pltpu.make_async_copy(
            source_refs[0].at[pl.ds(0, group)], own_ref.at[span], sems.at[step]
        ).wait()
        own = own_ref[span].reshape(rows, -1).astype(jnp.float32)
        far = far_ref[span].reshape(rows, -1).astype(jnp.float32)
        hidden = jnp.concatenate(
            [jnp.where(first, own, far), jnp.where(first, far, own)], axis=1
        )
        normed = norm_rows(hidden, gain_attn_ref[...]).astype(jnp.bfloat16)
        between()
        head = 0
        for qk_ref, value_ref, out_ref in (
            (qk_a_ref, value_a_ref, out_a_ref),
            (qk_b_ref, value_b_ref, out_b_ref),
        ):
            query = dot(normed, qk_ref[...]).astype(jnp.bfloat16)
            value = dot(normed, value_ref[...]).astype(jnp.bfloat16)
            between()
            mixed = []
            for at in range(0, query.shape[1], pair_dim):
                factors = [scale_ref[head + k] * (LOG2E / head_dim**0.5) for k in range(2)]
                head += 2
                q = query[:, at : at + pair_dim]
                v = value[:, at : at + pair_dim]
                sides = [slice(0, half), slice(half, rows)]
                mixed.append(
                    jnp.concatenate(
                        [mix(q, v, sides[k], sides[1 - k], factors) for k in range(2)], axis=0
                    )
                )
                between()
            hidden = hidden + dot(jnp.concatenate(mixed, axis=1), out_ref[...])
        hidden_ref[pair_rows(step), :] = jnp.sum(
            hidden.reshape(2, BLOCK, length, -1), axis=(0, 2)
        )
        normed_ref[step % 2] = norm_rows(hidden, gain_mlp_ref[...]).astype(jnp.bfloat16)
        between()

    def expand(step):
        offset = 0
        for in_ref, bias_ref in ((in_a_ref, bias_a_ref), (in_b_ref, bias_b_ref)):
            units = in_ref.shape[1]
            tile = units // 4
            for at in range(0, units, tile):
                cut = slice(at, at + tile)
                inner = dot(normed_ref[step % 2], in_ref[:, cut]) + bias_ref[:, cut]
                inner = inner.astype(jnp.bfloat16)
                cubic = inner * inner * jnp.bfloat16(0.0356774081) + jnp.bfloat16(0.7978845608)
                bent = (jnp.tanh(inner * cubic) + jnp.bfloat16(1.0)) * inner
                pooled = dot(pool, bent)
                pooled_ref[pair_rows(step), offset + at : offset + at + tile] = pooled[:BLOCK]
                yield
            offset += units

    def run(steps):
        for _ in steps:
            pass

    @pl.when(high > low)
    def _():
        for load in loads[:4]:
            load.start()
        begin(low, 0)
        for load in loads[4:]:
            load.start()
        lax.fori_loop(low + 1, high, begin, 0)
        for load in loads[:6]:
            load.wait()
        attend(low, lambda: None)
        for load in loads[6:8]:
            load.wait()

        def block(step, carry):
            tiles = expand(step - 1)
            attend(step, lambda: next(tiles, None))
            run(tiles)
            return carry

        lax.fori_loop(low + 1, high, block, 0)
        run(expand(high - 1))
        for load in loads[8:]:
            load.wait()
        pooled = pooled_ref[...] * (0.25 / length)
        coarse = pooled.astype(jnp.bfloat16)
        fine = (pooled - coarse.astype(jnp.float32)).astype(jnp.bfloat16)
        both = jnp.concatenate([coarse, fine], axis=0)
        units = back_a_ref.shape[0]
        back = dot(both[:, :units], back_a_ref[...]) + dot(both[:, units:], back_b_ref[...])
        mean = hidden_ref[...] * (0.5 / length)
        result = (mean + back[:count] + back[count:]).astype(jnp.bfloat16)
        if phase:
            line = lax.broadcasted_iota(jnp.int32, result.shape, 0)
            done = line < low * BLOCK
            result = jnp.where(done, earlier_ref[...].astype(jnp.float32), result.astype(jnp.float32))
        result_ref[...] = result.astype(jnp.bfloat16)

    if phase:

        @pl.when(high <= low)
        def _():
            result_ref[...] = earlier_ref[...]


def seat_kernel(core_ref, seats_ref, here_ref, there_ref, result_ref):
    first = core_ref[0] == 0
    here = here_ref[...].astype(jnp.float32)
    there = there_ref[...].astype(jnp.float32)
    both = jnp.concatenate([jnp.where(first, here, there), jnp.where(first, there, here)], axis=0)
    result_ref[...] = dot(seats_ref[...], both.astype(jnp.bfloat16)).astype(jnp.bfloat16)


def on_device(
    image_tokens,
    pair_owner,
    pair_slot,
    gain_attn,
    w_qk,
    w_value,
    logit_scale,
    w_out,
    gain_mlp,
    w_in,
    bias_in,
    w_back,
):
    owner_count = lax.axis_size("shard")
    groups = lax.axis_size("groups")
    core = lax.axis_index("mp").reshape(1)
    shard = lax.axis_index("shard").reshape(1)
    pair_count = pair_owner.shape[0]
    _, length, features = image_tokens.shape
    width = 2 * features
    head_dim = w_qk.shape[1] // logit_scale.shape[0]
    mine = pair_count // 2
    plan = Plan(pair_count, owner_count)

    def swap(values):
        return lax.ppermute(values, "mp", [(0, 1), (1, 0)])

    def across(values, distance):
        return lax.ppermute(values, "shard", [(k, k ^ distance) for k in range(owner_count)])

    def images(count):
        return jax.ShapeDtypeStruct((count, length, features), jnp.bfloat16)

    smem = pl.BlockSpec(memory_space=pltpu.SMEM)
    vmem = pl.BlockSpec(memory_space=pltpu.VMEM)
    hbm = pl.BlockSpec(memory_space=pltpu.HBM)

    wanted, info, seats = pl.pallas_call(
        functools.partial(place_kernel, plan, pair_count),
        out_shape=(
            jax.ShapeDtypeStruct((owner_count, 1, plan.row), jnp.int32),
            jax.ShapeDtypeStruct((8, 2 * pair_count), jnp.int32),
            jax.ShapeDtypeStruct((pair_count, pair_count), jnp.bfloat16),
        ),
        in_specs=[smem, vmem, vmem],
    )(shard, pair_owner.T, pair_slot.T)
    incoming = lax.all_to_all(wanted, "shard", split_axis=0, concat_axis=0, tiled=True)
    second = None
    if plan.extra:
        served = pl.pallas_call(
            functools.partial(serve_far_kernel, plan),
            out_shape=[images(plan.extra)] * plan.half + [images(plan.base)] * plan.half,
            in_specs=[smem, smem, vmem],
        )(shard, incoming, image_tokens)
        chunks = [served[0]] + [across(served[k], k) for k in range(1, plan.half)]
        direct = [across(served[k], k) for k in range(plan.half, owner_count)]
        incoming_again, _ = lax.optimization_barrier((incoming, served[0]))
        near = pl.pallas_call(
            functools.partial(serve_near_kernel, plan),
            out_shape=[images(plan.capacity)] * plan.half,
            in_specs=[smem, smem, vmem],
        )(shard, incoming_again, image_tokens)
        near = [near[0]] + [across(near[k], k) for k in range(1, plan.half)]
        first, second = pl.pallas_call(
            functools.partial(relay_kernel, plan),
            out_shape=[images(plan.part)] * 2,
            in_specs=[smem, smem] + [hbm] * plan.half,
            scratch_shapes=[pltpu.SemaphoreType.DMA],
        )(shard, incoming, *chunks)
        first = across(first, plan.half)
        crowded = jnp.max(jnp.sum(incoming[:, 0, plan.capacity :], axis=1)) > plan.part
        crowded = crowded.astype(jnp.int32)
        passed = crowded
        for _ in range(groups - 1):
            passed = lax.ppermute(passed, "groups", [(k, (k + 1) % groups) for k in range(groups)])
            crowded = jnp.maximum(crowded, passed)
        second = lax.cond(
            crowded > 0, lambda part: across(part, plan.half), lambda part: part, second
        )
        sources = near + direct
    else:
        served = pl.pallas_call(
            functools.partial(serve_all_kernel, plan),
            out_shape=jax.ShapeDtypeStruct(
                (owner_count, plan.base, length, features), jnp.bfloat16
            ),
            in_specs=[smem, vmem],
        )(incoming, image_tokens)
        returned = lax.all_to_all(served, "shard", split_axis=0, concat_axis=0, tiled=True)
        sources = [returned.reshape(-1, length, features)]
    weights = (w_qk, w_value, w_out, w_in, w_back, bias_in, logit_scale)
    swapped = [swap(w) for w in weights]
    sources, swapped = lax.optimization_barrier((sources, swapped))
    far_qk, far_value, far_out, far_in, far_back, far_bias, far_scale = swapped
    scale = jnp.concatenate([logit_scale, far_scale])
    vectors = [v.reshape(1, -1) for v in (gain_attn, gain_mlp, bias_in, far_bias)]
    matrices = [w_qk, far_qk, w_value, far_value, w_out, far_out, w_in, far_in, w_back, far_back]
    units = 2 * w_in.shape[1]

    def compare(phase, sources, earlier):
        picked = pl.pallas_call(
            functools.partial(pick_kernel, plan, phase),
            out_shape=images(pair_count),
            in_specs=[smem, smem] + [hbm] * len(sources),
            scratch_shapes=[pltpu.SemaphoreType.DMA],
        )(core, info, *sources)
        far = swap(picked)
        flops = 2 * mine * length * width * (3 * width + units)
        return pl.pallas_call(
            functools.partial(compare_kernel, plan, phase, length, head_dim),
            out_shape=jax.ShapeDtypeStruct((mine, width), jnp.bfloat16),
            in_specs=[smem] * 3 + [vmem] * (5 + len(earlier)) + [hbm] * (10 + len(sources)),
            out_specs=vmem,
            scratch_shapes=[pltpu.VMEM(m.shape, m.dtype) for m in matrices]
            + [
                pltpu.VMEM((pair_count, length, features), jnp.bfloat16),
                pltpu.VMEM((2, 2 * BLOCK * length, width), jnp.bfloat16),
                pltpu.VMEM((mine, units), jnp.float32),
                pltpu.VMEM((mine, width), jnp.float32),
                pltpu.SemaphoreType.DMA((mine // BLOCK,)),
                pltpu.SemaphoreType.DMA((10,)),
            ],
            compiler_params=pltpu.CompilerParams(vmem_limit_bytes=32 * 2**20),
            cost_estimate=pl.CostEstimate(
                flops=flops, bytes_accessed=8 * 2**20, transcendentals=mine * length * units
            ),
        )(core, scale, info, far, *vectors, *earlier, *matrices, *sources)

    if plan.extra:
        results = compare(0, sources, [])
        results = compare(1, sources + [first, second], [results])
    else:
        results = compare(1, sources, [jnp.zeros((mine, width), jnp.bfloat16)])
    return pl.pallas_call(
        seat_kernel,
        out_shape=jax.ShapeDtypeStruct((pair_count, width), jnp.bfloat16),
        in_specs=[smem, vmem, vmem, vmem],
    )(core, seats, results, swap(results))


def solution(mesh):
    in_specs = (
        P(("groups", "shard"), None, "mp"),
        P(("groups", "shard"), None),
        P(("groups", "shard"), None),
        P(),
        P(None, "mp"),
        P(None, "mp"),
        P("mp"),
        P("mp", None),
        P(),
        P(None, "mp"),
        P("mp"),
        P("mp", None),
    )
    out_specs = P(("groups", "shard"), None)
    return jax.shard_map(
        on_device, mesh=mesh, in_specs=in_specs, out_specs=out_specs, check_vma=False
    )
```

```python
import functools

import jax
import jax.numpy as jnp
from jax import lax
from jax.experimental import pallas as pl
from jax.experimental.pallas import tpu as pltpu
from jax.sharding import PartitionSpec as P

LOG2E = 1.4426950408889634
BLOCK = 8


def norm_rows(values, gain):
    center = values - jnp.mean(values, axis=-1, keepdims=True)
    spread = jnp.mean(center * center, axis=-1, keepdims=True)
    return center * lax.rsqrt(spread + 1e-05) * gain


def dot_nt(a, b):
    return lax.dot_general(a, b, (((1,), (1,)), ((), ())), preferred_element_type=jnp.float32)


def dot(a, b):
    return jnp.dot(a, b, preferred_element_type=jnp.float32)


class Plan:
    def __init__(self, pair_count, owner_count):
        self.owners = owner_count
        self.capacity = max(2, 4 * pair_count // owner_count)
        self.half = owner_count // 2
        split = self.capacity >= 32 and self.half & (self.half - 1) == 0 and self.half > 0
        self.base = self.capacity // 2 if split else self.capacity
        self.extra = self.capacity - self.base
        self.part = self.half * self.extra // 2
        self.near_at = owner_count * self.base
        self.rest_at = self.near_at + self.half * self.extra
        self.slots = self.rest_at + 2 * self.part
        self.row = self.capacity + (self.half if split else 0)


def place_kernel(plan, count, shard_ref, owner_ref, slot_ref, wanted_ref, list_ref):
    total = 2 * count
    owners = plan.owners
    owner = jnp.concatenate([owner_ref[0:1, :], owner_ref[1:2, :]], axis=1)
    slot = jnp.concatenate([slot_ref[0:1, :], slot_ref[1:2, :]], axis=1)

    def place(dim, size):
        return lax.broadcasted_iota(jnp.int32, (size, total), dim)

    def as_bf16(values):
        return values.astype(jnp.float32).astype(jnp.bfloat16)

    row = place(0, owners)
    named = row == owner
    until = as_bf16(jnp.where(place(0, total) <= place(1, total), 1, 0))
    tally = dot(as_bf16(jnp.where(named, 1, 0)), until).astype(jnp.int32)
    rank = jnp.sum(jnp.where(named, tally, 0), axis=0, keepdims=True) - 1
    ranked = as_bf16(jnp.where(place(0, total) == rank, 1, 0))
    wanted = dot_nt(as_bf16(jnp.where(named, slot, 0)), ranked).astype(jnp.int32)
    where = owner * plan.base + rank
    if plan.extra:
        me = shard_ref[0]
        half = plan.half
        over = jnp.maximum(jnp.max(tally, axis=1, keepdims=True) - plan.base, 0)
        far_over = jnp.where(row // half != me // half, over, 0)
        before = jnp.zeros((owners, total), jnp.int32)
        for index in range(owners - 1):
            before = before + jnp.where(row > index, far_over[index : index + 1], 0)
        before = jnp.sum(jnp.where(named, before, 0), axis=0, keepdims=True)
        rest = rank - plan.base
        near = plan.near_at + ((owner % half) ^ (me % half)) * plan.extra + rest
        late = jnp.where(owner // half == me // half, near, plan.rest_at + before + rest)
        where = jnp.where(rest < 0, where, late)
        told = place(1, owners) == plan.capacity + row % half
        wanted = wanted + jnp.sum(jnp.where(told, far_over, 0), axis=0, keepdims=True)
    for index in range(owners):
        wanted_ref[index] = wanted[index : index + 1, : plan.row]
    entry = place(1, 1)
    side = entry // count
    pair = entry % count
    mine = count // 2
    local = pair % mine
    position = pair // mine * count + local // BLOCK * (2 * BLOCK) + side * BLOCK + local % BLOCK
    seated = as_bf16(jnp.where(place(0, total) == position, 1, 0))
    parts = as_bf16(jnp.where(place(0, 8) == 0, where // 16, where % 16))
    listed = dot_nt(parts, seated).astype(jnp.int32)
    list_ref[...] = listed[0:1] * 16 + listed[1:2]


def serve(tokens_ref, incoming_ref, requester, start, served_ref):
    count = served_ref.shape[0]

    def copy(index, carry):
        served_ref[index] = tokens_ref[incoming_ref[requester, 0, start + index]]
        return carry

    lax.fori_loop(0, count, copy, 0, unroll=min(16, count))


def serve_relays_kernel(plan, shard_ref, incoming_ref, tokens_ref, *served_refs):
    for distance, served_ref in enumerate(served_refs):
        requester = shard_ref[0] ^ (distance + plan.half)
        serve(tokens_ref, incoming_ref, requester, plan.base, served_ref)


def serve_kernel(plan, shard_ref, incoming_ref, tokens_ref, served_ref, *near_refs):
    for requester in range(plan.owners):
        serve(tokens_ref, incoming_ref, requester, 0, served_ref.at[requester])
    for distance, near_ref in enumerate(near_refs):
        serve(tokens_ref, incoming_ref, shard_ref[0] ^ distance, plan.base, near_ref)


def relay_kernel(plan, shard_ref, incoming_ref, *refs):
    chunk_refs = refs[: plan.half]
    first_ref, second_ref = refs[plan.half :]
    client = shard_ref[0] ^ plan.half
    for distance, chunk_ref in enumerate(chunk_refs):
        owner = (shard_ref[0] % plan.half) ^ distance
        at = 0
        for index in range(plan.half):
            amount = incoming_ref[client, 0, plan.capacity + index]
            at = at + jnp.where(index < owner, amount, 0)
        amount = incoming_ref[client, 0, plan.capacity + owner]
        fit = jnp.clip(plan.part - at, 0, amount)

        def pack(index, carry, chunk_ref=chunk_ref, at=at):
            first_ref[at + index] = chunk_ref[index]
            return carry

        def pack_more(index, carry, chunk_ref=chunk_ref, at=at):
            second_ref[at + index - plan.part] = chunk_ref[index]
            return carry

        lax.fori_loop(0, fit, pack, 0)
        lax.fori_loop(fit, amount, pack_more, 0)


def pick_kernel(plan, core_ref, list_ref, *refs):
    source_refs = refs[:-4]
    own_ref, other_ref, held_ref, sems = refs[-4:]
    count = own_ref.shape[0]
    at = 0
    loads = []
    for index, source_ref in enumerate(source_refs):
        size = source_ref.shape[0]
        loads.append(
            pltpu.make_async_copy(source_ref, held_ref.at[pl.ds(at, size)], sems.at[index])
        )
        at += size
    for load in loads:
        load.start()
    for load in loads:
        load.wait()
    start = core_ref[0] * count

    def pick(index, carry):
        other_ref[index] = held_ref[list_ref[0, count - start + index]]
        own_ref[index] = held_ref[list_ref[0, start + index]]
        return carry

    lax.fori_loop(0, count, pick, 0, unroll=8)


def compare_kernel(
    length,
    head_dim,
    core_ref,
    scale_ref,
    own_ref,
    far_ref,
    gain_attn_ref,
    gain_mlp_ref,
    *refs,
):
    held_refs = refs[:12]
    result_ref, qkv_ref, out_ref, in_ref, back_ref, bias_ref = refs[12:18]
    normed_ref, heads_ref, mixed_ref, hidden_ref, pooled_ref, mean_ref, sems = refs[18:]
    depth, units = in_ref.shape
    width = depth
    wide = width // 2
    homes = [qkv_ref.at[:, pl.ds(k * wide, wide)] for k in range(4)]
    homes += [out_ref.at[pl.ds(k * wide, wide)] for k in range(2)]
    homes += [in_ref.at[:, pl.ds(k * units // 2, units // 2)] for k in range(2)]
    homes += [bias_ref.at[:, pl.ds(k * units // 2, units // 2)] for k in range(2)]
    homes += [back_ref.at[pl.ds(k * units // 2, units // 2)] for k in range(2)]
    loads = [
        pltpu.make_async_copy(held, home, sems.at[k])
        for k, (held, home) in enumerate(zip(held_refs, homes))
    ]
    for load in loads:
        load.start()
    half = BLOCK * length
    rows = 2 * half
    blocks = own_ref.shape[0] // (2 * BLOCK)
    count = result_ref.shape[0]
    long = 2 * rows
    tile = 256
    pair_dim = 2 * head_dim
    first = core_ref[0] == 0
    even = lax.broadcasted_iota(jnp.int32, (half, pair_dim), 1) < head_dim
    same = (
        lax.broadcasted_iota(jnp.int32, (half, half), 0) // length
        == lax.broadcasted_iota(jnp.int32, (half, half), 1) // length
    )
    row = lax.broadcasted_iota(jnp.int32, (2 * BLOCK, long), 1)
    row_pair = row // rows * BLOCK + row % half // length
    pool = jnp.where(row_pair == lax.broadcasted_iota(jnp.int32, row.shape, 0), 1.0, 0.0)
    pool = pool.astype(jnp.bfloat16)

    def span(step, size):
        return pl.ds(pl.multiple_of(step * size, size), size)

    def split(values):
        zero = jnp.zeros_like(values)
        return jnp.concatenate(
            [jnp.where(even, values, zero), jnp.where(even, zero, values)], axis=0
        )

    ones = split(jnp.ones((half, pair_dim), jnp.bfloat16))

    def start_block(step, carry):
        images = pl.ds(step * 2 * BLOCK, 2 * BLOCK)
        own = own_ref[images].reshape(rows, -1).astype(jnp.float32)
        far = far_ref[images].reshape(rows, -1).astype(jnp.float32)
        tokens = jnp.concatenate([jnp.where(first, own, far), jnp.where(first, far, own)], axis=1)
        hidden_ref[span(step, rows), :] = tokens
        normed_ref[span(step, rows), :] = norm_rows(tokens, gain_attn_ref[...]).astype(jnp.bfloat16)
        return carry

    def project(step, carry):
        here = span(step // 4, long)
        cut = span(step % 4, 2 * width // 4)
        heads_ref[here, cut] = dot(normed_ref[here, :], qkv_ref[:, cut]).astype(jnp.bfloat16)
        return carry

    def weigh(scores, factor):
        scores = jnp.where(same, scores, -1e30)
        top = jnp.max(scores, axis=1, keepdims=True)
        return jnp.exp2((scores - top) * factor).astype(jnp.bfloat16)

    def mix(query, key, value, factors):
        scores = dot_nt(query, split(key))
        weights = [weigh(scores[:, k * half : (k + 1) * half], factors[k]) for k in range(2)]
        mixed = dot(jnp.concatenate(weights, axis=1), jnp.concatenate([split(value), ones], axis=1))
        total = mixed[:, pair_dim:]
        inverse = pl.reciprocal(total, approx=True)
        inverse = inverse * (2.0 - total * inverse)
        return (mixed[:, :pair_dim] * inverse).astype(jnp.bfloat16)

    def attend(step, carry):
        for index in range(width // pair_dim):
            factors = [scale_ref[2 * index + k] * (LOG2E / head_dim**0.5) for k in range(2)]
            cut = slice(index * pair_dim, (index + 1) * pair_dim)
            beyond = slice(width + cut.start, width + cut.stop)
            sides = [span(2 * step + k, half) for k in range(2)]
            query = [heads_ref[side, cut] for side in sides]
            value = [heads_ref[side, beyond] for side in sides]
            for k in range(2):
                mixed_ref[sides[k], cut] = mix(query[k], query[1 - k], value[1 - k], factors)
        return carry

    def join(step, carry):
        here = span(step // 2, long)
        cut = span(step % 2, width // 2)
        hidden_ref[here, cut] += dot(mixed_ref[here, :], out_ref[:, cut])
        return carry

    def middle_block(step, carry):
        here = span(step, rows)
        hidden = hidden_ref[here, :]
        mean_ref[span(step, BLOCK), :] = jnp.sum(
            hidden.reshape(2, BLOCK, length, -1), axis=(0, 2)
        )
        normed_ref[here, :] = norm_rows(hidden, gain_mlp_ref[...]).astype(jnp.bfloat16)
        return carry

    def expand(step, carry):
        tiles = units // tile
        here = span(step // tiles, long)
        cut = span(step % tiles, tile)
        inner = dot(normed_ref[here, :], in_ref[:, cut]) + bias_ref[:, cut]
        inner = inner.astype(jnp.bfloat16)
        cubic = inner * inner * jnp.bfloat16(0.0356774081) + jnp.bfloat16(0.7978845608)
        bent = (jnp.tanh(inner * cubic) + jnp.bfloat16(1.0)) * inner
        pooled_ref[span(step // tiles, 2 * BLOCK), cut] = dot(pool, bent)
        return carry

    lax.fori_loop(0, blocks, start_block, 0)
    for load in loads[:4]:
        load.wait()
    lax.fori_loop(0, blocks // 2 * 4, project, 0)
    lax.fori_loop(0, blocks, attend, 0)
    for load in loads[4:6]:
        load.wait()
    lax.fori_loop(0, blocks // 2 * 2, join, 0)
    lax.fori_loop(0, blocks, middle_block, 0)
    for load in loads[6:10]:
        load.wait()
    lax.fori_loop(0, blocks // 2 * (units // tile), expand, 0)
    for load in loads[10:]:
        load.wait()
    pooled = pooled_ref[...] * (0.25 / length)
    coarse = pooled.astype(jnp.bfloat16)
    fine = (pooled - coarse.astype(jnp.float32)).astype(jnp.bfloat16)
    back = dot(jnp.concatenate([coarse, fine], axis=0), back_ref[...])
    mean = mean_ref[...] * (0.5 / length)
    result_ref[...] = (mean + back[:count] + back[count:]).astype(jnp.bfloat16)


def on_device(
    image_tokens,
    pair_owner,
    pair_slot,
    gain_attn,
    w_qk,
    w_value,
    logit_scale,
    w_out,
    gain_mlp,
    w_in,
    bias_in,
    w_back,
):
    owner_count = lax.axis_size("shard")
    groups = lax.axis_size("groups")
    core = lax.axis_index("mp").reshape(1)
    shard = lax.axis_index("shard").reshape(1)
    pair_count = pair_owner.shape[0]
    _, length, features = image_tokens.shape
    width = 2 * features
    head_dim = w_qk.shape[1] // logit_scale.shape[0]
    mine = pair_count // 2
    units = 2 * w_in.shape[1]
    plan = Plan(pair_count, owner_count)

    def swap(values):
        return lax.ppermute(values, "mp", [(0, 1), (1, 0)])

    def across(values, distance):
        return lax.ppermute(values, "shard", [(k, k ^ distance) for k in range(owner_count)])

    def images(*counts):
        return jax.ShapeDtypeStruct((*counts, length, features), jnp.bfloat16)

    smem = pl.BlockSpec(memory_space=pltpu.SMEM)
    vmem = pl.BlockSpec(memory_space=pltpu.VMEM)
    hbm = pl.BlockSpec(memory_space=pl.ANY)
    roomy = pltpu.CompilerParams(vmem_limit_bytes=56 * 2**20)

    wanted, order = pl.pallas_call(
        functools.partial(place_kernel, plan, pair_count),
        out_shape=(
            jax.ShapeDtypeStruct((owner_count, 1, plan.row), jnp.int32),
            jax.ShapeDtypeStruct((1, 2 * pair_count), jnp.int32),
        ),
        in_specs=[smem, vmem, vmem],
    )(shard, pair_owner.T, pair_slot.T)
    incoming = lax.all_to_all(wanted, "shard", split_axis=0, concat_axis=0, tiled=True)
    if plan.extra:
        chunks = pl.pallas_call(
            functools.partial(serve_relays_kernel, plan),
            out_shape=[images(plan.extra)] * plan.half,
            in_specs=[smem, smem, vmem],
        )(shard, incoming, image_tokens)
        incoming, chunks = lax.optimization_barrier((incoming, chunks))
        chunks = [chunks[0]] + [across(chunks[k], k) for k in range(1, plan.half)]
    served, *near = pl.pallas_call(
        functools.partial(serve_kernel, plan),
        out_shape=[images(owner_count, plan.base)]
        + [images(plan.extra)] * (plan.half if plan.extra else 0),
        in_specs=[smem, smem, vmem],
    )(shard, incoming, image_tokens)
    if plan.extra:
        served, near, chunks = lax.optimization_barrier((served, near, chunks))
    returned = lax.all_to_all(served, "shard", split_axis=0, concat_axis=0, tiled=True)
    sources = [returned.reshape(-1, length, features)]
    if plan.extra:
        first, second = pl.pallas_call(
            functools.partial(relay_kernel, plan),
            out_shape=[images(plan.part)] * 2,
            in_specs=[smem, smem] + [vmem] * plan.half,
        )(shard, incoming, *chunks)
        first = across(first, plan.half)
        near = [near[0]] + [across(near[k], k) for k in range(1, plan.half)]
        crowded = jnp.max(jnp.sum(incoming[:, 0, plan.capacity :], axis=1)) > plan.part
        crowded = crowded.astype(jnp.int32)
        passed = crowded
        for _ in range(groups - 1):
            passed = lax.ppermute(passed, "groups", [(k, (k + 1) % groups) for k in range(groups)])
            crowded = jnp.maximum(crowded, passed)
        second = lax.cond(
            crowded > 0, lambda part: across(part, plan.half), lambda part: part, second
        )
        sources += [*near, first, second]
    weights = (w_qk, w_value, w_out, w_in, w_back, bias_in, logit_scale)
    swapped = [swap(w) for w in weights]
    sources, swapped = lax.optimization_barrier((sources, swapped))
    far_qk, far_value, far_out, far_in, far_back, far_bias, far_scale = swapped
    own, other = pl.pallas_call(
        functools.partial(pick_kernel, plan),
        out_shape=[images(pair_count)] * 2,
        in_specs=[smem, smem] + [hbm] * len(sources),
        scratch_shapes=[
            pltpu.VMEM((plan.slots, length, features), jnp.bfloat16),
            pltpu.SemaphoreType.DMA((len(sources),)),
        ],
        compiler_params=roomy,
    )(core, order, *sources)
    far = swap(other)

    matrices = [w_qk, far_qk, w_value, far_value, w_out, far_out, w_in, far_in]
    matrices += [bias_in.reshape(1, -1), far_bias.reshape(1, -1), w_back, far_back]
    token_count = pair_count * length
    flops = 2 * token_count * width * (3 * width + units)
    here = pl.pallas_call(
        functools.partial(compare_kernel, length, head_dim),
        out_shape=jax.ShapeDtypeStruct((mine, width), jnp.bfloat16),
        in_specs=[smem] * 2 + [vmem] * 4 + [hbm] * 12,
        out_specs=vmem,
        scratch_shapes=[
            pltpu.VMEM((width, 2 * width), jnp.bfloat16),
            pltpu.VMEM((width, width), jnp.bfloat16),
            pltpu.VMEM((width, units), jnp.bfloat16),
            pltpu.VMEM((units, width), jnp.bfloat16),
            pltpu.VMEM((1, units), jnp.float32),
            pltpu.VMEM((token_count, width), jnp.bfloat16),
            pltpu.VMEM((token_count, 2 * width), jnp.bfloat16),
            pltpu.VMEM((token_count, width), jnp.bfloat16),
            pltpu.VMEM((token_count, width), jnp.float32),
            pltpu.VMEM((mine, units), jnp.float32),
            pltpu.VMEM((mine, width), jnp.float32),
            pltpu.SemaphoreType.DMA((12,)),
        ],
        compiler_params=roomy,
        cost_estimate=pl.CostEstimate(
            flops=flops, bytes_accessed=8 * 2**20, transcendentals=token_count * units
        ),
    )(
        core,
        jnp.concatenate([logit_scale, far_scale]),
        own,
        far,
        gain_attn.reshape(1, -1),
        gain_mlp.reshape(1, -1),
        *matrices,
    )
    there = swap(here)
    low = jnp.where(core == 0, here, there)
    high = jnp.where(core == 0, there, here)
    return jnp.concatenate([low, high], axis=0)


def solution(mesh):
    in_specs = (
        P(("groups", "shard"), None, "mp"),
        P(("groups", "shard"), None),
        P(("groups", "shard"), None),
        P(),
        P(None, "mp"),
        P(None, "mp"),
        P("mp"),
        P("mp", None),
        P(),
        P(None, "mp"),
        P("mp"),
        P("mp", None),
    )
    out_specs = P(("groups", "shard"), None)
    return jax.shard_map(
        on_device, mesh=mesh, in_specs=in_specs, out_specs=out_specs, check_vma=False
    )
```

```python
import functools

import jax
import jax.numpy as jnp
from jax import lax
from jax.experimental import pallas as pl
from jax.experimental.pallas import tpu as pltpu
from jax.sharding import PartitionSpec as P

LOG2E = 1.4426950408889634
BLOCK = 8


def norm_rows(values, gain):
    center = values - jnp.mean(values, axis=-1, keepdims=True)
    spread = jnp.mean(center * center, axis=-1, keepdims=True)
    return center * lax.rsqrt(spread + 1e-05) * gain


def dot_nt(a, b):
    return lax.dot_general(a, b, (((1,), (1,)), ((), ())), preferred_element_type=jnp.float32)


def dot(a, b):
    return jnp.dot(a, b, preferred_element_type=jnp.float32)


class Plan:
    def __init__(self, pair_count, owner_count):
        self.owners = owner_count
        self.capacity = max(2, 4 * pair_count // owner_count)
        self.half = owner_count // 2
        split = self.capacity >= 32 and self.half & (self.half - 1) == 0 and self.half > 0
        self.base = self.capacity // 2 if split else self.capacity
        self.extra = self.capacity - self.base
        self.part = self.half * self.extra // 2
        self.near_at = owner_count * self.base
        self.rest_at = self.near_at + self.half * self.extra
        self.slots = self.rest_at + 2 * self.part
        self.row = self.capacity + (self.half if split else 0)


def place_kernel(plan, count, shard_ref, owner_ref, slot_ref, wanted_ref, list_ref):
    total = 2 * count
    owners = plan.owners
    owner = jnp.concatenate([owner_ref[0:1, :], owner_ref[1:2, :]], axis=1)
    slot = jnp.concatenate([slot_ref[0:1, :], slot_ref[1:2, :]], axis=1)

    def place(dim, size):
        return lax.broadcasted_iota(jnp.int32, (size, total), dim)

    def as_bf16(values):
        return values.astype(jnp.float32).astype(jnp.bfloat16)

    row = place(0, owners)
    named = row == owner
    until = as_bf16(jnp.where(place(0, total) <= place(1, total), 1, 0))
    tally = dot(as_bf16(jnp.where(named, 1, 0)), until).astype(jnp.int32)
    rank = jnp.sum(jnp.where(named, tally, 0), axis=0, keepdims=True) - 1
    ranked = as_bf16(jnp.where(place(0, total) == rank, 1, 0))
    wanted = dot_nt(as_bf16(jnp.where(named, slot, 0)), ranked).astype(jnp.int32)
    where = owner * plan.base + rank
    if plan.extra:
        me = shard_ref[0]
        half = plan.half
        over = jnp.maximum(jnp.max(tally, axis=1, keepdims=True) - plan.base, 0)
        far_over = jnp.where(row // half != me // half, over, 0)
        before = jnp.zeros((owners, total), jnp.int32)
        for index in range(owners - 1):
            before = before + jnp.where(row > index, far_over[index : index + 1], 0)
        before = jnp.sum(jnp.where(named, before, 0), axis=0, keepdims=True)
        rest = rank - plan.base
        near = plan.near_at + ((owner % half) ^ (me % half)) * plan.extra + rest
        late = jnp.where(owner // half == me // half, near, plan.rest_at + before + rest)
        where = jnp.where(rest < 0, where, late)
        told = place(1, owners) == plan.capacity + row % half
        wanted = wanted + jnp.sum(jnp.where(told, far_over, 0), axis=0, keepdims=True)
    for index in range(owners):
        wanted_ref[index] = wanted[index : index + 1, : plan.row]
    entry = place(1, 1)
    side = entry // count
    pair = entry % count
    mine = count // 2
    local = pair % mine
    position = pair // mine * count + local // BLOCK * (2 * BLOCK) + side * BLOCK + local % BLOCK
    seated = as_bf16(jnp.where(place(0, total) == position, 1, 0))
    parts = as_bf16(jnp.where(place(0, 8) == 0, where // 16, where % 16))
    listed = dot_nt(parts, seated).astype(jnp.int32)
    list_ref[...] = listed[0:1] * 16 + listed[1:2]


def serve(tokens_ref, incoming_ref, requester, start, served_ref):
    count = served_ref.shape[0]

    def copy(index, carry):
        served_ref[index] = tokens_ref[incoming_ref[requester, 0, start + index]]
        return carry

    lax.fori_loop(0, count, copy, 0, unroll=min(16, count))


def serve_relays_kernel(plan, shard_ref, incoming_ref, tokens_ref, *served_refs):
    for distance, served_ref in enumerate(served_refs):
        requester = shard_ref[0] ^ (distance + plan.half)
        serve(tokens_ref, incoming_ref, requester, plan.base, served_ref)


def serve_kernel(plan, shard_ref, incoming_ref, tokens_ref, served_ref, *near_refs):
    for requester in range(plan.owners):
        serve(tokens_ref, incoming_ref, requester, 0, served_ref.at[requester])
    for distance, near_ref in enumerate(near_refs):
        serve(tokens_ref, incoming_ref, shard_ref[0] ^ distance, plan.base, near_ref)


def relay_kernel(plan, shard_ref, incoming_ref, *refs):
    chunk_refs = refs[: plan.half]
    first_ref, second_ref = refs[plan.half :]
    client = shard_ref[0] ^ plan.half
    for distance, chunk_ref in enumerate(chunk_refs):
        owner = (shard_ref[0] % plan.half) ^ distance
        at = 0
        for index in range(plan.half):
            amount = incoming_ref[client, 0, plan.capacity + index]
            at = at + jnp.where(index < owner, amount, 0)
        amount = incoming_ref[client, 0, plan.capacity + owner]
        fit = jnp.clip(plan.part - at, 0, amount)

        def pack(index, carry, chunk_ref=chunk_ref, at=at):
            first_ref[at + index] = chunk_ref[index]
            return carry

        def pack_more(index, carry, chunk_ref=chunk_ref, at=at):
            second_ref[at + index - plan.part] = chunk_ref[index]
            return carry

        lax.fori_loop(0, fit, pack, 0)
        lax.fori_loop(fit, amount, pack_more, 0)


def pick_kernel(core_ref, list_ref, *refs):
    source_refs = refs[:-3]
    picked_ref, held_ref, sems = refs[-3:]
    count = picked_ref.shape[0]
    at = 0
    loads = []
    for index, source_ref in enumerate(source_refs):
        size = source_ref.shape[0]
        loads.append(
            pltpu.make_async_copy(source_ref, held_ref.at[pl.ds(at, size)], sems.at[index])
        )
        at += size
    for load in loads:
        load.start()
    for load in loads:
        load.wait()
    start = core_ref[0] * count

    def pick(index, carry):
        picked_ref[index] = held_ref[list_ref[0, start + index]]
        return carry

    lax.fori_loop(0, count, pick, 0, unroll=16)


def attention_kernel(
    length,
    head_dim,
    core_ref,
    scale_ref,
    own_ref,
    far_ref,
    gain_attn_ref,
    gain_mlp_ref,
    *refs,
):
    held_refs = refs[:6]
    normed_ref, mean_ref, qkv_ref, out_ref = refs[6:10]
    heads_ref, mixed_ref, hidden_ref, sems = refs[10:]
    width = out_ref.shape[0]
    wide = width // 2
    homes = [qkv_ref.at[:, pl.ds(k * wide, wide)] for k in range(4)]
    homes += [out_ref.at[pl.ds(k * wide, wide)] for k in range(2)]
    loads = [
        pltpu.make_async_copy(held, home, sems.at[k])
        for k, (held, home) in enumerate(zip(held_refs, homes))
    ]
    for load in loads:
        load.start()
    half = BLOCK * length
    rows = 2 * half
    blocks = own_ref.shape[0] // (2 * BLOCK)
    long = 2 * rows
    pair_dim = 2 * head_dim
    first = core_ref[0] == 0
    even = lax.broadcasted_iota(jnp.int32, (half, pair_dim), 1) < head_dim
    same = (
        lax.broadcasted_iota(jnp.int32, (half, half), 0) // length
        == lax.broadcasted_iota(jnp.int32, (half, half), 1) // length
    )
    def span(step, size):
        return pl.ds(pl.multiple_of(step * size, size), size)

    def split(values):
        zero = jnp.zeros_like(values)
        return jnp.concatenate(
            [jnp.where(even, values, zero), jnp.where(even, zero, values)], axis=0
        )

    ones = split(jnp.ones((half, pair_dim), jnp.bfloat16))

    def start_block(step, carry):
        images = pl.ds(step * 2 * BLOCK, 2 * BLOCK)
        own = own_ref[images].reshape(rows, -1).astype(jnp.float32)
        far = far_ref[images].reshape(rows, -1).astype(jnp.float32)
        tokens = jnp.concatenate([jnp.where(first, own, far), jnp.where(first, far, own)], axis=1)
        hidden_ref[span(step, rows), :] = tokens
        normed_ref[span(step, rows), :] = norm_rows(tokens, gain_attn_ref[...]).astype(jnp.bfloat16)
        return carry

    def project(step, carry):
        here = span(step // 4, long)
        cut = span(step % 4, 2 * width // 4)
        heads_ref[here, cut] = dot(normed_ref[here, :], qkv_ref[:, cut]).astype(jnp.bfloat16)
        return carry

    def weigh(scores, factor):
        scores = jnp.where(same, scores, -1e30)
        top = jnp.max(scores, axis=1, keepdims=True)
        return jnp.exp2((scores - top) * factor).astype(jnp.bfloat16)

    def mix(query, key, value, factors):
        scores = dot_nt(query, split(key))
        weights = [weigh(scores[:, k * half : (k + 1) * half], factors[k]) for k in range(2)]
        mixed = dot(jnp.concatenate(weights, axis=1), jnp.concatenate([split(value), ones], axis=1))
        total = mixed[:, pair_dim:]
        inverse = pl.reciprocal(total, approx=True)
        inverse = inverse * (2.0 - total * inverse)
        return (mixed[:, :pair_dim] * inverse).astype(jnp.bfloat16)

    def attend(step, carry):
        for index in range(width // pair_dim):
            factors = [scale_ref[2 * index + k] * (LOG2E / head_dim**0.5) for k in range(2)]
            cut = slice(index * pair_dim, (index + 1) * pair_dim)
            beyond = slice(width + cut.start, width + cut.stop)
            sides = [span(2 * step + k, half) for k in range(2)]
            query = [heads_ref[side, cut] for side in sides]
            value = [heads_ref[side, beyond] for side in sides]
            for k in range(2):
                mixed_ref[sides[k], cut] = mix(query[k], query[1 - k], value[1 - k], factors)
        return carry

    def join(step, carry):
        here = span(step // 2, long)
        cut = span(step % 2, width // 2)
        hidden_ref[here, cut] += dot(mixed_ref[here, :], out_ref[:, cut])
        return carry

    def middle_block(step, carry):
        here = span(step, rows)
        hidden = hidden_ref[here, :]
        mean_ref[span(step, BLOCK), :] = jnp.sum(
            hidden.reshape(2, BLOCK, length, -1), axis=(0, 2)
        )
        normed_ref[here, :] = norm_rows(hidden, gain_mlp_ref[...]).astype(jnp.bfloat16)
        return carry

    lax.fori_loop(0, blocks, start_block, 0)
    for load in loads[:4]:
        load.wait()
    lax.fori_loop(0, blocks // 2 * 4, project, 0)
    lax.fori_loop(0, blocks, attend, 0)
    for load in loads[4:6]:
        load.wait()
    lax.fori_loop(0, blocks // 2 * 2, join, 0)
    lax.fori_loop(0, blocks, middle_block, 0)


def back_kernel(length, mean_ref, pooled_a_ref, pooled_b_ref, back_a_ref, back_b_ref, result_ref):
    count = mean_ref.shape[0]

    def spread(pooled_ref):
        pooled = pooled_ref[...] * (0.5 / length)
        coarse = pooled.astype(jnp.bfloat16)
        fine = (pooled - coarse.astype(jnp.float32)).astype(jnp.bfloat16)
        return jnp.concatenate([coarse, fine], axis=0)

    back = dot(spread(pooled_a_ref), back_a_ref[...]) + dot(spread(pooled_b_ref), back_b_ref[...])
    mean = mean_ref[...] * (0.5 / length)
    result_ref[...] = (mean + back[:count] + back[count:]).astype(jnp.bfloat16)


def expand(normed, w_in, bias, length):
    inner = dot(normed, w_in) + bias
    inner = jax.nn.gelu(inner, approximate=True).astype(jnp.bfloat16).astype(jnp.float32)
    inner = inner.reshape(-1, 2, BLOCK, length, inner.shape[-1])
    return jnp.sum(inner, axis=(1, 3)).reshape(-1, inner.shape[-1])


def on_device(
    image_tokens,
    pair_owner,
    pair_slot,
    gain_attn,
    w_qk,
    w_value,
    logit_scale,
    w_out,
    gain_mlp,
    w_in,
    bias_in,
    w_back,
):
    owner_count = lax.axis_size("shard")
    groups = lax.axis_size("groups")
    core = lax.axis_index("mp").reshape(1)
    shard = lax.axis_index("shard").reshape(1)
    pair_count = pair_owner.shape[0]
    _, length, features = image_tokens.shape
    width = 2 * features
    head_dim = w_qk.shape[1] // logit_scale.shape[0]
    mine = pair_count // 2
    units = 2 * w_in.shape[1]
    plan = Plan(pair_count, owner_count)

    def swap(values):
        return lax.ppermute(values, "mp", [(0, 1), (1, 0)])

    def across(values, distance):
        return lax.ppermute(values, "shard", [(k, k ^ distance) for k in range(owner_count)])

    def images(*counts):
        return jax.ShapeDtypeStruct((*counts, length, features), jnp.bfloat16)

    smem = pl.BlockSpec(memory_space=pltpu.SMEM)
    vmem = pl.BlockSpec(memory_space=pltpu.VMEM)
    hbm = pl.BlockSpec(memory_space=pl.ANY)

    def limit(mebibytes):
        return pltpu.CompilerParams(vmem_limit_bytes=mebibytes * 2**20)

    wanted, order = pl.pallas_call(
        functools.partial(place_kernel, plan, pair_count),
        out_shape=(
            jax.ShapeDtypeStruct((owner_count, 1, plan.row), jnp.int32),
            jax.ShapeDtypeStruct((1, 2 * pair_count), jnp.int32),
        ),
        in_specs=[smem, vmem, vmem],
        compiler_params=limit(8),
    )(shard, pair_owner.T, pair_slot.T)
    incoming = lax.all_to_all(wanted, "shard", split_axis=0, concat_axis=0, tiled=True)
    if plan.extra:
        chunks = pl.pallas_call(
            functools.partial(serve_relays_kernel, plan),
            out_shape=[images(plan.extra)] * plan.half,
            in_specs=[smem, smem, vmem],
            compiler_params=limit(8),
        )(shard, incoming, image_tokens)
        incoming, chunks = lax.optimization_barrier((incoming, chunks))
        chunks = [chunks[0]] + [across(chunks[k], k) for k in range(1, plan.half)]
    served, *near = pl.pallas_call(
        functools.partial(serve_kernel, plan),
        out_shape=[images(owner_count, plan.base)]
        + [images(plan.extra)] * (plan.half if plan.extra else 0),
        in_specs=[smem, smem, vmem],
        compiler_params=limit(12),
    )(shard, incoming, image_tokens)
    returned = lax.all_to_all(served, "shard", split_axis=0, concat_axis=0, tiled=True)
    sources = [returned.reshape(-1, length, features)]
    weights = (w_qk, w_value, w_out, w_in, w_back, bias_in, logit_scale)
    if plan.extra:
        first, second = pl.pallas_call(
            functools.partial(relay_kernel, plan),
            out_shape=[images(plan.part)] * 2,
            in_specs=[smem, smem] + [vmem] * plan.half,
            compiler_params=limit(8),
        )(shard, incoming, *chunks)
        first, incoming, weights, near = lax.optimization_barrier((first, incoming, weights, near))
        first = across(first, plan.half)
        near = [near[0]] + [across(near[k], k) for k in range(1, plan.half)]
        crowded = jnp.max(jnp.sum(incoming[:, 0, plan.capacity :], axis=1)) > plan.part
        crowded = crowded.astype(jnp.int32)
        passed = crowded
        for _ in range(groups - 1):
            passed = lax.ppermute(passed, "groups", [(k, (k + 1) % groups) for k in range(groups)])
            crowded = jnp.maximum(crowded, passed)
        second = lax.cond(
            crowded > 0, lambda part: across(part, plan.half), lambda part: part, second
        )
        sources += [*near, first, second]
    swapped = [swap(w) for w in weights]
    sources, swapped = lax.optimization_barrier((sources, swapped))
    far_qk, far_value, far_out, far_in, far_back, far_bias, far_scale = swapped

    def pick(core):
        return pl.pallas_call(
            pick_kernel,
            out_shape=images(pair_count),
            in_specs=[smem, smem] + [hbm] * len(sources),
            scratch_shapes=[
                pltpu.VMEM((plan.slots, length, features), jnp.bfloat16),
                pltpu.SemaphoreType.DMA((len(sources),)),
            ],
            compiler_params=limit(12),
        )(core, order, *sources)

    far = swap(pick(1 - core))
    own = pick(core)
    matrices = [w_qk, far_qk, w_value, far_value, w_out, far_out]
    token_count = pair_count * length
    flops = 6 * token_count * width * width
    normed, mean = pl.pallas_call(
        functools.partial(attention_kernel, length, head_dim),
        out_shape=(
            jax.ShapeDtypeStruct((token_count, width), jnp.bfloat16),
            jax.ShapeDtypeStruct((mine, width), jnp.float32),
        ),
        in_specs=[smem] * 2 + [vmem] * 4 + [hbm] * 6,
        scratch_shapes=[
            pltpu.VMEM((width, 2 * width), jnp.bfloat16),
            pltpu.VMEM((width, width), jnp.bfloat16),
            pltpu.VMEM((token_count, 2 * width), jnp.bfloat16),
            pltpu.VMEM((token_count, width), jnp.bfloat16),
            pltpu.VMEM((token_count, width), jnp.float32),
            pltpu.SemaphoreType.DMA((6,)),
        ],
        compiler_params=limit(24),
        cost_estimate=pl.CostEstimate(
            flops=flops, bytes_accessed=4 * 2**20, transcendentals=token_count * 1024
        ),
    )(
        core,
        jnp.concatenate([logit_scale, far_scale]),
        own,
        far,
        gain_attn.reshape(1, -1),
        gain_mlp.reshape(1, -1),
        *matrices,
    )
    here = pl.pallas_call(
        functools.partial(back_kernel, length),
        out_shape=jax.ShapeDtypeStruct((mine, width), jnp.bfloat16),
        compiler_params=limit(12),
    )(
        mean,
        expand(normed, w_in, bias_in, length),
        expand(normed, far_in, far_bias, length),
        w_back,
        far_back,
    )
    there = swap(here)
    low = jnp.where(core == 0, here, there)
    high = jnp.where(core == 0, there, here)
    return jnp.concatenate([low, high], axis=0)


def solution(mesh):
    in_specs = (
        P(("groups", "shard"), None, "mp"),
        P(("groups", "shard"), None),
        P(("groups", "shard"), None),
        P(),
        P(None, "mp"),
        P(None, "mp"),
        P("mp"),
        P("mp", None),
        P(),
        P(None, "mp"),
        P("mp"),
        P("mp", None),
    )
    out_specs = P(("groups", "shard"), None)
    return jax.shard_map(
        on_device, mesh=mesh, in_specs=in_specs, out_specs=out_specs, check_vma=False
    )
```

```python
import functools

import jax
import jax.numpy as jnp
from jax import lax
from jax.experimental import pallas as pl
from jax.experimental.pallas import tpu as pltpu
from jax.sharding import PartitionSpec as P

LOG2E = 1.4426950408889634
BLOCK = 8


def norm_rows(values, gain):
    center = values - jnp.mean(values, axis=-1, keepdims=True)
    spread = jnp.mean(center * center, axis=-1, keepdims=True)
    return center * lax.rsqrt(spread + 1e-05) * gain


def dot_nt(a, b):
    return lax.dot_general(a, b, (((1,), (1,)), ((), ())), preferred_element_type=jnp.float32)


def dot(a, b):
    return jnp.dot(a, b, preferred_element_type=jnp.float32)


class Plan:
    def __init__(self, pair_count, owner_count):
        self.owners = owner_count
        self.capacity = max(2, 4 * pair_count // owner_count)
        self.half = owner_count // 2
        split = self.capacity >= 32 and self.half & (self.half - 1) == 0 and self.half > 0
        self.base = self.capacity // 2 if split else self.capacity
        self.extra = self.capacity - self.base
        self.part = self.half * self.extra // 2
        self.near_at = owner_count * self.base
        self.rest_at = self.near_at + self.half * self.extra
        self.slots = self.rest_at + 2 * self.part
        self.row = self.capacity + (self.half if split else 0)


def place_kernel(plan, count, shard_ref, owner_ref, slot_ref, wanted_ref, list_ref):
    total = 2 * count
    owners = plan.owners
    owner = jnp.concatenate([owner_ref[0:1, :], owner_ref[1:2, :]], axis=1)
    slot = jnp.concatenate([slot_ref[0:1, :], slot_ref[1:2, :]], axis=1)

    def place(dim, size):
        return lax.broadcasted_iota(jnp.int32, (size, total), dim)

    def as_bf16(values):
        return values.astype(jnp.float32).astype(jnp.bfloat16)

    row = place(0, owners)
    named = row == owner
    until = as_bf16(jnp.where(place(0, total) <= place(1, total), 1, 0))
    tally = dot(as_bf16(jnp.where(named, 1, 0)), until).astype(jnp.int32)
    rank = jnp.sum(jnp.where(named, tally, 0), axis=0, keepdims=True) - 1
    ranked = as_bf16(jnp.where(place(0, total) == rank, 1, 0))
    wanted = dot_nt(as_bf16(jnp.where(named, slot, 0)), ranked).astype(jnp.int32)
    where = owner * plan.base + rank
    if plan.extra:
        me = shard_ref[0]
        half = plan.half
        over = jnp.maximum(jnp.max(tally, axis=1, keepdims=True) - plan.base, 0)
        far_over = jnp.where(row // half != me // half, over, 0)
        before = jnp.zeros((owners, total), jnp.int32)
        for index in range(owners - 1):
            before = before + jnp.where(row > index, far_over[index : index + 1], 0)
        before = jnp.sum(jnp.where(named, before, 0), axis=0, keepdims=True)
        rest = rank - plan.base
        near = plan.near_at + ((owner % half) ^ (me % half)) * plan.extra + rest
        late = jnp.where(owner // half == me // half, near, plan.rest_at + before + rest)
        where = jnp.where(rest < 0, where, late)
        told = place(1, owners) == plan.capacity + row % half
        wanted = wanted + jnp.sum(jnp.where(told, far_over, 0), axis=0, keepdims=True)
    for index in range(owners):
        wanted_ref[index] = wanted[index : index + 1, : plan.row]
    entry = place(1, 1)
    side = entry // count
    pair = entry % count
    mine = count // 2
    local = pair % mine
    position = pair // mine * count + local // BLOCK * (2 * BLOCK) + side * BLOCK + local % BLOCK
    seated = as_bf16(jnp.where(place(0, total) == position, 1, 0))
    parts = as_bf16(jnp.where(place(0, 8) == 0, where // 16, where % 16))
    listed = dot_nt(parts, seated).astype(jnp.int32)
    list_ref[...] = listed[0:1] * 16 + listed[1:2]


def serve(tokens_ref, incoming_ref, requester, start, served_ref):
    count = served_ref.shape[0]

    def copy(index, carry):
        served_ref[index] = tokens_ref[incoming_ref[requester, 0, start + index]]
        return carry

    lax.fori_loop(0, count, copy, 0, unroll=min(16, count))


def serve_relays_kernel(plan, shard_ref, incoming_ref, tokens_ref, *served_refs):
    for distance, served_ref in enumerate(served_refs):
        requester = shard_ref[0] ^ (distance + plan.half)
        serve(tokens_ref, incoming_ref, requester, plan.base, served_ref)


def serve_kernel(plan, shard_ref, incoming_ref, tokens_ref, served_ref, *near_refs):
    for requester in range(plan.owners):
        serve(tokens_ref, incoming_ref, requester, 0, served_ref.at[requester])
    for distance, near_ref in enumerate(near_refs):
        serve(tokens_ref, incoming_ref, shard_ref[0] ^ distance, plan.base, near_ref)


def relay_kernel(plan, shard_ref, incoming_ref, *refs):
    chunk_refs = refs[: plan.half]
    first_ref, second_ref = refs[plan.half :]
    client = shard_ref[0] ^ plan.half
    for distance, chunk_ref in enumerate(chunk_refs):
        owner = (shard_ref[0] % plan.half) ^ distance
        at = 0
        for index in range(plan.half):
            amount = incoming_ref[client, 0, plan.capacity + index]
            at = at + jnp.where(index < owner, amount, 0)
        amount = incoming_ref[client, 0, plan.capacity + owner]
        fit = jnp.clip(plan.part - at, 0, amount)

        def pack(index, carry, chunk_ref=chunk_ref, at=at):
            first_ref[at + index] = chunk_ref[index]
            return carry

        def pack_more(index, carry, chunk_ref=chunk_ref, at=at):
            second_ref[at + index - plan.part] = chunk_ref[index]
            return carry

        lax.fori_loop(0, fit, pack, 0)
        lax.fori_loop(fit, amount, pack_more, 0)


def pick_kernel(core_ref, list_ref, *refs):
    source_refs = refs[:-3]
    picked_ref, held_ref, sems = refs[-3:]
    count = picked_ref.shape[0]
    at = 0
    loads = []
    for index, source_ref in enumerate(source_refs):
        size = source_ref.shape[0]
        loads.append(
            pltpu.make_async_copy(source_ref, held_ref.at[pl.ds(at, size)], sems.at[index])
        )
        at += size
    for load in loads:
        load.start()
    for load in loads:
        load.wait()
    start = core_ref[0] * count

    def pick(index, carry):
        picked_ref[index] = held_ref[list_ref[0, start + index]]
        return carry

    lax.fori_loop(0, count, pick, 0, unroll=16)


def compare_kernel(
    length,
    head_dim,
    core_ref,
    scale_ref,
    gain_attn_ref,
    gain_mlp_ref,
    *refs,
):
    own_held_ref, far_held_ref, *held_refs = refs[:14]
    result_ref, qkv_ref, out_ref, in_ref, back_ref, bias_ref = refs[14:20]
    tokens_ref, normed_ref, heads_ref, mixed_ref, hidden_ref = refs[20:25]
    inner_ref, bent_ref, pooled_ref, mean_ref, sems, token_sems = refs[25:]
    width, units = in_ref.shape
    wide = width // 2
    homes = [qkv_ref.at[:, pl.ds(k * wide, wide)] for k in range(4)]
    homes += [out_ref.at[pl.ds(k * wide, wide)] for k in range(2)]
    homes += [in_ref.at[:, pl.ds(k * units // 2, units // 2)] for k in range(2)]
    homes += [bias_ref.at[:, pl.ds(k * units // 2, units // 2)] for k in range(2)]
    homes += [back_ref.at[pl.ds(k * units // 2, units // 2)] for k in range(2)]
    loads = [
        pltpu.make_async_copy(held, home, sems.at[k])
        for k, (held, home) in enumerate(zip(held_refs, homes))
    ]
    core = core_ref[0]
    token_loads = [
        pltpu.make_async_copy(own_held_ref, tokens_ref.at[core], token_sems.at[0]),
        pltpu.make_async_copy(far_held_ref, tokens_ref.at[1 - core], token_sems.at[1]),
    ]
    for load in token_loads + loads:
        load.start()
    half = BLOCK * length
    rows = 2 * half
    count = result_ref.shape[0]
    blocks = count // BLOCK
    tile = 256
    pair_dim = 2 * head_dim
    even = lax.broadcasted_iota(jnp.int32, (half, pair_dim), 1) < head_dim
    same = (
        lax.broadcasted_iota(jnp.int32, (half, half), 0) // length
        == lax.broadcasted_iota(jnp.int32, (half, half), 1) // length
    )

    def span(step, size):
        return pl.ds(pl.multiple_of(step * size, size), size)

    def split(values):
        zero = jnp.zeros_like(values)
        return jnp.concatenate(
            [jnp.where(even, values, zero), jnp.where(even, zero, values)], axis=0
        )

    ones = split(jnp.ones((half, pair_dim), jnp.bfloat16))

    def begin(step, carry):
        images = pl.ds(step * 2, 2)
        here = span(step, 2 * length)
        tokens = [
            tokens_ref[k, images].reshape(2 * length, -1).astype(jnp.float32) for k in range(2)
        ]
        tokens = jnp.concatenate(tokens, axis=1)
        hidden_ref[here, :] = tokens
        normed_ref[here, :] = norm_rows(tokens, gain_attn_ref[...]).astype(jnp.bfloat16)
        return carry

    def project(step, carry):
        here = span(step // 4, rows)
        cut = span(step % 4, 2 * width // 4)
        heads_ref[here, cut] = dot(normed_ref[here, :], qkv_ref[:, cut]).astype(jnp.bfloat16)
        return carry

    def weigh(scores, factor):
        scores = jnp.where(same, scores, -1e30)
        top = jnp.max(scores, axis=1, keepdims=True)
        return jnp.exp2((scores - top) * factor).astype(jnp.bfloat16)

    def mix(query, key, value, factors):
        scores = dot_nt(query, split(key))
        weights = [weigh(scores[:, k * half : (k + 1) * half], factors[k]) for k in range(2)]
        mixed = dot(jnp.concatenate(weights, axis=1), jnp.concatenate([split(value), ones], axis=1))
        total = mixed[:, pair_dim:]
        inverse = pl.reciprocal(total, approx=True)
        inverse = inverse * (2.0 - total * inverse)
        return (mixed[:, :pair_dim] * inverse).astype(jnp.bfloat16)

    def attend(step, carry):
        for index in range(width // pair_dim):
            factors = [scale_ref[2 * index + k] * (LOG2E / head_dim**0.5) for k in range(2)]
            cut = slice(index * pair_dim, (index + 1) * pair_dim)
            beyond = slice(width + cut.start, width + cut.stop)
            sides = [span(2 * step + k, half) for k in range(2)]
            query = [heads_ref[side, cut] for side in sides]
            value = [heads_ref[side, beyond] for side in sides]
            for k in range(2):
                mixed_ref[sides[k], cut] = mix(query[k], query[1 - k], value[1 - k], factors)
        return carry

    def join(step, carry):
        here = span(step // 2, rows)
        cut = span(step % 2, width // 2)
        hidden_ref[here, cut] += dot(mixed_ref[here, :], out_ref[:, cut])
        return carry

    def middle(step, carry):
        total = 0.0
        for side in range(2):
            at = (step // BLOCK * 2 + side) * BLOCK + step % BLOCK
            here = span(at, length)
            hidden = hidden_ref[here, :]
            total = total + jnp.sum(hidden, axis=0, keepdims=True)
            normed_ref[here, :] = norm_rows(hidden, gain_mlp_ref[...]).astype(jnp.bfloat16)
        mean_ref[pl.ds(step, 1), :] = total
        return carry

    long = inner_ref.shape[1]
    pairs = long // (2 * length)
    row = lax.broadcasted_iota(jnp.int32, (pairs, long), 1)
    row_pair = row // rows * BLOCK + row % half // length
    pool = jnp.where(row_pair == lax.broadcasted_iota(jnp.int32, row.shape, 0), 1.0, 0.0)
    pool = pool.astype(jnp.bfloat16)
    tiles = units // tile
    steps = count // pairs * tiles
    piece = 32

    def expand(step, carry):
        new = lax.rem(step, steps)
        here = span(new // tiles, long)
        cut = span(lax.rem(new, tiles), tile)
        inner_ref[lax.rem(step, 2)] = dot(normed_ref[here, :], in_ref[:, cut])
        pooled = dot(pool, bent_ref[lax.rem(step, 2)])
        last = lax.rem(step + steps - 1, steps)
        bias = bias_ref[:, span(lax.rem(last, tiles), tile)]
        for at in range(0, long, piece):
            inner = inner_ref[lax.rem(step + 1, 2), at : at + piece, :] + bias
            inner = inner.astype(jnp.bfloat16)
            cubic = inner * inner * jnp.bfloat16(0.0356774081) + jnp.bfloat16(0.7978845608)
            bent = (jnp.tanh(inner * cubic) + jnp.bfloat16(1.0)) * inner
            bent_ref[lax.rem(step + 1, 2), at : at + piece, :] = bent
        old = lax.rem(step + steps - 2, steps)
        pooled_ref[span(old // tiles, pairs), span(lax.rem(old, tiles), tile)] = pooled
        return carry

    for load in token_loads:
        load.wait()
    lax.fori_loop(0, count, begin, 0, unroll=8)
    for load in loads[:4]:
        load.wait()
    lax.fori_loop(0, blocks * 4, project, 0, unroll=2)
    lax.fori_loop(0, blocks, attend, 0)
    for load in loads[4:6]:
        load.wait()
    lax.fori_loop(0, blocks * 2, join, 0, unroll=2)
    lax.fori_loop(0, count, middle, 0, unroll=8)
    for load in loads[6:10]:
        load.wait()
    lax.fori_loop(0, steps + 2, expand, 0)
    for load in loads[10:]:
        load.wait()
    pooled = pooled_ref[...] * (0.25 / length)
    coarse = pooled.astype(jnp.bfloat16)
    fine = (pooled - coarse.astype(jnp.float32)).astype(jnp.bfloat16)
    back = dot(jnp.concatenate([coarse, fine], axis=0), back_ref[...])
    mean = mean_ref[...] * (0.5 / length)
    result_ref[...] = (mean + back[:count] + back[count:]).astype(jnp.bfloat16)


def on_device(
    image_tokens,
    pair_owner,
    pair_slot,
    gain_attn,
    w_qk,
    w_value,
    logit_scale,
    w_out,
    gain_mlp,
    w_in,
    bias_in,
    w_back,
):
    owner_count = lax.axis_size("shard")
    groups = lax.axis_size("groups")
    core = lax.axis_index("mp").reshape(1)
    shard = lax.axis_index("shard").reshape(1)
    pair_count = pair_owner.shape[0]
    _, length, features = image_tokens.shape
    width = 2 * features
    head_dim = w_qk.shape[1] // logit_scale.shape[0]
    mine = pair_count // 2
    units = 2 * w_in.shape[1]
    plan = Plan(pair_count, owner_count)

    def swap(values):
        return lax.ppermute(values, "mp", [(0, 1), (1, 0)])

    def across(values, distance):
        return lax.ppermute(values, "shard", [(k, k ^ distance) for k in range(owner_count)])

    def images(*counts):
        return jax.ShapeDtypeStruct((*counts, length, features), jnp.bfloat16)

    smem = pl.BlockSpec(memory_space=pltpu.SMEM)
    vmem = pl.BlockSpec(memory_space=pltpu.VMEM)
    hbm = pl.BlockSpec(memory_space=pl.ANY)

    wanted, order = pl.pallas_call(
        functools.partial(place_kernel, plan, pair_count),
        out_shape=(
            jax.ShapeDtypeStruct((owner_count, 1, plan.row), jnp.int32),
            jax.ShapeDtypeStruct((1, 2 * pair_count), jnp.int32),
        ),
        in_specs=[smem, vmem, vmem],
    )(shard, pair_owner.T, pair_slot.T)
    incoming = lax.all_to_all(wanted, "shard", split_axis=0, concat_axis=0, tiled=True)
    if plan.extra:
        chunks = pl.pallas_call(
            functools.partial(serve_relays_kernel, plan),
            out_shape=[images(plan.extra)] * plan.half,
            in_specs=[smem, smem, vmem],
        )(shard, incoming, image_tokens)
        incoming, chunks = lax.optimization_barrier((incoming, chunks))
        chunks = [chunks[0]] + [across(chunks[k], k) for k in range(1, plan.half)]
    served, *near = pl.pallas_call(
        functools.partial(serve_kernel, plan),
        out_shape=[images(owner_count, plan.base)]
        + [images(plan.extra)] * (plan.half if plan.extra else 0),
        in_specs=[smem, smem, vmem],
    )(shard, incoming, image_tokens)
    weights = (w_qk, w_value, w_out, w_in, w_back, bias_in, logit_scale)
    if plan.extra:
        first, second = pl.pallas_call(
            functools.partial(relay_kernel, plan),
            out_shape=[images(plan.part)] * 2,
            in_specs=[smem, smem] + [vmem] * plan.half,
        )(shard, incoming, *chunks)
        served, near, first, second, incoming, weights = lax.optimization_barrier(
            (served, near, first, second, incoming, weights)
        )
    returned = lax.all_to_all(served, "shard", split_axis=0, concat_axis=0, tiled=True)
    sources = [returned.reshape(-1, length, features)]
    if plan.extra:
        first = across(first, plan.half)
        near = [near[0]] + [across(near[k], k) for k in range(1, plan.half)]
        crowded = jnp.max(jnp.sum(incoming[:, 0, plan.capacity :], axis=1)) > plan.part
        crowded = crowded.astype(jnp.int32)
        passed = crowded
        for _ in range(groups - 1):
            passed = lax.ppermute(passed, "groups", [(k, (k + 1) % groups) for k in range(groups)])
            crowded = jnp.maximum(crowded, passed)
        second = lax.cond(
            crowded > 0, lambda part: across(part, plan.half), lambda part: part, second
        )
        sources += [*near, first, second]
    swapped = [swap(w) for w in weights]
    sources, swapped = lax.optimization_barrier((sources, swapped))
    far_qk, far_value, far_out, far_in, far_back, far_bias, far_scale = swapped

    def pick(core):
        return pl.pallas_call(
            pick_kernel,
            out_shape=images(pair_count),
            in_specs=[smem, smem] + [hbm] * len(sources),
            scratch_shapes=[
                pltpu.VMEM((plan.slots, length, features), jnp.bfloat16),
                pltpu.SemaphoreType.DMA((len(sources),)),
            ],
        )(core, order, *sources)

    far = swap(pick(1 - core))
    own = pick(core)
    matrices = [w_qk, far_qk, w_value, far_value, w_out, far_out, w_in, far_in]
    matrices += [bias_in.reshape(1, -1), far_bias.reshape(1, -1), w_back, far_back]
    token_count = pair_count * length
    long = token_count // 2
    here = pl.pallas_call(
        functools.partial(compare_kernel, length, head_dim),
        out_shape=jax.ShapeDtypeStruct((mine, width), jnp.bfloat16),
        in_specs=[smem] * 2 + [vmem] * 2 + [hbm] * 14,
        out_specs=vmem,
        scratch_shapes=[
            pltpu.VMEM((width, 2 * width), jnp.bfloat16),
            pltpu.VMEM((width, width), jnp.bfloat16),
            pltpu.VMEM((width, units), jnp.bfloat16),
            pltpu.VMEM((units, width), jnp.bfloat16),
            pltpu.VMEM((1, units), jnp.float32),
            pltpu.VMEM((2, pair_count, length, features), jnp.bfloat16),
            pltpu.VMEM((token_count, width), jnp.bfloat16),
            pltpu.VMEM((token_count, 2 * width), jnp.bfloat16),
            pltpu.VMEM((token_count, width), jnp.bfloat16),
            pltpu.VMEM((token_count, width), jnp.float32),
            pltpu.VMEM((2, long, 256), jnp.float32),
            pltpu.VMEM((2, long, 256), jnp.bfloat16),
            pltpu.VMEM((mine, units), jnp.float32),
            pltpu.VMEM((mine, width), jnp.float32),
            pltpu.SemaphoreType.DMA((12,)),
            pltpu.SemaphoreType.DMA((2,)),
        ],
        compiler_params=pltpu.CompilerParams(vmem_limit_bytes=56 * 2**20),
        cost_estimate=pl.CostEstimate(
            flops=2 * token_count * width * (3 * width + units),
            bytes_accessed=8 * 2**20,
            transcendentals=token_count * units,
        ),
    )(
        core,
        jnp.concatenate([logit_scale, far_scale]),
        gain_attn.reshape(1, -1),
        gain_mlp.reshape(1, -1),
        own,
        far,
        *matrices,
    )
    there = swap(here)
    low = jnp.where(core == 0, here, there)
    high = jnp.where(core == 0, there, here)
    return jnp.concatenate([low, high], axis=0)


def solution(mesh):
    in_specs = (
        P(("groups", "shard"), None, "mp"),
        P(("groups", "shard"), None),
        P(("groups", "shard"), None),
        P(),
        P(None, "mp"),
        P(None, "mp"),
        P("mp"),
        P("mp", None),
        P(),
        P(None, "mp"),
        P("mp"),
        P("mp", None),
    )
    out_specs = P(("groups", "shard"), None)
    return jax.shard_map(
        on_device, mesh=mesh, in_specs=in_specs, out_specs=out_specs, check_vma=False
    )
```

```python
import functools

import jax
import jax.numpy as jnp
from jax import lax
from jax.experimental import pallas as pl
from jax.experimental.pallas import tpu as pltpu
from jax.sharding import PartitionSpec as P

LOG2E = 1.4426950408889634
BLOCK = 8


def norm_rows(values, gain):
    center = values - jnp.mean(values, axis=-1, keepdims=True)
    spread = jnp.mean(center * center, axis=-1, keepdims=True)
    return center * lax.rsqrt(spread + 1e-05) * gain


def dot_nt(a, b):
    return lax.dot_general(a, b, (((1,), (1,)), ((), ())), preferred_element_type=jnp.float32)


def dot(a, b):
    return jnp.dot(a, b, preferred_element_type=jnp.float32)


class Plan:
    def __init__(self, pair_count, owner_count):
        self.owners = owner_count
        self.capacity = max(2, 4 * pair_count // owner_count)
        self.half = owner_count // 2
        split = self.capacity >= 32 and self.half & (self.half - 1) == 0 and self.half > 0
        self.base = self.capacity // 2 if split else self.capacity
        self.extra = self.capacity - self.base
        self.part = self.half * self.extra // 2
        self.near_at = owner_count * self.base
        self.rest_at = self.near_at + self.half * self.extra
        self.slots = self.rest_at + 2 * self.part
        self.row = self.capacity + (self.half if split else 0)


def place_kernel(plan, count, shard_ref, owner_ref, slot_ref, wanted_ref, list_ref):
    total = 2 * count
    owners = plan.owners
    owner = jnp.concatenate([owner_ref[0:1, :], owner_ref[1:2, :]], axis=1)
    slot = jnp.concatenate([slot_ref[0:1, :], slot_ref[1:2, :]], axis=1)

    def place(dim, size):
        return lax.broadcasted_iota(jnp.int32, (size, total), dim)

    def as_bf16(values):
        return values.astype(jnp.float32).astype(jnp.bfloat16)

    row = place(0, owners)
    named = row == owner
    until = as_bf16(jnp.where(place(0, total) <= place(1, total), 1, 0))
    tally = dot(as_bf16(jnp.where(named, 1, 0)), until).astype(jnp.int32)
    rank = jnp.sum(jnp.where(named, tally, 0), axis=0, keepdims=True) - 1
    ranked = as_bf16(jnp.where(place(0, total) == rank, 1, 0))
    wanted = dot_nt(as_bf16(jnp.where(named, slot, 0)), ranked).astype(jnp.int32)
    where = owner * plan.base + rank
    if plan.extra:
        me = shard_ref[0]
        half = plan.half
        over = jnp.maximum(jnp.max(tally, axis=1, keepdims=True) - plan.base, 0)
        far_over = jnp.where(row // half != me // half, over, 0)
        before = jnp.zeros((owners, total), jnp.int32)
        for index in range(owners - 1):
            before = before + jnp.where(row > index, far_over[index : index + 1], 0)
        before = jnp.sum(jnp.where(named, before, 0), axis=0, keepdims=True)
        rest = rank - plan.base
        near = plan.near_at + ((owner % half) ^ (me % half)) * plan.extra + rest
        late = jnp.where(owner // half == me // half, near, plan.rest_at + before + rest)
        where = jnp.where(rest < 0, where, late)
        told = place(1, owners) == plan.capacity + row % half
        wanted = wanted + jnp.sum(jnp.where(told, far_over, 0), axis=0, keepdims=True)
    for index in range(owners):
        wanted_ref[index] = wanted[index : index + 1, : plan.row]
    entry = place(1, 1)
    side = entry // count
    pair = entry % count
    mine = count // 2
    local = pair % mine
    position = pair // mine * count + local // BLOCK * (2 * BLOCK) + side * BLOCK + local % BLOCK
    seated = as_bf16(jnp.where(place(0, total) == position, 1, 0))
    parts = as_bf16(jnp.where(place(0, 8) == 0, where // 16, where % 16))
    listed = dot_nt(parts, seated).astype(jnp.int32)
    list_ref[...] = listed[0:1] * 16 + listed[1:2]


def serve(tokens_ref, incoming_ref, requester, start, served_ref):
    count = served_ref.shape[0]

    def copy(index, carry):
        served_ref[index] = tokens_ref[incoming_ref[requester, 0, start + index]]
        return carry

    lax.fori_loop(0, count, copy, 0, unroll=min(16, count))


def serve_kernel(plan, incoming_ref, tokens_ref, served_ref):
    for requester in range(plan.owners):
        serve(tokens_ref, incoming_ref, requester, 0, served_ref.at[requester])


def serve_rest_kernel(plan, shift, shard_ref, incoming_ref, tokens_ref, *served_refs):
    for distance, served_ref in enumerate(served_refs):
        serve(tokens_ref, incoming_ref, shard_ref[0] ^ (distance + shift), plan.base, served_ref)


def relay_kernel(plan, shard_ref, incoming_ref, *refs):
    chunk_refs = refs[: plan.half]
    first_ref, second_ref = refs[plan.half :]
    client = shard_ref[0] ^ plan.half
    for distance, chunk_ref in enumerate(chunk_refs):
        owner = (shard_ref[0] % plan.half) ^ distance
        at = 0
        for index in range(plan.half):
            amount = incoming_ref[client, 0, plan.capacity + index]
            at = at + jnp.where(index < owner, amount, 0)
        amount = incoming_ref[client, 0, plan.capacity + owner]
        fit = jnp.clip(plan.part - at, 0, amount)

        def pack(index, carry, chunk_ref=chunk_ref, at=at):
            first_ref[at + index] = chunk_ref[index]
            return carry

        def pack_more(index, carry, chunk_ref=chunk_ref, at=at):
            second_ref[at + index - plan.part] = chunk_ref[index]
            return carry

        lax.fori_loop(0, fit, pack, 0)
        lax.fori_loop(fit, amount, pack_more, 0)


def pick_kernel(core_ref, list_ref, *refs):
    source_refs = refs[:-3]
    picked_ref, held_ref, sems = refs[-3:]
    count = picked_ref.shape[0]
    at = 0
    loads = []
    for index, source_ref in enumerate(source_refs):
        size = source_ref.shape[0]
        loads.append(
            pltpu.make_async_copy(source_ref, held_ref.at[pl.ds(at, size)], sems.at[index])
        )
        at += size
    for load in loads:
        load.start()
    for load in loads:
        load.wait()
    start = core_ref[0] * count

    def pick(index, carry):
        picked_ref[index] = held_ref[list_ref[0, start + index]]
        return carry

    lax.fori_loop(0, count, pick, 0, unroll=16)


def compare_kernel(
    length,
    head_dim,
    core_ref,
    scale_a_ref,
    scale_b_ref,
    gain_attn_ref,
    gain_mlp_ref,
    *refs,
):
    own_held_ref, far_held_ref, *held_refs = refs[:14]
    result_ref, qkv_ref, out_ref, in_ref, back_ref, bias_ref = refs[14:20]
    tokens_ref, pooled_ref, mean_ref, sems, token_sems = refs[20:]
    width, units = in_ref.shape
    wide = width // 2
    homes = [qkv_ref.at[:, pl.ds(k * wide, wide)] for k in range(4)]
    homes += [out_ref.at[pl.ds(k * wide, wide)] for k in range(2)]
    homes += [in_ref.at[:, pl.ds(k * units // 2, units // 2)] for k in range(2)]
    homes += [bias_ref.at[:, pl.ds(k * units // 2, units // 2)] for k in range(2)]
    homes += [back_ref.at[pl.ds(k * units // 2, units // 2)] for k in range(2)]
    loads = [
        pltpu.make_async_copy(held, home, sems.at[k])
        for k, (held, home) in enumerate(zip(held_refs, homes))
    ]
    core = core_ref[0]
    token_loads = [
        pltpu.make_async_copy(own_held_ref, tokens_ref.at[core], token_sems.at[0]),
        pltpu.make_async_copy(far_held_ref, tokens_ref.at[1 - core], token_sems.at[1]),
    ]
    for load in token_loads + loads:
        load.start()
    half = BLOCK * length
    rows = 2 * half
    count = result_ref.shape[0]
    blocks = count // BLOCK
    tile = 256
    pair_dim = 2 * head_dim
    scale_refs = (scale_a_ref, scale_b_ref)
    per_core = width // head_dim // 2
    even = lax.broadcasted_iota(jnp.int32, (half, pair_dim), 1) < head_dim
    same = (
        lax.broadcasted_iota(jnp.int32, (half, half), 0) // length
        == lax.broadcasted_iota(jnp.int32, (half, half), 1) // length
    )

    def span(step, size):
        return pl.ds(pl.multiple_of(step * size, size), size)

    def split(values):
        zero = jnp.zeros_like(values)
        return jnp.concatenate(
            [jnp.where(even, values, zero), jnp.where(even, zero, values)], axis=0
        )

    ones = split(jnp.ones((half, pair_dim), jnp.bfloat16))

    def weigh(scores, factor):
        scores = jnp.where(same, scores, -1e30)
        top = jnp.max(scores, axis=1, keepdims=True)
        return jnp.exp2((scores - top) * factor).astype(jnp.bfloat16)

    def mix(query, key, value, factors):
        scores = dot_nt(query, split(key))
        weights = [weigh(scores[:, k * half : (k + 1) * half], factors[k]) for k in range(2)]
        mixed = dot(jnp.concatenate(weights, axis=1), jnp.concatenate([split(value), ones], axis=1))
        total = mixed[:, pair_dim:]
        inverse = pl.reciprocal(total, approx=True)
        inverse = inverse * (2.0 - total * inverse)
        return (mixed[:, :pair_dim] * inverse).astype(jnp.bfloat16)

    row_pair = lax.broadcasted_iota(jnp.int32, (2 * BLOCK, rows), 1) % half // length
    pool = jnp.where(row_pair == lax.broadcasted_iota(jnp.int32, row_pair.shape, 0), 1.0, 0.0)
    pool = pool.astype(jnp.bfloat16)

    def arrive(step, copies):
        @pl.when(step == 0)
        def _():
            for copy in copies:
                copy.wait()

    def block(step, carry):
        images = pl.ds(step * 2 * BLOCK, 2 * BLOCK)
        hidden = jnp.concatenate(
            [tokens_ref[k, images].reshape(rows, -1).astype(jnp.float32) for k in range(2)], axis=1
        )
        normed = norm_rows(hidden, gain_attn_ref[...]).astype(jnp.bfloat16)
        arrive(step, loads[:4])
        query = dot(normed, qkv_ref[:, :width]).astype(jnp.bfloat16)
        value = dot(normed, qkv_ref[:, width:]).astype(jnp.bfloat16)
        mixed = []
        for index in range(width // pair_dim):
            factors = [scale_refs[k // per_core][k % per_core] for k in (2 * index, 2 * index + 1)]
            factors = [factor * (LOG2E / head_dim**0.5) for factor in factors]
            cut = slice(index * pair_dim, (index + 1) * pair_dim)
            sides = [slice(0, half), slice(half, rows)]
            both = [
                mix(query[sides[k], cut], query[sides[1 - k], cut], value[sides[1 - k], cut], factors)
                for k in range(2)
            ]
            mixed.append(jnp.concatenate(both, axis=0))
        arrive(step, loads[4:6])
        hidden = hidden + dot(jnp.concatenate(mixed, axis=1), out_ref[...])
        here = span(step, BLOCK)
        mean_ref[here, :] = jnp.sum(hidden.reshape(2, BLOCK, length, -1), axis=(0, 2))
        normed = norm_rows(hidden, gain_mlp_ref[...]).astype(jnp.bfloat16)
        arrive(step, loads[6:10])
        for at in range(0, units, tile):
            cut = slice(at, at + tile)
            inner = dot(normed, in_ref[:, cut]) + bias_ref[:, cut]
            bent = jnp.tanh(inner * (0.7978845608028654 + 0.035677408136300125 * (inner * inner)))
            bent = (inner * bent + inner).astype(jnp.bfloat16)
            pooled_ref[here, cut] = dot(pool, bent)[:BLOCK]
        return carry

    for load in token_loads:
        load.wait()
    lax.fori_loop(0, blocks, block, 0)
    for load in loads[10:]:
        load.wait()
    pooled = pooled_ref[...] * (0.25 / length)
    coarse = pooled.astype(jnp.bfloat16)
    fine = (pooled - coarse.astype(jnp.float32)).astype(jnp.bfloat16)
    back = dot(jnp.concatenate([coarse, fine], axis=0), back_ref[...])
    mean = mean_ref[...] * (0.5 / length)
    result_ref[...] = (mean + back[:count] + back[count:]).astype(jnp.bfloat16)


def join_kernel(core_ref, here_ref, there_ref, result_ref):
    count = here_ref.shape[0]
    start = pl.multiple_of(core_ref[0] * count, count)
    result_ref[pl.ds(start, count), :] = here_ref[...]
    result_ref[pl.ds(pl.multiple_of(count - start, count), count), :] = there_ref[...]


def on_device(
    image_tokens,
    pair_owner,
    pair_slot,
    gain_attn,
    w_qk,
    w_value,
    logit_scale,
    w_out,
    gain_mlp,
    w_in,
    bias_in,
    w_back,
):
    owner_count = lax.axis_size("shard")
    groups = lax.axis_size("groups")
    core = lax.axis_index("mp").reshape(1)
    shard = lax.axis_index("shard").reshape(1)
    pair_count = pair_owner.shape[0]
    _, length, features = image_tokens.shape
    width = 2 * features
    head_dim = w_qk.shape[1] // logit_scale.shape[0]
    mine = pair_count // 2
    units = 2 * w_in.shape[1]
    plan = Plan(pair_count, owner_count)

    def swap(values):
        return lax.ppermute(values, "mp", [(0, 1), (1, 0)])

    def across(values, distance):
        return lax.ppermute(values, "shard", [(k, k ^ distance) for k in range(owner_count)])

    def images(*counts):
        return jax.ShapeDtypeStruct((*counts, length, features), jnp.bfloat16)

    smem = pl.BlockSpec(memory_space=pltpu.SMEM)
    vmem = pl.BlockSpec(memory_space=pltpu.VMEM)
    hbm = pl.BlockSpec(memory_space=pl.ANY)

    wanted, order = pl.pallas_call(
        functools.partial(place_kernel, plan, pair_count),
        out_shape=(
            jax.ShapeDtypeStruct((owner_count, 1, plan.row), jnp.int32),
            jax.ShapeDtypeStruct((1, 2 * pair_count), jnp.int32),
        ),
        in_specs=[smem, vmem, vmem],
    )(shard, pair_owner.T, pair_slot.T)
    incoming = lax.all_to_all(wanted, "shard", split_axis=0, concat_axis=0, tiled=True)
    served = pl.pallas_call(
        functools.partial(serve_kernel, plan),
        out_shape=images(owner_count, plan.base),
        in_specs=[smem, vmem],
    )(incoming, image_tokens)
    returned = lax.all_to_all(served, "shard", split_axis=0, concat_axis=0, tiled=True)
    sources = [returned.reshape(-1, length, features)]
    weights = (w_qk, w_value, w_out, w_in, w_back, bias_in, logit_scale)
    if plan.extra:

        def serve_rest(shift, incoming):
            return pl.pallas_call(
                functools.partial(serve_rest_kernel, plan, shift),
                out_shape=[images(plan.extra)] * plan.half,
                in_specs=[smem, smem, vmem],
            )(shard, incoming, image_tokens)

        incoming, served = lax.optimization_barrier((incoming, served))
        chunks = serve_rest(plan.half, incoming)
        chunks, weights = lax.optimization_barrier((chunks, weights))
        chunks = [chunks[0]] + [across(chunks[k], k) for k in range(1, plan.half)]
        first, second = pl.pallas_call(
            functools.partial(relay_kernel, plan),
            out_shape=[images(plan.part)] * 2,
            in_specs=[smem, smem] + [vmem] * plan.half,
        )(shard, incoming, *chunks)
        first, second, incoming = lax.optimization_barrier((first, second, incoming))
        first = across(first, plan.half)
        near = serve_rest(0, incoming)
        near = [near[0]] + [across(near[k], k) for k in range(1, plan.half)]
        crowded = jnp.max(jnp.sum(incoming[:, 0, plan.capacity :], axis=1)) > plan.part
        crowded = crowded.astype(jnp.int32)
        passed = crowded
        for _ in range(groups - 1):
            passed = lax.ppermute(passed, "groups", [(k, (k + 1) % groups) for k in range(groups)])
            crowded = jnp.maximum(crowded, passed)
        sources += [*near, first]
    swapped = [swap(w) for w in weights]
    sources, swapped = lax.optimization_barrier((sources, swapped))
    if plan.extra:
        second, sources = lax.optimization_barrier((second, sources))
        second = lax.cond(
            crowded > 0, lambda part: across(part, plan.half), lambda part: part, second
        )
        sources = [*sources, second]
    far_qk, far_value, far_out, far_in, far_back, far_bias, far_scale = swapped

    def pick(core):
        return pl.pallas_call(
            pick_kernel,
            out_shape=images(pair_count),
            in_specs=[smem, smem] + [hbm] * len(sources),
            scratch_shapes=[
                pltpu.VMEM((plan.slots, length, features), jnp.bfloat16),
                pltpu.SemaphoreType.DMA((len(sources),)),
            ],
        )(core, order, *sources)

    far = swap(pick(1 - core))
    own = pick(core)
    matrices = [w_qk, far_qk, w_value, far_value, w_out, far_out, w_in, far_in]
    matrices += [bias_in.reshape(1, -1), far_bias.reshape(1, -1), w_back, far_back]
    token_count = pair_count * length
    here = pl.pallas_call(
        functools.partial(compare_kernel, length, head_dim),
        out_shape=jax.ShapeDtypeStruct((mine, width), jnp.bfloat16),
        in_specs=[smem] * 3 + [vmem] * 2 + [hbm] * 14,
        out_specs=vmem,
        scratch_shapes=[
            pltpu.VMEM((width, 2 * width), jnp.bfloat16),
            pltpu.VMEM((width, width), jnp.bfloat16),
            pltpu.VMEM((width, units), jnp.bfloat16),
            pltpu.VMEM((units, width), jnp.bfloat16),
            pltpu.VMEM((1, units), jnp.float32),
            pltpu.VMEM((2, pair_count, length, features), jnp.bfloat16),
            pltpu.VMEM((mine, units), jnp.float32),
            pltpu.VMEM((mine, width), jnp.float32),
            pltpu.SemaphoreType.DMA((12,)),
            pltpu.SemaphoreType.DMA((2,)),
        ],
        compiler_params=pltpu.CompilerParams(vmem_limit_bytes=56 * 2**20),
        cost_estimate=pl.CostEstimate(
            flops=2 * token_count * width * (3 * width + units),
            bytes_accessed=8 * 2**20,
            transcendentals=token_count * units,
        ),
    )(
        core,
        logit_scale,
        far_scale,
        gain_attn.reshape(1, -1),
        gain_mlp.reshape(1, -1),
        own,
        far,
        *matrices,
    )
    there = swap(here)
    return pl.pallas_call(
        join_kernel,
        out_shape=jax.ShapeDtypeStruct((pair_count, width), jnp.bfloat16),
        in_specs=[smem, vmem, vmem],
    )(core, here, there)


def solution(mesh):
    in_specs = (
        P(("groups", "shard"), None, "mp"),
        P(("groups", "shard"), None),
        P(("groups", "shard"), None),
        P(),
        P(None, "mp"),
        P(None, "mp"),
        P("mp"),
        P("mp", None),
        P(),
        P(None, "mp"),
        P("mp"),
        P("mp", None),
    )
    out_specs = P(("groups", "shard"), None)
    return jax.shard_map(
        on_device, mesh=mesh, in_specs=in_specs, out_specs=out_specs, check_vma=False
    )
```

```python
import functools

import jax
import jax.numpy as jnp
from jax import lax
from jax.experimental import pallas as pl
from jax.experimental.pallas import tpu as pltpu
from jax.sharding import PartitionSpec as P

LOG2E = 1.4426950408889634
BLOCK = 8


def norm_rows(values, gain):
    center = values - jnp.mean(values, axis=-1, keepdims=True)
    spread = jnp.mean(center * center, axis=-1, keepdims=True)
    return center * lax.rsqrt(spread + 1e-05) * gain


def dot_nt(a, b):
    return lax.dot_general(a, b, (((1,), (1,)), ((), ())), preferred_element_type=jnp.float32)


def dot(a, b):
    return jnp.dot(a, b, preferred_element_type=jnp.float32)


class Plan:
    def __init__(self, pair_count, owner_count):
        self.owners = owner_count
        self.capacity = max(2, 4 * pair_count // owner_count)
        self.half = owner_count // 2
        split = self.capacity >= 32 and self.half & (self.half - 1) == 0 and self.half > 0
        self.base = self.capacity // 2 if split else self.capacity
        self.extra = self.capacity - self.base
        self.part = self.half * self.extra // 2
        self.near_at = owner_count * self.base
        self.rest_at = self.near_at + self.half * self.extra
        self.slots = self.rest_at + 2 * self.part
        self.row = self.capacity + (self.half if split else 0)


def place_kernel(plan, count, shard_ref, owner_ref, slot_ref, wanted_ref, list_ref):
    total = 2 * count
    owners = plan.owners
    owner = jnp.concatenate([owner_ref[0:1, :], owner_ref[1:2, :]], axis=1)
    slot = jnp.concatenate([slot_ref[0:1, :], slot_ref[1:2, :]], axis=1)

    def place(dim, size):
        return lax.broadcasted_iota(jnp.int32, (size, total), dim)

    def as_bf16(values):
        return values.astype(jnp.float32).astype(jnp.bfloat16)

    row = place(0, owners)
    named = row == owner
    until = as_bf16(jnp.where(place(0, total) <= place(1, total), 1, 0))
    tally = dot(as_bf16(jnp.where(named, 1, 0)), until).astype(jnp.int32)
    rank = jnp.sum(jnp.where(named, tally, 0), axis=0, keepdims=True) - 1
    ranked = as_bf16(jnp.where(place(0, total) == rank, 1, 0))
    wanted = dot_nt(as_bf16(jnp.where(named, slot, 0)), ranked).astype(jnp.int32)
    where = owner * plan.base + rank
    if plan.extra:
        me = shard_ref[0]
        half = plan.half
        over = jnp.maximum(jnp.max(tally, axis=1, keepdims=True) - plan.base, 0)
        far_over = jnp.where(row // half != me // half, over, 0)
        before = jnp.zeros((owners, total), jnp.int32)
        for index in range(owners - 1):
            before = before + jnp.where(row > index, far_over[index : index + 1], 0)
        before = jnp.sum(jnp.where(named, before, 0), axis=0, keepdims=True)
        rest = rank - plan.base
        near = plan.near_at + ((owner % half) ^ (me % half)) * plan.extra + rest
        late = jnp.where(owner // half == me // half, near, plan.rest_at + before + rest)
        where = jnp.where(rest < 0, where, late)
        told = place(1, owners) == plan.capacity + row % half
        wanted = wanted + jnp.sum(jnp.where(told, far_over, 0), axis=0, keepdims=True)
    for index in range(owners):
        wanted_ref[index] = wanted[index : index + 1, : plan.row]
    entry = place(1, 1)
    side = entry // count
    pair = entry % count
    mine = count // 2
    local = pair % mine
    position = pair // mine * count + local // BLOCK * (2 * BLOCK) + side * BLOCK + local % BLOCK
    seated = as_bf16(jnp.where(place(0, total) == position, 1, 0))
    parts = as_bf16(jnp.where(place(0, 8) == 0, where // 16, where % 16))
    listed = dot_nt(parts, seated).astype(jnp.int32)
    list_ref[...] = listed[0:1] * 16 + listed[1:2]


def serve(tokens_ref, incoming_ref, requester, start, served_ref):
    count = served_ref.shape[0]

    def copy(index, carry):
        served_ref[index] = tokens_ref[incoming_ref[requester, 0, start + index]]
        return carry

    lax.fori_loop(0, count, copy, 0, unroll=min(16, count))


def serve_relays_kernel(plan, shard_ref, incoming_ref, tokens_ref, *served_refs):
    for distance, served_ref in enumerate(served_refs):
        requester = shard_ref[0] ^ (distance + plan.half)
        serve(tokens_ref, incoming_ref, requester, plan.base, served_ref)


def serve_kernel(plan, shard_ref, incoming_ref, tokens_ref, served_ref, *near_refs):
    for requester in range(plan.owners):
        serve(tokens_ref, incoming_ref, requester, 0, served_ref.at[requester])
    for distance, near_ref in enumerate(near_refs):
        serve(tokens_ref, incoming_ref, shard_ref[0] ^ distance, plan.base, near_ref)


def relay_kernel(plan, shard_ref, incoming_ref, *refs):
    chunk_refs = refs[: plan.half]
    first_ref, second_ref = refs[plan.half :]
    client = shard_ref[0] ^ plan.half
    for distance, chunk_ref in enumerate(chunk_refs):
        owner = (shard_ref[0] % plan.half) ^ distance
        at = 0
        for index in range(plan.half):
            amount = incoming_ref[client, 0, plan.capacity + index]
            at = at + jnp.where(index < owner, amount, 0)
        amount = incoming_ref[client, 0, plan.capacity + owner]
        fit = jnp.clip(plan.part - at, 0, amount)

        def pack(index, carry, chunk_ref=chunk_ref, at=at):
            first_ref[at + index] = chunk_ref[index]
            return carry

        def pack_more(index, carry, chunk_ref=chunk_ref, at=at):
            second_ref[at + index - plan.part] = chunk_ref[index]
            return carry

        lax.fori_loop(0, fit, pack, 0)
        lax.fori_loop(fit, amount, pack_more, 0)


def pick_kernel(core_ref, list_ref, *refs):
    source_refs = refs[:-3]
    picked_ref, held_ref, sems = refs[-3:]
    count = picked_ref.shape[0]
    at = 0
    loads = []
    for index, source_ref in enumerate(source_refs):
        size = source_ref.shape[0]
        loads.append(
            pltpu.make_async_copy(source_ref, held_ref.at[pl.ds(at, size)], sems.at[index])
        )
        at += size
    for load in loads:
        load.start()
    for load in loads:
        load.wait()
    start = core_ref[0] * count

    def pick(index, carry):
        picked_ref[index] = held_ref[list_ref[0, start + index]]
        return carry

    lax.fori_loop(0, count, pick, 0, unroll=16)


def compare_kernel(
    length,
    head_dim,
    core_ref,
    scale_a_ref,
    scale_b_ref,
    gain_attn_ref,
    gain_mlp_ref,
    *refs,
):
    own_held_ref, far_held_ref, *held_refs = refs[:14]
    result_ref, qkv_ref, out_ref, in_ref, back_ref, bias_ref = refs[14:20]
    tokens_ref, normed_ref, heads_ref, mixed_ref, hidden_ref = refs[20:25]
    pooled_ref, mean_ref, sems, token_sems = refs[25:]
    width, units = in_ref.shape
    wide = width // 2
    homes = [qkv_ref.at[:, pl.ds(k * wide, wide)] for k in range(4)]
    homes += [out_ref.at[pl.ds(k * wide, wide)] for k in range(2)]
    homes += [in_ref.at[:, pl.ds(k * units // 2, units // 2)] for k in range(2)]
    homes += [bias_ref.at[:, pl.ds(k * units // 2, units // 2)] for k in range(2)]
    homes += [back_ref.at[pl.ds(k * units // 2, units // 2)] for k in range(2)]
    loads = [
        pltpu.make_async_copy(held, home, sems.at[k])
        for k, (held, home) in enumerate(zip(held_refs, homes))
    ]
    core = core_ref[0]
    token_loads = [
        pltpu.make_async_copy(own_held_ref, tokens_ref.at[core], token_sems.at[0]),
        pltpu.make_async_copy(far_held_ref, tokens_ref.at[1 - core], token_sems.at[1]),
    ]
    for load in token_loads + loads:
        load.start()
    half = BLOCK * length
    rows = 2 * half
    count = result_ref.shape[0]
    blocks = count // BLOCK
    tile = 256
    scale_refs = (scale_a_ref, scale_b_ref)
    lane_head = lax.broadcasted_iota(jnp.int32, (rows, wide), 1) // head_dim
    same = (
        lax.broadcasted_iota(jnp.int32, (half, half), 0) // length
        == lax.broadcasted_iota(jnp.int32, (half, half), 1) // length
    )
    empty = jnp.zeros((half, half), jnp.bfloat16)

    def span(step, size):
        return pl.ds(pl.multiple_of(step * size, size), size)

    def begin(step, carry):
        images = pl.ds(step * 2 * BLOCK, 2 * BLOCK)
        tokens = jnp.concatenate(
            [tokens_ref[k, images].reshape(rows, -1).astype(jnp.float32) for k in range(2)], axis=1
        )
        hidden_ref[span(step, rows), :] = tokens
        normed_ref[span(step, rows), :] = norm_rows(tokens, gain_attn_ref[...]).astype(jnp.bfloat16)
        return carry

    def project(step, carry):
        cut = span(step, tile)
        heads_ref[:, cut] = dot(normed_ref[...], qkv_ref[:, cut]).astype(jnp.bfloat16)
        return carry

    def weigh(scores, factor):
        scores = jnp.where(same, scores, -1e30)
        top = jnp.max(scores, axis=1, keepdims=True)
        weights = jnp.exp2((scores - top) * factor)
        return (weights * (1.0 / jnp.sum(weights, axis=1, keepdims=True))).astype(jnp.bfloat16)

    def attend(step, carry):
        here = span(step, rows)
        for core in range(2):
            query = heads_ref[here, core * wide : (core + 1) * wide]
            value = heads_ref[here, width + core * wide : width + (core + 1) * wide]
            zero = jnp.zeros_like(query)
            heads = range(wide // head_dim)
            masked = [jnp.where(lane_head == head, query, zero) for head in heads]
            scores = dot_nt(jnp.concatenate(masked, axis=0), query)
            probs = []
            for head in heads:
                factor = scale_refs[core][head] * (LOG2E / head_dim**0.5)
                at = head * rows
                ahead = weigh(scores[at : at + half, half:], factor)
                behind = weigh(scores[at + half : at + rows, :half], factor)
                probs.append(jnp.concatenate([empty, ahead], axis=1))
                probs.append(jnp.concatenate([behind, empty], axis=1))
            mixed = dot(jnp.concatenate(probs, axis=0), value)
            total = mixed[:rows]
            for head in heads[1:]:
                total = jnp.where(lane_head == head, mixed[head * rows : (head + 1) * rows], total)
            mixed_ref[here, core * wide : (core + 1) * wide] = total.astype(jnp.bfloat16)
        return carry

    def join(step, carry):
        cut = span(step, tile)
        hidden_ref[:, cut] += dot(mixed_ref[...], out_ref[:, cut])
        return carry

    def middle(step, carry):
        here = span(step, rows)
        hidden = hidden_ref[here, :]
        mean_ref[span(step, BLOCK), :] = jnp.sum(
            hidden.reshape(2, BLOCK, length, -1), axis=(0, 2)
        )
        normed_ref[here, :] = norm_rows(hidden, gain_mlp_ref[...]).astype(jnp.bfloat16)
        return carry

    def expand(step, carry):
        cut = span(step, tile)
        inner = dot(normed_ref[...], in_ref[:, cut])
        for index in range(blocks):
            piece = inner[index * rows : (index + 1) * rows] + bias_ref[:, cut]
            bent = jnp.tanh(piece * (0.7978845608028654 + 0.035677408136300125 * (piece * piece)))
            bent = (piece * bent + piece).reshape(2, BLOCK, length, -1)
            pooled_ref[index * BLOCK : (index + 1) * BLOCK, cut] = jnp.sum(bent, axis=(0, 2))
        return carry

    for load in token_loads:
        load.wait()
    lax.fori_loop(0, blocks, begin, 0)
    for load in loads[:4]:
        load.wait()
    lax.fori_loop(0, 2 * width // tile, project, 0)
    lax.fori_loop(0, blocks, attend, 0)
    for load in loads[4:6]:
        load.wait()
    lax.fori_loop(0, width // tile, join, 0)
    lax.fori_loop(0, blocks, middle, 0)
    for load in loads[6:10]:
        load.wait()
    lax.fori_loop(0, units // tile, expand, 0)
    for load in loads[10:]:
        load.wait()
    pooled = pooled_ref[...] * (0.25 / length)
    coarse = pooled.astype(jnp.bfloat16)
    fine = (pooled - coarse.astype(jnp.float32)).astype(jnp.bfloat16)
    back = dot(jnp.concatenate([coarse, fine], axis=0), back_ref[...])
    mean = mean_ref[...] * (0.5 / length)
    result_ref[...] = (mean + back[:count] + back[count:]).astype(jnp.bfloat16)


def on_device(
    image_tokens,
    pair_owner,
    pair_slot,
    gain_attn,
    w_qk,
    w_value,
    logit_scale,
    w_out,
    gain_mlp,
    w_in,
    bias_in,
    w_back,
):
    owner_count = lax.axis_size("shard")
    groups = lax.axis_size("groups")
    core = lax.axis_index("mp").reshape(1)
    shard = lax.axis_index("shard").reshape(1)
    pair_count = pair_owner.shape[0]
    _, length, features = image_tokens.shape
    width = 2 * features
    head_dim = w_qk.shape[1] // logit_scale.shape[0]
    mine = pair_count // 2
    units = 2 * w_in.shape[1]
    plan = Plan(pair_count, owner_count)

    def swap(values):
        return lax.ppermute(values, "mp", [(0, 1), (1, 0)])

    def across(values, distance):
        return lax.ppermute(values, "shard", [(k, k ^ distance) for k in range(owner_count)])

    def images(*counts):
        return jax.ShapeDtypeStruct((*counts, length, features), jnp.bfloat16)

    smem = pl.BlockSpec(memory_space=pltpu.SMEM)
    vmem = pl.BlockSpec(memory_space=pltpu.VMEM)
    hbm = pl.BlockSpec(memory_space=pl.ANY)

    wanted, order = pl.pallas_call(
        functools.partial(place_kernel, plan, pair_count),
        out_shape=(
            jax.ShapeDtypeStruct((owner_count, 1, plan.row), jnp.int32),
            jax.ShapeDtypeStruct((1, 2 * pair_count), jnp.int32),
        ),
        in_specs=[smem, vmem, vmem],
    )(shard, pair_owner.T, pair_slot.T)
    incoming = lax.all_to_all(wanted, "shard", split_axis=0, concat_axis=0, tiled=True)
    if plan.extra:
        chunks = pl.pallas_call(
            functools.partial(serve_relays_kernel, plan),
            out_shape=[images(plan.extra)] * plan.half,
            in_specs=[smem, smem, vmem],
        )(shard, incoming, image_tokens)
        incoming, chunks = lax.optimization_barrier((incoming, chunks))
        chunks = [chunks[0]] + [across(chunks[k], k) for k in range(1, plan.half)]
    served, *near = pl.pallas_call(
        functools.partial(serve_kernel, plan),
        out_shape=[images(owner_count, plan.base)]
        + [images(plan.extra)] * (plan.half if plan.extra else 0),
        in_specs=[smem, smem, vmem],
    )(shard, incoming, image_tokens)
    if plan.extra:
        served, near, chunks = lax.optimization_barrier((served, near, chunks))
    returned = lax.all_to_all(served, "shard", split_axis=0, concat_axis=0, tiled=True)
    sources = [returned.reshape(-1, length, features)]
    weights = (w_qk, w_value, w_out, w_in, w_back, bias_in, logit_scale)
    if plan.extra:
        first, second = pl.pallas_call(
            functools.partial(relay_kernel, plan),
            out_shape=[images(plan.part)] * 2,
            in_specs=[smem, smem] + [vmem] * plan.half,
        )(shard, incoming, *chunks)
        first = across(first, plan.half)
        near = [near[0]] + [across(near[k], k) for k in range(1, plan.half)]
        crowded = jnp.max(jnp.sum(incoming[:, 0, plan.capacity :], axis=1)) > plan.part
        crowded = crowded.astype(jnp.int32)
        passed = crowded
        for _ in range(groups - 1):
            passed = lax.ppermute(passed, "groups", [(k, (k + 1) % groups) for k in range(groups)])
            crowded = jnp.maximum(crowded, passed)
        sources += [*near, first]
    swapped = [swap(w) for w in weights]
    sources, swapped = lax.optimization_barrier((sources, swapped))
    if plan.extra:
        second, sources = lax.optimization_barrier((second, sources))
        second = lax.cond(
            crowded > 0, lambda part: across(part, plan.half), lambda part: part, second
        )
        sources = [*sources, second]
    far_qk, far_value, far_out, far_in, far_back, far_bias, far_scale = swapped

    def pick(core):
        return pl.pallas_call(
            pick_kernel,
            out_shape=images(pair_count),
            in_specs=[smem, smem] + [hbm] * len(sources),
            scratch_shapes=[
                pltpu.VMEM((plan.slots, length, features), jnp.bfloat16),
                pltpu.SemaphoreType.DMA((len(sources),)),
            ],
        )(core, order, *sources)

    far = swap(pick(1 - core))
    own = pick(core)
    matrices = [w_qk, far_qk, w_value, far_value, w_out, far_out, w_in, far_in]
    matrices += [bias_in.reshape(1, -1), far_bias.reshape(1, -1), w_back, far_back]
    token_count = pair_count * length
    here = pl.pallas_call(
        functools.partial(compare_kernel, length, head_dim),
        out_shape=jax.ShapeDtypeStruct((mine, width), jnp.bfloat16),
        in_specs=[smem] * 3 + [vmem] * 2 + [hbm] * 14,
        out_specs=vmem,
        scratch_shapes=[
            pltpu.VMEM((width, 2 * width), jnp.bfloat16),
            pltpu.VMEM((width, width), jnp.bfloat16),
            pltpu.VMEM((width, units), jnp.bfloat16),
            pltpu.VMEM((units, width), jnp.bfloat16),
            pltpu.VMEM((1, units), jnp.float32),
            pltpu.VMEM((2, pair_count, length, features), jnp.bfloat16),
            pltpu.VMEM((token_count, width), jnp.bfloat16),
            pltpu.VMEM((token_count, 2 * width), jnp.bfloat16),
            pltpu.VMEM((token_count, width), jnp.bfloat16),
            pltpu.VMEM((token_count, width), jnp.float32),
            pltpu.VMEM((mine, units), jnp.float32),
            pltpu.VMEM((mine, width), jnp.float32),
            pltpu.SemaphoreType.DMA((12,)),
            pltpu.SemaphoreType.DMA((2,)),
        ],
        compiler_params=pltpu.CompilerParams(vmem_limit_bytes=56 * 2**20),
        cost_estimate=pl.CostEstimate(
            flops=2 * token_count * width * (3 * width + units),
            bytes_accessed=8 * 2**20,
            transcendentals=token_count * units,
        ),
    )(
        core,
        logit_scale,
        far_scale,
        gain_attn.reshape(1, -1),
        gain_mlp.reshape(1, -1),
        own,
        far,
        *matrices,
    )
    there = swap(here)
    low = jnp.where(core == 0, here, there)
    high = jnp.where(core == 0, there, here)
    return jnp.concatenate([low, high], axis=0)


def solution(mesh):
    in_specs = (
        P(("groups", "shard"), None, "mp"),
        P(("groups", "shard"), None),
        P(("groups", "shard"), None),
        P(),
        P(None, "mp"),
        P(None, "mp"),
        P("mp"),
        P("mp", None),
        P(),
        P(None, "mp"),
        P("mp"),
        P("mp", None),
    )
    out_specs = P(("groups", "shard"), None)
    return jax.shard_map(
        on_device, mesh=mesh, in_specs=in_specs, out_specs=out_specs, check_vma=False
    )
```

```python
import functools

import jax
import jax.numpy as jnp
from jax import lax
from jax.experimental import pallas as pl
from jax.experimental.pallas import tpu as pltpu
from jax.sharding import PartitionSpec as P

LOG2E = 1.4426950408889634
BLOCK = 8


def norm_rows(values, gain):
    center = values - jnp.mean(values, axis=-1, keepdims=True)
    spread = jnp.mean(center * center, axis=-1, keepdims=True)
    return center * lax.rsqrt(spread + 1e-05) * gain


def dot_nt(a, b):
    return lax.dot_general(a, b, (((1,), (1,)), ((), ())), preferred_element_type=jnp.float32)


def dot(a, b):
    return jnp.dot(a, b, preferred_element_type=jnp.float32)


class Plan:
    def __init__(self, pair_count, owner_count):
        self.owners = owner_count
        self.capacity = max(2, 4 * pair_count // owner_count)
        self.half = owner_count // 2
        split = self.capacity >= 32 and self.half & (self.half - 1) == 0 and self.half > 0
        self.base = self.capacity // 2 if split else self.capacity
        self.extra = self.capacity - self.base
        self.part = self.half * self.extra // 2
        self.near_at = owner_count * self.base
        self.rest_at = self.near_at + self.half * self.extra
        self.slots = self.rest_at + 2 * self.part
        self.row = self.capacity + (self.half if split else 0)


def place_kernel(plan, count, shard_ref, owner_ref, slot_ref, wanted_ref, list_ref):
    total = 2 * count
    owners = plan.owners
    owner = jnp.concatenate([owner_ref[0:1, :], owner_ref[1:2, :]], axis=1)
    slot = jnp.concatenate([slot_ref[0:1, :], slot_ref[1:2, :]], axis=1)

    def place(dim, size):
        return lax.broadcasted_iota(jnp.int32, (size, total), dim)

    def as_bf16(values):
        return values.astype(jnp.float32).astype(jnp.bfloat16)

    row = place(0, owners)
    named = row == owner
    until = as_bf16(jnp.where(place(0, total) <= place(1, total), 1, 0))
    tally = dot(as_bf16(jnp.where(named, 1, 0)), until).astype(jnp.int32)
    rank = jnp.sum(jnp.where(named, tally, 0), axis=0, keepdims=True) - 1
    ranked = as_bf16(jnp.where(place(0, total) == rank, 1, 0))
    wanted = dot_nt(as_bf16(jnp.where(named, slot, 0)), ranked).astype(jnp.int32)
    where = owner * plan.base + rank
    if plan.extra:
        me = shard_ref[0]
        half = plan.half
        over = jnp.maximum(jnp.max(tally, axis=1, keepdims=True) - plan.base, 0)
        far_over = jnp.where(row // half != me // half, over, 0)
        before = jnp.zeros((owners, total), jnp.int32)
        for index in range(owners - 1):
            before = before + jnp.where(row > index, far_over[index : index + 1], 0)
        before = jnp.sum(jnp.where(named, before, 0), axis=0, keepdims=True)
        rest = rank - plan.base
        near = plan.near_at + ((owner % half) ^ (me % half)) * plan.extra + rest
        late = jnp.where(owner // half == me // half, near, plan.rest_at + before + rest)
        where = jnp.where(rest < 0, where, late)
        told = place(1, owners) == plan.capacity + row % half
        wanted = wanted + jnp.sum(jnp.where(told, far_over, 0), axis=0, keepdims=True)
    for index in range(owners):
        wanted_ref[index] = wanted[index : index + 1, : plan.row]
    entry = place(1, 1)
    side = entry // count
    pair = entry % count
    mine = count // 2
    local = pair % mine
    position = pair // mine * count + local // BLOCK * (2 * BLOCK) + side * BLOCK + local % BLOCK
    seated = as_bf16(jnp.where(place(0, total) == position, 1, 0))
    parts = as_bf16(jnp.where(place(0, 8) == 0, where // 16, where % 16))
    listed = dot_nt(parts, seated).astype(jnp.int32)
    list_ref[...] = listed[0:1] * 16 + listed[1:2]


def serve(tokens_ref, incoming_ref, requester, start, served_ref):
    count = served_ref.shape[0]

    def copy(index, carry):
        served_ref[index] = tokens_ref[incoming_ref[requester, 0, start + index]]
        return carry

    lax.fori_loop(0, count, copy, 0, unroll=min(16, count))


def serve_relays_kernel(plan, shard_ref, incoming_ref, tokens_ref, *served_refs):
    for distance, served_ref in enumerate(served_refs):
        requester = shard_ref[0] ^ (distance + plan.half)
        serve(tokens_ref, incoming_ref, requester, plan.base, served_ref)


def serve_kernel(plan, shard_ref, incoming_ref, tokens_ref, served_ref, *near_refs):
    for requester in range(plan.owners):
        serve(tokens_ref, incoming_ref, requester, 0, served_ref.at[requester])
    for distance, near_ref in enumerate(near_refs):
        serve(tokens_ref, incoming_ref, shard_ref[0] ^ distance, plan.base, near_ref)


def relay_kernel(plan, shard_ref, incoming_ref, *refs):
    chunk_refs = refs[: plan.half]
    first_ref, second_ref = refs[plan.half :]
    client = shard_ref[0] ^ plan.half
    for distance, chunk_ref in enumerate(chunk_refs):
        owner = (shard_ref[0] % plan.half) ^ distance
        at = 0
        for index in range(plan.half):
            amount = incoming_ref[client, 0, plan.capacity + index]
            at = at + jnp.where(index < owner, amount, 0)
        amount = incoming_ref[client, 0, plan.capacity + owner]
        fit = jnp.clip(plan.part - at, 0, amount)

        def pack(index, carry, chunk_ref=chunk_ref, at=at):
            first_ref[at + index] = chunk_ref[index]
            return carry

        def pack_more(index, carry, chunk_ref=chunk_ref, at=at):
            second_ref[at + index - plan.part] = chunk_ref[index]
            return carry

        lax.fori_loop(0, fit, pack, 0)
        lax.fori_loop(fit, amount, pack_more, 0)


def pick_kernel(core_ref, list_ref, *refs):
    *source_refs, picked_ref = refs
    count = picked_ref.shape[0]
    start = core_ref[0] * count
    starts = [0]
    for source_ref in source_refs:
        starts.append(starts[-1] + source_ref.shape[0])

    def pick(index, carry):
        where = list_ref[0, start + index]

        def among(low, high):
            if high - low == 1:
                picked_ref[index] = source_refs[low][where - starts[low]]
                return
            middle = (low + high) // 2

            @pl.when(where < starts[middle])
            def _():
                among(low, middle)

            @pl.when(where >= starts[middle])
            def _():
                among(middle, high)

        if len(source_refs) == 1:
            among(0, 1)
        else:

            @pl.when(where < starts[1])
            def _():
                among(0, 1)

            @pl.when(where >= starts[1])
            def _():
                among(1, len(source_refs))

        return carry

    lax.fori_loop(0, count, pick, 0)


def attention_kernel(
    length,
    head_dim,
    core_ref,
    scale_a_ref,
    scale_b_ref,
    gain_attn_ref,
    gain_mlp_ref,
    *refs,
):
    own_held_ref, far_held_ref, qk_ref, value_ref, part_ref, far_cols_ref, far_rows_ref = refs[:7]
    normed_ref, mean_ref, qkv_ref, out_ref = refs[7:11]
    tokens_ref, heads_ref, mixed_ref, hidden_ref, sems, token_sems = refs[11:]
    width = out_ref.shape[0]
    wide = width // 2
    homes = [qkv_ref.at[:, pl.ds(k * wide, wide)] for k in (0, 2, 1, 3)]
    homes += [out_ref.at[pl.ds(k * wide, wide)] for k in range(2)]
    held_refs = [qk_ref, value_ref]
    held_refs += [far_cols_ref.at[:, pl.ds(k * wide, wide)] for k in range(2)]
    held_refs += [part_ref, far_rows_ref.at[pl.ds(0, wide)]]
    loads = [
        pltpu.make_async_copy(held, home, sems.at[k])
        for k, (held, home) in enumerate(zip(held_refs, homes))
    ]
    core = core_ref[0]
    token_loads = [
        pltpu.make_async_copy(own_held_ref, tokens_ref.at[core], token_sems.at[0]),
        pltpu.make_async_copy(far_held_ref, tokens_ref.at[1 - core], token_sems.at[1]),
    ]
    for load in token_loads + loads:
        load.start()
    half = BLOCK * length
    rows = 2 * half
    blocks = tokens_ref.shape[1] // (2 * BLOCK)
    long = 2 * rows
    pair_dim = 2 * head_dim
    scale_refs = (scale_a_ref, scale_b_ref)
    per_core = wide // head_dim
    even = lax.broadcasted_iota(jnp.int32, (half, pair_dim), 1) < head_dim
    same = (
        lax.broadcasted_iota(jnp.int32, (half, half), 0) // length
        == lax.broadcasted_iota(jnp.int32, (half, half), 1) // length
    )

    def span(step, size):
        return pl.ds(pl.multiple_of(step * size, size), size)

    def split(values):
        zero = jnp.zeros_like(values)
        return jnp.concatenate(
            [jnp.where(even, values, zero), jnp.where(even, zero, values)], axis=0
        )

    ones = split(jnp.ones((half, pair_dim), jnp.bfloat16))

    def start_block(step, carry):
        images = pl.ds(step * 2 * BLOCK, 2 * BLOCK)
        tokens = jnp.concatenate(
            [tokens_ref[k, images].reshape(rows, -1).astype(jnp.float32) for k in range(2)], axis=1
        )
        hidden_ref[span(step, rows), :] = tokens
        normed_ref[span(step, rows), :] = norm_rows(tokens, gain_attn_ref[...]).astype(jnp.bfloat16)
        return carry

    def project(step, carry):
        here = span(step // 4, long)
        cut = span(step % 4, 2 * width // 4)
        heads_ref[here, cut] = dot(normed_ref[here, :], qkv_ref[:, cut]).astype(jnp.bfloat16)
        return carry

    def weigh(scores, factor):
        scores = jnp.where(same, scores, -1e30)
        top = jnp.max(scores, axis=1, keepdims=True)
        return jnp.exp2((scores - top) * factor).astype(jnp.bfloat16)

    def mix(query, key, value, factors):
        scores = dot_nt(query, split(key))
        weights = [weigh(scores[:, k * half : (k + 1) * half], factors[k]) for k in range(2)]
        mixed = dot(jnp.concatenate(weights, axis=1), jnp.concatenate([split(value), ones], axis=1))
        total = mixed[:, pair_dim:]
        inverse = pl.reciprocal(total, approx=True)
        inverse = inverse * (2.0 - total * inverse)
        return (mixed[:, :pair_dim] * inverse).astype(jnp.bfloat16)

    def attend(step, carry):
        for index in range(width // pair_dim):
            factors = [scale_refs[k // per_core][k % per_core] for k in (2 * index, 2 * index + 1)]
            factors = [factor * (LOG2E / head_dim**0.5) for factor in factors]
            cut = slice(index * pair_dim, (index + 1) * pair_dim)
            beyond = slice(width + cut.start, width + cut.stop)
            sides = [span(2 * step + k, half) for k in range(2)]
            query = [heads_ref[side, cut] for side in sides]
            value = [heads_ref[side, beyond] for side in sides]
            for k in range(2):
                mixed_ref[sides[k], cut] = mix(query[k], query[1 - k], value[1 - k], factors)
        return carry

    def join(step, carry):
        here = span(step // 2, long)
        cut = span(step % 2, width // 2)
        hidden_ref[here, cut] += dot(mixed_ref[here, :], out_ref[:, cut])
        return carry

    def middle_block(step, carry):
        here = span(step, rows)
        hidden = hidden_ref[here, :]
        mean_ref[span(step, BLOCK), :] = jnp.sum(
            hidden.reshape(2, BLOCK, length, -1), axis=(0, 2)
        )
        normed_ref[here, :] = norm_rows(hidden, gain_mlp_ref[...]).astype(jnp.bfloat16)
        return carry

    for load in token_loads:
        load.wait()
    lax.fori_loop(0, blocks, start_block, 0)
    for load in loads[:4]:
        load.wait()
    lax.fori_loop(0, blocks // 2 * 4, project, 0)
    lax.fori_loop(0, blocks, attend, 0)
    for load in loads[4:6]:
        load.wait()
    lax.fori_loop(0, blocks // 2 * 2, join, 0)
    lax.fori_loop(0, blocks, middle_block, 0)


def back_kernel(length, core_ref, mean_ref, pooled_ref, back_ref, far_rows_ref, result_ref):
    count = mean_ref.shape[0]
    units = back_ref.shape[0]
    skip = far_rows_ref.shape[0] - units
    pooled = pooled_ref[...] * (0.5 / length)
    coarse = pooled.astype(jnp.bfloat16)
    fine = (pooled - coarse.astype(jnp.float32)).astype(jnp.bfloat16)
    both = jnp.concatenate([coarse, fine], axis=0)
    back = dot(both[:, :units], back_ref[...]) + dot(both[:, units:], far_rows_ref[skip:, :])
    mean = mean_ref[...] * (0.5 / length)
    result = (mean + back[:count] + back[count:]).astype(jnp.bfloat16)
    start = pl.multiple_of(core_ref[0] * count, count)
    result_ref[pl.ds(start, count), :] = result
    result_ref[pl.ds(pl.multiple_of(count - start, count), count), :] = jnp.zeros_like(result)


def expand(normed, w_in, bias, length):
    inner = dot(normed, w_in) + bias
    inner = jax.nn.gelu(inner, approximate=True).astype(jnp.bfloat16).astype(jnp.float32)
    inner = inner.reshape(-1, 2, BLOCK, length, inner.shape[-1])
    return jnp.sum(inner, axis=(1, 3)).reshape(-1, inner.shape[-1])


def on_device(
    image_tokens,
    pair_owner,
    pair_slot,
    gain_attn,
    w_qk,
    w_value,
    logit_scale,
    w_out,
    gain_mlp,
    w_in,
    bias_in,
    w_back,
):
    owner_count = lax.axis_size("shard")
    groups = lax.axis_size("groups")
    core = lax.axis_index("mp").reshape(1)
    shard = lax.axis_index("shard").reshape(1)
    pair_count = pair_owner.shape[0]
    _, length, features = image_tokens.shape
    width = 2 * features
    head_dim = w_qk.shape[1] // logit_scale.shape[0]
    mine = pair_count // 2
    units = 2 * w_in.shape[1]
    plan = Plan(pair_count, owner_count)

    def swap(values):
        return lax.ppermute(values, "mp", [(0, 1), (1, 0)])

    def across(values, distance):
        return lax.ppermute(values, "shard", [(k, k ^ distance) for k in range(owner_count)])

    def images(*counts):
        return jax.ShapeDtypeStruct((*counts, length, features), jnp.bfloat16)

    smem = pl.BlockSpec(memory_space=pltpu.SMEM)
    vmem = pl.BlockSpec(memory_space=pltpu.VMEM)
    hbm = pl.BlockSpec(memory_space=pl.ANY)

    def limit(mebibytes):
        return pltpu.CompilerParams(vmem_limit_bytes=mebibytes * 2**20)

    wanted, order = pl.pallas_call(
        functools.partial(place_kernel, plan, pair_count),
        out_shape=(
            jax.ShapeDtypeStruct((owner_count, 1, plan.row), jnp.int32),
            jax.ShapeDtypeStruct((1, 2 * pair_count), jnp.int32),
        ),
        in_specs=[smem, vmem, vmem],
    )(shard, pair_owner.T, pair_slot.T)
    incoming = lax.all_to_all(wanted, "shard", split_axis=0, concat_axis=0, tiled=True)
    served, *near = pl.pallas_call(
        functools.partial(serve_kernel, plan),
        out_shape=[images(owner_count, plan.base)]
        + [images(plan.extra)] * (plan.half if plan.extra else 0),
        in_specs=[smem, smem, vmem],
    )(shard, incoming, image_tokens)
    returned = lax.all_to_all(served, "shard", split_axis=0, concat_axis=0, tiled=True)
    sources = [returned.reshape(-1, length, features)]
    weights = (w_qk, w_value, w_out, w_in, w_back, bias_in, logit_scale)
    if plan.extra:
        incoming, served = lax.optimization_barrier((incoming, served))
        chunks = pl.pallas_call(
            functools.partial(serve_relays_kernel, plan),
            out_shape=[images(plan.extra)] * plan.half,
            in_specs=[smem, smem, vmem],
        )(shard, incoming, image_tokens)
        chunks, weights, incoming = lax.optimization_barrier((chunks, weights, incoming))
        chunks = [chunks[0]] + [across(chunks[k], k) for k in range(1, plan.half)]
        first, second = pl.pallas_call(
            functools.partial(relay_kernel, plan),
            out_shape=[images(plan.part)] * 2,
            in_specs=[smem, smem] + [vmem] * plan.half,
        )(shard, incoming, *chunks)
        first, near = lax.optimization_barrier((first, near))
        first = across(first, plan.half)
        near = [near[0]] + [across(near[k], k) for k in range(1, plan.half)]
        crowded = jnp.max(jnp.sum(incoming[:, 0, plan.capacity :], axis=1)) > plan.part
        crowded = crowded.astype(jnp.int32)
        passed = crowded
        for _ in range(groups - 1):
            passed = lax.ppermute(passed, "groups", [(k, (k + 1) % groups) for k in range(groups)])
            crowded = jnp.maximum(crowded, passed)
        sources += [*near, first]
    near_qk, near_value, near_out, near_in, near_back, near_bias, near_scale = weights
    far_cols = swap(jnp.concatenate([near_qk, near_value, near_in], axis=1))
    far_rows = swap(jnp.concatenate([near_out, near_back], axis=0))
    far_small = swap(jnp.concatenate([near_bias, near_scale]))
    all_in = jnp.concatenate([near_in, far_cols[:, width:]], axis=1)
    all_bias = jnp.concatenate([near_bias, far_small[: near_bias.shape[0]]])
    far_scale = far_small[near_bias.shape[0] :]
    arrived = (sources, far_cols, far_rows, far_scale, all_in, all_bias)
    sources, far_cols, far_rows, far_scale, all_in, all_bias = lax.optimization_barrier(arrived)
    if plan.extra:
        second, sources = lax.optimization_barrier((second, sources))
        second = lax.cond(
            crowded > 0, lambda part: across(part, plan.half), lambda part: part, second
        )
        sources = [*sources, second]

    def pick(core):
        return pl.pallas_call(
            pick_kernel,
            out_shape=images(pair_count),
            in_specs=[smem, smem] + [vmem] * len(sources),
            compiler_params=limit(16),
        )(core, order, *sources)

    far = swap(pick(1 - core))
    own = pick(core)
    token_count = pair_count * length
    normed, mean = pl.pallas_call(
        functools.partial(attention_kernel, length, head_dim),
        out_shape=(
            jax.ShapeDtypeStruct((token_count, width), jnp.bfloat16),
            jax.ShapeDtypeStruct((mine, width), jnp.float32),
        ),
        in_specs=[smem] * 3 + [vmem] * 2 + [hbm] * 7,
        scratch_shapes=[
            pltpu.VMEM((width, 2 * width), jnp.bfloat16),
            pltpu.VMEM((width, width), jnp.bfloat16),
            pltpu.VMEM((2, pair_count, length, features), jnp.bfloat16),
            pltpu.VMEM((token_count, 2 * width), jnp.bfloat16),
            pltpu.VMEM((token_count, width), jnp.bfloat16),
            pltpu.VMEM((token_count, width), jnp.float32),
            pltpu.SemaphoreType.DMA((6,)),
            pltpu.SemaphoreType.DMA((2,)),
        ],
        compiler_params=limit(24),
        cost_estimate=pl.CostEstimate(
            flops=6 * token_count * width * width,
            bytes_accessed=4 * 2**20,
            transcendentals=token_count * 1024,
        ),
    )(
        core,
        near_scale,
        far_scale,
        gain_attn.reshape(1, -1),
        gain_mlp.reshape(1, -1),
        own,
        far,
        near_qk,
        near_value,
        near_out,
        far_cols,
        far_rows,
    )
    here = pl.pallas_call(
        functools.partial(back_kernel, length),
        out_shape=jax.ShapeDtypeStruct((pair_count, width), jnp.bfloat16),
        in_specs=[smem] + [vmem] * 4,
        compiler_params=limit(16),
    )(core, mean, expand(normed, all_in, all_bias, length), near_back, far_rows)
    return here + swap(here)


def solution(mesh):
    in_specs = (
        P(("groups", "shard"), None, "mp"),
        P(("groups", "shard"), None),
        P(("groups", "shard"), None),
        P(),
        P(None, "mp"),
        P(None, "mp"),
        P("mp"),
        P("mp", None),
        P(),
        P(None, "mp"),
        P("mp"),
        P("mp", None),
    )
    out_specs = P(("groups", "shard"), None)
    return jax.shard_map(
        on_device, mesh=mesh, in_specs=in_specs, out_specs=out_specs, check_vma=False
    )
```

```python
import functools

import jax
import jax.numpy as jnp
from jax import lax
from jax.experimental import pallas as pl
from jax.experimental.pallas import tpu as pltpu
from jax.sharding import PartitionSpec as P

LOG2E = 1.4426950408889634
BLOCK = 8


def norm_rows(values, gain):
    center = values - jnp.mean(values, axis=-1, keepdims=True)
    spread = jnp.mean(center * center, axis=-1, keepdims=True)
    return center * lax.rsqrt(spread + 1e-05) * gain


def dot_nt(a, b):
    return lax.dot_general(a, b, (((1,), (1,)), ((), ())), preferred_element_type=jnp.float32)


def dot(a, b):
    return jnp.dot(a, b, preferred_element_type=jnp.float32)


class Plan:
    def __init__(self, pair_count, owner_count):
        self.owners = owner_count
        self.capacity = max(2, 4 * pair_count // owner_count)
        self.half = owner_count // 2
        split = self.capacity >= 32 and self.half & (self.half - 1) == 0 and self.half > 0
        self.base = self.capacity // 2 if split else self.capacity
        self.extra = self.capacity - self.base
        self.part = self.half * self.extra // 2
        self.near_at = owner_count * self.base
        self.rest_at = self.near_at + self.half * self.extra
        self.slots = self.rest_at + 2 * self.part
        self.row = self.capacity + (self.half if split else 0)


def place_kernel(plan, count, shard_ref, owner_ref, slot_ref, list_ref, *wanted_refs):
    total = 2 * count
    owners = plan.owners
    owner = jnp.concatenate([owner_ref[0:1, :], owner_ref[1:2, :]], axis=1)
    slot = jnp.concatenate([slot_ref[0:1, :], slot_ref[1:2, :]], axis=1)

    def place(dim, size):
        return lax.broadcasted_iota(jnp.int32, (size, total), dim)

    def as_bf16(values):
        return values.astype(jnp.float32).astype(jnp.bfloat16)

    row = place(0, owners)
    named = row == owner
    until = as_bf16(jnp.where(place(0, total) <= place(1, total), 1, 0))
    tally = dot(as_bf16(jnp.where(named, 1, 0)), until).astype(jnp.int32)
    rank = jnp.sum(jnp.where(named, tally, 0), axis=0, keepdims=True) - 1
    ranked = as_bf16(jnp.where(place(0, total) == rank, 1, 0))
    wanted = dot_nt(as_bf16(jnp.where(named, slot, 0)), ranked).astype(jnp.int32)
    where = owner * plan.base + rank
    if plan.extra:
        me = shard_ref[0]
        half = plan.half
        over = jnp.maximum(jnp.max(tally, axis=1, keepdims=True) - plan.base, 0)
        far_over = jnp.where(row // half != me // half, over, 0)
        before = jnp.zeros((owners, total), jnp.int32)
        for index in range(owners - 1):
            before = before + jnp.where(row > index, far_over[index : index + 1], 0)
        before = jnp.sum(jnp.where(named, before, 0), axis=0, keepdims=True)
        rest = rank - plan.base
        near = plan.near_at + ((owner % half) ^ (me % half)) * plan.extra + rest
        late = jnp.where(owner // half == me // half, near, plan.rest_at + before + rest)
        where = jnp.where(rest < 0, where, late)
        told = place(1, owners) == plan.capacity + row % half
        wanted = wanted + jnp.sum(jnp.where(told, far_over, 0), axis=0, keepdims=True)
    if plan.extra:
        for distance, wanted_ref in enumerate(wanted_refs):
            chosen = jnp.where(row == me ^ distance, wanted, 0)
            wanted_ref[...] = jnp.sum(chosen, axis=0, keepdims=True)[:, : plan.row]
    else:
        for index in range(owners):
            wanted_refs[0][index] = wanted[index : index + 1, : plan.row]
    entry = place(1, 1)
    side = entry // count
    pair = entry % count
    mine = count // 2
    local = pair % mine
    position = pair // mine * count + local // BLOCK * (2 * BLOCK) + side * BLOCK + local % BLOCK
    seated = as_bf16(jnp.where(place(0, total) == position, 1, 0))
    parts = as_bf16(jnp.where(place(0, 8) == 0, where // 16, where % 16))
    listed = dot_nt(parts, seated).astype(jnp.int32)
    list_ref[...] = listed[0:1] * 16 + listed[1:2]


def serve(tokens_ref, incoming_ref, start, served_ref):
    count = served_ref.shape[0]

    def copy(index, carry):
        served_ref[index] = tokens_ref[incoming_ref[0, start + index]]
        return carry

    lax.fori_loop(0, count, copy, 0, unroll=min(16, count))


def serve_relays_kernel(plan, *refs):
    incoming_refs, (tokens_ref, *served_refs) = refs[: plan.owners], refs[plan.owners :]
    *served_refs, crowded_ref = served_refs
    for incoming_ref, served_ref in zip(incoming_refs[plan.half :], served_refs):
        serve(tokens_ref, incoming_ref, plan.base, served_ref)
    most = 0
    for incoming_ref in incoming_refs:
        total = 0
        for index in range(plan.half):
            total = total + incoming_ref[0, plan.capacity + index]
        most = jnp.maximum(most, total)
    crowded_ref[0] = jnp.where(most > plan.part, 1, 0)


def serve_kernel(plan, shard_ref, *refs):
    incoming_refs, (tokens_ref, served_ref, *near_refs) = refs[: plan.owners], refs[plan.owners :]
    for distance, incoming_ref in enumerate(incoming_refs):
        serve(tokens_ref, incoming_ref, 0, served_ref.at[shard_ref[0] ^ distance])
    for incoming_ref, near_ref in zip(incoming_refs, near_refs):
        serve(tokens_ref, incoming_ref, plan.base, near_ref)


def serve_all_kernel(plan, incoming_ref, tokens_ref, served_ref):
    for requester in range(plan.owners):
        serve(tokens_ref, incoming_ref.at[requester], 0, served_ref.at[requester])


def relay_kernel(plan, shard_ref, incoming_ref, *refs):
    chunk_refs = refs[: plan.half]
    first_ref, second_ref = refs[plan.half :]
    for distance, chunk_ref in enumerate(chunk_refs):
        owner = (shard_ref[0] % plan.half) ^ distance
        at = 0
        for index in range(plan.half):
            amount = incoming_ref[0, plan.capacity + index]
            at = at + jnp.where(index < owner, amount, 0)
        amount = incoming_ref[0, plan.capacity + owner]
        fit = jnp.clip(plan.part - at, 0, amount)

        def pack(index, carry, chunk_ref=chunk_ref, at=at):
            first_ref[at + index] = chunk_ref[index]
            return carry

        def pack_more(index, carry, chunk_ref=chunk_ref, at=at):
            second_ref[at + index - plan.part] = chunk_ref[index]
            return carry

        lax.fori_loop(0, fit, pack, 0)
        lax.fori_loop(fit, amount, pack_more, 0)


def pick_kernel(plan, core_ref, list_ref, *refs):
    source_refs = refs[:-4]
    own_ref, other_ref, held_ref, sems = refs[-4:]
    count = own_ref.shape[0]
    at = 0
    loads = []
    for index, source_ref in enumerate(source_refs):
        size = source_ref.shape[0]
        loads.append(
            pltpu.make_async_copy(source_ref, held_ref.at[pl.ds(at, size)], sems.at[index])
        )
        at += size
    for load in loads:
        load.start()
    for load in loads:
        load.wait()
    start = core_ref[0] * count

    def pick(index, carry):
        other_ref[index] = held_ref[list_ref[0, count - start + index]]
        own_ref[index] = held_ref[list_ref[0, start + index]]
        return carry

    lax.fori_loop(0, count, pick, 0, unroll=8)


def attention_kernel(
    length,
    head_dim,
    core_ref,
    scale_a_ref,
    scale_b_ref,
    gain_attn_ref,
    gain_mlp_ref,
    *refs,
):
    own_held_ref, far_held_ref, *held_refs = refs[:8]
    normed_ref, mean_ref, qkv_ref, out_ref = refs[8:12]
    tokens_ref, heads_ref, mixed_ref, hidden_ref, sems, token_sems = refs[12:]
    width = out_ref.shape[0]
    wide = width // 2
    homes = [qkv_ref.at[:, pl.ds(k * wide, wide)] for k in range(4)]
    homes += [out_ref.at[pl.ds(k * wide, wide)] for k in range(2)]
    loads = [
        pltpu.make_async_copy(held, home, sems.at[k])
        for k, (held, home) in enumerate(zip(held_refs, homes))
    ]
    core = core_ref[0]
    token_loads = [
        pltpu.make_async_copy(own_held_ref, tokens_ref.at[core], token_sems.at[0]),
        pltpu.make_async_copy(far_held_ref, tokens_ref.at[1 - core], token_sems.at[1]),
    ]
    for load in token_loads + loads:
        load.start()
    half = BLOCK * length
    rows = 2 * half
    blocks = tokens_ref.shape[1] // (2 * BLOCK)
    long = 2 * rows
    pair_dim = 2 * head_dim
    scale_refs = (scale_a_ref, scale_b_ref)
    per_core = wide // head_dim
    even = lax.broadcasted_iota(jnp.int32, (half, pair_dim), 1) < head_dim
    same = (
        lax.broadcasted_iota(jnp.int32, (half, half), 0) // length
        == lax.broadcasted_iota(jnp.int32, (half, half), 1) // length
    )

    def span(step, size):
        return pl.ds(pl.multiple_of(step * size, size), size)

    def split(values):
        zero = jnp.zeros_like(values)
        return jnp.concatenate(
            [jnp.where(even, values, zero), jnp.where(even, zero, values)], axis=0
        )

    ones = split(jnp.ones((half, pair_dim), jnp.bfloat16))

    def start_block(step, carry):
        images = pl.ds(step * 2 * BLOCK, 2 * BLOCK)
        tokens = jnp.concatenate(
            [tokens_ref[k, images].reshape(rows, -1).astype(jnp.float32) for k in range(2)], axis=1
        )
        hidden_ref[span(step, rows), :] = tokens
        normed_ref[span(step, rows), :] = norm_rows(tokens, gain_attn_ref[...]).astype(jnp.bfloat16)
        return carry

    def project(step, carry):
        here = span(step // 4, long)
        cut = span(step % 4, 2 * width // 4)
        heads_ref[here, cut] = dot(normed_ref[here, :], qkv_ref[:, cut]).astype(jnp.bfloat16)
        return carry

    def weigh(scores, factor):
        scores = jnp.where(same, scores, -1e30)
        top = jnp.max(scores, axis=1, keepdims=True)
        return jnp.exp2((scores - top) * factor).astype(jnp.bfloat16)

    def mix(query, key, value, factors):
        scores = dot_nt(query, split(key))
        weights = [weigh(scores[:, k * half : (k + 1) * half], factors[k]) for k in range(2)]
        mixed = dot(jnp.concatenate(weights, axis=1), jnp.concatenate([split(value), ones], axis=1))
        total = mixed[:, pair_dim:]
        inverse = pl.reciprocal(total, approx=True)
        inverse = inverse * (2.0 - total * inverse)
        return (mixed[:, :pair_dim] * inverse).astype(jnp.bfloat16)

    def attend(step, carry):
        for index in range(width // pair_dim):
            factors = [scale_refs[k // per_core][k % per_core] for k in (2 * index, 2 * index + 1)]
            factors = [factor * (LOG2E / head_dim**0.5) for factor in factors]
            cut = slice(index * pair_dim, (index + 1) * pair_dim)
            beyond = slice(width + cut.start, width + cut.stop)
            sides = [span(2 * step + k, half) for k in range(2)]
            query = [heads_ref[side, cut] for side in sides]
            value = [heads_ref[side, beyond] for side in sides]
            for k in range(2):
                mixed_ref[sides[k], cut] = mix(query[k], query[1 - k], value[1 - k], factors)
        return carry

    def join(step, carry):
        here = span(step // 2, long)
        cut = span(step % 2, width // 2)
        hidden_ref[here, cut] += dot(mixed_ref[here, :], out_ref[:, cut])
        return carry

    def middle_block(step, carry):
        here = span(step, rows)
        hidden = hidden_ref[here, :]
        mean_ref[span(step, BLOCK), :] = jnp.sum(
            hidden.reshape(2, BLOCK, length, -1), axis=(0, 2)
        )
        normed_ref[here, :] = norm_rows(hidden, gain_mlp_ref[...]).astype(jnp.bfloat16)
        return carry

    for load in token_loads:
        load.wait()
    lax.fori_loop(0, blocks, start_block, 0)
    for load in loads[:4]:
        load.wait()
    lax.fori_loop(0, blocks // 2 * 4, project, 0)
    lax.fori_loop(0, blocks, attend, 0)
    for load in loads[4:6]:
        load.wait()
    lax.fori_loop(0, blocks // 2 * 2, join, 0)
    lax.fori_loop(0, blocks, middle_block, 0)


def back_kernel(length, core_ref, mean_ref, pooled_ref, back_ref, far_back_ref, result_ref):
    count = mean_ref.shape[0]
    units = back_ref.shape[0]
    pooled = pooled_ref[...] * (0.5 / length)
    coarse = pooled.astype(jnp.bfloat16)
    fine = (pooled - coarse.astype(jnp.float32)).astype(jnp.bfloat16)
    both = jnp.concatenate([coarse, fine], axis=0)
    back = dot(both[:, :units], back_ref[...]) + dot(both[:, units:], far_back_ref[...])
    mean = mean_ref[...] * (0.5 / length)
    result = (mean + back[:count] + back[count:]).astype(jnp.bfloat16)
    start = pl.multiple_of(core_ref[0] * count, count)
    result_ref[pl.ds(start, count), :] = result
    result_ref[pl.ds(pl.multiple_of(count - start, count), count), :] = jnp.zeros_like(result)


def expand(normed, w_in, bias, length):
    inner = dot(normed, w_in) + bias
    inner = jax.nn.gelu(inner, approximate=True).astype(jnp.bfloat16).astype(jnp.float32)
    inner = inner.reshape(-1, 2, BLOCK, length, inner.shape[-1])
    return jnp.sum(inner, axis=(1, 3)).reshape(-1, inner.shape[-1])


def on_device(
    image_tokens,
    pair_owner,
    pair_slot,
    gain_attn,
    w_qk,
    w_value,
    logit_scale,
    w_out,
    gain_mlp,
    w_in,
    bias_in,
    w_back,
):
    owner_count = lax.axis_size("shard")
    groups = lax.axis_size("groups")
    core = lax.axis_index("mp").reshape(1)
    shard = lax.axis_index("shard").reshape(1)
    pair_count = pair_owner.shape[0]
    _, length, features = image_tokens.shape
    width = 2 * features
    head_dim = w_qk.shape[1] // logit_scale.shape[0]
    mine = pair_count // 2
    units = 2 * w_in.shape[1]
    plan = Plan(pair_count, owner_count)

    def swap(values):
        return lax.ppermute(values, "mp", [(0, 1), (1, 0)])

    def across(values, distance):
        return lax.ppermute(values, "shard", [(k, k ^ distance) for k in range(owner_count)])

    def images(*counts):
        return jax.ShapeDtypeStruct((*counts, length, features), jnp.bfloat16)

    smem = pl.BlockSpec(memory_space=pltpu.SMEM)
    vmem = pl.BlockSpec(memory_space=pltpu.VMEM)
    hbm = pl.BlockSpec(memory_space=pl.ANY)

    def limit(mebibytes):
        return pltpu.CompilerParams(vmem_limit_bytes=mebibytes * 2**20)

    if plan.extra:
        asked = [jax.ShapeDtypeStruct((1, plan.row), jnp.int32)] * owner_count
    else:
        asked = [jax.ShapeDtypeStruct((owner_count, 1, plan.row), jnp.int32)]
    order, *wanted = pl.pallas_call(
        functools.partial(place_kernel, plan, pair_count),
        out_shape=[jax.ShapeDtypeStruct((1, 2 * pair_count), jnp.int32), *asked],
        in_specs=[smem, vmem, vmem],
    )(shard, pair_owner.T, pair_slot.T)
    if plan.extra:
        incoming = [wanted[0]] + [across(wanted[k], k) for k in range(1, owner_count)]
        incoming = lax.optimization_barrier(incoming)
        *chunks, crowded = pl.pallas_call(
            functools.partial(serve_relays_kernel, plan),
            out_shape=[images(plan.extra)] * plan.half + [jax.ShapeDtypeStruct((1,), jnp.int32)],
            in_specs=[smem] * owner_count + [vmem],
            out_specs=[vmem] * plan.half + [smem],
        )(*incoming, image_tokens)
        incoming, chunks = lax.optimization_barrier((incoming, chunks))
        chunks = [chunks[0]] + [across(chunks[k], k) for k in range(1, plan.half)]
        served, *near = pl.pallas_call(
            functools.partial(serve_kernel, plan),
            out_shape=[images(owner_count, plan.base)] + [images(plan.extra)] * plan.half,
            in_specs=[smem] * (1 + owner_count) + [vmem],
        )(shard, *incoming, image_tokens)
        served, near, chunks = lax.optimization_barrier((served, near, chunks))
    else:
        incoming = lax.all_to_all(wanted[0], "shard", split_axis=0, concat_axis=0, tiled=True)
        served = pl.pallas_call(
            functools.partial(serve_all_kernel, plan),
            out_shape=images(owner_count, plan.base),
            in_specs=[smem, vmem],
        )(incoming, image_tokens)
    returned = lax.all_to_all(served, "shard", split_axis=0, concat_axis=0, tiled=True)
    sources = [returned.reshape(-1, length, features)]
    if plan.extra:
        first, second = pl.pallas_call(
            functools.partial(relay_kernel, plan),
            out_shape=[images(plan.part)] * 2,
            in_specs=[smem, smem] + [vmem] * plan.half,
        )(shard, incoming[plan.half], *chunks)
        first = across(first, plan.half)
        near = [near[0]] + [across(near[k], k) for k in range(1, plan.half)]
        passed = crowded
        for _ in range(groups - 1):
            passed = lax.ppermute(passed, "groups", [(k, (k + 1) % groups) for k in range(groups)])
            crowded = jnp.maximum(crowded, passed)
        sources += [*near, first]
    weights = (w_qk, w_value, w_out, w_in, w_back, bias_in, logit_scale)
    far_qk, far_value, far_out, far_in, far_back, far_bias, far_scale = [swap(w) for w in weights]
    all_in = jnp.concatenate([w_in, far_in], axis=1)
    all_bias = jnp.concatenate([bias_in, far_bias])
    swapped = (far_qk, far_value, far_out, all_in, far_back, all_bias, far_scale)
    sources, swapped = lax.optimization_barrier((sources, swapped))
    far_qk, far_value, far_out, all_in, far_back, all_bias, far_scale = swapped
    if plan.extra:
        second, sources = lax.optimization_barrier((second, sources))
        second = lax.cond(
            crowded[0] > 0, lambda part: across(part, plan.half), lambda part: part, second
        )
        sources = [*sources, second]
    own, other = pl.pallas_call(
        functools.partial(pick_kernel, plan),
        out_shape=[images(pair_count)] * 2,
        in_specs=[smem, smem] + [hbm] * len(sources),
        scratch_shapes=[
            pltpu.VMEM((plan.slots, length, features), jnp.bfloat16),
            pltpu.SemaphoreType.DMA((len(sources),)),
        ],
    )(core, order, *sources)
    far = swap(other)
    token_count = pair_count * length
    normed, mean = pl.pallas_call(
        functools.partial(attention_kernel, length, head_dim),
        out_shape=(
            jax.ShapeDtypeStruct((token_count, width), jnp.bfloat16),
            jax.ShapeDtypeStruct((mine, width), jnp.float32),
        ),
        in_specs=[smem] * 3 + [vmem] * 2 + [hbm] * 8,
        scratch_shapes=[
            pltpu.VMEM((width, 2 * width), jnp.bfloat16),
            pltpu.VMEM((width, width), jnp.bfloat16),
            pltpu.VMEM((2, pair_count, length, features), jnp.bfloat16),
            pltpu.VMEM((token_count, 2 * width), jnp.bfloat16),
            pltpu.VMEM((token_count, width), jnp.bfloat16),
            pltpu.VMEM((token_count, width), jnp.float32),
            pltpu.SemaphoreType.DMA((6,)),
            pltpu.SemaphoreType.DMA((2,)),
        ],
        compiler_params=limit(24),
        cost_estimate=pl.CostEstimate(
            flops=6 * token_count * width * width,
            bytes_accessed=4 * 2**20,
            transcendentals=token_count * 1024,
        ),
    )(
        core,
        logit_scale,
        far_scale,
        gain_attn.reshape(1, -1),
        gain_mlp.reshape(1, -1),
        own,
        far,
        w_qk,
        far_qk,
        w_value,
        far_value,
        w_out,
        far_out,
    )
    here = pl.pallas_call(
        functools.partial(back_kernel, length),
        out_shape=jax.ShapeDtypeStruct((pair_count, width), jnp.bfloat16),
        in_specs=[smem] + [vmem] * 4,
        compiler_params=limit(16),
    )(core, mean, expand(normed, all_in, all_bias, length), w_back, far_back)
    return here + swap(here)


def solution(mesh):
    in_specs = (
        P(("groups", "shard"), None, "mp"),
        P(("groups", "shard"), None),
        P(("groups", "shard"), None),
        P(),
        P(None, "mp"),
        P(None, "mp"),
        P("mp"),
        P("mp", None),
        P(),
        P(None, "mp"),
        P("mp"),
        P("mp", None),
    )
    out_specs = P(("groups", "shard"), None)
    return jax.shard_map(
        on_device, mesh=mesh, in_specs=in_specs, out_specs=out_specs, check_vma=False
    )
```

```python
import functools

import jax
import jax.numpy as jnp
from jax import lax
from jax.experimental import pallas as pl
from jax.experimental.pallas import tpu as pltpu
from jax.sharding import PartitionSpec as P

LOG2E = 1.4426950408889634
BLOCK = 8


def norm_rows(values, gain):
    center = values - jnp.mean(values, axis=-1, keepdims=True)
    spread = jnp.mean(center * center, axis=-1, keepdims=True)
    return center * lax.rsqrt(spread + 1e-05) * gain


def dot_nt(a, b):
    return lax.dot_general(a, b, (((1,), (1,)), ((), ())), preferred_element_type=jnp.float32)


def dot(a, b):
    return jnp.dot(a, b, preferred_element_type=jnp.float32)


class Plan:
    def __init__(self, pair_count, owner_count):
        self.owners = owner_count
        self.capacity = max(2, 4 * pair_count // owner_count)
        self.half = owner_count // 2
        split = self.capacity >= 32 and self.half & (self.half - 1) == 0 and self.half > 0
        self.base = self.capacity // 2 if split else self.capacity
        self.extra = self.capacity - self.base
        self.part = self.half * self.extra // 2
        self.far_at = self.half * self.capacity
        self.rest_at = self.far_at + self.half * self.base
        self.slots = self.rest_at + 2 * self.part
        self.row = self.capacity + (self.half if split else 0)


def place_kernel(plan, count, shard_ref, owner_ref, slot_ref, wanted_ref, list_ref):
    total = 2 * count
    owners = plan.owners
    owner = jnp.concatenate([owner_ref[0:1, :], owner_ref[1:2, :]], axis=1)
    slot = jnp.concatenate([slot_ref[0:1, :], slot_ref[1:2, :]], axis=1)

    def place(dim, size):
        return lax.broadcasted_iota(jnp.int32, (size, total), dim)

    def as_bf16(values):
        return values.astype(jnp.float32).astype(jnp.bfloat16)

    row = place(0, owners)
    named = row == owner
    until = as_bf16(jnp.where(place(0, total) <= place(1, total), 1, 0))
    tally = dot(as_bf16(jnp.where(named, 1, 0)), until).astype(jnp.int32)
    rank = jnp.sum(jnp.where(named, tally, 0), axis=0, keepdims=True) - 1
    ranked = as_bf16(jnp.where(place(0, total) == rank, 1, 0))
    wanted = dot_nt(as_bf16(jnp.where(named, slot, 0)), ranked).astype(jnp.int32)
    where = owner * plan.base + rank
    if plan.extra:
        me = shard_ref[0]
        half = plan.half
        over = jnp.maximum(jnp.max(tally, axis=1, keepdims=True) - plan.base, 0)
        far_over = jnp.where(row // half != me // half, over, 0)
        before = jnp.zeros((owners, total), jnp.int32)
        for index in range(owners - 1):
            before = before + jnp.where(row > index, far_over[index : index + 1], 0)
        before = jnp.sum(jnp.where(named, before, 0), axis=0, keepdims=True)
        distance = (owner % half) ^ (me % half)
        rest = plan.rest_at + before + rank - plan.base
        direct = plan.far_at + distance * plan.base + rank
        far = jnp.where(rank < plan.base, direct, rest)
        where = jnp.where(owner // half != me // half, far, distance * plan.capacity + rank)
        told = place(1, owners) == plan.capacity + row % half
        wanted = wanted + jnp.sum(jnp.where(told, far_over, 0), axis=0, keepdims=True)
    for index in range(owners):
        wanted_ref[index] = wanted[index : index + 1, : plan.row]
    entry = place(1, 1)
    side = entry // count
    pair = entry % count
    mine = count // 2
    local = pair % mine
    position = pair // mine * count + local // BLOCK * (2 * BLOCK) + side * BLOCK + local % BLOCK
    seated = as_bf16(jnp.where(place(0, total) == position, 1, 0))
    parts = as_bf16(jnp.where(place(0, 8) == 0, where // 16, where % 16))
    listed = dot_nt(parts, seated).astype(jnp.int32)
    list_ref[...] = listed[0:1] * 16 + listed[1:2]


def serve(tokens_ref, incoming_ref, requester, start, served_ref):
    count = served_ref.shape[0]

    def copy(index, carry):
        served_ref[index] = tokens_ref[incoming_ref[requester, 0, start + index]]
        return carry

    lax.fori_loop(0, count, copy, 0, unroll=min(16, count))


def serve_relays_kernel(plan, shard_ref, incoming_ref, tokens_ref, *served_refs):
    *served_refs, crowded_ref = served_refs
    for distance, served_ref in enumerate(served_refs):
        requester = shard_ref[0] ^ (distance + plan.half)
        serve(tokens_ref, incoming_ref, requester, plan.base, served_ref)
    most = 0
    for requester in range(plan.owners):
        total = 0
        for index in range(plan.half):
            total = total + incoming_ref[requester, 0, plan.capacity + index]
        most = jnp.maximum(most, total)
    crowded_ref[0] = jnp.where(most > plan.part, 1, 0)


def serve_direct_kernel(plan, shard_ref, incoming_ref, tokens_ref, *served_refs):
    for distance, served_ref in enumerate(served_refs):
        serve(tokens_ref, incoming_ref, shard_ref[0] ^ distance, 0, served_ref)


def serve_all_kernel(plan, incoming_ref, tokens_ref, served_ref):
    for requester in range(plan.owners):
        serve(tokens_ref, incoming_ref, requester, 0, served_ref.at[requester])


def relay_kernel(plan, shard_ref, incoming_ref, *refs):
    chunk_refs = refs[: plan.half]
    first_ref, second_ref = refs[plan.half :]
    client = shard_ref[0] ^ plan.half
    for distance, chunk_ref in enumerate(chunk_refs):
        owner = (shard_ref[0] % plan.half) ^ distance
        at = 0
        for index in range(plan.half):
            amount = incoming_ref[client, 0, plan.capacity + index]
            at = at + jnp.where(index < owner, amount, 0)
        amount = incoming_ref[client, 0, plan.capacity + owner]
        fit = jnp.clip(plan.part - at, 0, amount)

        def pack(index, carry, chunk_ref=chunk_ref, at=at):
            first_ref[at + index] = chunk_ref[index]
            return carry

        def pack_more(index, carry, chunk_ref=chunk_ref, at=at):
            second_ref[at + index - plan.part] = chunk_ref[index]
            return carry

        lax.fori_loop(0, fit, pack, 0)
        lax.fori_loop(fit, amount, pack_more, 0)


def pick_kernel(plan, core_ref, list_ref, *refs):
    source_refs = refs[:-4]
    own_ref, other_ref, held_ref, sems = refs[-4:]
    count = own_ref.shape[0]
    at = 0
    loads = []
    for index, source_ref in enumerate(source_refs):
        size = source_ref.shape[0]
        loads.append(
            pltpu.make_async_copy(source_ref, held_ref.at[pl.ds(at, size)], sems.at[index])
        )
        at += size
    for load in loads:
        load.start()
    for load in loads:
        load.wait()
    start = core_ref[0] * count

    def pick(index, carry):
        other_ref[index] = held_ref[list_ref[0, count - start + index]]
        own_ref[index] = held_ref[list_ref[0, start + index]]
        return carry

    lax.fori_loop(0, count, pick, 0, unroll=8)


def attention_kernel(
    length,
    head_dim,
    core_ref,
    scale_a_ref,
    scale_b_ref,
    gain_attn_ref,
    gain_mlp_ref,
    *refs,
):
    own_held_ref, far_held_ref, *held_refs = refs[:8]
    normed_ref, mean_ref, qkv_ref, out_ref = refs[8:12]
    tokens_ref, heads_ref, mixed_ref, hidden_ref, sems, token_sems = refs[12:]
    width = out_ref.shape[0]
    wide = width // 2
    homes = [qkv_ref.at[:, pl.ds(k * wide, wide)] for k in range(4)]
    homes += [out_ref.at[pl.ds(k * wide, wide)] for k in range(2)]
    loads = [
        pltpu.make_async_copy(held, home, sems.at[k])
        for k, (held, home) in enumerate(zip(held_refs, homes))
    ]
    core = core_ref[0]
    token_loads = [
        pltpu.make_async_copy(own_held_ref, tokens_ref.at[core], token_sems.at[0]),
        pltpu.make_async_copy(far_held_ref, tokens_ref.at[1 - core], token_sems.at[1]),
    ]
    for load in token_loads + loads:
        load.start()
    half = BLOCK * length
    rows = 2 * half
    blocks = tokens_ref.shape[1] // (2 * BLOCK)
    long = 2 * rows
    pair_dim = 2 * head_dim
    scale_refs = (scale_a_ref, scale_b_ref)
    per_core = wide // head_dim
    even = lax.broadcasted_iota(jnp.int32, (half, pair_dim), 1) < head_dim
    same = (
        lax.broadcasted_iota(jnp.int32, (half, half), 0) // length
        == lax.broadcasted_iota(jnp.int32, (half, half), 1) // length
    )

    def span(step, size):
        return pl.ds(pl.multiple_of(step * size, size), size)

    def split(values):
        zero = jnp.zeros_like(values)
        return jnp.concatenate(
            [jnp.where(even, values, zero), jnp.where(even, zero, values)], axis=0
        )

    ones = split(jnp.ones((half, pair_dim), jnp.bfloat16))

    def start_block(step, carry):
        images = pl.ds(step * 2 * BLOCK, 2 * BLOCK)
        tokens = jnp.concatenate(
            [tokens_ref[k, images].reshape(rows, -1).astype(jnp.float32) for k in range(2)], axis=1
        )
        hidden_ref[span(step, rows), :] = tokens
        normed_ref[span(step, rows), :] = norm_rows(tokens, gain_attn_ref[...]).astype(jnp.bfloat16)
        return carry

    def project(step, carry):
        here = span(step // 4, long)
        cut = span(step % 4, 2 * width // 4)
        heads_ref[here, cut] = dot(normed_ref[here, :], qkv_ref[:, cut]).astype(jnp.bfloat16)
        return carry

    def weigh(scores, factor):
        scores = jnp.where(same, scores, -1e30)
        top = jnp.max(scores, axis=1, keepdims=True)
        return jnp.exp2((scores - top) * factor).astype(jnp.bfloat16)

    def mix(query, key, value, factors):
        scores = dot_nt(query, split(key))
        weights = [weigh(scores[:, k * half : (k + 1) * half], factors[k]) for k in range(2)]
        mixed = dot(jnp.concatenate(weights, axis=1), jnp.concatenate([split(value), ones], axis=1))
        total = mixed[:, pair_dim:]
        inverse = pl.reciprocal(total, approx=True)
        inverse = inverse * (2.0 - total * inverse)
        return (mixed[:, :pair_dim] * inverse).astype(jnp.bfloat16)

    def attend(step, carry):
        for index in range(width // pair_dim):
            factors = [scale_refs[k // per_core][k % per_core] for k in (2 * index, 2 * index + 1)]
            factors = [factor * (LOG2E / head_dim**0.5) for factor in factors]
            cut = slice(index * pair_dim, (index + 1) * pair_dim)
            beyond = slice(width + cut.start, width + cut.stop)
            sides = [span(2 * step + k, half) for k in range(2)]
            query = [heads_ref[side, cut] for side in sides]
            value = [heads_ref[side, beyond] for side in sides]
            for k in range(2):
                mixed_ref[sides[k], cut] = mix(query[k], query[1 - k], value[1 - k], factors)
        return carry

    def join(step, carry):
        here = span(step // 2, long)
        cut = span(step % 2, width // 2)
        hidden_ref[here, cut] += dot(mixed_ref[here, :], out_ref[:, cut])
        return carry

    def middle_block(step, carry):
        here = span(step, rows)
        hidden = hidden_ref[here, :]
        mean_ref[span(step, BLOCK), :] = jnp.sum(
            hidden.reshape(2, BLOCK, length, -1), axis=(0, 2)
        )
        normed_ref[here, :] = norm_rows(hidden, gain_mlp_ref[...]).astype(jnp.bfloat16)
        return carry

    for load in token_loads:
        load.wait()
    lax.fori_loop(0, blocks, start_block, 0)
    for load in loads[:4]:
        load.wait()
    lax.fori_loop(0, blocks // 2 * 4, project, 0)
    lax.fori_loop(0, blocks, attend, 0)
    for load in loads[4:6]:
        load.wait()
    lax.fori_loop(0, blocks // 2 * 2, join, 0)
    lax.fori_loop(0, blocks, middle_block, 0)


def back_kernel(length, core_ref, mean_ref, pooled_ref, back_ref, far_back_ref, result_ref):
    count = mean_ref.shape[0]
    units = back_ref.shape[0]
    pooled = pooled_ref[...] * (0.5 / length)
    coarse = pooled.astype(jnp.bfloat16)
    fine = (pooled - coarse.astype(jnp.float32)).astype(jnp.bfloat16)
    both = jnp.concatenate([coarse, fine], axis=0)
    back = dot(both[:, :units], back_ref[...]) + dot(both[:, units:], far_back_ref[...])
    mean = mean_ref[...] * (0.5 / length)
    result = (mean + back[:count] + back[count:]).astype(jnp.bfloat16)
    start = pl.multiple_of(core_ref[0] * count, count)
    result_ref[pl.ds(start, count), :] = result
    result_ref[pl.ds(pl.multiple_of(count - start, count), count), :] = jnp.zeros_like(result)


def expand(normed, w_in, bias, length):
    inner = dot(normed, w_in) + bias
    inner = jax.nn.gelu(inner, approximate=True).astype(jnp.bfloat16).astype(jnp.float32)
    inner = inner.reshape(-1, 2, BLOCK, length, inner.shape[-1])
    return jnp.sum(inner, axis=(1, 3)).reshape(-1, inner.shape[-1])


def on_device(
    image_tokens,
    pair_owner,
    pair_slot,
    gain_attn,
    w_qk,
    w_value,
    logit_scale,
    w_out,
    gain_mlp,
    w_in,
    bias_in,
    w_back,
):
    owner_count = lax.axis_size("shard")
    groups = lax.axis_size("groups")
    core = lax.axis_index("mp").reshape(1)
    shard = lax.axis_index("shard").reshape(1)
    pair_count = pair_owner.shape[0]
    _, length, features = image_tokens.shape
    width = 2 * features
    head_dim = w_qk.shape[1] // logit_scale.shape[0]
    mine = pair_count // 2
    units = 2 * w_in.shape[1]
    plan = Plan(pair_count, owner_count)

    def swap(values):
        return lax.ppermute(values, "mp", [(0, 1), (1, 0)])

    def across(values, distance):
        return lax.ppermute(values, "shard", [(k, k ^ distance) for k in range(owner_count)])

    def images(*counts):
        return jax.ShapeDtypeStruct((*counts, length, features), jnp.bfloat16)

    smem = pl.BlockSpec(memory_space=pltpu.SMEM)
    vmem = pl.BlockSpec(memory_space=pltpu.VMEM)
    hbm = pl.BlockSpec(memory_space=pl.ANY)

    def limit(mebibytes):
        return pltpu.CompilerParams(vmem_limit_bytes=mebibytes * 2**20)

    wanted, order = pl.pallas_call(
        functools.partial(place_kernel, plan, pair_count),
        out_shape=(
            jax.ShapeDtypeStruct((owner_count, 1, plan.row), jnp.int32),
            jax.ShapeDtypeStruct((1, 2 * pair_count), jnp.int32),
        ),
        in_specs=[smem, vmem, vmem],
    )(shard, pair_owner.T, pair_slot.T)
    incoming = lax.all_to_all(wanted, "shard", split_axis=0, concat_axis=0, tiled=True)
    if not plan.extra:
        served = pl.pallas_call(
            functools.partial(serve_all_kernel, plan),
            out_shape=images(owner_count, plan.base),
            in_specs=[smem, vmem],
        )(incoming, image_tokens)
        returned = lax.all_to_all(served, "shard", split_axis=0, concat_axis=0, tiled=True)
        sources = [returned.reshape(-1, length, features)]
    else:
        *chunks, crowded = pl.pallas_call(
            functools.partial(serve_relays_kernel, plan),
            out_shape=[images(plan.extra)] * plan.half + [jax.ShapeDtypeStruct((1,), jnp.int32)],
            in_specs=[smem, smem, vmem],
            out_specs=[vmem] * plan.half + [smem],
        )(shard, incoming, image_tokens)
        incoming, chunks = lax.optimization_barrier((incoming, chunks))
        chunks = [chunks[0]] + [across(chunks[k], k) for k in range(1, plan.half)]
        served = pl.pallas_call(
            functools.partial(serve_direct_kernel, plan),
            out_shape=[images(plan.capacity)] * plan.half + [images(plan.base)] * plan.half,
            in_specs=[smem, smem, vmem],
        )(shard, incoming, image_tokens)
        served, chunks = lax.optimization_barrier((served, chunks))
        direct = [across(served[k], k) for k in range(plan.half, owner_count)]
        first, second = pl.pallas_call(
            functools.partial(relay_kernel, plan),
            out_shape=[images(plan.part)] * 2,
            in_specs=[smem, smem] + [vmem] * plan.half,
        )(shard, incoming, *chunks)
        near, first, crowded = lax.optimization_barrier((served[: plan.half], first, crowded))
        first = across(first, plan.half)
        near = [near[0]] + [across(near[k], k) for k in range(1, plan.half)]
        passed = crowded
        for _ in range(groups - 1):
            passed = lax.ppermute(passed, "groups", [(k, (k + 1) % groups) for k in range(groups)])
            crowded = jnp.maximum(crowded, passed)
        sources = [*near, *direct, first]
    weights = (w_qk, w_value, w_out, w_in, w_back, bias_in, logit_scale)
    far_qk, far_value, far_out, far_in, far_back, far_bias, far_scale = [swap(w) for w in weights]
    all_in = jnp.concatenate([w_in, far_in], axis=1)
    all_bias = jnp.concatenate([bias_in, far_bias])
    swapped = (far_qk, far_value, far_out, all_in, far_back, all_bias, far_scale)
    sources, swapped = lax.optimization_barrier((sources, swapped))
    far_qk, far_value, far_out, all_in, far_back, all_bias, far_scale = swapped
    if plan.extra:
        second, sources = lax.optimization_barrier((second, sources))
        second = lax.cond(
            crowded[0] > 0, lambda part: across(part, plan.half), lambda part: part, second
        )
        sources = [*sources, second]
    own, other = pl.pallas_call(
        functools.partial(pick_kernel, plan),
        out_shape=[images(pair_count)] * 2,
        in_specs=[smem, smem] + [hbm] * len(sources),
        scratch_shapes=[
            pltpu.VMEM((plan.slots, length, features), jnp.bfloat16),
            pltpu.SemaphoreType.DMA((len(sources),)),
        ],
    )(core, order, *sources)
    far = swap(other)
    token_count = pair_count * length
    normed, mean = pl.pallas_call(
        functools.partial(attention_kernel, length, head_dim),
        out_shape=(
            jax.ShapeDtypeStruct((token_count, width), jnp.bfloat16),
            jax.ShapeDtypeStruct((mine, width), jnp.float32),
        ),
        in_specs=[smem] * 3 + [vmem] * 2 + [hbm] * 8,
        scratch_shapes=[
            pltpu.VMEM((width, 2 * width), jnp.bfloat16),
            pltpu.VMEM((width, width), jnp.bfloat16),
            pltpu.VMEM((2, pair_count, length, features), jnp.bfloat16),
            pltpu.VMEM((token_count, 2 * width), jnp.bfloat16),
            pltpu.VMEM((token_count, width), jnp.bfloat16),
            pltpu.VMEM((token_count, width), jnp.float32),
            pltpu.SemaphoreType.DMA((6,)),
            pltpu.SemaphoreType.DMA((2,)),
        ],
        compiler_params=limit(24),
        cost_estimate=pl.CostEstimate(
            flops=6 * token_count * width * width,
            bytes_accessed=4 * 2**20,
            transcendentals=token_count * 1024,
        ),
    )(
        core,
        logit_scale,
        far_scale,
        gain_attn.reshape(1, -1),
        gain_mlp.reshape(1, -1),
        own,
        far,
        w_qk,
        far_qk,
        w_value,
        far_value,
        w_out,
        far_out,
    )
    here = pl.pallas_call(
        functools.partial(back_kernel, length),
        out_shape=jax.ShapeDtypeStruct((pair_count, width), jnp.bfloat16),
        in_specs=[smem] + [vmem] * 4,
        compiler_params=limit(16),
    )(core, mean, expand(normed, all_in, all_bias, length), w_back, far_back)
    return here + swap(here)


def solution(mesh):
    in_specs = (
        P(("groups", "shard"), None, "mp"),
        P(("groups", "shard"), None),
        P(("groups", "shard"), None),
        P(),
        P(None, "mp"),
        P(None, "mp"),
        P("mp"),
        P("mp", None),
        P(),
        P(None, "mp"),
        P("mp"),
        P("mp", None),
    )
    out_specs = P(("groups", "shard"), None)
    return jax.shard_map(
        on_device, mesh=mesh, in_specs=in_specs, out_specs=out_specs, check_vma=False
    )
```

```python
import functools

import jax
import jax.numpy as jnp
from jax import lax
from jax.experimental import pallas as pl
from jax.experimental.pallas import tpu as pltpu
from jax.sharding import PartitionSpec as P

LOG2E = 1.4426950408889634
BLOCK = 8


def norm_rows(values, gain):
    center = values - jnp.mean(values, axis=-1, keepdims=True)
    spread = jnp.mean(center * center, axis=-1, keepdims=True)
    return center * lax.rsqrt(spread + 1e-05) * gain


def dot_nt(a, b):
    return lax.dot_general(a, b, (((1,), (1,)), ((), ())), preferred_element_type=jnp.float32)


def dot(a, b):
    return jnp.dot(a, b, preferred_element_type=jnp.float32)


class Plan:
    def __init__(self, pair_count, owner_count):
        self.owners = owner_count
        self.capacity = max(2, 4 * pair_count // owner_count)
        self.half = owner_count // 2
        split = self.capacity >= 32 and self.half & (self.half - 1) == 0 and self.half > 0
        self.base = self.capacity // 2 if split else self.capacity
        self.extra = self.capacity - self.base
        self.part = self.half * self.extra // 2
        self.near_at = owner_count * self.base
        self.rest_at = self.near_at + self.half * self.extra
        self.slots = self.rest_at + 2 * self.part
        self.row = self.capacity + (self.half if split else 0)


def place_kernel(plan, count, shard_ref, owner_ref, slot_ref, wanted_ref, list_ref):
    total = 2 * count
    owners = plan.owners
    owner = jnp.concatenate([owner_ref[0:1, :], owner_ref[1:2, :]], axis=1)
    slot = jnp.concatenate([slot_ref[0:1, :], slot_ref[1:2, :]], axis=1)

    def place(dim, size):
        return lax.broadcasted_iota(jnp.int32, (size, total), dim)

    def as_bf16(values):
        return values.astype(jnp.float32).astype(jnp.bfloat16)

    row = place(0, owners)
    named = row == owner
    until = as_bf16(jnp.where(place(0, total) <= place(1, total), 1, 0))
    tally = dot(as_bf16(jnp.where(named, 1, 0)), until).astype(jnp.int32)
    rank = jnp.sum(jnp.where(named, tally, 0), axis=0, keepdims=True) - 1
    ranked = as_bf16(jnp.where(place(0, total) == rank, 1, 0))
    wanted = dot_nt(as_bf16(jnp.where(named, slot, 0)), ranked).astype(jnp.int32)
    where = owner * plan.base + rank
    if plan.extra:
        me = shard_ref[0]
        half = plan.half
        over = jnp.maximum(jnp.max(tally, axis=1, keepdims=True) - plan.base, 0)
        far_over = jnp.where(row // half != me // half, over, 0)
        before = jnp.zeros((owners, total), jnp.int32)
        for index in range(owners - 1):
            before = before + jnp.where(row > index, far_over[index : index + 1], 0)
        before = jnp.sum(jnp.where(named, before, 0), axis=0, keepdims=True)
        rest = rank - plan.base
        near = plan.near_at + ((owner % half) ^ (me % half)) * plan.extra + rest
        late = jnp.where(owner // half == me // half, near, plan.rest_at + before + rest)
        where = jnp.where(rest < 0, where, late)
        told = place(1, owners) == plan.capacity + row % half
        wanted = wanted + jnp.sum(jnp.where(told, far_over, 0), axis=0, keepdims=True)
    for index in range(owners):
        wanted_ref[index] = wanted[index : index + 1, : plan.row]
    entry = place(1, 1)
    side = entry // count
    pair = entry % count
    mine = count // 2
    local = pair % mine
    position = pair // mine * count + local // BLOCK * (2 * BLOCK) + side * BLOCK + local % BLOCK
    seated = as_bf16(jnp.where(place(0, total) == position, 1, 0))
    parts = as_bf16(jnp.where(place(0, 8) == 0, where // 16, where % 16))
    listed = dot_nt(parts, seated).astype(jnp.int32)
    list_ref[...] = listed[0:1] * 16 + listed[1:2]


def serve(tokens_ref, incoming_ref, requester, start, served_ref):
    count = served_ref.shape[0]

    def copy(index, carry):
        served_ref[index] = tokens_ref[incoming_ref[requester, 0, start + index]]
        return carry

    lax.fori_loop(0, count, copy, 0, unroll=min(16, count))


def serve_kernel(plan, shard_ref, incoming_ref, tokens_ref, *refs):
    relay_refs, near_refs = refs[: plan.half], refs[plan.half + 1 : -1]
    served_ref, crowded_ref = refs[plan.half], refs[-1]
    me = shard_ref[0]
    for distance, relay_ref in enumerate(relay_refs):
        serve(tokens_ref, incoming_ref, me ^ (distance + plan.half), plan.base, relay_ref)
    for requester in range(plan.owners):
        serve(tokens_ref, incoming_ref, requester, 0, served_ref.at[requester])
    for distance, near_ref in enumerate(near_refs):
        serve(tokens_ref, incoming_ref, me ^ distance, plan.base, near_ref)
    most = 0
    for requester in range(plan.owners):
        total = 0
        for index in range(plan.half):
            total = total + incoming_ref[requester, 0, plan.capacity + index]
        most = jnp.maximum(most, total)
    crowded_ref[0] = jnp.where(most > plan.part, 1, 0)


def serve_all_kernel(plan, incoming_ref, tokens_ref, served_ref):
    for requester in range(plan.owners):
        serve(tokens_ref, incoming_ref, requester, 0, served_ref.at[requester])


def relay_kernel(plan, shard_ref, incoming_ref, *refs):
    chunk_refs = refs[: plan.half]
    first_ref, second_ref = refs[plan.half :]
    client = shard_ref[0] ^ plan.half
    for distance, chunk_ref in enumerate(chunk_refs):
        owner = (shard_ref[0] % plan.half) ^ distance
        at = 0
        for index in range(plan.half):
            amount = incoming_ref[client, 0, plan.capacity + index]
            at = at + jnp.where(index < owner, amount, 0)
        amount = incoming_ref[client, 0, plan.capacity + owner]
        fit = jnp.clip(plan.part - at, 0, amount)

        def pack(index, carry, chunk_ref=chunk_ref, at=at):
            first_ref[at + index] = chunk_ref[index]
            return carry

        def pack_more(index, carry, chunk_ref=chunk_ref, at=at):
            second_ref[at + index - plan.part] = chunk_ref[index]
            return carry

        lax.fori_loop(0, fit, pack, 0)
        lax.fori_loop(fit, amount, pack_more, 0)


def pick_kernel(plan, core_ref, list_ref, *refs):
    source_refs = refs[:-4]
    own_ref, other_ref, held_ref, sems = refs[-4:]
    count = own_ref.shape[0]
    at = 0
    loads = []
    for index, source_ref in enumerate(source_refs):
        size = source_ref.shape[0]
        loads.append(
            pltpu.make_async_copy(source_ref, held_ref.at[pl.ds(at, size)], sems.at[index])
        )
        at += size
    for load in loads:
        load.start()
    for load in loads:
        load.wait()
    start = core_ref[0] * count

    def pick(index, carry):
        other_ref[index] = held_ref[list_ref[0, count - start + index]]
        own_ref[index] = held_ref[list_ref[0, start + index]]
        return carry

    lax.fori_loop(0, count, pick, 0, unroll=8)


def attention_kernel(
    length,
    head_dim,
    core_ref,
    scale_a_ref,
    scale_b_ref,
    gain_attn_ref,
    gain_mlp_ref,
    *refs,
):
    own_held_ref, far_held_ref, *held_refs = refs[:8]
    normed_ref, mean_ref, qkv_ref, out_ref = refs[8:12]
    tokens_ref, heads_ref, mixed_ref, hidden_ref, sems, token_sems = refs[12:]
    width = out_ref.shape[0]
    wide = width // 2
    homes = [qkv_ref.at[:, pl.ds(k * wide, wide)] for k in range(4)]
    homes += [out_ref.at[pl.ds(k * wide, wide)] for k in range(2)]
    loads = [
        pltpu.make_async_copy(held, home, sems.at[k])
        for k, (held, home) in enumerate(zip(held_refs, homes))
    ]
    core = core_ref[0]
    token_loads = [
        pltpu.make_async_copy(own_held_ref, tokens_ref.at[core], token_sems.at[0]),
        pltpu.make_async_copy(far_held_ref, tokens_ref.at[1 - core], token_sems.at[1]),
    ]
    for load in token_loads + loads:
        load.start()
    half = BLOCK * length
    rows = 2 * half
    blocks = tokens_ref.shape[1] // (2 * BLOCK)
    long = 2 * rows
    pair_dim = 2 * head_dim
    scale_refs = (scale_a_ref, scale_b_ref)
    per_core = wide // head_dim
    even = lax.broadcasted_iota(jnp.int32, (half, pair_dim), 1) < head_dim
    same = (
        lax.broadcasted_iota(jnp.int32, (half, half), 0) // length
        == lax.broadcasted_iota(jnp.int32, (half, half), 1) // length
    )

    def span(step, size):
        return pl.ds(pl.multiple_of(step * size, size), size)

    def split(values):
        zero = jnp.zeros_like(values)
        return jnp.concatenate(
            [jnp.where(even, values, zero), jnp.where(even, zero, values)], axis=0
        )

    ones = split(jnp.ones((half, pair_dim), jnp.bfloat16))

    def start_block(step, carry):
        images = pl.ds(step * 2 * BLOCK, 2 * BLOCK)
        tokens = jnp.concatenate(
            [tokens_ref[k, images].reshape(rows, -1).astype(jnp.float32) for k in range(2)], axis=1
        )
        hidden_ref[span(step, rows), :] = tokens
        normed_ref[span(step, rows), :] = norm_rows(tokens, gain_attn_ref[...]).astype(jnp.bfloat16)
        return carry

    def project(step, carry):
        here = span(step // 4, long)
        cut = span(step % 4, 2 * width // 4)
        heads_ref[here, cut] = dot(normed_ref[here, :], qkv_ref[:, cut]).astype(jnp.bfloat16)
        return carry

    def weigh(scores, factor):
        scores = jnp.where(same, scores, -1e30)
        top = jnp.max(scores, axis=1, keepdims=True)
        return jnp.exp2((scores - top) * factor).astype(jnp.bfloat16)

    def mix(query, key, value, factors):
        scores = dot_nt(query, split(key))
        weights = [weigh(scores[:, k * half : (k + 1) * half], factors[k]) for k in range(2)]
        mixed = dot(jnp.concatenate(weights, axis=1), jnp.concatenate([split(value), ones], axis=1))
        total = mixed[:, pair_dim:]
        inverse = pl.reciprocal(total, approx=True)
        inverse = inverse * (2.0 - total * inverse)
        return (mixed[:, :pair_dim] * inverse).astype(jnp.bfloat16)

    def attend(step, carry):
        for index in range(width // pair_dim):
            factors = [scale_refs[k // per_core][k % per_core] for k in (2 * index, 2 * index + 1)]
            factors = [factor * (LOG2E / head_dim**0.5) for factor in factors]
            cut = slice(index * pair_dim, (index + 1) * pair_dim)
            beyond = slice(width + cut.start, width + cut.stop)
            sides = [span(2 * step + k, half) for k in range(2)]
            query = [heads_ref[side, cut] for side in sides]
            value = [heads_ref[side, beyond] for side in sides]
            for k in range(2):
                mixed_ref[sides[k], cut] = mix(query[k], query[1 - k], value[1 - k], factors)
        return carry

    def join(step, carry):
        here = span(step // 2, long)
        cut = span(step % 2, width // 2)
        hidden_ref[here, cut] += dot(mixed_ref[here, :], out_ref[:, cut])
        return carry

    def middle_block(step, carry):
        here = span(step, rows)
        hidden = hidden_ref[here, :]
        mean_ref[span(step, BLOCK), :] = jnp.sum(
            hidden.reshape(2, BLOCK, length, -1), axis=(0, 2)
        )
        normed_ref[here, :] = norm_rows(hidden, gain_mlp_ref[...]).astype(jnp.bfloat16)
        return carry

    for load in token_loads:
        load.wait()
    lax.fori_loop(0, blocks, start_block, 0)
    for load in loads[:4]:
        load.wait()
    lax.fori_loop(0, blocks // 2 * 4, project, 0)
    lax.fori_loop(0, blocks, attend, 0)
    for load in loads[4:6]:
        load.wait()
    lax.fori_loop(0, blocks // 2 * 2, join, 0)
    lax.fori_loop(0, blocks, middle_block, 0)


def back_kernel(length, core_ref, mean_ref, pooled_ref, back_ref, far_back_ref, result_ref):
    count = mean_ref.shape[0]
    units = back_ref.shape[0]
    pooled = pooled_ref[...] * (0.5 / length)
    coarse = pooled.astype(jnp.bfloat16)
    fine = (pooled - coarse.astype(jnp.float32)).astype(jnp.bfloat16)
    both = jnp.concatenate([coarse, fine], axis=0)
    back = dot(both[:, :units], back_ref[...]) + dot(both[:, units:], far_back_ref[...])
    mean = mean_ref[...] * (0.5 / length)
    result = (mean + back[:count] + back[count:]).astype(jnp.bfloat16)
    start = pl.multiple_of(core_ref[0] * count, count)
    result_ref[pl.ds(start, count), :] = result
    result_ref[pl.ds(pl.multiple_of(count - start, count), count), :] = jnp.zeros_like(result)


def expand(normed, w_in, bias, length):
    inner = dot(normed, w_in) + bias
    inner = jax.nn.gelu(inner, approximate=True).astype(jnp.bfloat16).astype(jnp.float32)
    inner = inner.reshape(-1, 2, BLOCK, length, inner.shape[-1])
    return jnp.sum(inner, axis=(1, 3)).reshape(-1, inner.shape[-1])


def on_device(
    image_tokens,
    pair_owner,
    pair_slot,
    gain_attn,
    w_qk,
    w_value,
    logit_scale,
    w_out,
    gain_mlp,
    w_in,
    bias_in,
    w_back,
):
    owner_count = lax.axis_size("shard")
    groups = lax.axis_size("groups")
    core = lax.axis_index("mp").reshape(1)
    shard = lax.axis_index("shard").reshape(1)
    pair_count = pair_owner.shape[0]
    _, length, features = image_tokens.shape
    width = 2 * features
    head_dim = w_qk.shape[1] // logit_scale.shape[0]
    mine = pair_count // 2
    units = 2 * w_in.shape[1]
    plan = Plan(pair_count, owner_count)

    def swap(values):
        return lax.ppermute(values, "mp", [(0, 1), (1, 0)])

    def across(values, distance):
        return lax.ppermute(values, "shard", [(k, k ^ distance) for k in range(owner_count)])

    def images(*counts):
        return jax.ShapeDtypeStruct((*counts, length, features), jnp.bfloat16)

    smem = pl.BlockSpec(memory_space=pltpu.SMEM)
    vmem = pl.BlockSpec(memory_space=pltpu.VMEM)
    hbm = pl.BlockSpec(memory_space=pl.ANY)

    def limit(mebibytes):
        return pltpu.CompilerParams(vmem_limit_bytes=mebibytes * 2**20)

    wanted, order = pl.pallas_call(
        functools.partial(place_kernel, plan, pair_count),
        out_shape=(
            jax.ShapeDtypeStruct((owner_count, 1, plan.row), jnp.int32),
            jax.ShapeDtypeStruct((1, 2 * pair_count), jnp.int32),
        ),
        in_specs=[smem, vmem, vmem],
    )(shard, pair_owner.T, pair_slot.T)
    incoming = lax.all_to_all(wanted, "shard", split_axis=0, concat_axis=0, tiled=True)
    if not plan.extra:
        served = pl.pallas_call(
            functools.partial(serve_all_kernel, plan),
            out_shape=images(owner_count, plan.base),
            in_specs=[smem, vmem],
        )(incoming, image_tokens)
        returned = lax.all_to_all(served, "shard", split_axis=0, concat_axis=0, tiled=True)
        sources = [returned.reshape(-1, length, features)]
    else:
        outs = pl.pallas_call(
            functools.partial(serve_kernel, plan),
            out_shape=[images(plan.extra)] * plan.half
            + [images(owner_count, plan.base)]
            + [images(plan.extra)] * plan.half
            + [jax.ShapeDtypeStruct((1,), jnp.int32)],
            in_specs=[smem, smem, vmem],
            out_specs=[vmem] * (2 * plan.half + 1) + [smem],
        )(shard, incoming, image_tokens)
        chunks, near, crowded = outs[: plan.half], outs[plan.half + 1 : -1], outs[-1]
        chunks = [chunks[0]] + [across(chunks[k], k) for k in range(1, plan.half)]
        returned = lax.all_to_all(
            outs[plan.half], "shard", split_axis=0, concat_axis=0, tiled=True
        ).reshape(-1, length, features)
        first, second = pl.pallas_call(
            functools.partial(relay_kernel, plan),
            out_shape=[images(plan.part)] * 2,
            in_specs=[smem, smem] + [vmem] * plan.half,
            cost_estimate=pl.CostEstimate(
                flops=2 * 10**11, bytes_accessed=2**20, transcendentals=0
            ),
        )(shard, incoming, *chunks)
        near, first, crowded = lax.optimization_barrier((near, first, crowded))
        first = across(first, plan.half)
        near = [near[0]] + [across(near[k], k) for k in range(1, plan.half)]
        passed = crowded
        for _ in range(groups - 1):
            passed = lax.ppermute(passed, "groups", [(k, (k + 1) % groups) for k in range(groups)])
            crowded = jnp.maximum(crowded, passed)
        sources = [returned, *near, first]
    weights = (w_qk, w_value, w_out, w_in, w_back, bias_in, logit_scale)
    far_qk, far_value, far_out, far_in, far_back, far_bias, far_scale = [swap(w) for w in weights]
    all_in = jnp.concatenate([w_in, far_in], axis=1)
    all_bias = jnp.concatenate([bias_in, far_bias])
    swapped = (far_qk, far_value, far_out, all_in, far_back, all_bias, far_scale)
    sources, swapped = lax.optimization_barrier((sources, swapped))
    far_qk, far_value, far_out, all_in, far_back, all_bias, far_scale = swapped
    if plan.extra:
        second, sources = lax.optimization_barrier((second, sources))
        second = lax.cond(
            crowded[0] > 0, lambda part: across(part, plan.half), lambda part: part, second
        )
        sources = [*sources, second]
    own, other = pl.pallas_call(
        functools.partial(pick_kernel, plan),
        out_shape=[images(pair_count)] * 2,
        in_specs=[smem, smem] + [hbm] * len(sources),
        scratch_shapes=[
            pltpu.VMEM((plan.slots, length, features), jnp.bfloat16),
            pltpu.SemaphoreType.DMA((len(sources),)),
        ],
    )(core, order, *sources)
    far = swap(other)
    token_count = pair_count * length
    normed, mean = pl.pallas_call(
        functools.partial(attention_kernel, length, head_dim),
        out_shape=(
            jax.ShapeDtypeStruct((token_count, width), jnp.bfloat16),
            jax.ShapeDtypeStruct((mine, width), jnp.float32),
        ),
        in_specs=[smem] * 3 + [vmem] * 4 + [hbm] * 6,
        scratch_shapes=[
            pltpu.VMEM((width, 2 * width), jnp.bfloat16),
            pltpu.VMEM((width, width), jnp.bfloat16),
            pltpu.VMEM((2, pair_count, length, features), jnp.bfloat16),
            pltpu.VMEM((token_count, 2 * width), jnp.bfloat16),
            pltpu.VMEM((token_count, width), jnp.bfloat16),
            pltpu.VMEM((token_count, width), jnp.float32),
            pltpu.SemaphoreType.DMA((6,)),
            pltpu.SemaphoreType.DMA((2,)),
        ],
        compiler_params=limit(24),
        cost_estimate=pl.CostEstimate(
            flops=6 * token_count * width * width,
            bytes_accessed=4 * 2**20,
            transcendentals=token_count * 1024,
        ),
    )(
        core,
        logit_scale,
        far_scale,
        gain_attn.reshape(1, -1),
        gain_mlp.reshape(1, -1),
        own,
        far,
        w_qk,
        far_qk,
        w_value,
        far_value,
        w_out,
        far_out,
    )
    here = pl.pallas_call(
        functools.partial(back_kernel, length),
        out_shape=jax.ShapeDtypeStruct((pair_count, width), jnp.bfloat16),
        in_specs=[smem] + [vmem] * 4,
        compiler_params=limit(16),
    )(core, mean, expand(normed, all_in, all_bias, length), w_back, far_back)
    return here + swap(here)


def solution(mesh):
    in_specs = (
        P(("groups", "shard"), None, "mp"),
        P(("groups", "shard"), None),
        P(("groups", "shard"), None),
        P(),
        P(None, "mp"),
        P(None, "mp"),
        P("mp"),
        P("mp", None),
        P(),
        P(None, "mp"),
        P("mp"),
        P("mp", None),
    )
    out_specs = P(("groups", "shard"), None)
    return jax.shard_map(
        on_device, mesh=mesh, in_specs=in_specs, out_specs=out_specs, check_vma=False
    )
```

```python
import functools

import jax
import jax.numpy as jnp
from jax import lax
from jax.experimental import pallas as pl
from jax.experimental.pallas import tpu as pltpu
from jax.sharding import PartitionSpec as P

LOG2E = 1.4426950408889634
BLOCK = 8


def norm_rows(values, gain):
    center = values - jnp.mean(values, axis=-1, keepdims=True)
    spread = jnp.mean(center * center, axis=-1, keepdims=True)
    return center * lax.rsqrt(spread + 1e-05) * gain


def dot_nt(a, b):
    return lax.dot_general(a, b, (((1,), (1,)), ((), ())), preferred_element_type=jnp.float32)


def dot(a, b):
    return jnp.dot(a, b, preferred_element_type=jnp.float32)


class Plan:
    def __init__(self, pair_count, owner_count):
        self.owners = owner_count
        self.capacity = max(2, 4 * pair_count // owner_count)
        self.half = owner_count // 2
        split = self.capacity >= 32 and self.half & (self.half - 1) == 0 and self.half > 0
        self.base = self.capacity // 2 if split else self.capacity
        self.extra = self.capacity - self.base
        self.part = self.half * self.extra // 2
        self.near_at = owner_count * self.base
        self.rest_at = self.near_at + self.half * self.extra
        self.slots = self.rest_at + 2 * self.part
        self.row = self.capacity + (self.half if split else 0)


def place_kernel(plan, count, shard_ref, owner_ref, slot_ref, wanted_ref, list_ref):
    total = 2 * count
    owners = plan.owners
    owner = jnp.concatenate([owner_ref[0:1, :], owner_ref[1:2, :]], axis=1)
    slot = jnp.concatenate([slot_ref[0:1, :], slot_ref[1:2, :]], axis=1)

    def place(dim, size):
        return lax.broadcasted_iota(jnp.int32, (size, total), dim)

    def as_bf16(values):
        return values.astype(jnp.float32).astype(jnp.bfloat16)

    row = place(0, owners)
    named = row == owner
    until = as_bf16(jnp.where(place(0, total) <= place(1, total), 1, 0))
    tally = dot(as_bf16(jnp.where(named, 1, 0)), until).astype(jnp.int32)
    rank = jnp.sum(jnp.where(named, tally, 0), axis=0, keepdims=True) - 1
    ranked = as_bf16(jnp.where(place(0, total) == rank, 1, 0))
    wanted = dot_nt(as_bf16(jnp.where(named, slot, 0)), ranked).astype(jnp.int32)
    where = owner * plan.base + rank
    if plan.extra:
        me = shard_ref[0]
        half = plan.half
        over = jnp.maximum(jnp.max(tally, axis=1, keepdims=True) - plan.base, 0)
        far_over = jnp.where(row // half != me // half, over, 0)
        before = jnp.zeros((owners, total), jnp.int32)
        for index in range(owners - 1):
            before = before + jnp.where(row > index, far_over[index : index + 1], 0)
        before = jnp.sum(jnp.where(named, before, 0), axis=0, keepdims=True)
        rest = rank - plan.base
        near = plan.near_at + ((owner % half) ^ (me % half)) * plan.extra + rest
        late = jnp.where(owner // half == me // half, near, plan.rest_at + before + rest)
        where = jnp.where(rest < 0, where, late)
        told = place(1, owners) == plan.capacity + row % half
        wanted = wanted + jnp.sum(jnp.where(told, far_over, 0), axis=0, keepdims=True)
    for index in range(owners):
        wanted_ref[index] = wanted[index : index + 1, : plan.row]
    entry = place(1, 1)
    side = entry // count
    pair = entry % count
    mine = count // 2
    local = pair % mine
    position = pair // mine * count + local // BLOCK * (2 * BLOCK) + side * BLOCK + local % BLOCK
    seated = as_bf16(jnp.where(place(0, total) == position, 1, 0))
    parts = as_bf16(jnp.where(place(0, 8) == 0, where // 16, where % 16))
    listed = dot_nt(parts, seated).astype(jnp.int32)
    list_ref[...] = listed[0:1] * 16 + listed[1:2]


def serve(tokens_ref, incoming_ref, requester, start, served_ref):
    count = served_ref.shape[0]

    def copy(index, carry):
        served_ref[index] = tokens_ref[incoming_ref[requester, 0, start + index]]
        return carry

    lax.fori_loop(0, count, copy, 0, unroll=min(16, count))


def serve_kernel(plan, shard_ref, incoming_ref, tokens_ref, *refs):
    *chunk_refs, served_ref, crowded_ref = refs
    me = shard_ref[0]
    for distance, chunk_ref in enumerate(chunk_refs):
        for part in range(2):
            requester = me ^ (distance + (plan.half if part == 0 else 0))
            home = chunk_ref.at[pl.ds(part * plan.extra, plan.extra)]
            serve(tokens_ref, incoming_ref, requester, plan.base, home)
    for requester in range(plan.owners):
        serve(tokens_ref, incoming_ref, requester, 0, served_ref.at[requester])
    most = 0
    for requester in range(plan.owners):
        total = 0
        for index in range(plan.half):
            total = total + incoming_ref[requester, 0, plan.capacity + index]
        most = jnp.maximum(most, total)
    crowded_ref[0] = jnp.where(most > plan.part, 1, 0)


def serve_all_kernel(plan, incoming_ref, tokens_ref, served_ref):
    for requester in range(plan.owners):
        serve(tokens_ref, incoming_ref, requester, 0, served_ref.at[requester])


def relay_kernel(plan, shard_ref, incoming_ref, *refs):
    chunk_refs = refs[: plan.half]
    first_ref, second_ref = refs[plan.half :]
    client = shard_ref[0] ^ plan.half
    for distance, chunk_ref in enumerate(chunk_refs):
        owner = (shard_ref[0] % plan.half) ^ distance
        at = 0
        for index in range(plan.half):
            amount = incoming_ref[client, 0, plan.capacity + index]
            at = at + jnp.where(index < owner, amount, 0)
        amount = incoming_ref[client, 0, plan.capacity + owner]
        fit = jnp.clip(plan.part - at, 0, amount)

        def pack(index, carry, chunk_ref=chunk_ref, at=at):
            first_ref[at + index] = chunk_ref[index]
            return carry

        def pack_more(index, carry, chunk_ref=chunk_ref, at=at):
            second_ref[at + index - plan.part] = chunk_ref[index]
            return carry

        lax.fori_loop(0, fit, pack, 0)
        lax.fori_loop(fit, amount, pack_more, 0)


def pick_kernel(plan, core_ref, list_ref, *refs):
    source_refs = refs[:-4]
    own_ref, other_ref, held_ref, sems = refs[-4:]
    count = own_ref.shape[0]
    at = 0
    loads = []
    for index, source_ref in enumerate(source_refs):
        size = source_ref.shape[0]
        if 1 <= index <= plan.half:
            size = plan.extra
            source_ref = source_ref.at[pl.ds(plan.extra, plan.extra)]
        loads.append(
            pltpu.make_async_copy(source_ref, held_ref.at[pl.ds(at, size)], sems.at[index])
        )
        at += size
    for load in loads:
        load.start()
    for load in loads:
        load.wait()
    start = core_ref[0] * count

    def pick(index, carry):
        other_ref[index] = held_ref[list_ref[0, count - start + index]]
        own_ref[index] = held_ref[list_ref[0, start + index]]
        return carry

    lax.fori_loop(0, count, pick, 0, unroll=8)


def attention_kernel(
    length,
    head_dim,
    core_ref,
    scale_a_ref,
    scale_b_ref,
    gain_attn_ref,
    gain_mlp_ref,
    *refs,
):
    own_held_ref, far_held_ref, *held_refs = refs[:8]
    normed_ref, mean_ref, qkv_ref, out_ref = refs[8:12]
    tokens_ref, heads_ref, mixed_ref, hidden_ref, sems, token_sems = refs[12:]
    width = out_ref.shape[0]
    wide = width // 2
    homes = [qkv_ref.at[:, pl.ds(k * wide, wide)] for k in range(4)]
    homes += [out_ref.at[pl.ds(k * wide, wide)] for k in range(2)]
    loads = [
        pltpu.make_async_copy(held, home, sems.at[k])
        for k, (held, home) in enumerate(zip(held_refs, homes))
    ]
    core = core_ref[0]
    token_loads = [
        pltpu.make_async_copy(own_held_ref, tokens_ref.at[core], token_sems.at[0]),
        pltpu.make_async_copy(far_held_ref, tokens_ref.at[1 - core], token_sems.at[1]),
    ]
    for load in token_loads + loads:
        load.start()
    half = BLOCK * length
    rows = 2 * half
    blocks = tokens_ref.shape[1] // (2 * BLOCK)
    long = 2 * rows
    pair_dim = 2 * head_dim
    scale_refs = (scale_a_ref, scale_b_ref)
    per_core = wide // head_dim
    even = lax.broadcasted_iota(jnp.int32, (half, pair_dim), 1) < head_dim
    same = (
        lax.broadcasted_iota(jnp.int32, (half, half), 0) // length
        == lax.broadcasted_iota(jnp.int32, (half, half), 1) // length
    )

    def span(step, size):
        return pl.ds(pl.multiple_of(step * size, size), size)

    def split(values):
        zero = jnp.zeros_like(values)
        return jnp.concatenate(
            [jnp.where(even, values, zero), jnp.where(even, zero, values)], axis=0
        )

    ones = split(jnp.ones((half, pair_dim), jnp.bfloat16))

    def start_block(step, carry):
        images = pl.ds(step * 2 * BLOCK, 2 * BLOCK)
        tokens = jnp.concatenate(
            [tokens_ref[k, images].reshape(rows, -1).astype(jnp.float32) for k in range(2)], axis=1
        )
        hidden_ref[span(step, rows), :] = tokens
        normed_ref[span(step, rows), :] = norm_rows(tokens, gain_attn_ref[...]).astype(jnp.bfloat16)
        return carry

    def project(step, carry):
        here = span(step // 4, long)
        cut = span(step % 4, 2 * width // 4)
        heads_ref[here, cut] = dot(normed_ref[here, :], qkv_ref[:, cut]).astype(jnp.bfloat16)
        return carry

    def weigh(scores, factor):
        scores = jnp.where(same, scores, -1e30)
        top = jnp.max(scores, axis=1, keepdims=True)
        return jnp.exp2((scores - top) * factor).astype(jnp.bfloat16)

    def mix(query, key, value, factors):
        scores = dot_nt(query, split(key))
        weights = [weigh(scores[:, k * half : (k + 1) * half], factors[k]) for k in range(2)]
        mixed = dot(jnp.concatenate(weights, axis=1), jnp.concatenate([split(value), ones], axis=1))
        total = mixed[:, pair_dim:]
        inverse = pl.reciprocal(total, approx=True)
        inverse = inverse * (2.0 - total * inverse)
        return (mixed[:, :pair_dim] * inverse).astype(jnp.bfloat16)

    def attend(step, carry):
        for index in range(width // pair_dim):
            factors = [scale_refs[k // per_core][k % per_core] for k in (2 * index, 2 * index + 1)]
            factors = [factor * (LOG2E / head_dim**0.5) for factor in factors]
            cut = slice(index * pair_dim, (index + 1) * pair_dim)
            beyond = slice(width + cut.start, width + cut.stop)
            sides = [span(2 * step + k, half) for k in range(2)]
            query = [heads_ref[side, cut] for side in sides]
            value = [heads_ref[side, beyond] for side in sides]
            for k in range(2):
                mixed_ref[sides[k], cut] = mix(query[k], query[1 - k], value[1 - k], factors)
        return carry

    def join(step, carry):
        here = span(step // 2, long)
        cut = span(step % 2, width // 2)
        hidden_ref[here, cut] += dot(mixed_ref[here, :], out_ref[:, cut])
        return carry

    def middle_block(step, carry):
        here = span(step, rows)
        hidden = hidden_ref[here, :]
        mean_ref[span(step, BLOCK), :] = jnp.sum(
            hidden.reshape(2, BLOCK, length, -1), axis=(0, 2)
        )
        normed_ref[here, :] = norm_rows(hidden, gain_mlp_ref[...]).astype(jnp.bfloat16)
        return carry

    for load in token_loads:
        load.wait()
    lax.fori_loop(0, blocks, start_block, 0)
    for load in loads[:4]:
        load.wait()
    lax.fori_loop(0, blocks // 2 * 4, project, 0)
    lax.fori_loop(0, blocks, attend, 0)
    for load in loads[4:6]:
        load.wait()
    lax.fori_loop(0, blocks // 2 * 2, join, 0)
    lax.fori_loop(0, blocks, middle_block, 0)


def back_kernel(length, core_ref, mean_ref, pooled_a_ref, pooled_b_ref, back_a_ref, back_b_ref, result_ref):
    count = mean_ref.shape[0]

    def spread(pooled_ref):
        pooled = pooled_ref[...] * (0.5 / length)
        coarse = pooled.astype(jnp.bfloat16)
        fine = (pooled - coarse.astype(jnp.float32)).astype(jnp.bfloat16)
        return jnp.concatenate([coarse, fine], axis=0)

    back = dot(spread(pooled_a_ref), back_a_ref[...]) + dot(spread(pooled_b_ref), back_b_ref[...])
    mean = mean_ref[...] * (0.5 / length)
    result = (mean + back[:count] + back[count:]).astype(jnp.bfloat16)
    start = pl.multiple_of(core_ref[0] * count, count)
    result_ref[pl.ds(start, count), :] = result
    result_ref[pl.ds(pl.multiple_of(count - start, count), count), :] = jnp.zeros_like(result)


def expand(normed, w_in, bias, length):
    inner = dot(normed, w_in) + bias
    inner = jax.nn.gelu(inner, approximate=True).astype(jnp.bfloat16).astype(jnp.float32)
    inner = inner.reshape(-1, 2, BLOCK, length, inner.shape[-1])
    return jnp.sum(inner, axis=(1, 3)).reshape(-1, inner.shape[-1])


def on_device(
    image_tokens,
    pair_owner,
    pair_slot,
    gain_attn,
    w_qk,
    w_value,
    logit_scale,
    w_out,
    gain_mlp,
    w_in,
    bias_in,
    w_back,
):
    owner_count = lax.axis_size("shard")
    core = lax.axis_index("mp").reshape(1)
    shard = lax.axis_index("shard").reshape(1)
    pair_count = pair_owner.shape[0]
    _, length, features = image_tokens.shape
    width = 2 * features
    head_dim = w_qk.shape[1] // logit_scale.shape[0]
    mine = pair_count // 2
    units = 2 * w_in.shape[1]
    plan = Plan(pair_count, owner_count)

    def swap(values):
        return lax.ppermute(values, "mp", [(0, 1), (1, 0)])

    def across(values, distance):
        return lax.ppermute(values, "shard", [(k, k ^ distance) for k in range(owner_count)])

    def images(*counts):
        return jax.ShapeDtypeStruct((*counts, length, features), jnp.bfloat16)

    smem = pl.BlockSpec(memory_space=pltpu.SMEM)
    vmem = pl.BlockSpec(memory_space=pltpu.VMEM)
    hbm = pl.BlockSpec(memory_space=pl.ANY)

    def limit(mebibytes):
        return pltpu.CompilerParams(vmem_limit_bytes=mebibytes * 2**20)

    wanted, order = pl.pallas_call(
        functools.partial(place_kernel, plan, pair_count),
        out_shape=(
            jax.ShapeDtypeStruct((owner_count, 1, plan.row), jnp.int32),
            jax.ShapeDtypeStruct((1, 2 * pair_count), jnp.int32),
        ),
        in_specs=[smem, vmem, vmem],
    )(shard, pair_owner.T, pair_slot.T)
    incoming = lax.all_to_all(wanted, "shard", split_axis=0, concat_axis=0, tiled=True)
    if not plan.extra:
        served = pl.pallas_call(
            functools.partial(serve_all_kernel, plan),
            out_shape=images(owner_count, plan.base),
            in_specs=[smem, vmem],
        )(incoming, image_tokens)
        returned = lax.all_to_all(served, "shard", split_axis=0, concat_axis=0, tiled=True)
        sources = [returned.reshape(-1, length, features)]
    else:
        *chunks, served, crowded = pl.pallas_call(
            functools.partial(serve_kernel, plan),
            out_shape=[images(2 * plan.extra)] * plan.half
            + [images(owner_count, plan.base), jax.ShapeDtypeStruct((1,), jnp.int32)],
            in_specs=[smem, smem, vmem],
            out_specs=[vmem] * (plan.half + 1) + [smem],
        )(shard, incoming, image_tokens)
        chunks = [chunks[0]] + [across(chunks[k], k) for k in range(1, plan.half)]
        returned = lax.all_to_all(served, "shard", split_axis=0, concat_axis=0, tiled=True)
        returned = returned.reshape(-1, length, features)
        first, second = pl.pallas_call(
            functools.partial(relay_kernel, plan),
            out_shape=[images(plan.part)] * 2,
            in_specs=[smem, smem] + [vmem] * plan.half,
            cost_estimate=pl.CostEstimate(
                flops=2 * 10**11, bytes_accessed=2**20, transcendentals=0
            ),
        )(shard, incoming, *chunks)
        first = across(first, plan.half)
        sources = [returned, *chunks, first]
    weights = (w_qk, w_value, w_out, w_in, w_back, bias_in, logit_scale)
    if plan.extra:
        chunks, weights = lax.optimization_barrier((chunks, weights))
    swapped = [swap(w) for w in weights]
    sources, swapped = lax.optimization_barrier((sources, swapped))
    far_qk, far_value, far_out, far_in, far_back, far_bias, far_scale = swapped
    if plan.extra:
        second, sources = lax.optimization_barrier((second, sources))
        second = lax.cond(
            crowded[0] > 0, lambda part: across(part, plan.half), lambda part: part, second
        )
        sources = [*sources, second]
    own, other = pl.pallas_call(
        functools.partial(pick_kernel, plan),
        out_shape=[images(pair_count)] * 2,
        in_specs=[smem, smem] + [hbm] * len(sources),
        scratch_shapes=[
            pltpu.VMEM((plan.slots, length, features), jnp.bfloat16),
            pltpu.SemaphoreType.DMA((len(sources),)),
        ],
        compiler_params=limit(16),
    )(core, order, *sources)
    far = swap(other)
    token_count = pair_count * length
    normed, mean = pl.pallas_call(
        functools.partial(attention_kernel, length, head_dim),
        out_shape=(
            jax.ShapeDtypeStruct((token_count, width), jnp.bfloat16),
            jax.ShapeDtypeStruct((mine, width), jnp.float32),
        ),
        in_specs=[smem] * 3 + [vmem] * 4 + [hbm] * 6,
        scratch_shapes=[
            pltpu.VMEM((width, 2 * width), jnp.bfloat16),
            pltpu.VMEM((width, width), jnp.bfloat16),
            pltpu.VMEM((2, pair_count, length, features), jnp.bfloat16),
            pltpu.VMEM((token_count, 2 * width), jnp.bfloat16),
            pltpu.VMEM((token_count, width), jnp.bfloat16),
            pltpu.VMEM((token_count, width), jnp.float32),
            pltpu.SemaphoreType.DMA((6,)),
            pltpu.SemaphoreType.DMA((2,)),
        ],
        compiler_params=limit(24),
        cost_estimate=pl.CostEstimate(
            flops=6 * token_count * width * width,
            bytes_accessed=4 * 2**20,
            transcendentals=token_count * 1024,
        ),
    )(
        core,
        logit_scale,
        far_scale,
        gain_attn.reshape(1, -1),
        gain_mlp.reshape(1, -1),
        own,
        far,
        w_qk,
        far_qk,
        w_value,
        far_value,
        w_out,
        far_out,
    )
    here = pl.pallas_call(
        functools.partial(back_kernel, length),
        out_shape=jax.ShapeDtypeStruct((pair_count, width), jnp.bfloat16),
        in_specs=[smem] + [vmem] * 5,
        compiler_params=limit(16),
    )(
        core,
        mean,
        expand(normed, w_in, bias_in, length),
        expand(normed, far_in, far_bias, length),
        w_back,
        far_back,
    )
    return here + swap(here)


def solution(mesh):
    in_specs = (
        P(("groups", "shard"), None, "mp"),
        P(("groups", "shard"), None),
        P(("groups", "shard"), None),
        P(),
        P(None, "mp"),
        P(None, "mp"),
        P("mp"),
        P("mp", None),
        P(),
        P(None, "mp"),
        P("mp"),
        P("mp", None),
    )
    out_specs = P(("groups", "shard"), None)
    return jax.shard_map(
        on_device, mesh=mesh, in_specs=in_specs, out_specs=out_specs, check_vma=False
    )
```

```python
import functools

import jax
import jax.numpy as jnp
from jax import lax
from jax.experimental import pallas as pl
from jax.experimental.pallas import tpu as pltpu
from jax.sharding import PartitionSpec as P

LOG2E = 1.4426950408889634
BLOCK = 8


def norm_rows(values, gain):
    center = values - jnp.mean(values, axis=-1, keepdims=True)
    spread = jnp.mean(center * center, axis=-1, keepdims=True)
    return center * lax.rsqrt(spread + 1e-05) * gain


def dot_nt(a, b):
    return lax.dot_general(a, b, (((1,), (1,)), ((), ())), preferred_element_type=jnp.float32)


def dot(a, b):
    return jnp.dot(a, b, preferred_element_type=jnp.float32)


class Plan:
    def __init__(self, pair_count, owner_count):
        self.owners = owner_count
        self.capacity = max(2, 4 * pair_count // owner_count)
        self.half = owner_count // 2
        split = self.capacity >= 32 and self.half & (self.half - 1) == 0 and self.half > 0
        self.base = self.capacity // 2 if split else self.capacity
        self.extra = self.capacity - self.base
        self.part = self.half * self.extra // 2
        self.near_at = owner_count * self.base
        self.rest_at = self.near_at + self.half * self.extra
        self.slots = self.rest_at + 2 * self.part
        self.row = self.capacity + (self.half if split else 0)


def place_kernel(plan, count, shard_ref, owner_ref, slot_ref, wanted_ref, list_ref):
    total = 2 * count
    owners = plan.owners
    owner = jnp.concatenate([owner_ref[0:1, :], owner_ref[1:2, :]], axis=1)
    slot = jnp.concatenate([slot_ref[0:1, :], slot_ref[1:2, :]], axis=1)

    def place(dim, size):
        return lax.broadcasted_iota(jnp.int32, (size, total), dim)

    def as_bf16(values):
        return values.astype(jnp.float32).astype(jnp.bfloat16)

    row = place(0, owners)
    named = row == owner
    until = as_bf16(jnp.where(place(0, total) <= place(1, total), 1, 0))
    tally = dot(as_bf16(jnp.where(named, 1, 0)), until).astype(jnp.int32)
    rank = jnp.sum(jnp.where(named, tally, 0), axis=0, keepdims=True) - 1
    ranked = as_bf16(jnp.where(place(0, total) == rank, 1, 0))
    wanted = dot_nt(as_bf16(jnp.where(named, slot, 0)), ranked).astype(jnp.int32)
    where = owner * plan.base + rank
    if plan.extra:
        me = shard_ref[0]
        half = plan.half
        over = jnp.maximum(jnp.max(tally, axis=1, keepdims=True) - plan.base, 0)
        far_over = jnp.where(row // half != me // half, over, 0)
        before = jnp.zeros((owners, total), jnp.int32)
        for index in range(owners - 1):
            before = before + jnp.where(row > index, far_over[index : index + 1], 0)
        before = jnp.sum(jnp.where(named, before, 0), axis=0, keepdims=True)
        rest = rank - plan.base
        near = plan.near_at + ((owner % half) ^ (me % half)) * plan.extra + rest
        late = jnp.where(owner // half == me // half, near, plan.rest_at + before + rest)
        where = jnp.where(rest < 0, where, late)
        told = place(1, owners) == plan.capacity + row % half
        wanted = wanted + jnp.sum(jnp.where(told, far_over, 0), axis=0, keepdims=True)
    for index in range(owners):
        wanted_ref[index] = wanted[index : index + 1, : plan.row]
    entry = place(1, 1)
    side = entry // count
    pair = entry % count
    mine = count // 2
    local = pair % mine
    position = pair // mine * count + local // BLOCK * (2 * BLOCK) + side * BLOCK + local % BLOCK
    seated = as_bf16(jnp.where(place(0, total) == position, 1, 0))
    parts = as_bf16(jnp.where(place(0, 8) == 0, where // 16, where % 16))
    listed = dot_nt(parts, seated).astype(jnp.int32)
    list_ref[...] = listed[0:1] * 16 + listed[1:2]


def serve(tokens_ref, incoming_ref, requester, start, served_ref):
    count = served_ref.shape[0]

    def copy(index, carry):
        served_ref[index] = tokens_ref[incoming_ref[requester, 0, start + index]]
        return carry

    lax.fori_loop(0, count, copy, 0, unroll=min(16, count))


def serve_kernel(plan, shard_ref, incoming_ref, tokens_ref, *refs):
    *chunk_refs, served_ref, crowded_ref = refs
    me = shard_ref[0]
    for distance, chunk_ref in enumerate(chunk_refs):
        for part in range(2):
            requester = me ^ (distance + (plan.half if part == 0 else 0))
            home = chunk_ref.at[pl.ds(part * plan.extra, plan.extra)]
            serve(tokens_ref, incoming_ref, requester, plan.base, home)
    for requester in range(plan.owners):
        serve(tokens_ref, incoming_ref, requester, 0, served_ref.at[requester])
    most = 0
    for requester in range(plan.owners):
        total = 0
        for index in range(plan.half):
            total = total + incoming_ref[requester, 0, plan.capacity + index]
        most = jnp.maximum(most, total)
    crowded_ref[0] = jnp.where(most > plan.part, 1, 0)


def serve_all_kernel(plan, incoming_ref, tokens_ref, served_ref):
    for requester in range(plan.owners):
        serve(tokens_ref, incoming_ref, requester, 0, served_ref.at[requester])


def relay_kernel(plan, shard_ref, incoming_ref, *refs):
    chunk_refs = refs[: plan.half]
    first_ref, second_ref = refs[plan.half :]
    client = shard_ref[0] ^ plan.half
    for distance, chunk_ref in enumerate(chunk_refs):
        owner = (shard_ref[0] % plan.half) ^ distance
        at = 0
        for index in range(plan.half):
            amount = incoming_ref[client, 0, plan.capacity + index]
            at = at + jnp.where(index < owner, amount, 0)
        amount = incoming_ref[client, 0, plan.capacity + owner]
        fit = jnp.clip(plan.part - at, 0, amount)

        def pack(index, carry, chunk_ref=chunk_ref, at=at):
            first_ref[at + index] = chunk_ref[index]
            return carry

        def pack_more(index, carry, chunk_ref=chunk_ref, at=at):
            second_ref[at + index - plan.part] = chunk_ref[index]
            return carry

        lax.fori_loop(0, fit, pack, 0)
        lax.fori_loop(fit, amount, pack_more, 0)


def pick_kernel(plan, core_ref, list_ref, *refs):
    source_refs = refs[:-4]
    own_ref, other_ref, held_ref, sems = refs[-4:]
    count = own_ref.shape[0]
    at = 0
    loads = []
    for index, source_ref in enumerate(source_refs):
        size = source_ref.shape[0]
        if 1 <= index <= plan.half:
            size = plan.extra
            source_ref = source_ref.at[pl.ds(plan.extra, plan.extra)]
        loads.append(
            pltpu.make_async_copy(source_ref, held_ref.at[pl.ds(at, size)], sems.at[index])
        )
        at += size
    for load in loads:
        load.start()
    for load in loads:
        load.wait()
    start = core_ref[0] * count

    def pick(index, carry):
        other_ref[index] = held_ref[list_ref[0, count - start + index]]
        own_ref[index] = held_ref[list_ref[0, start + index]]
        return carry

    lax.fori_loop(0, count, pick, 0, unroll=8)


def attention_kernel(
    length,
    head_dim,
    core_ref,
    scale_a_ref,
    scale_b_ref,
    gain_attn_ref,
    gain_mlp_ref,
    *refs,
):
    own_held_ref, far_held_ref, *held_refs = refs[:14]
    normed_ref, mean_ref, in_ref, back_ref, bias_ref = refs[14:19]
    qkv_ref, out_ref, tokens_ref, heads_ref, mixed_ref, hidden_ref, sems, token_sems = refs[19:]
    units = in_ref.shape[1] // 2
    width = out_ref.shape[0]
    wide = width // 2
    homes = [qkv_ref.at[:, pl.ds(k * wide, wide)] for k in range(4)]
    homes += [out_ref.at[pl.ds(k * wide, wide)] for k in range(2)]
    homes += [in_ref.at[:, pl.ds(k * units, units)] for k in range(2)]
    homes += [back_ref.at[pl.ds(k * units, units)] for k in range(2)]
    homes += [bias_ref.at[:, pl.ds(k * units, units)] for k in range(2)]
    loads = [
        pltpu.make_async_copy(held, home, sems.at[k])
        for k, (held, home) in enumerate(zip(held_refs, homes))
    ]
    core = core_ref[0]
    token_loads = [
        pltpu.make_async_copy(own_held_ref, tokens_ref.at[core], token_sems.at[0]),
        pltpu.make_async_copy(far_held_ref, tokens_ref.at[1 - core], token_sems.at[1]),
    ]
    for load in token_loads + loads:
        load.start()
    half = BLOCK * length
    rows = 2 * half
    blocks = tokens_ref.shape[1] // (2 * BLOCK)
    long = 2 * rows
    pair_dim = 2 * head_dim
    scale_refs = (scale_a_ref, scale_b_ref)
    per_core = wide // head_dim
    even = lax.broadcasted_iota(jnp.int32, (half, pair_dim), 1) < head_dim
    same = (
        lax.broadcasted_iota(jnp.int32, (half, half), 0) // length
        == lax.broadcasted_iota(jnp.int32, (half, half), 1) // length
    )

    def span(step, size):
        return pl.ds(pl.multiple_of(step * size, size), size)

    def split(values):
        zero = jnp.zeros_like(values)
        return jnp.concatenate(
            [jnp.where(even, values, zero), jnp.where(even, zero, values)], axis=0
        )

    ones = split(jnp.ones((half, pair_dim), jnp.bfloat16))

    def start_block(step, carry):
        images = pl.ds(step * 2 * BLOCK, 2 * BLOCK)
        tokens = jnp.concatenate(
            [tokens_ref[k, images].reshape(rows, -1).astype(jnp.float32) for k in range(2)], axis=1
        )
        hidden_ref[span(step, rows), :] = tokens
        normed_ref[span(step, rows), :] = norm_rows(tokens, gain_attn_ref[...]).astype(jnp.bfloat16)
        return carry

    def project(step, carry):
        here = span(step // 4, long)
        cut = span(step % 4, 2 * width // 4)
        heads_ref[here, cut] = dot(normed_ref[here, :], qkv_ref[:, cut]).astype(jnp.bfloat16)
        return carry

    def weigh(scores, factor):
        scores = jnp.where(same, scores, -1e30)
        top = jnp.max(scores, axis=1, keepdims=True)
        return jnp.exp2((scores - top) * factor).astype(jnp.bfloat16)

    def mix(query, key, value, factors):
        scores = dot_nt(query, split(key))
        weights = [weigh(scores[:, k * half : (k + 1) * half], factors[k]) for k in range(2)]
        mixed = dot(jnp.concatenate(weights, axis=1), jnp.concatenate([split(value), ones], axis=1))
        total = mixed[:, pair_dim:]
        inverse = pl.reciprocal(total, approx=True)
        inverse = inverse * (2.0 - total * inverse)
        return (mixed[:, :pair_dim] * inverse).astype(jnp.bfloat16)

    def attend(step, carry):
        for index in range(width // pair_dim):
            factors = [scale_refs[k // per_core][k % per_core] for k in (2 * index, 2 * index + 1)]
            factors = [factor * (LOG2E / head_dim**0.5) for factor in factors]
            cut = slice(index * pair_dim, (index + 1) * pair_dim)
            beyond = slice(width + cut.start, width + cut.stop)
            sides = [span(2 * step + k, half) for k in range(2)]
            query = [heads_ref[side, cut] for side in sides]
            value = [heads_ref[side, beyond] for side in sides]
            for k in range(2):
                mixed_ref[sides[k], cut] = mix(query[k], query[1 - k], value[1 - k], factors)
        return carry

    def join(step, carry):
        here = span(step // 2, long)
        cut = span(step % 2, width // 2)
        hidden_ref[here, cut] += dot(mixed_ref[here, :], out_ref[:, cut])
        return carry

    def middle_block(step, carry):
        here = span(step, rows)
        hidden = hidden_ref[here, :]
        mean_ref[span(step, BLOCK), :] = jnp.sum(
            hidden.reshape(2, BLOCK, length, -1), axis=(0, 2)
        )
        normed_ref[here, :] = norm_rows(hidden, gain_mlp_ref[...]).astype(jnp.bfloat16)
        return carry

    for load in token_loads:
        load.wait()
    lax.fori_loop(0, blocks, start_block, 0)
    for load in loads[:4]:
        load.wait()
    lax.fori_loop(0, blocks // 2 * 4, project, 0)
    lax.fori_loop(0, blocks, attend, 0)
    for load in loads[4:]:
        load.wait()
    lax.fori_loop(0, blocks // 2 * 2, join, 0)
    lax.fori_loop(0, blocks, middle_block, 0)


def back_kernel(length, core_ref, mean_ref, pooled_ref, back_ref, result_ref):
    count = mean_ref.shape[0]
    pooled = pooled_ref[...] * (0.5 / length)
    coarse = pooled.astype(jnp.bfloat16)
    fine = (pooled - coarse.astype(jnp.float32)).astype(jnp.bfloat16)
    back = dot(jnp.concatenate([coarse, fine], axis=0), back_ref[...])
    mean = mean_ref[...] * (0.5 / length)
    result = (mean + back[:count] + back[count:]).astype(jnp.bfloat16)
    start = pl.multiple_of(core_ref[0] * count, count)
    result_ref[pl.ds(start, count), :] = result
    result_ref[pl.ds(pl.multiple_of(count - start, count), count), :] = jnp.zeros_like(result)


def expand(normed, w_in, bias, length):
    inner = dot(normed, w_in) + bias
    inner = jax.nn.gelu(inner, approximate=True).astype(jnp.bfloat16).astype(jnp.float32)
    inner = inner.reshape(-1, 2, BLOCK, length, inner.shape[-1])
    return jnp.sum(inner, axis=(1, 3)).reshape(-1, inner.shape[-1])


def on_device(
    image_tokens,
    pair_owner,
    pair_slot,
    gain_attn,
    w_qk,
    w_value,
    logit_scale,
    w_out,
    gain_mlp,
    w_in,
    bias_in,
    w_back,
):
    owner_count = lax.axis_size("shard")
    core = lax.axis_index("mp").reshape(1)
    shard = lax.axis_index("shard").reshape(1)
    pair_count = pair_owner.shape[0]
    _, length, features = image_tokens.shape
    width = 2 * features
    head_dim = w_qk.shape[1] // logit_scale.shape[0]
    mine = pair_count // 2
    units = 2 * w_in.shape[1]
    plan = Plan(pair_count, owner_count)

    def swap(values):
        return lax.ppermute(values, "mp", [(0, 1), (1, 0)])

    def across(values, distance):
        return lax.ppermute(values, "shard", [(k, k ^ distance) for k in range(owner_count)])

    def images(*counts):
        return jax.ShapeDtypeStruct((*counts, length, features), jnp.bfloat16)

    smem = pl.BlockSpec(memory_space=pltpu.SMEM)
    vmem = pl.BlockSpec(memory_space=pltpu.VMEM)
    hbm = pl.BlockSpec(memory_space=pl.ANY)

    def limit(mebibytes):
        return pltpu.CompilerParams(vmem_limit_bytes=mebibytes * 2**20)

    wanted, order = pl.pallas_call(
        functools.partial(place_kernel, plan, pair_count),
        out_shape=(
            jax.ShapeDtypeStruct((owner_count, 1, plan.row), jnp.int32),
            jax.ShapeDtypeStruct((1, 2 * pair_count), jnp.int32),
        ),
        in_specs=[smem, vmem, vmem],
    )(shard, pair_owner.T, pair_slot.T)
    incoming = lax.all_to_all(wanted, "shard", split_axis=0, concat_axis=0, tiled=True)
    if not plan.extra:
        served = pl.pallas_call(
            functools.partial(serve_all_kernel, plan),
            out_shape=images(owner_count, plan.base),
            in_specs=[smem, vmem],
        )(incoming, image_tokens)
        returned = lax.all_to_all(served, "shard", split_axis=0, concat_axis=0, tiled=True)
        sources = [returned.reshape(-1, length, features)]
    else:
        *chunks, served, crowded = pl.pallas_call(
            functools.partial(serve_kernel, plan),
            out_shape=[images(2 * plan.extra)] * plan.half
            + [images(owner_count, plan.base), jax.ShapeDtypeStruct((1,), jnp.int32)],
            in_specs=[smem, smem, vmem],
            out_specs=[vmem] * (plan.half + 1) + [smem],
        )(shard, incoming, image_tokens)
        chunks = [chunks[0]] + [across(chunks[k], k) for k in range(1, plan.half)]
        returned = lax.all_to_all(served, "shard", split_axis=0, concat_axis=0, tiled=True)
        returned = returned.reshape(-1, length, features)
        first, second = pl.pallas_call(
            functools.partial(relay_kernel, plan),
            out_shape=[images(plan.part)] * 2,
            in_specs=[smem, smem] + [vmem] * plan.half,
            cost_estimate=pl.CostEstimate(
                flops=2 * 10**11, bytes_accessed=2**20, transcendentals=0
            ),
        )(shard, incoming, *chunks)
        first = across(first, plan.half)
        sources = [returned, *chunks, first]
    weights = (w_qk, w_value, w_out, w_in, w_back, bias_in, logit_scale)
    if plan.extra:
        chunks, weights = lax.optimization_barrier((chunks, weights))
    swapped = [swap(w) for w in weights]
    sources, swapped = lax.optimization_barrier((sources, swapped))
    far_qk, far_value, far_out, far_in, far_back, far_bias, far_scale = swapped
    if plan.extra:
        second, sources = lax.optimization_barrier((second, sources))
        second = lax.cond(
            crowded[0] > 0, lambda part: across(part, plan.half), lambda part: part, second
        )
        sources = [*sources, second]
    own, other = pl.pallas_call(
        functools.partial(pick_kernel, plan),
        out_shape=[images(pair_count)] * 2,
        in_specs=[smem, smem] + [hbm] * len(sources),
        scratch_shapes=[
            pltpu.VMEM((plan.slots, length, features), jnp.bfloat16),
            pltpu.SemaphoreType.DMA((len(sources),)),
        ],
    )(core, order, *sources)
    far = swap(other)
    token_count = pair_count * length
    units = 2 * w_in.shape[1]
    normed, mean, all_in, all_back, all_bias = pl.pallas_call(
        functools.partial(attention_kernel, length, head_dim),
        out_shape=(
            jax.ShapeDtypeStruct((token_count, width), jnp.bfloat16),
            jax.ShapeDtypeStruct((mine, width), jnp.float32),
            jax.ShapeDtypeStruct((width, units), jnp.bfloat16),
            jax.ShapeDtypeStruct((units, width), jnp.bfloat16),
            jax.ShapeDtypeStruct((1, units), jnp.float32),
        ),
        in_specs=[smem] * 3 + [vmem] * 4 + [hbm] * 12,
        scratch_shapes=[
            pltpu.VMEM((width, 2 * width), jnp.bfloat16),
            pltpu.VMEM((width, width), jnp.bfloat16),
            pltpu.VMEM((2, pair_count, length, features), jnp.bfloat16),
            pltpu.VMEM((token_count, 2 * width), jnp.bfloat16),
            pltpu.VMEM((token_count, width), jnp.bfloat16),
            pltpu.VMEM((token_count, width), jnp.float32),
            pltpu.SemaphoreType.DMA((12,)),
            pltpu.SemaphoreType.DMA((2,)),
        ],
        compiler_params=limit(32),
        cost_estimate=pl.CostEstimate(
            flops=6 * token_count * width * width,
            bytes_accessed=4 * 2**20,
            transcendentals=token_count * 1024,
        ),
    )(
        core,
        logit_scale,
        far_scale,
        gain_attn.reshape(1, -1),
        gain_mlp.reshape(1, -1),
        own,
        far,
        w_qk,
        far_qk,
        w_value,
        far_value,
        w_out,
        far_out,
        w_in,
        far_in,
        w_back,
        far_back,
        bias_in.reshape(1, -1),
        far_bias.reshape(1, -1),
    )
    here = pl.pallas_call(
        functools.partial(back_kernel, length),
        out_shape=jax.ShapeDtypeStruct((pair_count, width), jnp.bfloat16),
        in_specs=[smem] + [vmem] * 3,
        compiler_params=limit(16),
    )(core, mean, expand(normed, all_in, all_bias, length), all_back)
    return here + swap(here)


def solution(mesh):
    in_specs = (
        P(("groups", "shard"), None, "mp"),
        P(("groups", "shard"), None),
        P(("groups", "shard"), None),
        P(),
        P(None, "mp"),
        P(None, "mp"),
        P("mp"),
        P("mp", None),
        P(),
        P(None, "mp"),
        P("mp"),
        P("mp", None),
    )
    out_specs = P(("groups", "shard"), None)
    return jax.shard_map(
        on_device, mesh=mesh, in_specs=in_specs, out_specs=out_specs, check_vma=False
    )
```

```python
import functools

import jax
import jax.numpy as jnp
from jax import lax
from jax.experimental import pallas as pl
from jax.experimental.pallas import tpu as pltpu
from jax.sharding import PartitionSpec as P

LOG2E = 1.4426950408889634
BLOCK = 8


def norm_rows(values, gain):
    center = values - jnp.mean(values, axis=-1, keepdims=True)
    spread = jnp.mean(center * center, axis=-1, keepdims=True)
    return center * lax.rsqrt(spread + 1e-05) * gain


def dot_nt(a, b):
    return lax.dot_general(a, b, (((1,), (1,)), ((), ())), preferred_element_type=jnp.float32)


def dot(a, b):
    return jnp.dot(a, b, preferred_element_type=jnp.float32)


class Plan:
    def __init__(self, pair_count, owner_count):
        self.owners = owner_count
        self.capacity = max(2, 4 * pair_count // owner_count)
        self.half = owner_count // 2
        split = self.capacity >= 32 and self.half & (self.half - 1) == 0 and self.half > 0
        self.base = self.capacity // 2 if split else self.capacity
        self.extra = self.capacity - self.base
        self.part = self.half * self.extra // 2
        self.near_at = owner_count * self.base
        self.rest_at = self.near_at + self.half * self.extra
        self.slots = self.rest_at + 2 * self.part
        self.row = self.capacity + (self.half if split else 0)


def place_kernel(plan, count, shard_ref, owner_ref, slot_ref, wanted_ref, list_ref):
    total = 2 * count
    owners = plan.owners
    owner = jnp.concatenate([owner_ref[0:1, :], owner_ref[1:2, :]], axis=1)
    slot = jnp.concatenate([slot_ref[0:1, :], slot_ref[1:2, :]], axis=1)

    def place(dim, size):
        return lax.broadcasted_iota(jnp.int32, (size, total), dim)

    def as_bf16(values):
        return values.astype(jnp.float32).astype(jnp.bfloat16)

    row = place(0, owners)
    named = row == owner
    until = as_bf16(jnp.where(place(0, total) <= place(1, total), 1, 0))
    tally = dot(as_bf16(jnp.where(named, 1, 0)), until).astype(jnp.int32)
    rank = jnp.sum(jnp.where(named, tally, 0), axis=0, keepdims=True) - 1
    ranked = as_bf16(jnp.where(place(0, total) == rank, 1, 0))
    wanted = dot_nt(as_bf16(jnp.where(named, slot, 0)), ranked).astype(jnp.int32)
    where = owner * plan.base + rank
    if plan.extra:
        me = shard_ref[0]
        half = plan.half
        over = jnp.maximum(jnp.max(tally, axis=1, keepdims=True) - plan.base, 0)
        far_over = jnp.where(row // half != me // half, over, 0)
        before = jnp.zeros((owners, total), jnp.int32)
        for index in range(owners - 1):
            before = before + jnp.where(row > index, far_over[index : index + 1], 0)
        before = jnp.sum(jnp.where(named, before, 0), axis=0, keepdims=True)
        rest = rank - plan.base
        near = plan.near_at + ((owner % half) ^ (me % half)) * plan.extra + rest
        late = jnp.where(owner // half == me // half, near, plan.rest_at + before + rest)
        where = jnp.where(rest < 0, where, late)
        told = place(1, owners) == plan.capacity + row % half
        wanted = wanted + jnp.sum(jnp.where(told, far_over, 0), axis=0, keepdims=True)
    for index in range(owners):
        wanted_ref[index] = wanted[index : index + 1, : plan.row]
    entry = place(1, 1)
    side = entry // count
    pair = entry % count
    mine = count // 2
    local = pair % mine
    position = pair // mine * count + local // BLOCK * (2 * BLOCK) + side * BLOCK + local % BLOCK
    seated = as_bf16(jnp.where(place(0, total) == position, 1, 0))
    parts = as_bf16(jnp.where(place(0, 8) == 0, where // 16, where % 16))
    listed = dot_nt(parts, seated).astype(jnp.int32)
    list_ref[...] = listed[0:1] * 16 + listed[1:2]


def serve(tokens_ref, incoming_ref, requester, start, served_ref):
    count = served_ref.shape[0]

    def copy(index, carry):
        served_ref[index] = tokens_ref[incoming_ref[requester, 0, start + index]]
        return carry

    lax.fori_loop(0, count, copy, 0, unroll=min(16, count))


def serve_kernel(plan, shard_ref, incoming_ref, tokens_ref, *refs):
    *chunk_refs, served_ref, crowded_ref = refs
    me = shard_ref[0]
    for distance, chunk_ref in enumerate(chunk_refs):
        for part in range(2):
            requester = me ^ (distance + (plan.half if part == 0 else 0))
            home = chunk_ref.at[pl.ds(part * plan.extra, plan.extra)]
            serve(tokens_ref, incoming_ref, requester, plan.base, home)
    for requester in range(plan.owners):
        serve(tokens_ref, incoming_ref, requester, 0, served_ref.at[requester])
    most = 0
    for requester in range(plan.owners):
        total = 0
        for index in range(plan.half):
            total = total + incoming_ref[requester, 0, plan.capacity + index]
        most = jnp.maximum(most, total)
    crowded_ref[0] = jnp.where(most > plan.part, 1, 0)


def serve_all_kernel(plan, incoming_ref, tokens_ref, served_ref):
    for requester in range(plan.owners):
        serve(tokens_ref, incoming_ref, requester, 0, served_ref.at[requester])


def relay_kernel(plan, shard_ref, incoming_ref, *refs):
    chunk_refs = refs[: plan.half]
    first_ref, second_ref = refs[plan.half :]
    client = shard_ref[0] ^ plan.half
    for distance, chunk_ref in enumerate(chunk_refs):
        owner = (shard_ref[0] % plan.half) ^ distance
        at = 0
        for index in range(plan.half):
            amount = incoming_ref[client, 0, plan.capacity + index]
            at = at + jnp.where(index < owner, amount, 0)
        amount = incoming_ref[client, 0, plan.capacity + owner]
        fit = jnp.clip(plan.part - at, 0, amount)

        def pack(index, carry, chunk_ref=chunk_ref, at=at):
            first_ref[at + index] = chunk_ref[index]
            return carry

        def pack_more(index, carry, chunk_ref=chunk_ref, at=at):
            second_ref[at + index - plan.part] = chunk_ref[index]
            return carry

        lax.fori_loop(0, fit, pack, 0)
        lax.fori_loop(fit, amount, pack_more, 0)


def pick_kernel(plan, core_ref, list_ref, *refs):
    source_refs = refs[:-4]
    own_ref, other_ref, held_ref, sems = refs[-4:]
    count = own_ref.shape[0]
    at = 0
    loads = []
    for index, source_ref in enumerate(source_refs):
        size = source_ref.shape[0]
        if 1 <= index <= plan.half:
            size = plan.extra
            source_ref = source_ref.at[pl.ds(plan.extra, plan.extra)]
        loads.append(
            pltpu.make_async_copy(source_ref, held_ref.at[pl.ds(at, size)], sems.at[index])
        )
        at += size
    for load in loads:
        load.start()
    for load in loads:
        load.wait()
    start = core_ref[0] * count

    def pick(index, carry):
        other_ref[index] = held_ref[list_ref[0, count - start + index]]
        own_ref[index] = held_ref[list_ref[0, start + index]]
        return carry

    lax.fori_loop(0, count, pick, 0, unroll=8)


def attention_kernel(
    plan,
    length,
    head_dim,
    core_ref,
    list_ref,
    crowded_ref,
    scale_a_ref,
    scale_b_ref,
    gain_attn_ref,
    gain_mlp_ref,
    *refs,
):
    if plan.extra:
        rest_held_refs, refs = refs[:4], refs[4:]
        *refs, rest_ref, rest_sems = refs
    own_held_ref, far_held_ref, *held_refs = refs[:14]
    normed_ref, mean_ref, in_ref, back_ref, bias_ref = refs[14:19]
    qkv_ref, out_ref, tokens_ref, heads_ref, mixed_ref, hidden_ref, sems, token_sems = refs[19:]
    units = in_ref.shape[1] // 2
    width = out_ref.shape[0]
    wide = width // 2
    homes = [qkv_ref.at[:, pl.ds(k * wide, wide)] for k in range(4)]
    homes += [out_ref.at[pl.ds(k * wide, wide)] for k in range(2)]
    homes += [in_ref.at[:, pl.ds(k * units, units)] for k in range(2)]
    homes += [back_ref.at[pl.ds(k * units, units)] for k in range(2)]
    homes += [bias_ref.at[:, pl.ds(k * units, units)] for k in range(2)]
    loads = [
        pltpu.make_async_copy(held, home, sems.at[k])
        for k, (held, home) in enumerate(zip(held_refs, homes))
    ]
    core = core_ref[0]
    token_loads = [
        pltpu.make_async_copy(own_held_ref, tokens_ref.at[core], token_sems.at[0]),
        pltpu.make_async_copy(far_held_ref, tokens_ref.at[1 - core], token_sems.at[1]),
    ]
    for load in token_loads:
        load.start()
    if plan.extra:
        rest_loads = [
            pltpu.make_async_copy(
                held, rest_ref.at[side, pl.ds(at * plan.part, plan.part)], rest_sems.at[index]
            )
            for index, (held, side, at) in enumerate(
                zip(rest_held_refs, (core, 1 - core, core, 1 - core), (0, 0, 1, 1))
            )
        ]
        for load in rest_loads[:2]:
            load.start()

        @pl.when(crowded_ref[0] > 0)
        def _():
            for load in rest_loads[2:]:
                load.start()

    for load in loads:
        load.start()
    half = BLOCK * length
    rows = 2 * half
    blocks = tokens_ref.shape[1] // (2 * BLOCK)
    long = 2 * rows
    pair_dim = 2 * head_dim
    scale_refs = (scale_a_ref, scale_b_ref)
    per_core = wide // head_dim
    even = lax.broadcasted_iota(jnp.int32, (half, pair_dim), 1) < head_dim
    same = (
        lax.broadcasted_iota(jnp.int32, (half, half), 0) // length
        == lax.broadcasted_iota(jnp.int32, (half, half), 1) // length
    )

    def span(step, size):
        return pl.ds(pl.multiple_of(step * size, size), size)

    def split(values):
        zero = jnp.zeros_like(values)
        return jnp.concatenate(
            [jnp.where(even, values, zero), jnp.where(even, zero, values)], axis=0
        )

    ones = split(jnp.ones((half, pair_dim), jnp.bfloat16))

    def start_block(step, carry):
        images = pl.ds(step * 2 * BLOCK, 2 * BLOCK)
        tokens = jnp.concatenate(
            [tokens_ref[k, images].reshape(rows, -1).astype(jnp.float32) for k in range(2)], axis=1
        )
        hidden_ref[span(step, rows), :] = tokens
        normed_ref[span(step, rows), :] = norm_rows(tokens, gain_attn_ref[...]).astype(jnp.bfloat16)
        return carry

    def project(step, carry):
        here = span(step // 4, long)
        cut = span(step % 4, 2 * width // 4)
        heads_ref[here, cut] = dot(normed_ref[here, :], qkv_ref[:, cut]).astype(jnp.bfloat16)
        return carry

    def weigh(scores, factor):
        scores = jnp.where(same, scores, -1e30)
        top = jnp.max(scores, axis=1, keepdims=True)
        return jnp.exp2((scores - top) * factor).astype(jnp.bfloat16)

    def mix(query, key, value, factors):
        scores = dot_nt(query, split(key))
        weights = [weigh(scores[:, k * half : (k + 1) * half], factors[k]) for k in range(2)]
        mixed = dot(jnp.concatenate(weights, axis=1), jnp.concatenate([split(value), ones], axis=1))
        total = mixed[:, pair_dim:]
        inverse = pl.reciprocal(total, approx=True)
        inverse = inverse * (2.0 - total * inverse)
        return (mixed[:, :pair_dim] * inverse).astype(jnp.bfloat16)

    def attend(step, carry):
        for index in range(width // pair_dim):
            factors = [scale_refs[k // per_core][k % per_core] for k in (2 * index, 2 * index + 1)]
            factors = [factor * (LOG2E / head_dim**0.5) for factor in factors]
            cut = slice(index * pair_dim, (index + 1) * pair_dim)
            beyond = slice(width + cut.start, width + cut.stop)
            sides = [span(2 * step + k, half) for k in range(2)]
            query = [heads_ref[side, cut] for side in sides]
            value = [heads_ref[side, beyond] for side in sides]
            for k in range(2):
                mixed_ref[sides[k], cut] = mix(query[k], query[1 - k], value[1 - k], factors)
        return carry

    def join(step, carry):
        here = span(step // 2, long)
        cut = span(step % 2, width // 2)
        hidden_ref[here, cut] += dot(mixed_ref[here, :], out_ref[:, cut])
        return carry

    def middle_block(step, carry):
        here = span(step, rows)
        hidden = hidden_ref[here, :]
        mean_ref[span(step, BLOCK), :] = jnp.sum(
            hidden.reshape(2, BLOCK, length, -1), axis=(0, 2)
        )
        normed_ref[here, :] = norm_rows(hidden, gain_mlp_ref[...]).astype(jnp.bfloat16)
        return carry

    for load in token_loads:
        load.wait()
    if plan.extra:
        for load in rest_loads[:2]:
            load.wait()

        @pl.when(crowded_ref[0] > 0)
        def _():
            for load in rest_loads[2:]:
                load.wait()

        def put(index, carry):
            where = list_ref[0, core * tokens_ref.shape[1] + index] - plan.rest_at

            @pl.when(where >= 0)
            def _():
                for side in range(2):
                    tokens_ref[side, index] = rest_ref[side, where]

            return carry

        lax.fori_loop(0, tokens_ref.shape[1], put, 0, unroll=4)
    lax.fori_loop(0, blocks, start_block, 0)
    for load in loads[:4]:
        load.wait()
    lax.fori_loop(0, blocks // 2 * 4, project, 0)
    lax.fori_loop(0, blocks, attend, 0)
    for load in loads[4:]:
        load.wait()
    lax.fori_loop(0, blocks // 2 * 2, join, 0)
    lax.fori_loop(0, blocks, middle_block, 0)


def back_kernel(length, core_ref, mean_ref, pooled_ref, back_ref, result_ref):
    count = mean_ref.shape[0]
    pooled = pooled_ref[...] * (0.5 / length)
    coarse = pooled.astype(jnp.bfloat16)
    fine = (pooled - coarse.astype(jnp.float32)).astype(jnp.bfloat16)
    back = dot(jnp.concatenate([coarse, fine], axis=0), back_ref[...])
    mean = mean_ref[...] * (0.5 / length)
    result = (mean + back[:count] + back[count:]).astype(jnp.bfloat16)
    start = pl.multiple_of(core_ref[0] * count, count)
    result_ref[pl.ds(start, count), :] = result
    result_ref[pl.ds(pl.multiple_of(count - start, count), count), :] = jnp.zeros_like(result)


def expand(normed, w_in, bias, length):
    inner = dot(normed, w_in) + bias
    inner = jax.nn.gelu(inner, approximate=True).astype(jnp.bfloat16).astype(jnp.float32)
    inner = inner.reshape(-1, 2, BLOCK, length, inner.shape[-1])
    return jnp.sum(inner, axis=(1, 3)).reshape(-1, inner.shape[-1])


def on_device(
    image_tokens,
    pair_owner,
    pair_slot,
    gain_attn,
    w_qk,
    w_value,
    logit_scale,
    w_out,
    gain_mlp,
    w_in,
    bias_in,
    w_back,
):
    owner_count = lax.axis_size("shard")
    core = lax.axis_index("mp").reshape(1)
    shard = lax.axis_index("shard").reshape(1)
    pair_count = pair_owner.shape[0]
    _, length, features = image_tokens.shape
    width = 2 * features
    head_dim = w_qk.shape[1] // logit_scale.shape[0]
    mine = pair_count // 2
    units = 2 * w_in.shape[1]
    plan = Plan(pair_count, owner_count)

    def swap(values):
        return lax.ppermute(values, "mp", [(0, 1), (1, 0)])

    def across(values, distance):
        return lax.ppermute(values, "shard", [(k, k ^ distance) for k in range(owner_count)])

    def images(*counts):
        return jax.ShapeDtypeStruct((*counts, length, features), jnp.bfloat16)

    smem = pl.BlockSpec(memory_space=pltpu.SMEM)
    vmem = pl.BlockSpec(memory_space=pltpu.VMEM)
    hbm = pl.BlockSpec(memory_space=pl.ANY)

    def limit(mebibytes):
        return pltpu.CompilerParams(vmem_limit_bytes=mebibytes * 2**20)

    wanted, order = pl.pallas_call(
        functools.partial(place_kernel, plan, pair_count),
        out_shape=(
            jax.ShapeDtypeStruct((owner_count, 1, plan.row), jnp.int32),
            jax.ShapeDtypeStruct((1, 2 * pair_count), jnp.int32),
        ),
        in_specs=[smem, vmem, vmem],
    )(shard, pair_owner.T, pair_slot.T)
    incoming = lax.all_to_all(wanted, "shard", split_axis=0, concat_axis=0, tiled=True)
    if not plan.extra:
        served = pl.pallas_call(
            functools.partial(serve_all_kernel, plan),
            out_shape=images(owner_count, plan.base),
            in_specs=[smem, vmem],
        )(incoming, image_tokens)
        returned = lax.all_to_all(served, "shard", split_axis=0, concat_axis=0, tiled=True)
        sources = [returned.reshape(-1, length, features)]
    else:
        *chunks, served, crowded = pl.pallas_call(
            functools.partial(serve_kernel, plan),
            out_shape=[images(2 * plan.extra)] * plan.half
            + [images(owner_count, plan.base), jax.ShapeDtypeStruct((1,), jnp.int32)],
            in_specs=[smem, smem, vmem],
            out_specs=[vmem] * (plan.half + 1) + [smem],
        )(shard, incoming, image_tokens)
        chunks = [chunks[0]] + [across(chunks[k], k) for k in range(1, plan.half)]
        returned = lax.all_to_all(served, "shard", split_axis=0, concat_axis=0, tiled=True)
        returned = returned.reshape(-1, length, features)
        first, second = pl.pallas_call(
            functools.partial(relay_kernel, plan),
            out_shape=[images(plan.part)] * 2,
            in_specs=[smem, smem] + [vmem] * plan.half,
            cost_estimate=pl.CostEstimate(
                flops=2 * 10**11, bytes_accessed=2**20, transcendentals=0
            ),
        )(shard, incoming, *chunks)
        first = across(first, plan.half)
        sources = [returned, *chunks]
    weights = (w_qk, w_value, w_out, w_in, w_back, bias_in, logit_scale)
    if plan.extra:
        chunks, weights = lax.optimization_barrier((chunks, weights))
    swapped = [swap(w) for w in weights]
    own, other = pl.pallas_call(
        functools.partial(pick_kernel, plan),
        out_shape=[images(pair_count)] * 2,
        in_specs=[smem, smem] + [hbm] * len(sources),
        scratch_shapes=[
            pltpu.VMEM((plan.slots, length, features), jnp.bfloat16),
            pltpu.SemaphoreType.DMA((len(sources),)),
        ],
    )(core, order, *sources)
    far = swap(other)
    rest = []
    if plan.extra:
        first, second, swapped = lax.optimization_barrier((first, second, swapped))
        far_first = swap(first)

        def fetch_second(part):
            part = across(part, plan.half)
            return part, swap(part)

        second, far_second = lax.cond(
            crowded[0] > 0, fetch_second, lambda part: (part, part), second
        )
        rest = [first, far_first, second, far_second]
    else:
        crowded = jnp.zeros((1,), jnp.int32)
    far_qk, far_value, far_out, far_in, far_back, far_bias, far_scale = swapped
    token_count = pair_count * length
    units = 2 * w_in.shape[1]
    normed, mean, all_in, all_back, all_bias = pl.pallas_call(
        functools.partial(attention_kernel, plan, length, head_dim),
        out_shape=(
            jax.ShapeDtypeStruct((token_count, width), jnp.bfloat16),
            jax.ShapeDtypeStruct((mine, width), jnp.float32),
            jax.ShapeDtypeStruct((width, units), jnp.bfloat16),
            jax.ShapeDtypeStruct((units, width), jnp.bfloat16),
            jax.ShapeDtypeStruct((1, units), jnp.float32),
        ),
        in_specs=[smem] * 5 + [vmem] * 2 + [hbm] * len(rest) + [vmem] * 2 + [hbm] * 12,
        scratch_shapes=[
            pltpu.VMEM((width, 2 * width), jnp.bfloat16),
            pltpu.VMEM((width, width), jnp.bfloat16),
            pltpu.VMEM((2, pair_count, length, features), jnp.bfloat16),
            pltpu.VMEM((token_count, 2 * width), jnp.bfloat16),
            pltpu.VMEM((token_count, width), jnp.bfloat16),
            pltpu.VMEM((token_count, width), jnp.float32),
            pltpu.SemaphoreType.DMA((12,)),
            pltpu.SemaphoreType.DMA((2,)),
        ]
        + (
            [
                pltpu.VMEM((2, 2 * plan.part, length, features), jnp.bfloat16),
                pltpu.SemaphoreType.DMA((4,)),
            ]
            if rest
            else []
        ),
        compiler_params=limit(32),
        cost_estimate=pl.CostEstimate(
            flops=6 * token_count * width * width,
            bytes_accessed=4 * 2**20,
            transcendentals=token_count * 1024,
        ),
    )(
        core,
        order,
        crowded,
        logit_scale,
        far_scale,
        gain_attn.reshape(1, -1),
        gain_mlp.reshape(1, -1),
        *rest,
        own,
        far,
        w_qk,
        far_qk,
        w_value,
        far_value,
        w_out,
        far_out,
        w_in,
        far_in,
        w_back,
        far_back,
        bias_in.reshape(1, -1),
        far_bias.reshape(1, -1),
    )
    here = pl.pallas_call(
        functools.partial(back_kernel, length),
        out_shape=jax.ShapeDtypeStruct((pair_count, width), jnp.bfloat16),
        in_specs=[smem] + [vmem] * 3,
        compiler_params=limit(16),
    )(core, mean, expand(normed, all_in, all_bias, length), all_back)
    return here + swap(here)


def solution(mesh):
    in_specs = (
        P(("groups", "shard"), None, "mp"),
        P(("groups", "shard"), None),
        P(("groups", "shard"), None),
        P(),
        P(None, "mp"),
        P(None, "mp"),
        P("mp"),
        P("mp", None),
        P(),
        P(None, "mp"),
        P("mp"),
        P("mp", None),
    )
    out_specs = P(("groups", "shard"), None)
    return jax.shard_map(
        on_device, mesh=mesh, in_specs=in_specs, out_specs=out_specs, check_vma=False
    )
```

```python
import functools

import jax
import jax.numpy as jnp
from jax import lax
from jax.experimental import pallas as pl
from jax.experimental.pallas import tpu as pltpu
from jax.sharding import PartitionSpec as P

LOG2E = 1.4426950408889634
BLOCK = 8


def norm_rows(values, gain):
    center = values - jnp.mean(values, axis=-1, keepdims=True)
    spread = jnp.mean(center * center, axis=-1, keepdims=True)
    return center * lax.rsqrt(spread + 1e-05) * gain


def dot_nt(a, b):
    return lax.dot_general(a, b, (((1,), (1,)), ((), ())), preferred_element_type=jnp.float32)


def dot(a, b):
    return jnp.dot(a, b, preferred_element_type=jnp.float32)


class Plan:
    def __init__(self, pair_count, owner_count):
        self.owners = owner_count
        self.capacity = max(2, 4 * pair_count // owner_count)
        self.half = owner_count // 2
        split = self.capacity >= 32 and self.half & (self.half - 1) == 0 and self.half > 0
        self.base = self.capacity // 2 if split else self.capacity
        self.extra = self.capacity - self.base
        self.part = self.half * self.extra // 2
        self.near_at = owner_count * self.base
        self.rest_at = self.near_at + self.half * self.extra
        self.slots = self.rest_at + 2 * self.part
        self.row = self.capacity + (self.half if split else 0)


def place_kernel(plan, count, shard_ref, owner_ref, slot_ref, wanted_ref, list_ref):
    total = 2 * count
    owners = plan.owners
    owner = jnp.concatenate([owner_ref[0:1, :], owner_ref[1:2, :]], axis=1)
    slot = jnp.concatenate([slot_ref[0:1, :], slot_ref[1:2, :]], axis=1)

    def place(dim, size):
        return lax.broadcasted_iota(jnp.int32, (size, total), dim)

    def as_bf16(values):
        return values.astype(jnp.float32).astype(jnp.bfloat16)

    row = place(0, owners)
    named = row == owner
    until = as_bf16(jnp.where(place(0, total) <= place(1, total), 1, 0))
    tally = dot(as_bf16(jnp.where(named, 1, 0)), until).astype(jnp.int32)
    rank = jnp.sum(jnp.where(named, tally, 0), axis=0, keepdims=True) - 1
    ranked = as_bf16(jnp.where(place(0, total) == rank, 1, 0))
    wanted = dot_nt(as_bf16(jnp.where(named, slot, 0)), ranked).astype(jnp.int32)
    where = owner * plan.base + rank
    if plan.extra:
        me = shard_ref[0]
        half = plan.half
        over = jnp.maximum(jnp.max(tally, axis=1, keepdims=True) - plan.base, 0)
        far_over = jnp.where(row // half != me // half, over, 0)
        before = jnp.zeros((owners, total), jnp.int32)
        for index in range(owners - 1):
            before = before + jnp.where(row > index, far_over[index : index + 1], 0)
        before = jnp.sum(jnp.where(named, before, 0), axis=0, keepdims=True)
        rest = rank - plan.base
        near = plan.near_at + ((owner % half) ^ (me % half)) * plan.extra + rest
        late = jnp.where(owner // half == me // half, near, plan.rest_at + before + rest)
        where = jnp.where(rest < 0, where, late)
        told = place(1, owners) == plan.capacity + row % half
        wanted = wanted + jnp.sum(jnp.where(told, far_over, 0), axis=0, keepdims=True)
    for index in range(owners):
        wanted_ref[index] = wanted[index : index + 1, : plan.row]
    entry = place(1, 1)
    side = entry // count
    pair = entry % count
    mine = count // 2
    local = pair % mine
    position = pair // mine * count + local // BLOCK * (2 * BLOCK) + side * BLOCK + local % BLOCK
    seated = as_bf16(jnp.where(place(0, total) == position, 1, 0))
    parts = as_bf16(jnp.where(place(0, 8) == 0, where // 16, where % 16))
    listed = dot_nt(parts, seated).astype(jnp.int32)
    list_ref[...] = listed[0:1] * 16 + listed[1:2]


def serve(tokens_ref, incoming_ref, requester, start, served_ref):
    count = served_ref.shape[0]

    def copy(index, carry):
        served_ref[index] = tokens_ref[incoming_ref[requester, 0, start + index]]
        return carry

    lax.fori_loop(0, count, copy, 0, unroll=min(16, count))


def serve_kernel(plan, shard_ref, incoming_ref, tokens_ref, *refs):
    *chunk_refs, served_ref, crowded_ref = refs
    me = shard_ref[0]
    for distance, chunk_ref in enumerate(chunk_refs):
        for part in range(2):
            requester = me ^ (distance + (plan.half if part == 0 else 0))
            home = chunk_ref.at[pl.ds(part * plan.extra, plan.extra)]
            serve(tokens_ref, incoming_ref, requester, plan.base, home)
    for requester in range(plan.owners):
        serve(tokens_ref, incoming_ref, requester, 0, served_ref.at[requester])
    most = 0
    for requester in range(plan.owners):
        total = 0
        for index in range(plan.half):
            total = total + incoming_ref[requester, 0, plan.capacity + index]
        most = jnp.maximum(most, total)
    crowded_ref[0] = jnp.where(most > plan.part, 1, 0)


def serve_all_kernel(plan, incoming_ref, tokens_ref, served_ref):
    for requester in range(plan.owners):
        serve(tokens_ref, incoming_ref, requester, 0, served_ref.at[requester])


def relay_kernel(plan, shard_ref, incoming_ref, *refs):
    chunk_refs = refs[: plan.half]
    first_ref, second_ref = refs[plan.half :]
    client = shard_ref[0] ^ plan.half
    for distance, chunk_ref in enumerate(chunk_refs):
        owner = (shard_ref[0] % plan.half) ^ distance
        at = 0
        for index in range(plan.half):
            amount = incoming_ref[client, 0, plan.capacity + index]
            at = at + jnp.where(index < owner, amount, 0)
        amount = incoming_ref[client, 0, plan.capacity + owner]
        fit = jnp.clip(plan.part - at, 0, amount)

        def pack(index, carry, chunk_ref=chunk_ref, at=at):
            first_ref[at + index] = chunk_ref[index]
            return carry

        def pack_more(index, carry, chunk_ref=chunk_ref, at=at):
            second_ref[0, at + index - plan.part] = chunk_ref[index]
            return carry

        lax.fori_loop(0, fit, pack, 0)
        lax.fori_loop(fit, amount, pack_more, 0)


def pick_kernel(plan, core_ref, list_ref, *refs):
    source_refs = refs[:-4]
    own_ref, other_ref, held_ref, sems = refs[-4:]
    count = own_ref.shape[0]
    at = 0
    loads = []
    for index, source_ref in enumerate(source_refs):
        size = source_ref.shape[0]
        if 1 <= index <= plan.half:
            size = plan.extra
            source_ref = source_ref.at[pl.ds(plan.extra, plan.extra)]
        loads.append(
            pltpu.make_async_copy(source_ref, held_ref.at[pl.ds(at, size)], sems.at[index])
        )
        at += size
    for load in loads:
        load.start()
    for load in loads:
        load.wait()
    start = core_ref[0] * count

    def pick(index, carry):
        other_ref[index] = held_ref[list_ref[0, count - start + index]]
        own_ref[index] = held_ref[list_ref[0, start + index]]
        return carry

    lax.fori_loop(0, count, pick, 0, unroll=8)


def attention_kernel(
    plan,
    length,
    head_dim,
    core_ref,
    list_ref,
    crowded_ref,
    scale_a_ref,
    scale_b_ref,
    gain_attn_ref,
    gain_mlp_ref,
    *refs,
):
    if plan.extra:
        first_held_ref, far_first_held_ref, second_held_ref, *refs = refs
        *refs, rest_ref, rest_sems = refs
    own_held_ref, far_held_ref, *held_refs = refs[:14]
    normed_ref, mean_ref, in_ref, back_ref, bias_ref = refs[14:19]
    qkv_ref, out_ref, tokens_ref, heads_ref, mixed_ref, hidden_ref, sems, token_sems = refs[19:]
    units = in_ref.shape[1] // 2
    width = out_ref.shape[0]
    wide = width // 2
    homes = [qkv_ref.at[:, pl.ds(k * wide, wide)] for k in range(4)]
    homes += [out_ref.at[pl.ds(k * wide, wide)] for k in range(2)]
    homes += [in_ref.at[:, pl.ds(k * units, units)] for k in range(2)]
    homes += [back_ref.at[pl.ds(k * units, units)] for k in range(2)]
    homes += [bias_ref.at[:, pl.ds(k * units, units)] for k in range(2)]
    loads = [
        pltpu.make_async_copy(held, home, sems.at[k])
        for k, (held, home) in enumerate(zip(held_refs, homes))
    ]
    core = core_ref[0]
    token_loads = [
        pltpu.make_async_copy(own_held_ref, tokens_ref.at[core], token_sems.at[0]),
        pltpu.make_async_copy(far_held_ref, tokens_ref.at[1 - core], token_sems.at[1]),
    ]
    for load in token_loads:
        load.start()
    if plan.extra:
        rest_held_refs = [first_held_ref, far_first_held_ref]
        rest_held_refs += [second_held_ref.at[0], second_held_ref.at[1]]
        rest_loads = [
            pltpu.make_async_copy(
                held, rest_ref.at[side, pl.ds(at * plan.part, plan.part)], rest_sems.at[index]
            )
            for index, (held, side, at) in enumerate(
                zip(rest_held_refs, (core, 1 - core, core, 1 - core), (0, 0, 1, 1))
            )
        ]
        for load in rest_loads[:2]:
            load.start()

        @pl.when(crowded_ref[0] > 0)
        def _():
            for load in rest_loads[2:]:
                load.start()

    for load in loads:
        load.start()
    half = BLOCK * length
    rows = 2 * half
    blocks = tokens_ref.shape[1] // (2 * BLOCK)
    long = 2 * rows
    pair_dim = 2 * head_dim
    scale_refs = (scale_a_ref, scale_b_ref)
    per_core = wide // head_dim
    even = lax.broadcasted_iota(jnp.int32, (half, pair_dim), 1) < head_dim
    same = (
        lax.broadcasted_iota(jnp.int32, (half, half), 0) // length
        == lax.broadcasted_iota(jnp.int32, (half, half), 1) // length
    )

    def span(step, size):
        return pl.ds(pl.multiple_of(step * size, size), size)

    def split(values):
        zero = jnp.zeros_like(values)
        return jnp.concatenate(
            [jnp.where(even, values, zero), jnp.where(even, zero, values)], axis=0
        )

    ones = split(jnp.ones((half, pair_dim), jnp.bfloat16))

    def start_block(step, carry):
        images = pl.ds(step * 2 * BLOCK, 2 * BLOCK)
        tokens = jnp.concatenate(
            [tokens_ref[k, images].reshape(rows, -1).astype(jnp.float32) for k in range(2)], axis=1
        )
        hidden_ref[span(step, rows), :] = tokens
        normed_ref[span(step, rows), :] = norm_rows(tokens, gain_attn_ref[...]).astype(jnp.bfloat16)
        return carry

    def project(step, carry):
        here = span(step // 4, long)
        cut = span(step % 4, 2 * width // 4)
        heads_ref[here, cut] = dot(normed_ref[here, :], qkv_ref[:, cut]).astype(jnp.bfloat16)
        return carry

    def weigh(scores, factor):
        scores = jnp.where(same, scores, -1e30)
        top = jnp.max(scores, axis=1, keepdims=True)
        return jnp.exp2((scores - top) * factor).astype(jnp.bfloat16)

    def mix(query, key, value, factors):
        scores = dot_nt(query, split(key))
        weights = [weigh(scores[:, k * half : (k + 1) * half], factors[k]) for k in range(2)]
        mixed = dot(jnp.concatenate(weights, axis=1), jnp.concatenate([split(value), ones], axis=1))
        total = mixed[:, pair_dim:]
        inverse = pl.reciprocal(total, approx=True)
        inverse = inverse * (2.0 - total * inverse)
        return (mixed[:, :pair_dim] * inverse).astype(jnp.bfloat16)

    def attend(step, carry):
        for index in range(width // pair_dim):
            factors = [scale_refs[k // per_core][k % per_core] for k in (2 * index, 2 * index + 1)]
            factors = [factor * (LOG2E / head_dim**0.5) for factor in factors]
            cut = slice(index * pair_dim, (index + 1) * pair_dim)
            beyond = slice(width + cut.start, width + cut.stop)
            sides = [span(2 * step + k, half) for k in range(2)]
            query = [heads_ref[side, cut] for side in sides]
            value = [heads_ref[side, beyond] for side in sides]
            for k in range(2):
                mixed_ref[sides[k], cut] = mix(query[k], query[1 - k], value[1 - k], factors)
        return carry

    def join(step, carry):
        here = span(step // 2, long)
        cut = span(step % 2, width // 2)
        hidden_ref[here, cut] += dot(mixed_ref[here, :], out_ref[:, cut])
        return carry

    def middle_block(step, carry):
        here = span(step, rows)
        hidden = hidden_ref[here, :]
        mean_ref[span(step, BLOCK), :] = jnp.sum(
            hidden.reshape(2, BLOCK, length, -1), axis=(0, 2)
        )
        normed_ref[here, :] = norm_rows(hidden, gain_mlp_ref[...]).astype(jnp.bfloat16)
        return carry

    for load in token_loads:
        load.wait()
    if plan.extra:
        for load in rest_loads[:2]:
            load.wait()

        @pl.when(crowded_ref[0] > 0)
        def _():
            for load in rest_loads[2:]:
                load.wait()

        def put(index, carry):
            where = list_ref[0, core * tokens_ref.shape[1] + index] - plan.rest_at

            @pl.when(where >= 0)
            def _():
                for side in range(2):
                    tokens_ref[side, index] = rest_ref[side, where]

            return carry

        lax.fori_loop(0, tokens_ref.shape[1], put, 0, unroll=4)
    lax.fori_loop(0, blocks, start_block, 0)
    for load in loads[:4]:
        load.wait()
    lax.fori_loop(0, blocks // 2 * 4, project, 0)
    lax.fori_loop(0, blocks, attend, 0)
    for load in loads[4:]:
        load.wait()
    lax.fori_loop(0, blocks // 2 * 2, join, 0)
    lax.fori_loop(0, blocks, middle_block, 0)


def back_kernel(length, core_ref, mean_ref, pooled_ref, back_ref, result_ref):
    count = mean_ref.shape[0]
    pooled = pooled_ref[...] * (0.5 / length)
    coarse = pooled.astype(jnp.bfloat16)
    fine = (pooled - coarse.astype(jnp.float32)).astype(jnp.bfloat16)
    back = dot(jnp.concatenate([coarse, fine], axis=0), back_ref[...])
    mean = mean_ref[...] * (0.5 / length)
    result = (mean + back[:count] + back[count:]).astype(jnp.bfloat16)
    start = pl.multiple_of(core_ref[0] * count, count)
    result_ref[pl.ds(start, count), :] = result
    result_ref[pl.ds(pl.multiple_of(count - start, count), count), :] = jnp.zeros_like(result)


def expand(normed, w_in, bias, length):
    inner = dot(normed, w_in) + bias
    inner = jax.nn.gelu(inner, approximate=True).astype(jnp.bfloat16).astype(jnp.float32)
    inner = inner.reshape(-1, 2, BLOCK, length, inner.shape[-1])
    return jnp.sum(inner, axis=(1, 3)).reshape(-1, inner.shape[-1])


def on_device(
    image_tokens,
    pair_owner,
    pair_slot,
    gain_attn,
    w_qk,
    w_value,
    logit_scale,
    w_out,
    gain_mlp,
    w_in,
    bias_in,
    w_back,
):
    owner_count = lax.axis_size("shard")
    core = lax.axis_index("mp").reshape(1)
    shard = lax.axis_index("shard").reshape(1)
    pair_count = pair_owner.shape[0]
    _, length, features = image_tokens.shape
    width = 2 * features
    head_dim = w_qk.shape[1] // logit_scale.shape[0]
    mine = pair_count // 2
    units = 2 * w_in.shape[1]
    plan = Plan(pair_count, owner_count)

    def swap(values):
        return lax.ppermute(values, "mp", [(0, 1), (1, 0)])

    def across(values, distance):
        return lax.ppermute(values, "shard", [(k, k ^ distance) for k in range(owner_count)])

    def images(*counts):
        return jax.ShapeDtypeStruct((*counts, length, features), jnp.bfloat16)

    smem = pl.BlockSpec(memory_space=pltpu.SMEM)
    vmem = pl.BlockSpec(memory_space=pltpu.VMEM)
    hbm = pl.BlockSpec(memory_space=pl.ANY)

    def limit(mebibytes):
        return pltpu.CompilerParams(vmem_limit_bytes=mebibytes * 2**20)

    wanted, order = pl.pallas_call(
        functools.partial(place_kernel, plan, pair_count),
        out_shape=(
            jax.ShapeDtypeStruct((owner_count, 1, plan.row), jnp.int32),
            jax.ShapeDtypeStruct((1, 2 * pair_count), jnp.int32),
        ),
        in_specs=[smem, vmem, vmem],
    )(shard, pair_owner.T, pair_slot.T)
    incoming = lax.all_to_all(wanted, "shard", split_axis=0, concat_axis=0, tiled=True)
    if not plan.extra:
        served = pl.pallas_call(
            functools.partial(serve_all_kernel, plan),
            out_shape=images(owner_count, plan.base),
            in_specs=[smem, vmem],
        )(incoming, image_tokens)
        returned = lax.all_to_all(served, "shard", split_axis=0, concat_axis=0, tiled=True)
        sources = [returned.reshape(-1, length, features)]
    else:
        *chunks, served, crowded = pl.pallas_call(
            functools.partial(serve_kernel, plan),
            out_shape=[images(2 * plan.extra)] * plan.half
            + [images(owner_count, plan.base), jax.ShapeDtypeStruct((1,), jnp.int32)],
            in_specs=[smem, smem, vmem],
            out_specs=[vmem] * (plan.half + 1) + [smem],
        )(shard, incoming, image_tokens)
        passed = [across(chunks[k], k) for k in reversed(range(1, plan.half))]
        chunks = [chunks[0], *reversed(passed)]
        returned = lax.all_to_all(served, "shard", split_axis=0, concat_axis=0, tiled=True)
        returned = returned.reshape(-1, length, features)
        first, second = pl.pallas_call(
            functools.partial(relay_kernel, plan),
            out_shape=[images(plan.part), images(2, plan.part)],
            in_specs=[smem, smem] + [vmem] * plan.half,
            cost_estimate=pl.CostEstimate(
                flops=2 * 10**11, bytes_accessed=2**20, transcendentals=0
            ),
        )(shard, incoming, *chunks)
        first = across(first, plan.half)
        sources = [returned, *chunks]
    weights = (w_qk, w_value, w_out, w_in, w_back, bias_in, logit_scale)
    if plan.extra:
        chunks, weights = lax.optimization_barrier((chunks, weights))
    swapped = [swap(w) for w in weights]
    own, other = pl.pallas_call(
        functools.partial(pick_kernel, plan),
        out_shape=[images(pair_count)] * 2,
        in_specs=[smem, smem] + [hbm] * len(sources),
        scratch_shapes=[
            pltpu.VMEM((plan.slots, length, features), jnp.bfloat16),
            pltpu.SemaphoreType.DMA((len(sources),)),
        ],
        compiler_params=limit(16),
    )(core, order, *sources)
    far = swap(other)
    rest = []
    if plan.extra:
        first, second, swapped = lax.optimization_barrier((first, second, swapped))
        far_first = swap(first)

        def fetch_second(parts):
            part = across(parts[0], plan.half)
            return jnp.stack([part, swap(part)])

        second = lax.cond(crowded[0] > 0, fetch_second, lambda parts: parts, second)
        rest = [first, far_first, second]
    else:
        crowded = jnp.zeros((1,), jnp.int32)
    far_qk, far_value, far_out, far_in, far_back, far_bias, far_scale = swapped
    token_count = pair_count * length
    units = 2 * w_in.shape[1]
    normed, mean, all_in, all_back, all_bias = pl.pallas_call(
        functools.partial(attention_kernel, plan, length, head_dim),
        out_shape=(
            jax.ShapeDtypeStruct((token_count, width), jnp.bfloat16),
            jax.ShapeDtypeStruct((mine, width), jnp.float32),
            jax.ShapeDtypeStruct((width, units), jnp.bfloat16),
            jax.ShapeDtypeStruct((units, width), jnp.bfloat16),
            jax.ShapeDtypeStruct((1, units), jnp.float32),
        ),
        in_specs=[smem] * 5 + [vmem] * 2 + [hbm] * len(rest) + [vmem] * 2 + [hbm] * 12,
        scratch_shapes=[
            pltpu.VMEM((width, 2 * width), jnp.bfloat16),
            pltpu.VMEM((width, width), jnp.bfloat16),
            pltpu.VMEM((2, pair_count, length, features), jnp.bfloat16),
            pltpu.VMEM((token_count, 2 * width), jnp.bfloat16),
            pltpu.VMEM((token_count, width), jnp.bfloat16),
            pltpu.VMEM((token_count, width), jnp.float32),
            pltpu.SemaphoreType.DMA((12,)),
            pltpu.SemaphoreType.DMA((2,)),
        ]
        + (
            [
                pltpu.VMEM((2, 2 * plan.part, length, features), jnp.bfloat16),
                pltpu.SemaphoreType.DMA((4,)),
            ]
            if rest
            else []
        ),
        compiler_params=limit(32),
        cost_estimate=pl.CostEstimate(
            flops=6 * token_count * width * width,
            bytes_accessed=4 * 2**20,
            transcendentals=token_count * 1024,
        ),
    )(
        core,
        order,
        crowded,
        logit_scale,
        far_scale,
        gain_attn.reshape(1, -1),
        gain_mlp.reshape(1, -1),
        *rest,
        own,
        far,
        w_qk,
        far_qk,
        w_value,
        far_value,
        w_out,
        far_out,
        w_in,
        far_in,
        w_back,
        far_back,
        bias_in.reshape(1, -1),
        far_bias.reshape(1, -1),
    )
    here = pl.pallas_call(
        functools.partial(back_kernel, length),
        out_shape=jax.ShapeDtypeStruct((pair_count, width), jnp.bfloat16),
        in_specs=[smem] + [vmem] * 3,
        compiler_params=limit(16),
    )(core, mean, expand(normed, all_in, all_bias, length), all_back)
    return here + swap(here)


def solution(mesh):
    in_specs = (
        P(("groups", "shard"), None, "mp"),
        P(("groups", "shard"), None),
        P(("groups", "shard"), None),
        P(),
        P(None, "mp"),
        P(None, "mp"),
        P("mp"),
        P("mp", None),
        P(),
        P(None, "mp"),
        P("mp"),
        P("mp", None),
    )
    out_specs = P(("groups", "shard"), None)
    return jax.shard_map(
        on_device, mesh=mesh, in_specs=in_specs, out_specs=out_specs, check_vma=False
    )
```

```python
import functools

import jax
import jax.numpy as jnp
from jax import lax
from jax.experimental import pallas as pl
from jax.experimental.pallas import tpu as pltpu
from jax.sharding import PartitionSpec as P

LOG2E = 1.4426950408889634
BLOCK = 8


def norm_rows(values, gain):
    center = values - jnp.mean(values, axis=-1, keepdims=True)
    spread = jnp.mean(center * center, axis=-1, keepdims=True)
    return center * lax.rsqrt(spread + 1e-05) * gain


def dot_nt(a, b):
    return lax.dot_general(a, b, (((1,), (1,)), ((), ())), preferred_element_type=jnp.float32)


def dot(a, b):
    return jnp.dot(a, b, preferred_element_type=jnp.float32)


class Plan:
    def __init__(self, pair_count, owner_count):
        self.owners = owner_count
        self.capacity = max(2, 4 * pair_count // owner_count)
        self.half = owner_count // 2
        split = self.capacity >= 32 and self.half & (self.half - 1) == 0 and self.half > 0
        self.base = self.capacity // 2 if split else self.capacity
        self.extra = self.capacity - self.base
        self.part = self.half * self.extra // 2
        self.near_at = owner_count * self.base
        self.rest_at = self.near_at + self.half * self.extra
        self.slots = self.rest_at + 2 * self.part
        self.row = self.capacity + (self.half if split else 0)


def place_kernel(plan, count, shard_ref, owner_ref, slot_ref, wanted_ref, list_ref):
    total = 2 * count
    owners = plan.owners
    owner = jnp.concatenate([owner_ref[0:1, :], owner_ref[1:2, :]], axis=1)
    slot = jnp.concatenate([slot_ref[0:1, :], slot_ref[1:2, :]], axis=1)

    def place(dim, size):
        return lax.broadcasted_iota(jnp.int32, (size, total), dim)

    def as_bf16(values):
        return values.astype(jnp.float32).astype(jnp.bfloat16)

    row = place(0, owners)
    named = row == owner
    until = as_bf16(jnp.where(place(0, total) <= place(1, total), 1, 0))
    tally = dot(as_bf16(jnp.where(named, 1, 0)), until).astype(jnp.int32)
    rank = jnp.sum(jnp.where(named, tally, 0), axis=0, keepdims=True) - 1
    ranked = as_bf16(jnp.where(place(0, total) == rank, 1, 0))
    wanted = dot_nt(as_bf16(jnp.where(named, slot, 0)), ranked).astype(jnp.int32)
    where = owner * plan.base + rank
    if plan.extra:
        me = shard_ref[0]
        half = plan.half
        over = jnp.maximum(jnp.max(tally, axis=1, keepdims=True) - plan.base, 0)
        far_over = jnp.where(row // half != me // half, over, 0)
        before = jnp.zeros((owners, total), jnp.int32)
        for index in range(owners - 1):
            before = before + jnp.where(row > index, far_over[index : index + 1], 0)
        before = jnp.sum(jnp.where(named, before, 0), axis=0, keepdims=True)
        rest = rank - plan.base
        near = plan.near_at + ((owner % half) ^ (me % half)) * plan.extra + rest
        late = jnp.where(owner // half == me // half, near, plan.rest_at + before + rest)
        where = jnp.where(rest < 0, where, late)
        told = place(1, owners) == plan.capacity + row % half
        wanted = wanted + jnp.sum(jnp.where(told, far_over, 0), axis=0, keepdims=True)
    for index in range(owners):
        wanted_ref[index] = wanted[index : index + 1, : plan.row]
    entry = place(1, 1)
    side = entry // count
    pair = entry % count
    mine = count // 2
    local = pair % mine
    position = pair // mine * count + local // BLOCK * (2 * BLOCK) + side * BLOCK + local % BLOCK
    seated = as_bf16(jnp.where(place(0, total) == position, 1, 0))
    parts = as_bf16(jnp.where(place(0, 8) == 0, where // 16, where % 16))
    listed = dot_nt(parts, seated).astype(jnp.int32)
    list_ref[...] = listed[0:1] * 16 + listed[1:2]


def serve(tokens_ref, incoming_ref, requester, start, served_ref):
    count = served_ref.shape[0]

    def copy(index, carry):
        served_ref[index] = tokens_ref[incoming_ref[requester, 0, start + index]]
        return carry

    lax.fori_loop(0, count, copy, 0, unroll=min(16, count))


def serve_kernel(plan, shard_ref, incoming_ref, tokens_ref, *refs):
    *chunk_refs, served_ref, crowded_ref = refs
    me = shard_ref[0]
    for distance, chunk_ref in enumerate(chunk_refs):
        for part in range(2):
            requester = me ^ (distance + (plan.half if part == 0 else 0))
            home = chunk_ref.at[pl.ds(part * plan.extra, plan.extra)]
            serve(tokens_ref, incoming_ref, requester, plan.base, home)
    for requester in range(plan.owners):
        serve(tokens_ref, incoming_ref, requester, 0, served_ref.at[requester])
    most = 0
    for requester in range(plan.owners):
        total = 0
        for index in range(plan.half):
            total = total + incoming_ref[requester, 0, plan.capacity + index]
        most = jnp.maximum(most, total)
    crowded_ref[0] = jnp.where(most > plan.part, 1, 0)


def serve_all_kernel(plan, incoming_ref, tokens_ref, served_ref):
    for requester in range(plan.owners):
        serve(tokens_ref, incoming_ref, requester, 0, served_ref.at[requester])


def relay_kernel(plan, shard_ref, incoming_ref, *refs):
    chunk_refs = refs[: plan.half]
    first_ref, second_ref = refs[plan.half :]
    client = shard_ref[0] ^ plan.half
    for distance, chunk_ref in enumerate(chunk_refs):
        owner = (shard_ref[0] % plan.half) ^ distance
        at = 0
        for index in range(plan.half):
            amount = incoming_ref[client, 0, plan.capacity + index]
            at = at + jnp.where(index < owner, amount, 0)
        amount = incoming_ref[client, 0, plan.capacity + owner]
        fit = jnp.clip(plan.part - at, 0, amount)

        def pack(index, carry, chunk_ref=chunk_ref, at=at):
            first_ref[at + index] = chunk_ref[index]
            return carry

        def pack_more(index, carry, chunk_ref=chunk_ref, at=at):
            second_ref[0, at + index - plan.part] = chunk_ref[index]
            return carry

        lax.fori_loop(0, fit, pack, 0)
        lax.fori_loop(fit, amount, pack_more, 0)


def pick_kernel(plan, core_ref, list_ref, *refs):
    source_refs = refs[:-4]
    own_ref, other_ref, held_ref, sems = refs[-4:]
    count = own_ref.shape[0]
    at = 0
    loads = []
    for index, source_ref in enumerate(source_refs):
        size = source_ref.shape[0]
        if 1 <= index <= plan.half:
            size = plan.extra
            source_ref = source_ref.at[pl.ds(plan.extra, plan.extra)]
        loads.append(
            pltpu.make_async_copy(source_ref, held_ref.at[pl.ds(at, size)], sems.at[index])
        )
        at += size
    for load in loads:
        load.start()
    for load in loads:
        load.wait()
    start = core_ref[0] * count

    def pick(index, carry):
        other_ref[index] = held_ref[list_ref[0, count - start + index]]
        own_ref[index] = held_ref[list_ref[0, start + index]]
        return carry

    lax.fori_loop(0, count, pick, 0, unroll=8)


def attention_kernel(
    plan,
    length,
    head_dim,
    core_ref,
    list_ref,
    crowded_ref,
    scale_a_ref,
    scale_b_ref,
    gain_attn_ref,
    gain_mlp_ref,
    *refs,
):
    if plan.extra:
        first_held_ref, far_first_held_ref, second_held_ref, *refs = refs
        *refs, rest_ref, rest_sems = refs
    own_held_ref, far_held_ref, *held_refs = refs[:14]
    normed_ref, mean_ref, in_ref, back_ref, bias_ref = refs[14:19]
    qkv_ref, out_ref, tokens_ref, heads_ref, mixed_ref, hidden_ref, sems, token_sems = refs[19:]
    units = in_ref.shape[1] // 2
    width = out_ref.shape[0]
    wide = width // 2
    homes = [qkv_ref.at[:, pl.ds(k * wide, wide)] for k in range(4)]
    homes += [out_ref.at[pl.ds(k * wide, wide)] for k in range(2)]
    homes += [in_ref.at[:, pl.ds(k * units, units)] for k in range(2)]
    homes += [back_ref.at[pl.ds(k * units, units)] for k in range(2)]
    homes += [bias_ref.at[:, pl.ds(k * units, units)] for k in range(2)]
    loads = [
        pltpu.make_async_copy(held, home, sems.at[k])
        for k, (held, home) in enumerate(zip(held_refs, homes))
    ]
    core = core_ref[0]
    token_loads = [
        pltpu.make_async_copy(own_held_ref, tokens_ref.at[core], token_sems.at[0]),
        pltpu.make_async_copy(far_held_ref, tokens_ref.at[1 - core], token_sems.at[1]),
    ]
    for load in token_loads:
        load.start()
    if plan.extra:
        rest_held_refs = [first_held_ref, far_first_held_ref]
        rest_held_refs += [second_held_ref.at[0], second_held_ref.at[1]]
        rest_loads = [
            pltpu.make_async_copy(
                held, rest_ref.at[side, pl.ds(at * plan.part, plan.part)], rest_sems.at[index]
            )
            for index, (held, side, at) in enumerate(
                zip(rest_held_refs, (core, 1 - core, core, 1 - core), (0, 0, 1, 1))
            )
        ]
        for load in rest_loads[:2]:
            load.start()

        @pl.when(crowded_ref[0] > 0)
        def _():
            for load in rest_loads[2:]:
                load.start()

    for load in loads:
        load.start()
    half = BLOCK * length
    rows = 2 * half
    blocks = tokens_ref.shape[1] // (2 * BLOCK)
    pair_dim = 2 * head_dim
    scale_refs = (scale_a_ref, scale_b_ref)
    per_core = wide // head_dim
    even = lax.broadcasted_iota(jnp.int32, (half, pair_dim), 1) < head_dim
    same = (
        lax.broadcasted_iota(jnp.int32, (half, half), 0) // length
        == lax.broadcasted_iota(jnp.int32, (half, half), 1) // length
    )

    def span(step, size):
        return pl.ds(step * size, size)

    def split(values):
        zero = jnp.zeros_like(values)
        return jnp.concatenate(
            [jnp.where(even, values, zero), jnp.where(even, zero, values)], axis=0
        )

    ones = split(jnp.ones((half, pair_dim), jnp.bfloat16))

    def begin(step):
        images = pl.ds(step * 2 * BLOCK, 2 * BLOCK)
        tokens = jnp.concatenate(
            [tokens_ref[k, images].reshape(rows, -1).astype(jnp.float32) for k in range(2)], axis=1
        )
        hidden_ref[span(step, rows), :] = tokens
        normed_ref[span(step, rows), :] = norm_rows(tokens, gain_attn_ref[...]).astype(jnp.bfloat16)

    def project(step):
        here = span(step, rows)
        for index in range(4):
            cut = span(index, wide)
            heads_ref[here, cut] = dot(normed_ref[here, :], qkv_ref[:, cut]).astype(jnp.bfloat16)

    def weigh(scores, factor):
        scores = jnp.where(same, scores, -1e30)
        top = jnp.max(scores, axis=1, keepdims=True)
        return jnp.exp2((scores - top) * factor).astype(jnp.bfloat16)

    def mix(query, key, value, factors):
        scores = dot_nt(query, split(key))
        weights = [weigh(scores[:, k * half : (k + 1) * half], factors[k]) for k in range(2)]
        mixed = dot(jnp.concatenate(weights, axis=1), jnp.concatenate([split(value), ones], axis=1))
        total = mixed[:, pair_dim:]
        inverse = pl.reciprocal(total, approx=True)
        inverse = inverse * (2.0 - total * inverse)
        return (mixed[:, :pair_dim] * inverse).astype(jnp.bfloat16)

    def attend(step):
        for index in range(width // pair_dim):
            factors = [scale_refs[k // per_core][k % per_core] for k in (2 * index, 2 * index + 1)]
            factors = [factor * (LOG2E / head_dim**0.5) for factor in factors]
            cut = slice(index * pair_dim, (index + 1) * pair_dim)
            beyond = slice(width + cut.start, width + cut.stop)
            sides = [span(2 * step + k, half) for k in range(2)]
            query = [heads_ref[side, cut] for side in sides]
            value = [heads_ref[side, beyond] for side in sides]
            for k in range(2):
                mixed_ref[sides[k], cut] = mix(query[k], query[1 - k], value[1 - k], factors)

    def join(step):
        here = span(step, rows)
        for index in range(2):
            cut = span(index, wide)
            hidden_ref[here, cut] += dot(mixed_ref[here, :], out_ref[:, cut])

    def middle(step):
        here = span(step, rows)
        hidden = hidden_ref[here, :]
        mean_ref[span(step, BLOCK), :] = jnp.sum(
            hidden.reshape(2, BLOCK, length, -1), axis=(0, 2)
        )
        normed_ref[here, :] = norm_rows(hidden, gain_mlp_ref[...]).astype(jnp.bfloat16)

    for load in token_loads:
        load.wait()
    if plan.extra:
        for load in rest_loads[:2]:
            load.wait()

        @pl.when(crowded_ref[0] > 0)
        def _():
            for load in rest_loads[2:]:
                load.wait()

        def put(index, carry):
            where = list_ref[0, core * tokens_ref.shape[1] + index] - plan.rest_at

            @pl.when(where >= 0)
            def _():
                for side in range(2):
                    tokens_ref[side, index] = rest_ref[side, where]

            return carry

        lax.fori_loop(0, tokens_ref.shape[1], put, 0, unroll=4)
    stages = (begin, project, attend, join, middle)
    for turn in range(blocks + len(stages) - 1):
        if turn == 1:
            for load in loads[:4]:
                load.wait()
        if turn == 3:
            for load in loads[4:]:
                load.wait()
        for index, stage in enumerate(stages):
            if 0 <= turn - index < blocks:
                stage(turn - index)


def back_kernel(length, core_ref, mean_ref, pooled_ref, back_ref, result_ref):
    count = mean_ref.shape[0]
    pooled = pooled_ref[...] * (0.5 / length)
    coarse = pooled.astype(jnp.bfloat16)
    fine = (pooled - coarse.astype(jnp.float32)).astype(jnp.bfloat16)
    back = dot(jnp.concatenate([coarse, fine], axis=0), back_ref[...])
    mean = mean_ref[...] * (0.5 / length)
    result = (mean + back[:count] + back[count:]).astype(jnp.bfloat16)
    start = pl.multiple_of(core_ref[0] * count, count)
    result_ref[pl.ds(start, count), :] = result
    result_ref[pl.ds(pl.multiple_of(count - start, count), count), :] = jnp.zeros_like(result)


def expand(normed, w_in, bias, length):
    inner = dot(normed, w_in) + bias
    inner = jax.nn.gelu(inner, approximate=True).astype(jnp.bfloat16).astype(jnp.float32)
    inner = inner.reshape(-1, 2, BLOCK, length, inner.shape[-1])
    return jnp.sum(inner, axis=(1, 3)).reshape(-1, inner.shape[-1])


def on_device(
    image_tokens,
    pair_owner,
    pair_slot,
    gain_attn,
    w_qk,
    w_value,
    logit_scale,
    w_out,
    gain_mlp,
    w_in,
    bias_in,
    w_back,
):
    owner_count = lax.axis_size("shard")
    core = lax.axis_index("mp").reshape(1)
    shard = lax.axis_index("shard").reshape(1)
    pair_count = pair_owner.shape[0]
    _, length, features = image_tokens.shape
    width = 2 * features
    head_dim = w_qk.shape[1] // logit_scale.shape[0]
    mine = pair_count // 2
    units = 2 * w_in.shape[1]
    plan = Plan(pair_count, owner_count)

    def swap(values):
        return lax.ppermute(values, "mp", [(0, 1), (1, 0)])

    def across(values, distance):
        return lax.ppermute(values, "shard", [(k, k ^ distance) for k in range(owner_count)])

    def images(*counts):
        return jax.ShapeDtypeStruct((*counts, length, features), jnp.bfloat16)

    smem = pl.BlockSpec(memory_space=pltpu.SMEM)
    vmem = pl.BlockSpec(memory_space=pltpu.VMEM)
    hbm = pl.BlockSpec(memory_space=pl.ANY)

    def limit(mebibytes):
        return pltpu.CompilerParams(vmem_limit_bytes=mebibytes * 2**20)

    wanted, order = pl.pallas_call(
        functools.partial(place_kernel, plan, pair_count),
        out_shape=(
            jax.ShapeDtypeStruct((owner_count, 1, plan.row), jnp.int32),
            jax.ShapeDtypeStruct((1, 2 * pair_count), jnp.int32),
        ),
        in_specs=[smem, vmem, vmem],
    )(shard, pair_owner.T, pair_slot.T)
    incoming = lax.all_to_all(wanted, "shard", split_axis=0, concat_axis=0, tiled=True)
    if not plan.extra:
        served = pl.pallas_call(
            functools.partial(serve_all_kernel, plan),
            out_shape=images(owner_count, plan.base),
            in_specs=[smem, vmem],
        )(incoming, image_tokens)
        returned = lax.all_to_all(served, "shard", split_axis=0, concat_axis=0, tiled=True)
        sources = [returned.reshape(-1, length, features)]
    else:
        *chunks, served, crowded = pl.pallas_call(
            functools.partial(serve_kernel, plan),
            out_shape=[images(2 * plan.extra)] * plan.half
            + [images(owner_count, plan.base), jax.ShapeDtypeStruct((1,), jnp.int32)],
            in_specs=[smem, smem, vmem],
            out_specs=[vmem] * (plan.half + 1) + [smem],
        )(shard, incoming, image_tokens)
        passed = [across(chunks[k], k) for k in reversed(range(1, plan.half))]
        chunks = [chunks[0], *reversed(passed)]
        returned = lax.all_to_all(served, "shard", split_axis=0, concat_axis=0, tiled=True)
        returned = returned.reshape(-1, length, features)
        first, second = pl.pallas_call(
            functools.partial(relay_kernel, plan),
            out_shape=[images(plan.part), images(2, plan.part)],
            in_specs=[smem, smem] + [vmem] * plan.half,
            compiler_params=limit(16),
            cost_estimate=pl.CostEstimate(
                flops=2 * 10**11, bytes_accessed=2**20, transcendentals=0
            ),
        )(shard, incoming, *chunks)
        first = across(first, plan.half)
        sources = [returned, *chunks]
    weights = (w_qk, w_value, w_out, w_in, w_back, bias_in, logit_scale)
    if plan.extra:
        chunks, weights = lax.optimization_barrier((chunks, weights))
    swapped = [swap(w) for w in weights]
    own, other = pl.pallas_call(
        functools.partial(pick_kernel, plan),
        out_shape=[images(pair_count)] * 2,
        in_specs=[smem, smem] + [hbm] * len(sources),
        scratch_shapes=[
            pltpu.VMEM((plan.slots, length, features), jnp.bfloat16),
            pltpu.SemaphoreType.DMA((len(sources),)),
        ],
        compiler_params=limit(16),
    )(core, order, *sources)
    far = swap(other)
    rest = []
    if plan.extra:
        first, second, swapped = lax.optimization_barrier((first, second, swapped))
        far_first = swap(first)

        def fetch_second(parts):
            part = across(parts[0], plan.half)
            return jnp.stack([part, swap(part)])

        second = lax.cond(crowded[0] > 0, fetch_second, lambda parts: parts, second)
        rest = [first, far_first, second]
    else:
        crowded = jnp.zeros((1,), jnp.int32)
    far_qk, far_value, far_out, far_in, far_back, far_bias, far_scale = swapped
    token_count = pair_count * length
    units = 2 * w_in.shape[1]
    normed, mean, all_in, all_back, all_bias = pl.pallas_call(
        functools.partial(attention_kernel, plan, length, head_dim),
        out_shape=(
            jax.ShapeDtypeStruct((token_count, width), jnp.bfloat16),
            jax.ShapeDtypeStruct((mine, width), jnp.float32),
            jax.ShapeDtypeStruct((width, units), jnp.bfloat16),
            jax.ShapeDtypeStruct((units, width), jnp.bfloat16),
            jax.ShapeDtypeStruct((1, units), jnp.float32),
        ),
        in_specs=[smem] * 5 + [vmem] * 2 + [hbm] * len(rest) + [vmem] * 2 + [hbm] * 12,
        scratch_shapes=[
            pltpu.VMEM((width, 2 * width), jnp.bfloat16),
            pltpu.VMEM((width, width), jnp.bfloat16),
            pltpu.VMEM((2, pair_count, length, features), jnp.bfloat16),
            pltpu.VMEM((token_count, 2 * width), jnp.bfloat16),
            pltpu.VMEM((token_count, width), jnp.bfloat16),
            pltpu.VMEM((token_count, width), jnp.float32),
            pltpu.SemaphoreType.DMA((12,)),
            pltpu.SemaphoreType.DMA((2,)),
        ]
        + (
            [
                pltpu.VMEM((2, 2 * plan.part, length, features), jnp.bfloat16),
                pltpu.SemaphoreType.DMA((4,)),
            ]
            if rest
            else []
        ),
        compiler_params=limit(32),
        cost_estimate=pl.CostEstimate(
            flops=6 * token_count * width * width,
            bytes_accessed=4 * 2**20,
            transcendentals=token_count * 1024,
        ),
    )(
        core,
        order,
        crowded,
        logit_scale,
        far_scale,
        gain_attn.reshape(1, -1),
        gain_mlp.reshape(1, -1),
        *rest,
        own,
        far,
        w_qk,
        far_qk,
        w_value,
        far_value,
        w_out,
        far_out,
        w_in,
        far_in,
        w_back,
        far_back,
        bias_in.reshape(1, -1),
        far_bias.reshape(1, -1),
    )
    here = pl.pallas_call(
        functools.partial(back_kernel, length),
        out_shape=jax.ShapeDtypeStruct((pair_count, width), jnp.bfloat16),
        in_specs=[smem] + [vmem] * 3,
        compiler_params=limit(16),
    )(core, mean, expand(normed, all_in, all_bias, length), all_back)
    return here + swap(here)


def solution(mesh):
    in_specs = (
        P(("groups", "shard"), None, "mp"),
        P(("groups", "shard"), None),
        P(("groups", "shard"), None),
        P(),
        P(None, "mp"),
        P(None, "mp"),
        P("mp"),
        P("mp", None),
        P(),
        P(None, "mp"),
        P("mp"),
        P("mp", None),
    )
    out_specs = P(("groups", "shard"), None)
    return jax.shard_map(
        on_device, mesh=mesh, in_specs=in_specs, out_specs=out_specs, check_vma=False
    )
```

```python
import functools

import jax
import jax.numpy as jnp
from jax import lax
from jax.experimental import pallas as pl
from jax.experimental.pallas import tpu as pltpu
from jax.sharding import PartitionSpec as P

LOG2E = 1.4426950408889634
BLOCK = 8


def norm_rows(values, gain):
    center = values - jnp.mean(values, axis=-1, keepdims=True)
    spread = jnp.mean(center * center, axis=-1, keepdims=True)
    return center * lax.rsqrt(spread + 1e-05) * gain


def dot_nt(a, b):
    return lax.dot_general(a, b, (((1,), (1,)), ((), ())), preferred_element_type=jnp.float32)


def dot(a, b):
    return jnp.dot(a, b, preferred_element_type=jnp.float32)


class Plan:
    def __init__(self, pair_count, owner_count):
        self.owners = owner_count
        self.capacity = max(2, 4 * pair_count // owner_count)
        self.half = owner_count // 2
        split = self.capacity >= 32 and self.half & (self.half - 1) == 0 and self.half > 0
        self.base = self.capacity // 2 if split else self.capacity
        self.extra = self.capacity - self.base
        self.part = self.half * self.extra // 2
        self.near_at = owner_count * self.base
        self.rest_at = self.near_at + self.half * self.extra
        self.slots = self.rest_at + 2 * self.part
        self.row = self.capacity + (self.half if split else 0)


def place_kernel(plan, count, shard_ref, owner_ref, slot_ref, wanted_ref, list_ref):
    total = 2 * count
    owners = plan.owners
    owner = jnp.concatenate([owner_ref[0:1, :], owner_ref[1:2, :]], axis=1)
    slot = jnp.concatenate([slot_ref[0:1, :], slot_ref[1:2, :]], axis=1)

    def place(dim, size):
        return lax.broadcasted_iota(jnp.int32, (size, total), dim)

    def as_bf16(values):
        return values.astype(jnp.float32).astype(jnp.bfloat16)

    row = place(0, owners)
    named = row == owner
    until = as_bf16(jnp.where(place(0, total) <= place(1, total), 1, 0))
    tally = dot(as_bf16(jnp.where(named, 1, 0)), until).astype(jnp.int32)
    rank = jnp.sum(jnp.where(named, tally, 0), axis=0, keepdims=True) - 1
    ranked = as_bf16(jnp.where(place(0, total) == rank, 1, 0))
    wanted = dot_nt(as_bf16(jnp.where(named, slot, 0)), ranked).astype(jnp.int32)
    where = owner * plan.base + rank
    if plan.extra:
        me = shard_ref[0]
        half = plan.half
        over = jnp.maximum(jnp.max(tally, axis=1, keepdims=True) - plan.base, 0)
        far_over = jnp.where(row // half != me // half, over, 0)
        before = jnp.zeros((owners, total), jnp.int32)
        for index in range(owners - 1):
            before = before + jnp.where(row > index, far_over[index : index + 1], 0)
        before = jnp.sum(jnp.where(named, before, 0), axis=0, keepdims=True)
        rest = rank - plan.base
        near = plan.near_at + ((owner % half) ^ (me % half)) * plan.extra + rest
        late = jnp.where(owner // half == me // half, near, plan.rest_at + before + rest)
        where = jnp.where(rest < 0, where, late)
        told = place(1, owners) == plan.capacity + row % half
        wanted = wanted + jnp.sum(jnp.where(told, far_over, 0), axis=0, keepdims=True)
    for index in range(owners):
        wanted_ref[index] = wanted[index : index + 1, : plan.row]
    entry = place(1, 1)
    side = entry // count
    pair = entry % count
    mine = count // 2
    local = pair % mine
    position = pair // mine * count + local // BLOCK * (2 * BLOCK) + side * BLOCK + local % BLOCK
    seated = as_bf16(jnp.where(place(0, total) == position, 1, 0))
    parts = as_bf16(jnp.where(place(0, 8) == 0, where // 16, where % 16))
    listed = dot_nt(parts, seated).astype(jnp.int32)
    list_ref[...] = listed[0:1] * 16 + listed[1:2]


def serve(tokens_ref, incoming_ref, requester, start, served_ref):
    count = served_ref.shape[0]

    def copy(index, carry):
        served_ref[index] = tokens_ref[incoming_ref[requester, 0, start + index]]
        return carry

    lax.fori_loop(0, count, copy, 0, unroll=min(16, count))


def serve_kernel(plan, shard_ref, incoming_ref, tokens_ref, *refs):
    *chunk_refs, served_ref, crowded_ref = refs
    me = shard_ref[0]
    for distance, chunk_ref in enumerate(chunk_refs):
        for part in range(2):
            requester = me ^ (distance + (plan.half if part == 0 else 0))
            home = chunk_ref.at[pl.ds(part * plan.extra, plan.extra)]
            serve(tokens_ref, incoming_ref, requester, plan.base, home)
    for requester in range(plan.owners):
        serve(tokens_ref, incoming_ref, requester, 0, served_ref.at[requester])
    most = 0
    for requester in range(plan.owners):
        total = 0
        for index in range(plan.half):
            total = total + incoming_ref[requester, 0, plan.capacity + index]
        most = jnp.maximum(most, total)
    crowded_ref[0] = jnp.where(most > plan.part, 1, 0)


def serve_all_kernel(plan, incoming_ref, tokens_ref, served_ref):
    for requester in range(plan.owners):
        serve(tokens_ref, incoming_ref, requester, 0, served_ref.at[requester])


def relay_kernel(plan, shard_ref, incoming_ref, *refs):
    chunk_refs = refs[: plan.half]
    first_ref, second_ref = refs[plan.half :]
    client = shard_ref[0] ^ plan.half
    for distance, chunk_ref in enumerate(chunk_refs):
        owner = (shard_ref[0] % plan.half) ^ distance
        at = 0
        for index in range(plan.half):
            amount = incoming_ref[client, 0, plan.capacity + index]
            at = at + jnp.where(index < owner, amount, 0)
        amount = incoming_ref[client, 0, plan.capacity + owner]
        fit = jnp.clip(plan.part - at, 0, amount)

        def pack(index, carry, chunk_ref=chunk_ref, at=at):
            first_ref[at + index] = chunk_ref[index]
            return carry

        def pack_more(index, carry, chunk_ref=chunk_ref, at=at):
            second_ref[0, at + index - plan.part] = chunk_ref[index]
            return carry

        lax.fori_loop(0, fit, pack, 0)
        lax.fori_loop(fit, amount, pack_more, 0)


def pick_kernel(plan, core_ref, list_ref, *refs):
    source_refs = refs[:-4]
    own_ref, other_ref, held_ref, sems = refs[-4:]
    count = own_ref.shape[0]
    at = 0
    loads = []
    for index, source_ref in enumerate(source_refs):
        size = source_ref.shape[0]
        if 1 <= index <= plan.half:
            size = plan.extra
            source_ref = source_ref.at[pl.ds(plan.extra, plan.extra)]
        loads.append(
            pltpu.make_async_copy(source_ref, held_ref.at[pl.ds(at, size)], sems.at[index])
        )
        at += size
    for load in loads:
        load.start()
    for load in loads:
        load.wait()
    start = core_ref[0] * count

    def pick(index, carry):
        other_ref[index] = held_ref[list_ref[0, count - start + index]]
        own_ref[index] = held_ref[list_ref[0, start + index]]
        return carry

    lax.fori_loop(0, count, pick, 0, unroll=8)


def compare_kernel(
    plan,
    length,
    head_dim,
    core_ref,
    list_ref,
    crowded_ref,
    scale_a_ref,
    scale_b_ref,
    gain_attn_ref,
    gain_mlp_ref,
    *refs,
):
    if plan.extra:
        first_held_ref, far_first_held_ref, second_held_ref, *refs = refs
        *refs, rest_ref, rest_sems = refs
    own_held_ref, far_held_ref, *held_refs = refs[:14]
    result_ref, normed_ref, mean_ref, pooled_ref, in_ref, back_ref, bias_ref = refs[14:21]
    qkv_ref, out_ref, tokens_ref, heads_ref, mixed_ref, hidden_ref, sems, token_sems = refs[21:]
    units = in_ref.shape[1] // 2
    width = out_ref.shape[0]
    wide = width // 2
    homes = [qkv_ref.at[:, pl.ds(k * wide, wide)] for k in range(4)]
    homes += [out_ref.at[pl.ds(k * wide, wide)] for k in range(2)]
    homes += [in_ref.at[:, pl.ds(k * units, units)] for k in range(2)]
    homes += [bias_ref.at[:, pl.ds(k * units, units)] for k in range(2)]
    homes += [back_ref.at[pl.ds(k * units, units)] for k in range(2)]
    loads = [
        pltpu.make_async_copy(held, home, sems.at[k])
        for k, (held, home) in enumerate(zip(held_refs, homes))
    ]
    core = core_ref[0]
    token_loads = [
        pltpu.make_async_copy(own_held_ref, tokens_ref.at[core], token_sems.at[0]),
        pltpu.make_async_copy(far_held_ref, tokens_ref.at[1 - core], token_sems.at[1]),
    ]
    for load in token_loads:
        load.start()
    if plan.extra:
        rest_held_refs = [first_held_ref, far_first_held_ref]
        rest_held_refs += [second_held_ref.at[0], second_held_ref.at[1]]
        rest_loads = [
            pltpu.make_async_copy(
                held, rest_ref.at[side, pl.ds(at * plan.part, plan.part)], rest_sems.at[index]
            )
            for index, (held, side, at) in enumerate(
                zip(rest_held_refs, (core, 1 - core, core, 1 - core), (0, 0, 1, 1))
            )
        ]
        for load in rest_loads[:2]:
            load.start()

        @pl.when(crowded_ref[0] > 0)
        def _():
            for load in rest_loads[2:]:
                load.start()

    for load in loads:
        load.start()
    half = BLOCK * length
    rows = 2 * half
    blocks = tokens_ref.shape[1] // (2 * BLOCK)
    pair_dim = 2 * head_dim
    scale_refs = (scale_a_ref, scale_b_ref)
    per_core = wide // head_dim
    even = lax.broadcasted_iota(jnp.int32, (half, pair_dim), 1) < head_dim
    same = (
        lax.broadcasted_iota(jnp.int32, (half, half), 0) // length
        == lax.broadcasted_iota(jnp.int32, (half, half), 1) // length
    )

    def span(step, size):
        return pl.ds(step * size, size)

    def split(values):
        zero = jnp.zeros_like(values)
        return jnp.concatenate(
            [jnp.where(even, values, zero), jnp.where(even, zero, values)], axis=0
        )

    ones = split(jnp.ones((half, pair_dim), jnp.bfloat16))

    def begin(step):
        images = pl.ds(step * 2 * BLOCK, 2 * BLOCK)
        tokens = jnp.concatenate(
            [tokens_ref[k, images].reshape(rows, -1).astype(jnp.float32) for k in range(2)], axis=1
        )
        hidden_ref[span(step, rows), :] = tokens
        normed_ref[span(step, rows), :] = norm_rows(tokens, gain_attn_ref[...]).astype(jnp.bfloat16)
        yield

    def project(step):
        here = span(step, rows)
        for index in range(4):
            cut = span(index, wide)
            heads_ref[here, cut] = dot(normed_ref[here, :], qkv_ref[:, cut]).astype(jnp.bfloat16)
            yield

    def weigh(scores, factor):
        scores = jnp.where(same, scores, -1e30)
        top = jnp.max(scores, axis=1, keepdims=True)
        return jnp.exp2((scores - top) * factor).astype(jnp.bfloat16)

    def mix(query, key, value, factors):
        scores = dot_nt(query, split(key))
        weights = [weigh(scores[:, k * half : (k + 1) * half], factors[k]) for k in range(2)]
        mixed = dot(jnp.concatenate(weights, axis=1), jnp.concatenate([split(value), ones], axis=1))
        total = mixed[:, pair_dim:]
        inverse = pl.reciprocal(total, approx=True)
        inverse = inverse * (2.0 - total * inverse)
        return (mixed[:, :pair_dim] * inverse).astype(jnp.bfloat16)

    def attend(step):
        for index in range(width // pair_dim):
            factors = [scale_refs[k // per_core][k % per_core] for k in (2 * index, 2 * index + 1)]
            factors = [factor * (LOG2E / head_dim**0.5) for factor in factors]
            cut = slice(index * pair_dim, (index + 1) * pair_dim)
            beyond = slice(width + cut.start, width + cut.stop)
            sides = [span(2 * step + k, half) for k in range(2)]
            query = [heads_ref[side, cut] for side in sides]
            value = [heads_ref[side, beyond] for side in sides]
            for k in range(2):
                mixed_ref[sides[k], cut] = mix(query[k], query[1 - k], value[1 - k], factors)
                yield

    def join(step):
        here = span(step, rows)
        for index in range(2):
            cut = span(index, wide)
            hidden_ref[here, cut] += dot(mixed_ref[here, :], out_ref[:, cut])
            yield

    def middle(step):
        here = span(step, rows)
        hidden = hidden_ref[here, :]
        mean_ref[span(step, BLOCK), :] = jnp.sum(
            hidden.reshape(2, BLOCK, length, -1), axis=(0, 2)
        )
        normed_ref[here, :] = norm_rows(hidden, gain_mlp_ref[...]).astype(jnp.bfloat16)
        yield

    def expand(step):
        here = span(step, rows)
        for at in range(0, 2 * units, 256):
            cut = pl.ds(at, 256)
            inner = dot(normed_ref[here, :], in_ref[:, cut]) + bias_ref[:, cut]
            bent = jnp.tanh(inner * (0.7978845608028654 + 0.035677408136300125 * (inner * inner)))
            bent = (inner * bent + inner).reshape(2, BLOCK, length, -1)
            pooled_ref[span(step, BLOCK), cut] = jnp.sum(bent, axis=(0, 2))
            yield

    for load in token_loads:
        load.wait()
    if plan.extra:
        for load in rest_loads[:2]:
            load.wait()

        @pl.when(crowded_ref[0] > 0)
        def _():
            for load in rest_loads[2:]:
                load.wait()

        def put(index, carry):
            where = list_ref[0, core * tokens_ref.shape[1] + index] - plan.rest_at

            @pl.when(where >= 0)
            def _():
                for side in range(2):
                    tokens_ref[side, index] = rest_ref[side, where]

            return carry

        lax.fori_loop(0, tokens_ref.shape[1], put, 0, unroll=4)
    stages = (begin, project, attend, join, middle, expand)
    needs = {1: loads[:4], 3: loads[4:6], 5: loads[6:10]}
    for turn in range(blocks + len(stages) - 1):
        for load in needs.get(turn, []):
            load.wait()
        active = [
            stage(turn - index)
            for index, stage in enumerate(stages)
            if 0 <= turn - index < blocks
        ]
        while active:
            active = [steps for steps in active if next(steps, 0) is None]
    for load in loads[10:]:
        load.wait()
    count = mean_ref.shape[0]
    pooled = pooled_ref[...] * (0.25 / length)
    coarse = pooled.astype(jnp.bfloat16)
    fine = (pooled - coarse.astype(jnp.float32)).astype(jnp.bfloat16)
    back = dot(jnp.concatenate([coarse, fine], axis=0), back_ref[...])
    mean = mean_ref[...] * (0.5 / length)
    result = (mean + back[:count] + back[count:]).astype(jnp.bfloat16)
    at = pl.multiple_of(core * count, count)
    result_ref[pl.ds(at, count), :] = result
    result_ref[pl.ds(pl.multiple_of(count - at, count), count), :] = jnp.zeros_like(result)


def on_device(
    image_tokens,
    pair_owner,
    pair_slot,
    gain_attn,
    w_qk,
    w_value,
    logit_scale,
    w_out,
    gain_mlp,
    w_in,
    bias_in,
    w_back,
):
    owner_count = lax.axis_size("shard")
    core = lax.axis_index("mp").reshape(1)
    shard = lax.axis_index("shard").reshape(1)
    pair_count = pair_owner.shape[0]
    _, length, features = image_tokens.shape
    width = 2 * features
    head_dim = w_qk.shape[1] // logit_scale.shape[0]
    mine = pair_count // 2
    units = 2 * w_in.shape[1]
    plan = Plan(pair_count, owner_count)

    def swap(values):
        return lax.ppermute(values, "mp", [(0, 1), (1, 0)])

    def across(values, distance):
        return lax.ppermute(values, "shard", [(k, k ^ distance) for k in range(owner_count)])

    def images(*counts):
        return jax.ShapeDtypeStruct((*counts, length, features), jnp.bfloat16)

    smem = pl.BlockSpec(memory_space=pltpu.SMEM)
    vmem = pl.BlockSpec(memory_space=pltpu.VMEM)
    hbm = pl.BlockSpec(memory_space=pl.ANY)

    def limit(mebibytes):
        return pltpu.CompilerParams(vmem_limit_bytes=mebibytes * 2**20)

    wanted, order = pl.pallas_call(
        functools.partial(place_kernel, plan, pair_count),
        out_shape=(
            jax.ShapeDtypeStruct((owner_count, 1, plan.row), jnp.int32),
            jax.ShapeDtypeStruct((1, 2 * pair_count), jnp.int32),
        ),
        in_specs=[smem, vmem, vmem],
    )(shard, pair_owner.T, pair_slot.T)
    incoming = lax.all_to_all(wanted, "shard", split_axis=0, concat_axis=0, tiled=True)
    if not plan.extra:
        served = pl.pallas_call(
            functools.partial(serve_all_kernel, plan),
            out_shape=images(owner_count, plan.base),
            in_specs=[smem, vmem],
        )(incoming, image_tokens)
        returned = lax.all_to_all(served, "shard", split_axis=0, concat_axis=0, tiled=True)
        sources = [returned.reshape(-1, length, features)]
    else:
        *chunks, served, crowded = pl.pallas_call(
            functools.partial(serve_kernel, plan),
            out_shape=[images(2 * plan.extra)] * plan.half
            + [images(owner_count, plan.base), jax.ShapeDtypeStruct((1,), jnp.int32)],
            in_specs=[smem, smem, vmem],
            out_specs=[vmem] * (plan.half + 1) + [smem],
        )(shard, incoming, image_tokens)
        passed = [across(chunks[k], k) for k in reversed(range(1, plan.half))]
        chunks = [chunks[0], *reversed(passed)]
        returned = lax.all_to_all(served, "shard", split_axis=0, concat_axis=0, tiled=True)
        returned = returned.reshape(-1, length, features)
        first, second = pl.pallas_call(
            functools.partial(relay_kernel, plan),
            out_shape=[images(plan.part), images(2, plan.part)],
            in_specs=[smem, smem] + [vmem] * plan.half,
            compiler_params=limit(16),
            cost_estimate=pl.CostEstimate(
                flops=2 * 10**11, bytes_accessed=2**20, transcendentals=0
            ),
        )(shard, incoming, *chunks)
        first = across(first, plan.half)
        sources = [returned, *chunks]
    weights = (w_qk, w_value, w_out, w_in, w_back, bias_in, logit_scale)
    if plan.extra:
        chunks, weights = lax.optimization_barrier((chunks, weights))
    swapped = [swap(w) for w in weights]
    own, other = pl.pallas_call(
        functools.partial(pick_kernel, plan),
        out_shape=[images(pair_count)] * 2,
        in_specs=[smem, smem] + [hbm] * len(sources),
        scratch_shapes=[
            pltpu.VMEM((plan.slots, length, features), jnp.bfloat16),
            pltpu.SemaphoreType.DMA((len(sources),)),
        ],
        compiler_params=limit(16),
    )(core, order, *sources)
    far = swap(other)
    rest = []
    if plan.extra:
        first, second, swapped = lax.optimization_barrier((first, second, swapped))
        far_first = swap(first)

        def fetch_second(parts):
            part = across(parts[0], plan.half)
            return jnp.stack([part, swap(part)])

        second = lax.cond(crowded[0] > 0, fetch_second, lambda parts: parts, second)
        rest = [first, far_first, second]
    else:
        crowded = jnp.zeros((1,), jnp.int32)
    far_qk, far_value, far_out, far_in, far_back, far_bias, far_scale = swapped
    token_count = pair_count * length
    units = 2 * w_in.shape[1]
    here = pl.pallas_call(
        functools.partial(compare_kernel, plan, length, head_dim),
        out_shape=jax.ShapeDtypeStruct((pair_count, width), jnp.bfloat16),
        in_specs=[smem] * 5 + [vmem] * 2 + [hbm] * len(rest) + [vmem] * 2 + [hbm] * 12,
        scratch_shapes=[
            pltpu.VMEM((token_count, width), jnp.bfloat16),
            pltpu.VMEM((mine, width), jnp.float32),
            pltpu.VMEM((mine, units), jnp.float32),
            pltpu.VMEM((width, units), jnp.bfloat16),
            pltpu.VMEM((units, width), jnp.bfloat16),
            pltpu.VMEM((1, units), jnp.float32),
            pltpu.VMEM((width, 2 * width), jnp.bfloat16),
            pltpu.VMEM((width, width), jnp.bfloat16),
            pltpu.VMEM((2, pair_count, length, features), jnp.bfloat16),
            pltpu.VMEM((token_count, 2 * width), jnp.bfloat16),
            pltpu.VMEM((token_count, width), jnp.bfloat16),
            pltpu.VMEM((token_count, width), jnp.float32),
            pltpu.SemaphoreType.DMA((12,)),
            pltpu.SemaphoreType.DMA((2,)),
        ]
        + (
            [
                pltpu.VMEM((2, 2 * plan.part, length, features), jnp.bfloat16),
                pltpu.SemaphoreType.DMA((4,)),
            ]
            if rest
            else []
        ),
        compiler_params=limit(32),
        cost_estimate=pl.CostEstimate(
            flops=2 * token_count * width * (3 * width + units),
            bytes_accessed=8 * 2**20,
            transcendentals=token_count * units,
        ),
    )(
        core,
        order,
        crowded,
        logit_scale,
        far_scale,
        gain_attn.reshape(1, -1),
        gain_mlp.reshape(1, -1),
        *rest,
        own,
        far,
        w_qk,
        far_qk,
        w_value,
        far_value,
        w_out,
        far_out,
        w_in,
        far_in,
        bias_in.reshape(1, -1),
        far_bias.reshape(1, -1),
        w_back,
        far_back,
    )
    return here + swap(here)


def solution(mesh):
    in_specs = (
        P(("groups", "shard"), None, "mp"),
        P(("groups", "shard"), None),
        P(("groups", "shard"), None),
        P(),
        P(None, "mp"),
        P(None, "mp"),
        P("mp"),
        P("mp", None),
        P(),
        P(None, "mp"),
        P("mp"),
        P("mp", None),
    )
    out_specs = P(("groups", "shard"), None)
    return jax.shard_map(
        on_device, mesh=mesh, in_specs=in_specs, out_specs=out_specs, check_vma=False
    )
```

```python
import functools

import jax
import jax.numpy as jnp
from jax import lax
from jax.experimental import pallas as pl
from jax.experimental.pallas import tpu as pltpu
from jax.sharding import PartitionSpec as P

LOG2E = 1.4426950408889634
BLOCK = 8


def norm_rows(values, gain):
    center = values - jnp.mean(values, axis=-1, keepdims=True)
    spread = jnp.mean(center * center, axis=-1, keepdims=True)
    return center * lax.rsqrt(spread + 1e-05) * gain


def dot_nt(a, b):
    return lax.dot_general(a, b, (((1,), (1,)), ((), ())), preferred_element_type=jnp.float32)


def dot(a, b):
    return jnp.dot(a, b, preferred_element_type=jnp.float32)


class Plan:
    def __init__(self, pair_count, owner_count):
        self.owners = owner_count
        self.capacity = max(2, 4 * pair_count // owner_count)
        self.half = owner_count // 2
        split = self.capacity >= 32 and self.half & (self.half - 1) == 0 and self.half > 0
        self.base = self.capacity // 2 if split else self.capacity
        self.extra = self.capacity - self.base
        self.part = self.half * self.extra // 2
        self.near_at = owner_count * self.base
        self.rest_at = self.near_at + self.half * self.extra
        self.slots = self.rest_at + 2 * self.part
        self.row = self.capacity + (self.half if split else 0)


def place_kernel(plan, count, shard_ref, owner_ref, slot_ref, wanted_ref, list_ref):
    total = 2 * count
    owners = plan.owners
    owner = jnp.concatenate([owner_ref[0:1, :], owner_ref[1:2, :]], axis=1)
    slot = jnp.concatenate([slot_ref[0:1, :], slot_ref[1:2, :]], axis=1)

    def place(dim, size):
        return lax.broadcasted_iota(jnp.int32, (size, total), dim)

    def as_bf16(values):
        return values.astype(jnp.float32).astype(jnp.bfloat16)

    row = place(0, owners)
    named = row == owner
    until = as_bf16(jnp.where(place(0, total) <= place(1, total), 1, 0))
    tally = dot(as_bf16(jnp.where(named, 1, 0)), until).astype(jnp.int32)
    rank = jnp.sum(jnp.where(named, tally, 0), axis=0, keepdims=True) - 1
    ranked = as_bf16(jnp.where(place(0, total) == rank, 1, 0))
    wanted = dot_nt(as_bf16(jnp.where(named, slot, 0)), ranked).astype(jnp.int32)
    where = owner * plan.base + rank
    if plan.extra:
        me = shard_ref[0]
        half = plan.half
        over = jnp.maximum(jnp.max(tally, axis=1, keepdims=True) - plan.base, 0)
        far_over = jnp.where(row // half != me // half, over, 0)
        before = jnp.zeros((owners, total), jnp.int32)
        for index in range(owners - 1):
            before = before + jnp.where(row > index, far_over[index : index + 1], 0)
        before = jnp.sum(jnp.where(named, before, 0), axis=0, keepdims=True)
        rest = rank - plan.base
        near = plan.near_at + ((owner % half) ^ (me % half)) * plan.extra + rest
        late = jnp.where(owner // half == me // half, near, plan.rest_at + before + rest)
        where = jnp.where(rest < 0, where, late)
        told = place(1, owners) == plan.capacity + row % half
        wanted = wanted + jnp.sum(jnp.where(told, far_over, 0), axis=0, keepdims=True)
    for index in range(owners):
        wanted_ref[index] = wanted[index : index + 1, : plan.row]
    entry = place(1, 1)
    side = entry // count
    pair = entry % count
    mine = count // 2
    local = pair % mine
    position = pair // mine * count + local // BLOCK * (2 * BLOCK) + side * BLOCK + local % BLOCK
    seated = as_bf16(jnp.where(place(0, total) == position, 1, 0))
    parts = as_bf16(jnp.where(place(0, 8) == 0, where // 16, where % 16))
    listed = dot_nt(parts, seated).astype(jnp.int32)
    list_ref[...] = listed[0:1] * 16 + listed[1:2]


def serve(tokens_ref, incoming_ref, requester, start, served_ref):
    count = served_ref.shape[0]

    def copy(index, carry):
        served_ref[index] = tokens_ref[incoming_ref[requester, 0, start + index]]
        return carry

    lax.fori_loop(0, count, copy, 0, unroll=min(16, count))


def serve_kernel(plan, shard_ref, incoming_ref, tokens_ref, *refs):
    *chunk_refs, served_ref, crowded_ref = refs
    me = shard_ref[0]
    for distance, chunk_ref in enumerate(chunk_refs):
        for part in range(2):
            requester = me ^ (distance + (plan.half if part == 0 else 0))
            home = chunk_ref.at[pl.ds(part * plan.extra, plan.extra)]
            serve(tokens_ref, incoming_ref, requester, plan.base, home)
    for requester in range(plan.owners):
        serve(tokens_ref, incoming_ref, requester, 0, served_ref.at[requester])
    most = 0
    for requester in range(plan.owners):
        total = 0
        for index in range(plan.half):
            total = total + incoming_ref[requester, 0, plan.capacity + index]
        most = jnp.maximum(most, total)
    crowded_ref[0] = jnp.where(most > plan.part, 1, 0)


def serve_all_kernel(plan, incoming_ref, tokens_ref, served_ref):
    for requester in range(plan.owners):
        serve(tokens_ref, incoming_ref, requester, 0, served_ref.at[requester])


def relay_kernel(plan, shard_ref, incoming_ref, *refs):
    chunk_refs = refs[: plan.half]
    first_ref, second_ref = refs[plan.half :]
    client = shard_ref[0] ^ plan.half
    for distance, chunk_ref in enumerate(chunk_refs):
        owner = (shard_ref[0] % plan.half) ^ distance
        at = 0
        for index in range(plan.half):
            amount = incoming_ref[client, 0, plan.capacity + index]
            at = at + jnp.where(index < owner, amount, 0)
        amount = incoming_ref[client, 0, plan.capacity + owner]
        fit = jnp.clip(plan.part - at, 0, amount)

        def pack(index, carry, chunk_ref=chunk_ref, at=at):
            first_ref[at + index] = chunk_ref[index]
            return carry

        def pack_more(index, carry, chunk_ref=chunk_ref, at=at):
            second_ref[0, at + index - plan.part] = chunk_ref[index]
            return carry

        lax.fori_loop(0, fit, pack, 0)
        lax.fori_loop(fit, amount, pack_more, 0)


def pick_kernel(plan, core_ref, list_ref, *refs):
    source_refs = refs[:-4]
    own_ref, other_ref, held_ref, sems = refs[-4:]
    count = own_ref.shape[0]
    at = 0
    loads = []
    for index, source_ref in enumerate(source_refs):
        size = source_ref.shape[0]
        if 1 <= index <= plan.half:
            size = plan.extra
            source_ref = source_ref.at[pl.ds(plan.extra, plan.extra)]
        loads.append(
            pltpu.make_async_copy(source_ref, held_ref.at[pl.ds(at, size)], sems.at[index])
        )
        at += size
    for load in loads:
        load.start()
    for load in loads:
        load.wait()
    start = core_ref[0] * count

    def pick(index, carry):
        other_ref[index] = held_ref[list_ref[0, count - start + index]]
        own_ref[index] = held_ref[list_ref[0, start + index]]
        return carry

    lax.fori_loop(0, count, pick, 0, unroll=8)


def compare_kernel(
    plan,
    length,
    head_dim,
    core_ref,
    list_ref,
    crowded_ref,
    scale_a_ref,
    scale_b_ref,
    gain_attn_ref,
    gain_mlp_ref,
    *refs,
):
    if plan.extra:
        first_held_ref, far_first_held_ref, second_held_ref, *refs = refs
        *refs, rest_ref, rest_sems = refs
    own_held_ref, far_held_ref, *held_refs = refs[:14]
    result_ref, normed_ref, mean_ref, pooled_ref, in_ref, back_ref, bias_ref = refs[14:21]
    qkv_ref, out_ref, tokens_ref, heads_ref, mixed_ref, hidden_ref, sems, token_sems = refs[21:]
    units = in_ref.shape[1] // 2
    width = out_ref.shape[0]
    wide = width // 2
    homes = [qkv_ref.at[:, pl.ds(k * wide, wide)] for k in range(4)]
    homes += [out_ref.at[pl.ds(k * wide, wide)] for k in range(2)]
    homes += [in_ref.at[:, pl.ds(k * units, units)] for k in range(2)]
    homes += [bias_ref.at[:, pl.ds(k * units, units)] for k in range(2)]
    homes += [back_ref.at[pl.ds(k * units, units)] for k in range(2)]
    loads = [
        pltpu.make_async_copy(held, home, sems.at[k])
        for k, (held, home) in enumerate(zip(held_refs, homes))
    ]
    core = core_ref[0]
    token_loads = [
        pltpu.make_async_copy(own_held_ref, tokens_ref.at[core], token_sems.at[0]),
        pltpu.make_async_copy(far_held_ref, tokens_ref.at[1 - core], token_sems.at[1]),
    ]
    for load in token_loads:
        load.start()
    if plan.extra:
        rest_held_refs = [first_held_ref, far_first_held_ref]
        rest_held_refs += [second_held_ref.at[0], second_held_ref.at[1]]
        rest_loads = [
            pltpu.make_async_copy(
                held, rest_ref.at[side, pl.ds(at * plan.part, plan.part)], rest_sems.at[index]
            )
            for index, (held, side, at) in enumerate(
                zip(rest_held_refs, (core, 1 - core, core, 1 - core), (0, 0, 1, 1))
            )
        ]
        for load in rest_loads[:2]:
            load.start()

        @pl.when(crowded_ref[0] > 0)
        def _():
            for load in rest_loads[2:]:
                load.start()

    for load in loads:
        load.start()
    half = BLOCK * length
    rows = 2 * half
    blocks = tokens_ref.shape[1] // (2 * BLOCK)
    pair_dim = 2 * head_dim
    scale_refs = (scale_a_ref, scale_b_ref)
    per_core = wide // head_dim
    even = lax.broadcasted_iota(jnp.int32, (half, pair_dim), 1) < head_dim
    same = (
        lax.broadcasted_iota(jnp.int32, (half, half), 0) // length
        == lax.broadcasted_iota(jnp.int32, (half, half), 1) // length
    )

    def span(step, size):
        return pl.ds(step * size, size)

    def split(values):
        zero = jnp.zeros_like(values)
        return jnp.concatenate(
            [jnp.where(even, values, zero), jnp.where(even, zero, values)], axis=0
        )

    ones = split(jnp.ones((half, pair_dim), jnp.bfloat16))

    def begin(step):
        images = pl.ds(step * 2 * BLOCK, 2 * BLOCK)
        tokens = jnp.concatenate(
            [tokens_ref[k, images].reshape(rows, -1).astype(jnp.float32) for k in range(2)], axis=1
        )
        hidden_ref[span(step, rows), :] = tokens
        normed_ref[span(step, rows), :] = norm_rows(tokens, gain_attn_ref[...]).astype(jnp.bfloat16)
        yield

    def project(step):
        here = span(step, rows)
        for index in range(4):
            cut = span(index, wide)
            heads_ref[here, cut] = dot(normed_ref[here, :], qkv_ref[:, cut]).astype(jnp.bfloat16)
            yield

    def weigh(scores, factor):
        scores = jnp.where(same, scores, -1e30)
        top = jnp.max(scores, axis=1, keepdims=True)
        return jnp.exp2((scores - top) * factor).astype(jnp.bfloat16)

    def mix(query, key, value, factors):
        scores = dot_nt(query, split(key))
        weights = [weigh(scores[:, k * half : (k + 1) * half], factors[k]) for k in range(2)]
        mixed = dot(jnp.concatenate(weights, axis=1), jnp.concatenate([split(value), ones], axis=1))
        total = mixed[:, pair_dim:]
        inverse = pl.reciprocal(total, approx=True)
        inverse = inverse * (2.0 - total * inverse)
        return (mixed[:, :pair_dim] * inverse).astype(jnp.bfloat16)

    def attend(step):
        for index in range(width // pair_dim):
            factors = [scale_refs[k // per_core][k % per_core] for k in (2 * index, 2 * index + 1)]
            factors = [factor * (LOG2E / head_dim**0.5) for factor in factors]
            cut = slice(index * pair_dim, (index + 1) * pair_dim)
            beyond = slice(width + cut.start, width + cut.stop)
            sides = [span(2 * step + k, half) for k in range(2)]
            query = [heads_ref[side, cut] for side in sides]
            value = [heads_ref[side, beyond] for side in sides]
            for k in range(2):
                mixed_ref[sides[k], cut] = mix(query[k], query[1 - k], value[1 - k], factors)
                yield

    def join(step):
        here = span(step, rows)
        for index in range(2):
            cut = span(index, wide)
            hidden_ref[here, cut] += dot(mixed_ref[here, :], out_ref[:, cut])
            yield

    def middle(step):
        here = span(step, rows)
        hidden = hidden_ref[here, :]
        mean_ref[span(step, BLOCK), :] = jnp.sum(
            hidden.reshape(2, BLOCK, length, -1), axis=(0, 2)
        )
        normed_ref[here, :] = norm_rows(hidden, gain_mlp_ref[...]).astype(jnp.bfloat16)
        yield

    row_pair = lax.broadcasted_iota(jnp.int32, (2 * BLOCK, rows), 1) % half // length
    pool = jnp.where(row_pair == lax.broadcasted_iota(jnp.int32, row_pair.shape, 0), 1.0, 0.0)
    pool = pool.astype(jnp.bfloat16)

    def expand(step):
        here = span(step, rows)
        for at in range(0, 2 * units, 256):
            cut = pl.ds(at, 256)
            inner = dot(normed_ref[here, :], in_ref[:, cut]) + bias_ref[:, cut]
            inner = inner.astype(jnp.bfloat16)
            cubic = inner * inner * jnp.bfloat16(0.0356774081) + jnp.bfloat16(0.7978845608)
            bent = (jnp.tanh(inner * cubic) + jnp.bfloat16(1.0)) * inner
            pooled_ref[span(step, BLOCK), cut] = dot(pool, bent)[:BLOCK]
            yield

    for load in token_loads:
        load.wait()
    if plan.extra:
        for load in rest_loads[:2]:
            load.wait()

        @pl.when(crowded_ref[0] > 0)
        def _():
            for load in rest_loads[2:]:
                load.wait()

        def put(index, carry):
            where = list_ref[0, core * tokens_ref.shape[1] + index] - plan.rest_at

            @pl.when(where >= 0)
            def _():
                for side in range(2):
                    tokens_ref[side, index] = rest_ref[side, where]

            return carry

        lax.fori_loop(0, tokens_ref.shape[1], put, 0, unroll=4)
    stages = (begin, project, attend, join, middle, expand)
    needs = {1: loads[:4], 3: loads[4:6], 5: loads[6:10]}
    for turn in range(blocks + len(stages) - 1):
        for load in needs.get(turn, []):
            load.wait()
        active = [
            stage(turn - index)
            for index, stage in enumerate(stages)
            if 0 <= turn - index < blocks
        ]
        while active:
            active = [steps for steps in active if next(steps, 0) is None]
    for load in loads[10:]:
        load.wait()
    count = mean_ref.shape[0]
    pooled = pooled_ref[...] * (0.25 / length)
    coarse = pooled.astype(jnp.bfloat16)
    fine = (pooled - coarse.astype(jnp.float32)).astype(jnp.bfloat16)
    back = dot(jnp.concatenate([coarse, fine], axis=0), back_ref[...])
    mean = mean_ref[...] * (0.5 / length)
    result = (mean + back[:count] + back[count:]).astype(jnp.bfloat16)
    at = pl.multiple_of(core * count, count)
    result_ref[pl.ds(at, count), :] = result
    result_ref[pl.ds(pl.multiple_of(count - at, count), count), :] = jnp.zeros_like(result)


def on_device(
    image_tokens,
    pair_owner,
    pair_slot,
    gain_attn,
    w_qk,
    w_value,
    logit_scale,
    w_out,
    gain_mlp,
    w_in,
    bias_in,
    w_back,
):
    owner_count = lax.axis_size("shard")
    core = lax.axis_index("mp").reshape(1)
    shard = lax.axis_index("shard").reshape(1)
    pair_count = pair_owner.shape[0]
    _, length, features = image_tokens.shape
    width = 2 * features
    head_dim = w_qk.shape[1] // logit_scale.shape[0]
    mine = pair_count // 2
    units = 2 * w_in.shape[1]
    plan = Plan(pair_count, owner_count)

    def swap(values):
        return lax.ppermute(values, "mp", [(0, 1), (1, 0)])

    def across(values, distance):
        return lax.ppermute(values, "shard", [(k, k ^ distance) for k in range(owner_count)])

    def images(*counts):
        return jax.ShapeDtypeStruct((*counts, length, features), jnp.bfloat16)

    smem = pl.BlockSpec(memory_space=pltpu.SMEM)
    vmem = pl.BlockSpec(memory_space=pltpu.VMEM)
    hbm = pl.BlockSpec(memory_space=pl.ANY)

    def limit(mebibytes):
        return pltpu.CompilerParams(vmem_limit_bytes=mebibytes * 2**20)

    wanted, order = pl.pallas_call(
        functools.partial(place_kernel, plan, pair_count),
        out_shape=(
            jax.ShapeDtypeStruct((owner_count, 1, plan.row), jnp.int32),
            jax.ShapeDtypeStruct((1, 2 * pair_count), jnp.int32),
        ),
        in_specs=[smem, vmem, vmem],
    )(shard, pair_owner.T, pair_slot.T)
    incoming = lax.all_to_all(wanted, "shard", split_axis=0, concat_axis=0, tiled=True)
    if not plan.extra:
        served = pl.pallas_call(
            functools.partial(serve_all_kernel, plan),
            out_shape=images(owner_count, plan.base),
            in_specs=[smem, vmem],
        )(incoming, image_tokens)
        returned = lax.all_to_all(served, "shard", split_axis=0, concat_axis=0, tiled=True)
        sources = [returned.reshape(-1, length, features)]
    else:
        *chunks, served, crowded = pl.pallas_call(
            functools.partial(serve_kernel, plan),
            out_shape=[images(2 * plan.extra)] * plan.half
            + [images(owner_count, plan.base), jax.ShapeDtypeStruct((1,), jnp.int32)],
            in_specs=[smem, smem, vmem],
            out_specs=[vmem] * (plan.half + 1) + [smem],
        )(shard, incoming, image_tokens)
        passed = [across(chunks[k], k) for k in reversed(range(1, plan.half))]
        chunks = [chunks[0], *reversed(passed)]
        returned = lax.all_to_all(served, "shard", split_axis=0, concat_axis=0, tiled=True)
        returned = returned.reshape(-1, length, features)
        first, second = pl.pallas_call(
            functools.partial(relay_kernel, plan),
            out_shape=[images(plan.part), images(2, plan.part)],
            in_specs=[smem, smem] + [vmem] * plan.half,
            compiler_params=limit(16),
            cost_estimate=pl.CostEstimate(
                flops=2 * 10**11, bytes_accessed=2**20, transcendentals=0
            ),
        )(shard, incoming, *chunks)
        first = across(first, plan.half)
        sources = [returned, *chunks]
    weights = (w_qk, w_value, w_out, w_in, w_back, bias_in, logit_scale)
    if plan.extra:
        chunks, weights = lax.optimization_barrier((chunks, weights))
    swapped = [swap(w) for w in weights]
    own, other = pl.pallas_call(
        functools.partial(pick_kernel, plan),
        out_shape=[images(pair_count)] * 2,
        in_specs=[smem, smem] + [hbm] * len(sources),
        scratch_shapes=[
            pltpu.VMEM((plan.slots, length, features), jnp.bfloat16),
            pltpu.SemaphoreType.DMA((len(sources),)),
        ],
        compiler_params=limit(16),
    )(core, order, *sources)
    far = swap(other)
    rest = []
    if plan.extra:
        first, second, swapped = lax.optimization_barrier((first, second, swapped))
        far_first = swap(first)

        def fetch_second(parts):
            part = across(parts[0], plan.half)
            return jnp.stack([part, swap(part)])

        second = lax.cond(crowded[0] > 0, fetch_second, lambda parts: parts, second)
        rest = [first, far_first, second]
    else:
        crowded = jnp.zeros((1,), jnp.int32)
    far_qk, far_value, far_out, far_in, far_back, far_bias, far_scale = swapped
    token_count = pair_count * length
    units = 2 * w_in.shape[1]
    here = pl.pallas_call(
        functools.partial(compare_kernel, plan, length, head_dim),
        out_shape=jax.ShapeDtypeStruct((pair_count, width), jnp.bfloat16),
        in_specs=[smem] * 5 + [vmem] * 2 + [hbm] * len(rest) + [vmem] * 2 + [hbm] * 12,
        scratch_shapes=[
            pltpu.VMEM((token_count, width), jnp.bfloat16),
            pltpu.VMEM((mine, width), jnp.float32),
            pltpu.VMEM((mine, units), jnp.float32),
            pltpu.VMEM((width, units), jnp.bfloat16),
            pltpu.VMEM((units, width), jnp.bfloat16),
            pltpu.VMEM((1, units), jnp.float32),
            pltpu.VMEM((width, 2 * width), jnp.bfloat16),
            pltpu.VMEM((width, width), jnp.bfloat16),
            pltpu.VMEM((2, pair_count, length, features), jnp.bfloat16),
            pltpu.VMEM((token_count, 2 * width), jnp.bfloat16),
            pltpu.VMEM((token_count, width), jnp.bfloat16),
            pltpu.VMEM((token_count, width), jnp.float32),
            pltpu.SemaphoreType.DMA((12,)),
            pltpu.SemaphoreType.DMA((2,)),
        ]
        + (
            [
                pltpu.VMEM((2, 2 * plan.part, length, features), jnp.bfloat16),
                pltpu.SemaphoreType.DMA((4,)),
            ]
            if rest
            else []
        ),
        compiler_params=limit(32),
        cost_estimate=pl.CostEstimate(
            flops=2 * token_count * width * (3 * width + units),
            bytes_accessed=8 * 2**20,
            transcendentals=token_count * units,
        ),
    )(
        core,
        order,
        crowded,
        logit_scale,
        far_scale,
        gain_attn.reshape(1, -1),
        gain_mlp.reshape(1, -1),
        *rest,
        own,
        far,
        w_qk,
        far_qk,
        w_value,
        far_value,
        w_out,
        far_out,
        w_in,
        far_in,
        bias_in.reshape(1, -1),
        far_bias.reshape(1, -1),
        w_back,
        far_back,
    )
    return here + swap(here)


def solution(mesh):
    in_specs = (
        P(("groups", "shard"), None, "mp"),
        P(("groups", "shard"), None),
        P(("groups", "shard"), None),
        P(),
        P(None, "mp"),
        P(None, "mp"),
        P("mp"),
        P("mp", None),
        P(),
        P(None, "mp"),
        P("mp"),
        P("mp", None),
    )
    out_specs = P(("groups", "shard"), None)
    return jax.shard_map(
        on_device, mesh=mesh, in_specs=in_specs, out_specs=out_specs, check_vma=False
    )
```

```python
import functools

import jax
import jax.numpy as jnp
from jax import lax
from jax.experimental import pallas as pl
from jax.experimental.pallas import tpu as pltpu
from jax.sharding import PartitionSpec as P

LOG2E = 1.4426950408889634
BLOCK = 8


def norm_rows(values, gain):
    center = values - jnp.mean(values, axis=-1, keepdims=True)
    spread = jnp.mean(center * center, axis=-1, keepdims=True)
    return center * lax.rsqrt(spread + 1e-05) * gain


def dot_nt(a, b):
    return lax.dot_general(a, b, (((1,), (1,)), ((), ())), preferred_element_type=jnp.float32)


def dot(a, b):
    return jnp.dot(a, b, preferred_element_type=jnp.float32)


class Plan:
    def __init__(self, pair_count, owner_count):
        self.owners = owner_count
        self.capacity = max(2, 4 * pair_count // owner_count)
        self.half = owner_count // 2
        split = self.capacity >= 32 and self.half & (self.half - 1) == 0 and self.half > 0
        self.base = self.capacity // 2 if split else self.capacity
        self.extra = self.capacity - self.base
        self.part = self.half * self.extra // 2
        self.near_at = owner_count * self.base
        self.rest_at = self.near_at + self.half * self.extra
        self.slots = self.rest_at + 2 * self.part
        self.row = self.capacity + (self.half if split else 0)


def place_kernel(plan, count, shard_ref, owner_ref, slot_ref, wanted_ref, list_ref):
    total = 2 * count
    owners = plan.owners
    owner = jnp.concatenate([owner_ref[0:1, :], owner_ref[1:2, :]], axis=1)
    slot = jnp.concatenate([slot_ref[0:1, :], slot_ref[1:2, :]], axis=1)

    def place(dim, size):
        return lax.broadcasted_iota(jnp.int32, (size, total), dim)

    def as_bf16(values):
        return values.astype(jnp.float32).astype(jnp.bfloat16)

    row = place(0, owners)
    named = row == owner
    until = as_bf16(jnp.where(place(0, total) <= place(1, total), 1, 0))
    tally = dot(as_bf16(jnp.where(named, 1, 0)), until).astype(jnp.int32)
    rank = jnp.sum(jnp.where(named, tally, 0), axis=0, keepdims=True) - 1
    ranked = as_bf16(jnp.where(place(0, total) == rank, 1, 0))
    wanted = dot_nt(as_bf16(jnp.where(named, slot, 0)), ranked).astype(jnp.int32)
    where = owner * plan.base + rank
    if plan.extra:
        me = shard_ref[0]
        half = plan.half
        over = jnp.maximum(jnp.max(tally, axis=1, keepdims=True) - plan.base, 0)
        far_over = jnp.where(row // half != me // half, over, 0)
        before = jnp.zeros((owners, total), jnp.int32)
        for index in range(owners - 1):
            before = before + jnp.where(row > index, far_over[index : index + 1], 0)
        before = jnp.sum(jnp.where(named, before, 0), axis=0, keepdims=True)
        rest = rank - plan.base
        near = plan.near_at + ((owner % half) ^ (me % half)) * plan.extra + rest
        late = jnp.where(owner // half == me // half, near, plan.rest_at + before + rest)
        where = jnp.where(rest < 0, where, late)
        told = place(1, owners) == plan.capacity + row % half
        wanted = wanted + jnp.sum(jnp.where(told, far_over, 0), axis=0, keepdims=True)
    for index in range(owners):
        wanted_ref[index] = wanted[index : index + 1, : plan.row]
    entry = place(1, 1)
    side = entry // count
    pair = entry % count
    mine = count // 2
    local = pair % mine
    position = pair // mine * count + local // BLOCK * (2 * BLOCK) + side * BLOCK + local % BLOCK
    seated = as_bf16(jnp.where(place(0, total) == position, 1, 0))
    parts = as_bf16(jnp.where(place(0, 8) == 0, where // 16, where % 16))
    listed = dot_nt(parts, seated).astype(jnp.int32)
    list_ref[...] = listed[0:1] * 16 + listed[1:2]


def serve(tokens_ref, incoming_ref, requester, start, served_ref):
    count = served_ref.shape[0]

    def copy(index, carry):
        served_ref[index] = tokens_ref[incoming_ref[requester, 0, start + index]]
        return carry

    lax.fori_loop(0, count, copy, 0, unroll=min(16, count))


def serve_kernel(plan, shard_ref, incoming_ref, tokens_ref, *refs):
    *chunk_refs, served_ref, crowded_ref = refs
    me = shard_ref[0]
    for distance, chunk_ref in enumerate(chunk_refs):
        for part in range(2):
            requester = me ^ (distance + (plan.half if part == 0 else 0))
            home = chunk_ref.at[pl.ds(part * plan.extra, plan.extra)]
            serve(tokens_ref, incoming_ref, requester, plan.base, home)
    for requester in range(plan.owners):
        serve(tokens_ref, incoming_ref, requester, 0, served_ref.at[requester])
    most = 0
    for requester in range(plan.owners):
        total = 0
        for index in range(plan.half):
            total = total + incoming_ref[requester, 0, plan.capacity + index]
        most = jnp.maximum(most, total)
    crowded_ref[0] = jnp.where(most > plan.part, 1, 0)


def serve_all_kernel(plan, incoming_ref, tokens_ref, served_ref):
    for requester in range(plan.owners):
        serve(tokens_ref, incoming_ref, requester, 0, served_ref.at[requester])


def relay_kernel(plan, shard_ref, incoming_ref, *refs):
    chunk_refs = refs[: plan.half]
    first_ref, second_ref = refs[plan.half :]
    client = shard_ref[0] ^ plan.half
    for distance, chunk_ref in enumerate(chunk_refs):
        owner = (shard_ref[0] % plan.half) ^ distance
        at = 0
        for index in range(plan.half):
            amount = incoming_ref[client, 0, plan.capacity + index]
            at = at + jnp.where(index < owner, amount, 0)
        amount = incoming_ref[client, 0, plan.capacity + owner]
        fit = jnp.clip(plan.part - at, 0, amount)

        def pack(index, carry, chunk_ref=chunk_ref, at=at):
            first_ref[at + index] = chunk_ref[index]
            return carry

        def pack_more(index, carry, chunk_ref=chunk_ref, at=at):
            second_ref[0, at + index - plan.part] = chunk_ref[index]
            return carry

        lax.fori_loop(0, fit, pack, 0)
        lax.fori_loop(fit, amount, pack_more, 0)


def pick_kernel(plan, core_ref, list_ref, *refs):
    source_refs = refs[:-4]
    own_ref, other_ref, held_ref, sems = refs[-4:]
    count = own_ref.shape[0]
    at = 0
    loads = []
    for index, source_ref in enumerate(source_refs):
        size = source_ref.shape[0]
        if 1 <= index <= plan.half:
            size = plan.extra
            source_ref = source_ref.at[pl.ds(plan.extra, plan.extra)]
        loads.append(
            pltpu.make_async_copy(source_ref, held_ref.at[pl.ds(at, size)], sems.at[index])
        )
        at += size
    for load in loads:
        load.start()
    for load in loads:
        load.wait()
    start = core_ref[0] * count

    def pick(index, carry):
        other_ref[index] = held_ref[list_ref[0, count - start + index]]
        own_ref[index] = held_ref[list_ref[0, start + index]]
        return carry

    lax.fori_loop(0, count, pick, 0, unroll=8)


def compare_kernel(
    plan,
    length,
    head_dim,
    core_ref,
    list_ref,
    crowded_ref,
    scale_a_ref,
    scale_b_ref,
    gain_attn_ref,
    gain_mlp_ref,
    *refs,
):
    if plan.extra:
        first_held_ref, far_first_held_ref, second_held_ref, *refs = refs
        *refs, rest_ref, rest_sems = refs
    own_held_ref, far_held_ref, *held_refs = refs[:14]
    result_ref, normed_ref, mean_ref, pooled_ref, in_ref, back_ref, bias_ref = refs[14:21]
    qkv_ref, out_ref, tokens_ref, heads_ref, mixed_ref, hidden_ref, sems, token_sems = refs[21:]
    units = in_ref.shape[1] // 2
    width = out_ref.shape[0]
    wide = width // 2
    homes = [qkv_ref.at[:, pl.ds(k * wide, wide)] for k in range(4)]
    homes += [out_ref.at[pl.ds(k * wide, wide)] for k in range(2)]
    homes += [in_ref.at[:, pl.ds(k * units, units)] for k in range(2)]
    homes += [bias_ref.at[:, pl.ds(k * units, units)] for k in range(2)]
    homes += [back_ref.at[pl.ds(k * units, units)] for k in range(2)]
    loads = [
        pltpu.make_async_copy(held, home, sems.at[k])
        for k, (held, home) in enumerate(zip(held_refs, homes))
    ]
    core = core_ref[0]
    token_loads = [
        pltpu.make_async_copy(own_held_ref, tokens_ref.at[core], token_sems.at[0]),
        pltpu.make_async_copy(far_held_ref, tokens_ref.at[1 - core], token_sems.at[1]),
    ]
    for load in token_loads:
        load.start()
    if plan.extra:
        rest_held_refs = [first_held_ref, far_first_held_ref]
        rest_held_refs += [second_held_ref.at[0], second_held_ref.at[1]]
        rest_loads = [
            pltpu.make_async_copy(
                held, rest_ref.at[side, pl.ds(at * plan.part, plan.part)], rest_sems.at[index]
            )
            for index, (held, side, at) in enumerate(
                zip(rest_held_refs, (core, 1 - core, core, 1 - core), (0, 0, 1, 1))
            )
        ]
        for load in rest_loads[:2]:
            load.start()

        @pl.when(crowded_ref[0] > 0)
        def _():
            for load in rest_loads[2:]:
                load.start()

    for load in loads:
        load.start()
    half = BLOCK * length
    rows = 2 * half
    blocks = tokens_ref.shape[1] // (2 * BLOCK)
    pair_dim = 2 * head_dim
    scale_refs = (scale_a_ref, scale_b_ref)
    per_core = wide // head_dim
    even = lax.broadcasted_iota(jnp.int32, (half, pair_dim), 1) < head_dim
    same = (
        lax.broadcasted_iota(jnp.int32, (half, half), 0) // length
        == lax.broadcasted_iota(jnp.int32, (half, half), 1) // length
    )

    def span(step, size):
        return pl.ds(step * size, size)

    def split(values):
        zero = jnp.zeros_like(values)
        return jnp.concatenate(
            [jnp.where(even, values, zero), jnp.where(even, zero, values)], axis=0
        )

    def begin(step):
        images = pl.ds(step * 2 * BLOCK, 2 * BLOCK)
        tokens = jnp.concatenate(
            [tokens_ref[k, images].reshape(rows, -1).astype(jnp.float32) for k in range(2)], axis=1
        )
        hidden_ref[span(step, rows), :] = tokens
        normed_ref[span(step, rows), :] = norm_rows(tokens, gain_attn_ref[...]).astype(jnp.bfloat16)
        yield

    def project(step):
        here = span(step, rows)
        for index in range(4):
            cut = span(index, wide)
            heads_ref[here, cut] = dot(normed_ref[here, :], qkv_ref[:, cut]).astype(jnp.bfloat16)
            yield

    def weigh(scores, factor):
        scores = jnp.where(same, scores, -1e30)
        top = jnp.max(scores, axis=1, keepdims=True)
        weights = jnp.exp2((scores - top) * factor)
        return (weights * (1.0 / jnp.sum(weights, axis=1, keepdims=True))).astype(jnp.bfloat16)

    def mix(query, key, value, factors):
        scores = dot_nt(query, split(key))
        weights = [weigh(scores[:, k * half : (k + 1) * half], factors[k]) for k in range(2)]
        mixed = dot(jnp.concatenate(weights, axis=1), split(value))
        return mixed.astype(jnp.bfloat16)

    def attend(step):
        for index in range(width // pair_dim):
            factors = [scale_refs[k // per_core][k % per_core] for k in (2 * index, 2 * index + 1)]
            factors = [factor * (LOG2E / head_dim**0.5) for factor in factors]
            cut = slice(index * pair_dim, (index + 1) * pair_dim)
            beyond = slice(width + cut.start, width + cut.stop)
            sides = [span(2 * step + k, half) for k in range(2)]
            query = [heads_ref[side, cut] for side in sides]
            value = [heads_ref[side, beyond] for side in sides]
            for k in range(2):
                mixed_ref[sides[k], cut] = mix(query[k], query[1 - k], value[1 - k], factors)
                yield

    def join(step):
        here = span(step, rows)
        for index in range(2):
            cut = span(index, wide)
            hidden_ref[here, cut] += dot(mixed_ref[here, :], out_ref[:, cut])
            yield

    def middle(step):
        here = span(step, rows)
        hidden = hidden_ref[here, :]
        mean_ref[span(step, BLOCK), :] = jnp.sum(
            hidden.reshape(2, BLOCK, length, -1), axis=(0, 2)
        )
        normed_ref[here, :] = norm_rows(hidden, gain_mlp_ref[...]).astype(jnp.bfloat16)
        yield

    def expand(step):
        here = span(step, rows)
        for at in range(0, 2 * units, 256):
            cut = pl.ds(at, 256)
            inner = dot(normed_ref[here, :], in_ref[:, cut]) + bias_ref[:, cut]
            bent = jnp.tanh(inner * (0.7978845608028654 + 0.035677408136300125 * (inner * inner)))
            bent = (inner * bent + inner).reshape(2, BLOCK, length, -1)
            pooled_ref[span(step, BLOCK), cut] = jnp.sum(bent, axis=(0, 2))
            yield

    for load in token_loads:
        load.wait()
    if plan.extra:
        for load in rest_loads[:2]:
            load.wait()

        @pl.when(crowded_ref[0] > 0)
        def _():
            for load in rest_loads[2:]:
                load.wait()

        def put(index, carry):
            where = list_ref[0, core * tokens_ref.shape[1] + index] - plan.rest_at

            @pl.when(where >= 0)
            def _():
                for side in range(2):
                    tokens_ref[side, index] = rest_ref[side, where]

            return carry

        lax.fori_loop(0, tokens_ref.shape[1], put, 0, unroll=4)
    stages = (begin, project, attend, join, middle, expand)
    needs = {1: loads[:4], 3: loads[4:6], 5: loads[6:10]}
    for turn in range(blocks + len(stages) - 1):
        for load in needs.get(turn, []):
            load.wait()
        active = [
            stage(turn - index)
            for index, stage in enumerate(stages)
            if 0 <= turn - index < blocks
        ]
        while active:
            active = [steps for steps in active if next(steps, 0) is None]
    for load in loads[10:]:
        load.wait()
    count = mean_ref.shape[0]
    pooled = pooled_ref[...] * (0.25 / length)
    coarse = pooled.astype(jnp.bfloat16)
    fine = (pooled - coarse.astype(jnp.float32)).astype(jnp.bfloat16)
    back = dot(jnp.concatenate([coarse, fine], axis=0), back_ref[...])
    mean = mean_ref[...] * (0.5 / length)
    result = (mean + back[:count] + back[count:]).astype(jnp.bfloat16)
    at = pl.multiple_of(core * count, count)
    result_ref[pl.ds(at, count), :] = result
    result_ref[pl.ds(pl.multiple_of(count - at, count), count), :] = jnp.zeros_like(result)


def on_device(
    image_tokens,
    pair_owner,
    pair_slot,
    gain_attn,
    w_qk,
    w_value,
    logit_scale,
    w_out,
    gain_mlp,
    w_in,
    bias_in,
    w_back,
):
    owner_count = lax.axis_size("shard")
    core = lax.axis_index("mp").reshape(1)
    shard = lax.axis_index("shard").reshape(1)
    pair_count = pair_owner.shape[0]
    _, length, features = image_tokens.shape
    width = 2 * features
    head_dim = w_qk.shape[1] // logit_scale.shape[0]
    mine = pair_count // 2
    units = 2 * w_in.shape[1]
    plan = Plan(pair_count, owner_count)

    def swap(values):
        return lax.ppermute(values, "mp", [(0, 1), (1, 0)])

    def across(values, distance):
        return lax.ppermute(values, "shard", [(k, k ^ distance) for k in range(owner_count)])

    def images(*counts):
        return jax.ShapeDtypeStruct((*counts, length, features), jnp.bfloat16)

    smem = pl.BlockSpec(memory_space=pltpu.SMEM)
    vmem = pl.BlockSpec(memory_space=pltpu.VMEM)
    hbm = pl.BlockSpec(memory_space=pl.ANY)

    def limit(mebibytes):
        return pltpu.CompilerParams(vmem_limit_bytes=mebibytes * 2**20)

    wanted, order = pl.pallas_call(
        functools.partial(place_kernel, plan, pair_count),
        out_shape=(
            jax.ShapeDtypeStruct((owner_count, 1, plan.row), jnp.int32),
            jax.ShapeDtypeStruct((1, 2 * pair_count), jnp.int32),
        ),
        in_specs=[smem, vmem, vmem],
    )(shard, pair_owner.T, pair_slot.T)
    incoming = lax.all_to_all(wanted, "shard", split_axis=0, concat_axis=0, tiled=True)
    if not plan.extra:
        served = pl.pallas_call(
            functools.partial(serve_all_kernel, plan),
            out_shape=images(owner_count, plan.base),
            in_specs=[smem, vmem],
        )(incoming, image_tokens)
        returned = lax.all_to_all(served, "shard", split_axis=0, concat_axis=0, tiled=True)
        sources = [returned.reshape(-1, length, features)]
    else:
        *chunks, served, crowded = pl.pallas_call(
            functools.partial(serve_kernel, plan),
            out_shape=[images(2 * plan.extra)] * plan.half
            + [images(owner_count, plan.base), jax.ShapeDtypeStruct((1,), jnp.int32)],
            in_specs=[smem, smem, vmem],
            out_specs=[vmem] * (plan.half + 1) + [smem],
        )(shard, incoming, image_tokens)
        passed = [across(chunks[k], k) for k in reversed(range(1, plan.half))]
        chunks = [chunks[0], *reversed(passed)]
        returned = lax.all_to_all(served, "shard", split_axis=0, concat_axis=0, tiled=True)
        returned = returned.reshape(-1, length, features)
        first, second = pl.pallas_call(
            functools.partial(relay_kernel, plan),
            out_shape=[images(plan.part), images(2, plan.part)],
            in_specs=[smem, smem] + [vmem] * plan.half,
            compiler_params=limit(16),
            cost_estimate=pl.CostEstimate(
                flops=2 * 10**11, bytes_accessed=2**20, transcendentals=0
            ),
        )(shard, incoming, *chunks)
        first = across(first, plan.half)
        sources = [returned, *chunks]
    weights = (w_qk, w_value, w_out, w_in, w_back, bias_in, logit_scale)
    if plan.extra:
        chunks, weights = lax.optimization_barrier((chunks, weights))
    swapped = [swap(w) for w in weights]
    own, other = pl.pallas_call(
        functools.partial(pick_kernel, plan),
        out_shape=[images(pair_count)] * 2,
        in_specs=[smem, smem] + [hbm] * len(sources),
        scratch_shapes=[
            pltpu.VMEM((plan.slots, length, features), jnp.bfloat16),
            pltpu.SemaphoreType.DMA((len(sources),)),
        ],
        compiler_params=limit(16),
    )(core, order, *sources)
    far = swap(other)
    rest = []
    if plan.extra:
        first, second, swapped = lax.optimization_barrier((first, second, swapped))
        far_first = swap(first)

        def fetch_second(parts):
            part = across(parts[0], plan.half)
            return jnp.stack([part, swap(part)])

        second = lax.cond(crowded[0] > 0, fetch_second, lambda parts: parts, second)
        rest = [first, far_first, second]
    else:
        crowded = jnp.zeros((1,), jnp.int32)
    far_qk, far_value, far_out, far_in, far_back, far_bias, far_scale = swapped
    token_count = pair_count * length
    units = 2 * w_in.shape[1]
    here = pl.pallas_call(
        functools.partial(compare_kernel, plan, length, head_dim),
        out_shape=jax.ShapeDtypeStruct((pair_count, width), jnp.bfloat16),
        in_specs=[smem] * 5 + [vmem] * 2 + [hbm] * len(rest) + [vmem] * 2 + [hbm] * 12,
        scratch_shapes=[
            pltpu.VMEM((token_count, width), jnp.bfloat16),
            pltpu.VMEM((mine, width), jnp.float32),
            pltpu.VMEM((mine, units), jnp.float32),
            pltpu.VMEM((width, units), jnp.bfloat16),
            pltpu.VMEM((units, width), jnp.bfloat16),
            pltpu.VMEM((1, units), jnp.float32),
            pltpu.VMEM((width, 2 * width), jnp.bfloat16),
            pltpu.VMEM((width, width), jnp.bfloat16),
            pltpu.VMEM((2, pair_count, length, features), jnp.bfloat16),
            pltpu.VMEM((token_count, 2 * width), jnp.bfloat16),
            pltpu.VMEM((token_count, width), jnp.bfloat16),
            pltpu.VMEM((token_count, width), jnp.float32),
            pltpu.SemaphoreType.DMA((12,)),
            pltpu.SemaphoreType.DMA((2,)),
        ]
        + (
            [
                pltpu.VMEM((2, 2 * plan.part, length, features), jnp.bfloat16),
                pltpu.SemaphoreType.DMA((4,)),
            ]
            if rest
            else []
        ),
        compiler_params=limit(32),
        cost_estimate=pl.CostEstimate(
            flops=2 * token_count * width * (3 * width + units),
            bytes_accessed=8 * 2**20,
            transcendentals=token_count * units,
        ),
    )(
        core,
        order,
        crowded,
        logit_scale,
        far_scale,
        gain_attn.reshape(1, -1),
        gain_mlp.reshape(1, -1),
        *rest,
        own,
        far,
        w_qk,
        far_qk,
        w_value,
        far_value,
        w_out,
        far_out,
        w_in,
        far_in,
        bias_in.reshape(1, -1),
        far_bias.reshape(1, -1),
        w_back,
        far_back,
    )
    return here + swap(here)


def solution(mesh):
    in_specs = (
        P(("groups", "shard"), None, "mp"),
        P(("groups", "shard"), None),
        P(("groups", "shard"), None),
        P(),
        P(None, "mp"),
        P(None, "mp"),
        P("mp"),
        P("mp", None),
        P(),
        P(None, "mp"),
        P("mp"),
        P("mp", None),
    )
    out_specs = P(("groups", "shard"), None)
    return jax.shard_map(
        on_device, mesh=mesh, in_specs=in_specs, out_specs=out_specs, check_vma=False
    )
```
